256 devices in a mesh: section: 2 (over z_hi), grp: 8 (over z_lo, core), tp: 16 (over x, y).
Axes of the slice: x: 4, y: 4, z: 8 (z_hi: 2, z_lo: 4; z = z_hi * 4 + z_lo), core: 2. Of those that a mesh axis runs over, the one named last changes fastest.
Arguments:
- heads_in: bfloat16 [2, 3072, 8192], P('section', 'grp', 'tp'), may hold values from -6 to 6
- weights: bfloat16 [2, 8192, 8192], P('section', 'tp'), may hold values from -0.0625 to 0.0625
- residual: bfloat16 [3072, 8192], P(('grp', 'tp')), may hold values from -50 to 50
- norm_gain: float32 [8192], replicated, may hold values from 0.1 to 1.9
Outputs:
- heads_out: bfloat16 [2, 3072, 8192], P('section', 'grp', 'tp')
- weight_grad: float32 [2, 8192, 8192], P('section', 'grp', 'tp')
- boundary_grad: bfloat16 [3072, 8192], P(('grp', 'tp'))
- gain_grad: float32 [8192], replicated
The draws below stay inside these ranges and needn't reach their ends.
All inputs are finite; a program needn't handle non-finite values.
Results may differ from the reference program's by a relative error of at most 0.027.
Values may be sent and summed in bfloat16 or wider, within the bound.
A program may use at most 128 MiB of HBM per device.

```python
import math
import jax
import jax.numpy as jnp
from jax import lax

D = 8192
HW = 8192
TOKENS = 3072
N_GRP = 8
N_TP = 16


def draw_residual(key, part):
    key = jax.random.fold_in(key, 7)
    row_key, col_key, base_key = jax.random.split(key, 3)
    col_scale = jnp.exp(jax.random.uniform(col_key, (1, D), jnp.float32, math.log(0.4), math.log(2.5)))
    row_scale = jnp.exp(jax.random.uniform(row_key, (TOKENS, 1), jnp.float32, math.log(0.4), math.log(2.5)))
    base_draw = jnp.clip(jax.random.normal(base_key, (TOKENS, D), jnp.float32), -4.0, 4.0)
    values = base_draw * row_scale * col_scale
    return values.astype(jnp.bfloat16)


def steps_of(own_key, dims, shards, least, high):
    loudness = 1.0
    for axis_at, parts in shards:
        draws = jax.random.uniform(jax.random.fold_in(jax.random.fold_in(own_key, 6), axis_at), (parts,), jnp.float32, least / len(shards), high / len(shards))
        loudness = loudness * jnp.repeat(jnp.exp(draws), dims[axis_at] // parts).reshape((-1,) + (1,) * (len(dims) - 1 - axis_at))
    return loudness


def normal_values(stream_key, shape, scale, reach, cuts=(), dtype=jnp.bfloat16):
    result = jax.random.normal(stream_key, shape, jnp.float32) * scale
    if len(cuts) > 0:
        result = steps_of(stream_key, shape, cuts, -0.22, 0.18) * result
    return jnp.clip(result, min=-reach, max=reach).astype(dtype)


def setup_inputs(seed: int = 0) -> dict:
    key_list = jax.random.split(jax.random.key(seed), 5)
    return {
        "heads_in": normal_values(key_list[0], (2, TOKENS, HW), 1.0, 6.0, ((0, 2), (1, 8), (2, 16))),
        "weights": normal_values(key_list[1], (2, HW, D), HW ** -0.5, 0.0625, ((0, 2), (1, 16))),
        "residual": draw_residual(jax.random.fold_in(key_list[4], 71), 0),
        "norm_gain": jnp.clip(1.0 + 0.18 * jax.random.normal(key_list[3], (D,), jnp.float32), 0.1, 1.9),
    }


EPSILON = 1e-05

def head_block_sum(heads_side, weight_side):
    head_blocks = jnp.transpose(heads_side.reshape(heads_side.shape[0], N_TP, -1), (1, 0, 2))
    weight_blocks = weight_side.reshape(N_TP, -1, weight_side.shape[1])

    def add_block(running, operands):
        partial_value = jnp.dot(operands[0], operands[1], preferred_element_type=jnp.float32)
        partial_value = lax.optimization_barrier(partial_value.astype(jnp.bfloat16)).astype(jnp.float32)
        return (running + partial_value, None)
    start_value = jnp.zeros((heads_side.shape[0], weight_side.shape[1]), jnp.float32)
    running, _ = lax.scan(add_block, start_value, (head_blocks, weight_blocks))
    return running

def token_block_grad(value_side, heads_side, grad_scale):
    value_blocks = value_side.reshape(N_GRP, -1, value_side.shape[1])
    head_blocks = heads_side.reshape(N_GRP, -1, heads_side.shape[1])

    def add_block(running, operands):
        partial_value = jnp.dot(operands[0].T, operands[1], preferred_element_type=jnp.float32) * grad_scale
        partial_value = lax.optimization_barrier(partial_value.astype(jnp.bfloat16)).astype(jnp.float32)
        return (running + partial_value, None)
    start_value = jnp.zeros((value_side.shape[1], heads_side.shape[1]), jnp.float32)
    running, _ = lax.scan(add_block, start_value, (value_blocks, head_blocks))
    return running

def norm_both(boundary, d_normed, norm_gain):
    wide = boundary.astype(jnp.float32)
    row_mean = lax.optimization_barrier(jnp.mean(wide, axis=1, keepdims=True))
    centred = wide - row_mean
    inv_scale = lax.rsqrt(lax.optimization_barrier(jnp.mean(centred * centred, axis=1, keepdims=True)) + EPSILON)
    unit_rows = centred * inv_scale
    normed = (unit_rows * norm_gain).astype(jnp.bfloat16)
    grad_wide = d_normed.astype(jnp.float32)
    scaled = norm_gain * grad_wide
    inner = scaled - lax.optimization_barrier(jnp.mean(scaled, axis=1, keepdims=True)) - unit_rows * lax.optimization_barrier(jnp.mean(scaled * unit_rows, axis=1, keepdims=True))
    boundary_grad = (inv_scale * inner).astype(jnp.bfloat16)
    return (boundary_grad, normed, lax.optimization_barrier(jnp.sum(grad_wide * unit_rows, axis=0)))

def reference(heads_in, weights, residual, norm_gain):
    grad_scale = 1.0 / math.sqrt(heads_in.shape[1])
    forward_sum = head_block_sum(heads_in[0], weights[0])
    boundary = (residual.astype(jnp.float32) + forward_sum).astype(jnp.bfloat16)
    back_sum = head_block_sum(heads_in[1], weights[1])
    d_normed = back_sum.astype(jnp.bfloat16)
    boundary_grad, normed, gain_sum = norm_both(boundary, d_normed, norm_gain)
    gain_grad = gain_sum * grad_scale
    context_grad = jnp.dot(boundary_grad, weights[0].T, preferred_element_type=jnp.float32).astype(jnp.bfloat16)
    queries = jnp.dot(normed, weights[1].T, preferred_element_type=jnp.float32).astype(jnp.bfloat16)
    first_grad = token_block_grad(boundary_grad, heads_in[0], grad_scale)
    second_grad = token_block_grad(normed, heads_in[1], grad_scale)
    heads_out = jnp.stack([context_grad, queries])
    weight_grad = jnp.stack([first_grad, second_grad])
    return (heads_out, weight_grad, boundary_grad, gain_grad)
```

```python
import math

import jax
import jax.numpy as jnp
from jax import lax
from jax.sharding import PartitionSpec as P

EPSILON = 1e-05


def swapped(block, axis, stride):
    count = lax.axis_size(axis)
    route = []
    for low in range(count):
        high = low | 1 << stride
        if high != low and high < count:
            route += [(low, high), (high, low)]
    return lax.ppermute(block, axis, route)


def norm_both(boundary, d_normed, norm_gain):
    wide = boundary.astype(jnp.float32)
    row_mean = jnp.mean(wide, axis=1, keepdims=True)
    centred = wide - row_mean
    inv_scale = lax.rsqrt(jnp.mean(centred * centred, axis=1, keepdims=True) + EPSILON)
    unit_rows = centred * inv_scale
    normed = (unit_rows * norm_gain).astype(jnp.bfloat16)
    grad_wide = d_normed.astype(jnp.float32)
    scaled = norm_gain * grad_wide
    inner = (
        scaled
        - jnp.mean(scaled, axis=1, keepdims=True)
        - unit_rows * jnp.mean(scaled * unit_rows, axis=1, keepdims=True)
    )
    boundary_grad = (inv_scale * inner).astype(jnp.bfloat16)
    return (boundary_grad, normed, jnp.sum(grad_wide * unit_rows, axis=0))


def per_device(heads_in, weights, residual, norm_gain):
    heads_local = heads_in[0]
    weight_local = weights[0]
    rows_dev = heads_local.shape[0]
    grp_count = lax.axis_size("grp")
    grad_scale = 1.0 / math.sqrt(rows_dev * grp_count)
    section_first = lax.axis_index("section") == 0
    segment = heads_local
    summed = lax.psum_scatter(
        jnp.dot(segment, weight_local, preferred_element_type=jnp.float32).astype(jnp.bfloat16),
        "tp",
        scatter_dimension=0,
        tiled=True,
    ).astype(jnp.float32)
    forward_rows = (residual.astype(jnp.float32) + summed).astype(jnp.bfloat16)
    backward_rows = summed.astype(jnp.bfloat16)
    outgoing = jnp.where(section_first, forward_rows, backward_rows)
    arrived = swapped(outgoing, "section", 0)
    boundary = jnp.where(section_first, outgoing, arrived)
    d_normed = jnp.where(section_first, arrived, outgoing)
    boundary_grad, normed, gain_part = norm_both(boundary, d_normed, norm_gain)
    own_values = jnp.where(section_first, boundary_grad, normed)
    values = lax.all_gather(own_values, "tp", axis=0, tiled=True)
    gain_grad = lax.psum(gain_part, ("grp", "tp")) * grad_scale
    heads_out = lax.dot_general(
        values, weight_local, (((1,), (1,)), ((), ())), preferred_element_type=jnp.float32
    )
    heads_out = heads_out.astype(jnp.bfloat16)
    segment = values
    product = lax.dot_general(
        segment, heads_local, (((0,), (0,)), ((), ())), preferred_element_type=jnp.float32
    )
    weight_grad = lax.psum_scatter(
        (product * grad_scale).astype(jnp.bfloat16), "grp", scatter_dimension=0, tiled=True
    ).astype(jnp.float32)
    return (heads_out[None], weight_grad[None], boundary_grad, gain_grad)


def solution(mesh):
    placed = (P("section", "grp", "tp"), P("section", "tp", None), P(("grp", "tp"), None), P())
    return jax.shard_map(
        per_device,
        mesh=mesh,
        in_specs=placed,
        out_specs=(
            P("section", "grp", "tp"),
            P("section", "grp", "tp"),
            P(("grp", "tp"), None),
            P(),
        ),
        check_vma=False,
    )
```

```python
import math

import jax
import jax.numpy as jnp
from jax import lax
from jax.experimental import pallas as pl
from jax.experimental.pallas import tpu as pltpu
from jax.sharding import PartitionSpec as P

EPSILON = 1e-05
MESH = pl.DeviceIdType.MESH

SIDE = 4
PAIRS = 4
CHUNKS = 2 * PAIRS
WIDE = 512
HALF = WIDE // 2
OWN = 24
TALL = 2 * OWN


def lower_start(t, h):
    return pl.multiple_of((2 * t + h) * WIDE, WIDE)


def upper_start(t, h):
    return pl.multiple_of((2 * (2 * PAIRS - 1 - t) + h) * WIDE, WIDE)


def place_on_plane():
    tp = lax.axis_index("tp")
    return tp // SIDE, tp % SIDE


def plane_device(h, first, second):
    x, y = (first, second) if h == 0 else (second, first)
    return {"tp": x * SIDE + y}


def stacked(lower, upper):
    return jnp.concatenate([lower, upper], axis=0)


def both_halves(row_pair):
    total = row_pair[:OWN] + row_pair[OWN:]
    return stacked(total, total)


def lanes(value):
    return sum(value[:, 128 * i : 128 * (i + 1)] for i in range(value.shape[1] // 128))


def wide(value):
    return value.astype(jnp.float32)


def greet(peers):
    barrier = pltpu.get_barrier_semaphore()
    for peer in peers:
        pl.semaphore_signal(barrier, inc=1, device_id=peer, device_id_type=MESH)
    pl.semaphore_wait(barrier, len(peers))


def plane_neighbours(x, y):
    return [
        {"tp": ((x + 1) % SIDE) * SIDE + y},
        {"tp": ((x + 3) % SIDE) * SIDE + y},
        {"tp": x * SIDE + (y + 1) % SIDE},
        {"tp": x * SIDE + (y + 3) % SIDE},
    ]


def reduce_kernel(
    heads, weights, residual, gain, values_out, grad_out, gain_out,
    weight_buf, part, from1, from2, from3, from4, both, weight_sem, send_sem, recv_sem,
):
    x, y = place_on_plane()
    section = lax.axis_index("section")
    other = {"section": 1 - section}

    def weight_copy(t, h, upper):
        start = upper_start(t, h) if upper else lower_start(t, h)
        cols = pl.ds(start, WIDE)
        return pltpu.make_async_copy(
            weights.at[:, cols], weight_buf.at[:, cols], weight_sem.at[2 * t + h, upper]
        )

    def start_weights(t, carry):
        for h in range(2):
            for upper in range(2):
                weight_copy(t, h, upper).start()
        return carry

    lax.fori_loop(0, PAIRS, start_weights, 0)
    greet(plane_neighbours(x, y) + [other])

    def copy(t, h, step):
        chunk = 2 * t + h
        a, b = (x, y) if h == 0 else (y, x)
        right, left = (a + 1) % SIDE, (a + 3) % SIDE
        up, down = (b + 1) % SIDE, (b + 3) % SIDE
        low, high = pl.ds(0, HALF), pl.ds(HALF, HALF)
        far_a, far_b = (a + 2) % SIDE, (b + 2) % SIDE
        source, target, device = [
            lambda: (part.at[chunk, far_a, :, :, low], from1.at[chunk, 0], plane_device(h, right, b)),
            lambda: (part.at[chunk, far_a, :, :, high], from1.at[chunk, 1], plane_device(h, left, b)),
            lambda: (part.at[chunk, right], from2.at[chunk, 0], plane_device(h, right, b)),
            lambda: (part.at[chunk, left], from2.at[chunk, 1], plane_device(h, left, b)),
            lambda: (part.at[chunk, a, far_b, :, low], from3.at[chunk, 0], plane_device(h, a, up)),
            lambda: (part.at[chunk, a, far_b, :, high], from3.at[chunk, 1], plane_device(h, a, down)),
            lambda: (part.at[chunk, a, up], from4.at[chunk, 0], plane_device(h, a, up)),
            lambda: (part.at[chunk, a, down], from4.at[chunk, 1], plane_device(h, a, down)),
            lambda: (both.at[section, chunk], both.at[section, chunk], other),
        ][step]()
        return pltpu.make_async_remote_copy(
            src_ref=source,
            dst_ref=target,
            send_sem=send_sem.at[chunk, step],
            recv_sem=recv_sem.at[chunk, step],
            device_id=device,
            device_id_type=MESH,
        )

    def arrive(t, h, steps):
        for step in steps:
            copy(t, h, step).wait_recv()

    def multiply(t, carry):
        for h in range(2):
            weight_copy(t, h, 0).wait()
            weight_copy(t, h, 1).wait()
            lower = jnp.dot(
                heads[...], weight_buf[:, pl.ds(lower_start(t, h), WIDE)],
                preferred_element_type=jnp.float32,
            )
            upper = jnp.dot(
                heads[...], weight_buf[:, pl.ds(upper_start(t, h), WIDE)],
                preferred_element_type=jnp.float32,
            )
            for i in range(SIDE * SIDE):
                rows = slice(OWN * i, OWN * (i + 1))
                a, b = (i // SIDE, i % SIDE) if h == 0 else (i % SIDE, i // SIDE)
                part[2 * t + h, a, b] = stacked(lower[rows], upper[rows]).astype(jnp.bfloat16)
            copy(t, h, 0).start()
            copy(t, h, 1).start()
        return carry

    def near_first(t, carry):
        for h in range(2):
            chunk = 2 * t + h
            a = x if h == 0 else y
            right, left = (a + 1) % SIDE, (a + 3) % SIDE
            arrive(t, h, (0, 1))
            part[chunk, right, :, :, :HALF] = (
                wide(part[chunk, right, :, :, :HALF]) + wide(from1[chunk, 0])
            ).astype(jnp.bfloat16)
            copy(t, h, 2).start()
            part[chunk, left, :, :, HALF:] = (
                wide(part[chunk, left, :, :, HALF:]) + wide(from1[chunk, 1])
            ).astype(jnp.bfloat16)
            copy(t, h, 3).start()
        return carry

    def far_second(t, carry):
        for h in range(2):
            chunk = 2 * t + h
            a = x if h == 0 else y
            arrive(t, h, (2, 3))
            part[chunk, a] = (
                wide(part[chunk, a]) + (wide(from2[chunk, 0]) + wide(from2[chunk, 1]))
            ).astype(jnp.bfloat16)
            copy(t, h, 4).start()
            copy(t, h, 5).start()
        return carry

    def near_second(t, carry):
        for h in range(2):
            chunk = 2 * t + h
            a, b = (x, y) if h == 0 else (y, x)
            up, down = (b + 1) % SIDE, (b + 3) % SIDE
            arrive(t, h, (4, 5))
            part[chunk, a, up, :, :HALF] = (
                wide(part[chunk, a, up, :, :HALF]) + wide(from3[chunk, 0])
            ).astype(jnp.bfloat16)
            copy(t, h, 6).start()
            part[chunk, a, down, :, HALF:] = (
                wide(part[chunk, a, down, :, HALF:]) + wide(from3[chunk, 1])
            ).astype(jnp.bfloat16)
            copy(t, h, 7).start()
        return carry

    def finish(t, carry):
        for h in range(2):
            chunk = 2 * t + h
            a, b = (x, y) if h == 0 else (y, x)
            arrive(t, h, (6, 7))
            total = wide(part[chunk, a, b]) + (wide(from4[chunk, 0]) + wide(from4[chunk, 1]))
            stream = stacked(
                wide(residual[:, pl.ds(lower_start(t, h), WIDE)]),
                wide(residual[:, pl.ds(upper_start(t, h), WIDE)]),
            )
            total = total + jnp.where(section == 0, stream, 0.0)
            both[section, chunk] = total.astype(jnp.bfloat16)
            copy(t, h, 8).start()
        return carry

    for stage in (multiply, near_first, far_second, near_second, finish):
        lax.fori_loop(0, PAIRS, stage, 0)

    zero = jnp.zeros((TALL, 128), jnp.float32)

    def row_mean(total):
        return both_halves(jnp.sum(total, axis=1, keepdims=True)) / (2 * CHUNKS * WIDE)

    def add_sums(t, total):
        for h in range(2):
            copy(t, h, 8).wait_recv()
            total = total + lanes(wide(both[0, 2 * t + h]))
        return total

    mean = row_mean(lax.fori_loop(0, PAIRS, add_sums, zero))

    def add_squares(t, total):
        for h in range(2):
            centred = wide(both[0, 2 * t + h]) - mean
            total = total + lanes(centred * centred)
        return total

    inv_scale = lax.rsqrt(row_mean(lax.fori_loop(0, PAIRS, add_squares, zero)) + EPSILON)

    def gain_rows(t, h):
        return stacked(
            jnp.broadcast_to(gain[:, pl.ds(lower_start(t, h), WIDE)], (OWN, WIDE)),
            jnp.broadcast_to(gain[:, pl.ds(upper_start(t, h), WIDE)], (OWN, WIDE)),
        )

    def add_means(t, totals):
        for h in range(2):
            unit = (wide(both[0, 2 * t + h]) - mean) * inv_scale
            scaled = gain_rows(t, h) * wide(both[1, 2 * t + h])
            totals = (totals[0] + lanes(scaled), totals[1] + lanes(scaled * unit))
        return totals

    sums = lax.fori_loop(0, PAIRS, add_means, (zero, zero))
    mean_scaled, mean_product = row_mean(sums[0]), row_mean(sums[1])

    def write(t, carry):
        for h in range(2):
            chunk = 2 * t + h
            rows = gain_rows(t, h)
            unit = (wide(both[0, chunk]) - mean) * inv_scale
            d_normed = wide(both[1, chunk])
            normed = unit * rows
            grad = inv_scale * (rows * d_normed - mean_scaled - unit * mean_product)
            values_out[chunk] = jnp.where(section == 0, grad, normed).astype(jnp.bfloat16)
            grad_out[:, pl.ds(lower_start(t, h), WIDE)] = grad[:OWN].astype(jnp.bfloat16)
            grad_out[:, pl.ds(upper_start(t, h), WIDE)] = grad[OWN:].astype(jnp.bfloat16)
            product = d_normed * unit
            gain_out[chunk, 0:1] = jnp.sum(product[:OWN], axis=0, keepdims=True)
            gain_out[chunk, 1:2] = jnp.sum(product[OWN:], axis=0, keepdims=True)
        return carry

    lax.fori_loop(0, PAIRS, write, 0)

    def sent(t, carry):
        for h in range(2):
            for step in range(9):
                copy(t, h, step).wait_send()
        return carry

    lax.fori_loop(0, PAIRS, sent, 0)


def reduced_rows(heads, weights, residual, gain):
    vmem = pl.BlockSpec(memory_space=pltpu.VMEM)
    bf16 = jnp.bfloat16
    return pl.pallas_call(
        reduce_kernel,
        out_shape=(
            jax.ShapeDtypeStruct((CHUNKS, TALL, WIDE), bf16),
            jax.ShapeDtypeStruct(residual.shape, bf16),
            jax.ShapeDtypeStruct((CHUNKS, 2, WIDE), jnp.float32),
        ),
        in_specs=[vmem, pl.BlockSpec(memory_space=pl.ANY), vmem, vmem],
        out_specs=(vmem, vmem, vmem),
        scratch_shapes=[
            pltpu.VMEM(weights.shape, bf16),
            pltpu.VMEM((CHUNKS, SIDE, SIDE, TALL, WIDE), bf16),
            pltpu.VMEM((CHUNKS, 2, SIDE, TALL, HALF), bf16),
            pltpu.VMEM((CHUNKS, 2, SIDE, TALL, WIDE), bf16),
            pltpu.VMEM((CHUNKS, 2, TALL, HALF), bf16),
            pltpu.VMEM((CHUNKS, 2, TALL, WIDE), bf16),
            pltpu.VMEM((2, CHUNKS, TALL, WIDE), bf16),
            pltpu.SemaphoreType.DMA((CHUNKS, 2)),
            pltpu.SemaphoreType.DMA((CHUNKS, 9)),
            pltpu.SemaphoreType.DMA((CHUNKS, 9)),
        ],
        compiler_params=pltpu.CompilerParams(
            collective_id=0, has_side_effects=True, vmem_limit_bytes=48 * 1024 * 1024
        ),
        name="reduced_rows",
    )(heads, weights, residual, gain)


def plain_rows(chunks):
    rows = chunks.shape[1] // 2
    parts = chunks.reshape(PAIRS, 2, 2, rows, WIDE)
    lower = parts[:, :, 0].transpose(2, 0, 1, 3).reshape(rows, -1)
    upper = parts[::-1, :, 1].transpose(2, 0, 1, 3).reshape(rows, -1)
    return jnp.concatenate([lower, upper], axis=1)


def swapped(block, axis, stride):
    count = lax.axis_size(axis)
    route = [(low, low ^ 1 << stride) for low in range(count)]
    return lax.ppermute(block, axis, route)


def per_device(heads_in, weights, residual, norm_gain):
    heads_local = heads_in[0]
    weight_local = weights[0]
    rows_dev = heads_local.shape[0]
    grad_scale = 1.0 / math.sqrt(rows_dev * lax.axis_size("grp"))
    own_values, boundary_grad, gain_part = reduced_rows(
        heads_local, weight_local, residual, norm_gain[None]
    )
    values = lax.all_gather(plain_rows(own_values), "tp", axis=0, tiled=True)
    gain_sum = gain_part
    for axis, strides in (("tp", 4), ("grp", 3)):
        for stride in range(strides):
            gain_sum = gain_sum + swapped(gain_sum, axis, stride)
    gain_grad = plain_rows(gain_sum)[0] * grad_scale
    heads_out = lax.dot_general(
        values, weight_local, (((1,), (1,)), ((), ())), preferred_element_type=jnp.float32
    )
    heads_out = heads_out.astype(jnp.bfloat16)
    product = lax.dot_general(
        values, heads_local, (((0,), (0,)), ((), ())), preferred_element_type=jnp.float32
    )
    weight_grad = lax.psum_scatter(
        (product * grad_scale).astype(jnp.bfloat16), "grp", scatter_dimension=0, tiled=True
    ).astype(jnp.float32)
    return (heads_out[None], weight_grad[None], boundary_grad, gain_grad)


def solution(mesh):
    placed = (P("section", "grp", "tp"), P("section", "tp", None), P(("grp", "tp"), None), P())
    return jax.shard_map(
        per_device,
        mesh=mesh,
        in_specs=placed,
        out_specs=(
            P("section", "grp", "tp"),
            P("section", "grp", "tp"),
            P(("grp", "tp"), None),
            P(),
        ),
        check_vma=False,
    )
```

```python
import math

import jax
import jax.numpy as jnp
from jax import lax
from jax.experimental import pallas as pl
from jax.experimental.pallas import tpu as pltpu
from jax.sharding import PartitionSpec as P

EPSILON = 1e-05
MESH = pl.DeviceIdType.MESH

SIDE = 4
GATHERS = 7
GROUPS = 8

PAIRS = 4
CHUNKS = 2 * PAIRS
WIDE = 512
HALF = WIDE // 2
OWN = 24
TALL = 2 * OWN


def lower_start(t, h):
    return pl.multiple_of((2 * t + h) * WIDE, WIDE)


def upper_start(t, h):
    return pl.multiple_of((2 * (2 * PAIRS - 1 - t) + h) * WIDE, WIDE)


def place_on_plane():
    tp = lax.axis_index("tp")
    return tp // SIDE, tp % SIDE


def plane_device(h, first, second):
    x, y = (first, second) if h == 0 else (second, first)
    return {"tp": x * SIDE + y}


def stacked(lower, upper):
    return jnp.concatenate([lower, upper], axis=0)


def both_halves(row_pair):
    total = row_pair[:OWN] + row_pair[OWN:]
    return stacked(total, total)


def lanes(value):
    return sum(value[:, 128 * i : 128 * (i + 1)] for i in range(value.shape[1] // 128))


def wide(value):
    return value.astype(jnp.float32)


def greet(peers):
    barrier = pltpu.get_barrier_semaphore()
    for peer in peers:
        pl.semaphore_signal(barrier, inc=1, device_id=peer, device_id_type=MESH)
    pl.semaphore_wait(barrier, len(peers))


def plane_neighbours(x, y):
    return [
        {"tp": ((x + 1) % SIDE) * SIDE + y},
        {"tp": ((x + 3) % SIDE) * SIDE + y},
        {"tp": x * SIDE + (y + 1) % SIDE},
        {"tp": x * SIDE + (y + 3) % SIDE},
    ]


def boundary_kernel(
    heads_in, weights, residual, gain_in, heads_out, grads_out, grad_out, gain_out,
    heads, gain, weight_buf, part, from1, from2, from3, from4, both,
    values, exchange, tokens, to_sibling, from_sibling, heads_all, heads_total, gain_own, gain_got,
    input_sem, weight_sem, send_sem, recv_sem, gather_send, gather_recv, exchange_send, exchange_recv,
    heads_send, heads_recv, sibling_send, sibling_recv, gain_send, gain_recv,
):
    x, y = place_on_plane()
    section = lax.axis_index("section")
    other = {"section": 1 - section}
    group = lax.axis_index("grp")
    z, core = group // 2, group % 2
    sibling = {"grp": 2 * z + 1 - core}
    grad_scale = 1.0 / math.sqrt(heads.shape[0] * GROUPS)

    def weight_copy(t, h, upper):
        start = upper_start(t, h) if upper else lower_start(t, h)
        cols = pl.ds(start, WIDE)
        return pltpu.make_async_copy(
            weights.at[:, cols], weight_buf.at[:, cols], weight_sem.at[2 * t + h, upper]
        )

    def start_weights(t, carry):
        for h in range(2):
            for upper in range(2):
                weight_copy(t, h, upper).start()
        return carry

    heads_load = pltpu.make_async_copy(heads_in, heads, input_sem.at[0])
    gain_load = pltpu.make_async_copy(gain_in, gain, input_sem.at[1])
    heads_load.start()
    gain_load.start()
    lax.fori_loop(0, PAIRS, start_weights, 0)
    far_groups = [{"grp": 2 * ((z + hop) % SIDE) + k} for hop in range(1, SIDE) for k in range(2)]
    greet(plane_neighbours(x, y) + [other, sibling] + far_groups)
    heads_load.wait()

    def heads_copy(slot, source, device):
        return pltpu.make_async_remote_copy(
            src_ref=source,
            dst_ref=heads_all.at[slot],
            send_sem=heads_send.at[slot],
            recv_sem=heads_recv.at[slot],
            device_id=device,
            device_id_type=MESH,
        )

    def own_heads(hop):
        return heads_copy(2 * (SIDE - 1 - hop) + core, heads, {"grp": 2 * ((z + hop) % SIDE) + core})

    def passed_heads(j):
        slot = 2 * j + core
        return pltpu.make_async_remote_copy(
            src_ref=heads_all.at[slot],
            dst_ref=heads_all.at[slot],
            send_sem=heads_send.at[GATHERS + j],
            recv_sem=heads_recv.at[slot],
            device_id=sibling,
            device_id_type=MESH,
        )

    for hop in range(1, SIDE):
        own_heads(hop).start()
    heads_copy(GATHERS - 1, heads, sibling).start()

    def copy(t, h, step):
        chunk = 2 * t + h
        a, b = (x, y) if h == 0 else (y, x)
        right, left = (a + 1) % SIDE, (a + 3) % SIDE
        up, down = (b + 1) % SIDE, (b + 3) % SIDE
        low, high = pl.ds(0, HALF), pl.ds(HALF, HALF)
        far_a, far_b = (a + 2) % SIDE, (b + 2) % SIDE
        source, target, device = [
            lambda: (part.at[chunk, far_a, :, :, low], from1.at[chunk, 0], plane_device(h, right, b)),
            lambda: (part.at[chunk, far_a, :, :, high], from1.at[chunk, 1], plane_device(h, left, b)),
            lambda: (part.at[chunk, right], from2.at[chunk, 0], plane_device(h, right, b)),
            lambda: (part.at[chunk, left], from2.at[chunk, 1], plane_device(h, left, b)),
            lambda: (part.at[chunk, a, far_b, :, low], from3.at[chunk, 0], plane_device(h, a, up)),
            lambda: (part.at[chunk, a, far_b, :, high], from3.at[chunk, 1], plane_device(h, a, down)),
            lambda: (part.at[chunk, a, up], from4.at[chunk, 0], plane_device(h, a, up)),
            lambda: (part.at[chunk, a, down], from4.at[chunk, 1], plane_device(h, a, down)),
            lambda: (both.at[section, chunk], both.at[section, chunk], other),
        ][step]()
        return pltpu.make_async_remote_copy(
            src_ref=source,
            dst_ref=target,
            send_sem=send_sem.at[chunk, step],
            recv_sem=recv_sem.at[chunk, step],
            device_id=device,
            device_id_type=MESH,
        )

    def arrive(t, h, steps):
        for step in steps:
            copy(t, h, step).wait_recv()

    def multiply(t, carry):
        for h in range(2):
            weight_copy(t, h, 0).wait()
            weight_copy(t, h, 1).wait()
            lower = jnp.dot(
                heads[...], weight_buf[:, pl.ds(lower_start(t, h), WIDE)],
                preferred_element_type=jnp.float32,
            )
            upper = jnp.dot(
                heads[...], weight_buf[:, pl.ds(upper_start(t, h), WIDE)],
                preferred_element_type=jnp.float32,
            )
            for i in range(SIDE * SIDE):
                rows = slice(OWN * i, OWN * (i + 1))
                a, b = (i // SIDE, i % SIDE) if h == 0 else (i % SIDE, i // SIDE)
                part[2 * t + h, a, b] = stacked(lower[rows], upper[rows]).astype(jnp.bfloat16)
            copy(t, h, 0).start()
            copy(t, h, 1).start()
        return carry

    def near_first(t, carry):
        for h in range(2):
            chunk = 2 * t + h
            a = x if h == 0 else y
            right, left = (a + 1) % SIDE, (a + 3) % SIDE
            arrive(t, h, (0, 1))
            part[chunk, right, :, :, :HALF] = (
                wide(part[chunk, right, :, :, :HALF]) + wide(from1[chunk, 0])
            ).astype(jnp.bfloat16)
            copy(t, h, 2).start()
            part[chunk, left, :, :, HALF:] = (
                wide(part[chunk, left, :, :, HALF:]) + wide(from1[chunk, 1])
            ).astype(jnp.bfloat16)
            copy(t, h, 3).start()
        return carry

    def far_second(t, carry):
        for h in range(2):
            chunk = 2 * t + h
            a = x if h == 0 else y
            arrive(t, h, (2, 3))
            part[chunk, a] = (
                wide(part[chunk, a]) + (wide(from2[chunk, 0]) + wide(from2[chunk, 1]))
            ).astype(jnp.bfloat16)
            copy(t, h, 4).start()
            copy(t, h, 5).start()
        return carry

    def near_second(t, carry):
        for h in range(2):
            chunk = 2 * t + h
            a, b = (x, y) if h == 0 else (y, x)
            up, down = (b + 1) % SIDE, (b + 3) % SIDE
            arrive(t, h, (4, 5))
            part[chunk, a, up, :, :HALF] = (
                wide(part[chunk, a, up, :, :HALF]) + wide(from3[chunk, 0])
            ).astype(jnp.bfloat16)
            copy(t, h, 6).start()
            part[chunk, a, down, :, HALF:] = (
                wide(part[chunk, a, down, :, HALF:]) + wide(from3[chunk, 1])
            ).astype(jnp.bfloat16)
            copy(t, h, 7).start()
        return carry

    def finish(t, carry):
        for h in range(2):
            chunk = 2 * t + h
            a, b = (x, y) if h == 0 else (y, x)
            arrive(t, h, (6, 7))
            total = wide(part[chunk, a, b]) + (wide(from4[chunk, 0]) + wide(from4[chunk, 1]))
            stream = stacked(
                wide(residual[:, pl.ds(lower_start(t, h), WIDE)]),
                wide(residual[:, pl.ds(upper_start(t, h), WIDE)]),
            )
            total = total + jnp.where(section == 0, stream, 0.0)
            both[section, chunk] = total.astype(jnp.bfloat16)
            copy(t, h, 8).start()
        return carry

    for stage in (multiply, near_first, far_second, near_second, finish):
        lax.fori_loop(0, PAIRS, stage, 0)

    heads_total[...] = jnp.zeros_like(heads_total)
    grads_out[...] = jnp.zeros_like(grads_out)
    gain_load.wait()
    zero = jnp.zeros((TALL, 128), jnp.float32)

    def row_mean(total):
        return both_halves(jnp.sum(total, axis=1, keepdims=True)) / (2 * CHUNKS * WIDE)

    def add_sums(t, total):
        for h in range(2):
            copy(t, h, 8).wait_recv()
            total = total + lanes(wide(both[0, 2 * t + h]))
        return total

    mean = row_mean(lax.fori_loop(0, PAIRS, add_sums, zero))

    def add_squares(t, total):
        for h in range(2):
            centred = wide(both[0, 2 * t + h]) - mean
            total = total + lanes(centred * centred)
        return total

    inv_scale = lax.rsqrt(row_mean(lax.fori_loop(0, PAIRS, add_squares, zero)) + EPSILON)

    def gain_rows(t, h):
        return stacked(
            jnp.broadcast_to(gain[:, pl.ds(lower_start(t, h), WIDE)], (OWN, WIDE)),
            jnp.broadcast_to(gain[:, pl.ds(upper_start(t, h), WIDE)], (OWN, WIDE)),
        )

    def add_means(t, totals):
        for h in range(2):
            unit = (wide(both[0, 2 * t + h]) - mean) * inv_scale
            scaled = gain_rows(t, h) * wide(both[1, 2 * t + h])
            totals = (totals[0] + lanes(scaled), totals[1] + lanes(scaled * unit))
        return totals

    sums = lax.fori_loop(0, PAIRS, add_means, (zero, zero))
    mean_scaled, mean_product = row_mean(sums[0]), row_mean(sums[1])

    def gather(p, h, step):
        chunk = 2 * p + h
        a, b = (x, y) if h == 0 else (y, x)
        right, left = (a + 1) % SIDE, (a + 3) % SIDE
        up, down = (b + 1) % SIDE, (b + 3) % SIDE
        low, high = pl.ds(0, HALF), pl.ds(HALF, HALF)
        block, device = [
            lambda: (values.at[chunk, b, a], plane_device(h, right, b)),
            lambda: (values.at[chunk, b, a], plane_device(h, left, b)),
            lambda: (values.at[chunk, b, left, :, low], plane_device(h, right, b)),
            lambda: (values.at[chunk, b, right, :, high], plane_device(h, left, b)),
            lambda: (values.at[chunk, b], plane_device(h, a, up)),
            lambda: (values.at[chunk, b], plane_device(h, a, down)),
            lambda: (values.at[chunk, down, :, :, low], plane_device(h, a, up)),
            lambda: (values.at[chunk, up, :, :, high], plane_device(h, a, down)),
        ][step]()
        return pltpu.make_async_remote_copy(
            src_ref=block,
            dst_ref=block,
            send_sem=gather_send.at[chunk, step],
            recv_sem=gather_recv.at[chunk, step],
            device_id=device,
            device_id_type=MESH,
        )

    def gather_stage(p, waits, starts):
        for h in range(2):
            for step in waits:
                gather(p, h, step).wait_recv()
            for step in starts:
                gather(p, h, step).start()

    def exchanged(target):
        slot = 2 * ((z + SIDE - 1 - target // 2) % SIDE) + core
        a, b = x + core * (y - x), y + core * (x - y)
        return pltpu.make_async_remote_copy(
            src_ref=exchange.at[target],
            dst_ref=values.at[CHUNKS + slot, b, a],
            send_sem=exchange_send.at[target],
            recv_sem=exchange_recv.at[slot],
            device_id={"grp": target},
            device_id_type=MESH,
        )

    def arrived_exchange(slot, h):
        a, b = (x, y) if h == 0 else (y, x)
        return pltpu.make_async_remote_copy(
            src_ref=exchange.at[0],
            dst_ref=values.at[CHUNKS + slot, b, a],
            send_sem=exchange_send.at[0],
            recv_sem=exchange_recv.at[slot],
            device_id=sibling,
            device_id_type=MESH,
        )

    def write(t, carry):
        kept = []
        for h in range(2):
            chunk = 2 * t + h
            a, b = (x, y) if h == 0 else (y, x)
            rows = gain_rows(t, h)
            unit = (wide(both[0, chunk]) - mean) * inv_scale
            d_normed = wide(both[1, chunk])
            normed = unit * rows
            grad = inv_scale * (rows * d_normed - mean_scaled - unit * mean_product)
            value = jnp.where(section == 0, grad, normed)
            values[chunk, b, a] = value.astype(jnp.bfloat16)
            gather(t, h, 0).start()
            gather(t, h, 1).start()
            kept.append(value)
            grad_out[:, pl.ds(lower_start(t, h), WIDE)] = grad[:OWN].astype(jnp.bfloat16)
            grad_out[:, pl.ds(upper_start(t, h), WIDE)] = grad[OWN:].astype(jnp.bfloat16)
            product = d_normed * unit
            gain_own[0, chunk, 0:1] = jnp.sum(product[:OWN], axis=0, keepdims=True)
            gain_own[0, chunk, 1:2] = jnp.sum(product[OWN:], axis=0, keepdims=True)
        for target, rows in ((t, slice(0, OWN)), (GROUPS - 1 - t, slice(OWN, TALL))):
            exchange[target] = stacked(kept[0][rows], kept[1][rows]).astype(jnp.bfloat16)

            @pl.when(target // 2 != z)
            def _():
                exchanged(target).start()
        return carry

    lax.fori_loop(0, PAIRS, write, 0)

    for j in range(SIDE - 1):
        heads_copy(2 * j + core, heads, sibling).wait_recv()
        passed_heads(j).start()

    gain_partners = [
        {"tp": x * SIDE + y + 1 - 2 * (y % 2)},
        {"tp": x * SIDE + SIDE - 1 - y},
        {"tp": (x + 1 - 2 * (x % 2)) * SIDE + y},
        {"tp": (SIDE - 1 - x) * SIDE + y},
        sibling,
        {"grp": 2 * (z + 1 - 2 * (z % 2)) + core},
        {"grp": 2 * (SIDE - 1 - z) + core},
    ]

    def gain_copy(step):
        return pltpu.make_async_remote_copy(
            src_ref=gain_own.at[step],
            dst_ref=gain_got.at[step],
            send_sem=gain_send.at[step],
            recv_sem=gain_recv.at[step],
            device_id=gain_partners[step],
            device_id_type=MESH,
        )

    def sibling_copy(h):
        return pltpu.make_async_remote_copy(
            src_ref=to_sibling.at[h],
            dst_ref=from_sibling.at[h],
            send_sem=sibling_send.at[h],
            recv_sem=sibling_recv.at[h],
            device_id=sibling,
            device_id_type=MESH,
        )

    rows_dev = heads.shape[0]

    def unpack(p):
        for h in range(2):
            for i in range(0, SIDE * SIDE, 2):
                pair = []
                for at in (i, i + 1):
                    a, b = (at // SIDE, at % SIDE) if h == 0 else (at % SIDE, at // SIDE)
                    pair.append(wide(values[2 * p + h, b, a]))
                rows = slice(h * rows_dev + OWN * i, h * rows_dev + OWN * (i + 2))
                tokens[0, rows] = stacked(pair[0][:OWN], pair[1][:OWN]).astype(jnp.bfloat16)
                tokens[1, rows] = stacked(pair[0][OWN:], pair[1][OWN:]).astype(jnp.bfloat16)

    def add_grads(part_at, token_rows, head_rows):
        grads_out[part_at * WIDE : (part_at + 1) * WIDE] += grad_scale * lax.dot_general(
            token_rows, head_rows, (((0,), (0,)), ((), ())), preferred_element_type=jnp.float32
        )

    def use_rows(t):
        total = heads_total[...]
        for h in range(2):
            rows = slice(h * rows_dev, (h + 1) * rows_dev)
            for upper in range(2):
                start = upper_start(t, h) if upper else lower_start(t, h)
                total = total + lax.dot_general(
                    tokens[upper, rows], weight_buf[:, pl.ds(start, WIDE)],
                    (((1,), (1,)), ((), ())), preferred_element_type=jnp.float32,
                )
        heads_total[...] = total
        for upper in range(2):
            target = GROUPS - 1 - t if upper else t

            @pl.when(target == group)
            def _():
                for h in range(2):
                    add_grads(h, tokens[upper, h * rows_dev : (h + 1) * rows_dev], heads[...])

            @pl.when(target == 2 * z + 1 - core)
            def _():
                for h in range(2):
                    to_sibling[h] = tokens[upper, h * rows_dev : (h + 1) * rows_dev]
                    sibling_copy(h).start()

    def use_columns(j):
        heads_copy(2 * j + 1 - core, heads, sibling).wait_recv()
        head_rows = heads_all[pl.ds(2 * j, 2)].reshape(2 * rows_dev, -1)
        for upper in range(2):
            add_grads(upper, tokens[upper], head_rows)

    def use_sibling():
        heads_copy(GATHERS - 1, heads, sibling).wait_recv()
        for h in range(2):
            sibling_copy(h).wait_recv()
            add_grads(h, from_sibling[h], heads_all[GATHERS - 1])

    def inside(p, first=0):
        return jnp.logical_and(p >= first, p < GATHERS)

    def turn(n, carry):
        for step in range(len(gain_partners) + 1):

            @pl.when(n == step + 1)
            def _():
                if step > 0:
                    gain_copy(step - 1).wait_recv()
                    gain_own[step] = gain_own[step - 1] + gain_got[step - 1]
                if step < len(gain_partners):
                    gain_copy(step).start()

        @pl.when(inside(n, PAIRS))
        def _():
            for h in range(2):
                arrived_exchange(2 * (n - PAIRS) + h, h).wait_recv()
            gather_stage(n, (), (0, 1))

        @pl.when(inside(n - 1))
        def _():
            gather_stage(n - 1, (0, 1), (2, 3))

        @pl.when(inside(n - 2))
        def _():
            gather_stage(n - 2, (2, 3), (4, 5))

        @pl.when(inside(n - 3))
        def _():
            gather_stage(n - 3, (4, 5), (6, 7))

        @pl.when(inside(n - 4))
        def _():
            gather_stage(n - 4, (6, 7), ())
            unpack(n - 4)

            @pl.when(n - 4 < PAIRS)
            def _():
                use_rows(n - 4)

            @pl.when(n - 4 >= PAIRS)
            def _():
                use_columns(n - 4 - PAIRS)

            @pl.when(n - 4 == PAIRS)
            def _():
                use_sibling()

        return carry

    lax.fori_loop(1, GATHERS + 4, turn, 0)
    heads_out[...] = heads_total[...].astype(jnp.bfloat16)
    gain_out[...] = gain_own[len(gain_partners)] * grad_scale

    def sent(t, carry):
        for h in range(2):
            for step in range(9):
                copy(t, h, step).wait_send()
            target = t + h * (GROUPS - 1 - 2 * t)

            @pl.when(target // 2 != z)
            def _():
                exchanged(target).wait_send()
        return carry

    lax.fori_loop(0, PAIRS, sent, 0)

    def sent_gathers(p, carry):
        for h in range(2):
            for step in range(8):
                gather(p, h, step).wait_send()
        return carry

    lax.fori_loop(0, GATHERS, sent_gathers, 0)
    for hop in range(1, SIDE):
        own_heads(hop).wait_send()
        passed_heads(hop - 1).wait_send()
    heads_copy(GATHERS - 1, heads, sibling).wait_send()
    for h in range(2):
        sibling_copy(h).wait_send()
    for step in range(len(gain_partners)):
        gain_copy(step).wait_send()


def fused(heads, weights, residual, gain):
    vmem = pl.BlockSpec(memory_space=pltpu.VMEM)
    hbm = pl.BlockSpec(memory_space=pl.ANY)
    bf16, f32 = jnp.bfloat16, jnp.float32
    rows_dev, depth = heads.shape
    owned = weights.shape[1] // GROUPS
    dma = pltpu.SemaphoreType.DMA
    return pl.pallas_call(
        boundary_kernel,
        out_shape=(
            jax.ShapeDtypeStruct(heads.shape, bf16),
            jax.ShapeDtypeStruct((owned, depth), f32),
            jax.ShapeDtypeStruct(residual.shape, bf16),
            jax.ShapeDtypeStruct((CHUNKS, 2, WIDE), f32),
        ),
        in_specs=[hbm, hbm, vmem, hbm],
        out_specs=(vmem, vmem, vmem, vmem),
        scratch_shapes=[
            pltpu.VMEM(heads.shape, bf16),
            pltpu.VMEM(gain.shape, f32),
            pltpu.VMEM(weights.shape, bf16),
            pltpu.VMEM((CHUNKS, SIDE, SIDE, TALL, WIDE), bf16),
            pltpu.VMEM((CHUNKS, 2, SIDE, TALL, HALF), bf16),
            pltpu.VMEM((CHUNKS, 2, SIDE, TALL, WIDE), bf16),
            pltpu.VMEM((CHUNKS, 2, TALL, HALF), bf16),
            pltpu.VMEM((CHUNKS, 2, TALL, WIDE), bf16),
            pltpu.VMEM((2, CHUNKS, TALL, WIDE), bf16),
            pltpu.VMEM((2 * GATHERS, SIDE, SIDE, TALL, WIDE), bf16),
            pltpu.VMEM((GROUPS, TALL, WIDE), bf16),
            pltpu.VMEM((2, 2 * rows_dev, WIDE), bf16),
            pltpu.VMEM((2, rows_dev, WIDE), bf16),
            pltpu.VMEM((2, rows_dev, WIDE), bf16),
            pltpu.VMEM((GATHERS, rows_dev, depth), bf16),
            pltpu.VMEM((rows_dev, depth), f32),
            pltpu.VMEM((8, CHUNKS, 2, WIDE), f32),
            pltpu.VMEM((7, CHUNKS, 2, WIDE), f32),
            dma((2,)),
            dma((CHUNKS, 2)),
            dma((CHUNKS, 9)),
            dma((CHUNKS, 9)),
            dma((2 * GATHERS, 8)),
            dma((2 * GATHERS, 8)),
            dma((GROUPS,)),
            dma((GROUPS - 2,)),
            dma((GATHERS + 3,)),
            dma((GATHERS,)),
            dma((2,)),
            dma((2,)),
            dma((7,)),
            dma((7,)),
        ],
        compiler_params=pltpu.CompilerParams(
            collective_id=0, has_side_effects=True, vmem_limit_bytes=60 * 1024 * 1024
        ),
        name="boundary",
    )(heads, weights, residual, gain)


def plain_rows(chunks):
    rows = chunks.shape[1] // 2
    parts = chunks.reshape(PAIRS, 2, 2, rows, WIDE)
    lower = parts[:, :, 0].transpose(2, 0, 1, 3).reshape(rows, -1)
    upper = parts[::-1, :, 1].transpose(2, 0, 1, 3).reshape(rows, -1)
    return jnp.concatenate([lower, upper], axis=1)


def per_device(heads_in, weights, residual, norm_gain):
    heads_out, weight_grad, boundary_grad, gain_sum = fused(
        heads_in[0], weights[0], residual, norm_gain[None]
    )
    return (heads_out[None], weight_grad[None], boundary_grad, plain_rows(gain_sum)[0])


def solution(mesh):
    placed = (P("section", "grp", "tp"), P("section", "tp", None), P(("grp", "tp"), None), P())
    return jax.shard_map(
        per_device,
        mesh=mesh,
        in_specs=placed,
        out_specs=(
            P("section", "grp", "tp"),
            P("section", "grp", "tp"),
            P(("grp", "tp"), None),
            P(),
        ),
        check_vma=False,
    )
```

```python
import math

import jax
import jax.numpy as jnp
from jax import lax
from jax.experimental import pallas as pl
from jax.experimental.pallas import tpu as pltpu
from jax.sharding import PartitionSpec as P

EPSILON = 1e-05
MESH = pl.DeviceIdType.MESH

SIDE = 4
GATHERS = 7
GROUPS = 8

PAIRS = 4
CHUNKS = 2 * PAIRS
WIDE = 512
HALF = WIDE // 2
OWN = 24
TALL = 2 * OWN


def lower_start(t, h):
    return pl.multiple_of((2 * t + h) * WIDE, WIDE)


def upper_start(t, h):
    return pl.multiple_of((2 * (2 * PAIRS - 1 - t) + h) * WIDE, WIDE)


def place_on_plane():
    tp = lax.axis_index("tp")
    return tp // SIDE, tp % SIDE


def plane_device(h, first, second):
    x, y = (first, second) if h == 0 else (second, first)
    return {"tp": x * SIDE + y}


def stacked(lower, upper):
    return jnp.concatenate([lower, upper], axis=0)


def both_halves(row_pair):
    total = row_pair[:OWN] + row_pair[OWN:]
    return stacked(total, total)


def lanes(value):
    return sum(value[:, 128 * i : 128 * (i + 1)] for i in range(value.shape[1] // 128))


def wide(value):
    return value.astype(jnp.float32)


def greet(peers):
    barrier = pltpu.get_barrier_semaphore()
    for peer in peers:
        pl.semaphore_signal(barrier, inc=1, device_id=peer, device_id_type=MESH)
    pl.semaphore_wait(barrier, len(peers))


def plane_neighbours(x, y):
    return [
        {"tp": ((x + 1) % SIDE) * SIDE + y},
        {"tp": ((x + 3) % SIDE) * SIDE + y},
        {"tp": x * SIDE + (y + 1) % SIDE},
        {"tp": x * SIDE + (y + 3) % SIDE},
    ]


def boundary_kernel(
    heads_in, weights, residual_in, gain_in, heads_out, grads_out, grad_out, gain_out,
    heads, residual, gain, heads_done, grads, own_grad, gain_done, weight_buf, part, from1, from2, from3, from4, both,
    values, exchange, tokens, to_sibling, from_sibling, heads_all, heads_total, gain_own, gain_got,
    input_sem, output_sem, weight_sem, send_sem, recv_sem, gather_send, gather_recv, exchange_send, exchange_recv,
    heads_send, heads_recv, sibling_send, sibling_recv, gain_send, gain_recv,
):
    x, y = place_on_plane()
    section = lax.axis_index("section")
    other = {"section": 1 - section}
    group = lax.axis_index("grp")
    z, core = group // 2, group % 2
    sibling = {"grp": 2 * z + 1 - core}
    grad_scale = 1.0 / math.sqrt(heads.shape[0] * GROUPS)

    def weight_copy(t, h, upper):
        start = upper_start(t, h) if upper else lower_start(t, h)
        cols = pl.ds(start, WIDE)
        return pltpu.make_async_copy(
            weights.at[:, cols], weight_buf.at[:, cols], weight_sem.at[2 * t + h, upper]
        )

    def start_weights(t, carry):
        for h in range(2):
            for upper in range(2):
                weight_copy(t, h, upper).start()
        return carry

    heads_load = pltpu.make_async_copy(heads_in, heads, input_sem.at[0])
    gain_load = pltpu.make_async_copy(gain_in, gain, input_sem.at[1])
    residual_load = pltpu.make_async_copy(residual_in, residual, input_sem.at[2])
    heads_load.start()
    lax.fori_loop(0, PAIRS, start_weights, 0)
    residual_load.start()
    gain_load.start()
    far_groups = [{"grp": 2 * ((z + hop) % SIDE) + k} for hop in range(1, SIDE) for k in range(2)]
    greet(plane_neighbours(x, y) + [other, sibling] + far_groups)
    heads_load.wait()
    residual_load.wait()
    gain_load.wait()

    def heads_copy(slot, source, device):
        return pltpu.make_async_remote_copy(
            src_ref=source,
            dst_ref=heads_all.at[slot],
            send_sem=heads_send.at[slot],
            recv_sem=heads_recv.at[slot],
            device_id=device,
            device_id_type=MESH,
        )

    def slot_of(origin, at):
        return 2 * ((origin + SIDE - 1 - at) % SIDE) + core

    def relayed_heads(origin, target, source, at):
        return pltpu.make_async_remote_copy(
            src_ref=source,
            dst_ref=heads_all.at[slot_of(origin, target)],
            send_sem=heads_send.at[GATHERS + at],
            recv_sem=heads_recv.at[slot_of(origin, target)],
            device_id={"grp": 2 * target + core},
            device_id_type=MESH,
        )

    relays = ((1, 0), (-1, 0), (1, 1), (-1, 1), (1, 2), (-1, 2))

    def each_relay(wanted, act):
        for at, (step, away) in enumerate(relays):
            if away not in wanted:
                continue
            first, last = (away, SIDE - 2) if step > 0 else (1, SIDE - 1 - away)

            @pl.when(jnp.logical_and(z >= first, z <= last))
            def _():
                origin = z - step * away
                source = heads_all.at[slot_of(origin, z)] if away else heads
                act(relayed_heads(origin, z + step, source, at), slot_of(origin, z))

    def start_relay(relay, slot):
        relay.start()

    def pass_relay(relay, slot):
        heads_copy(slot, heads, sibling).wait_recv()
        relay.start()

    def passed_heads(j):
        slot = 2 * j + core
        return pltpu.make_async_remote_copy(
            src_ref=heads_all.at[slot],
            dst_ref=heads_all.at[slot],
            send_sem=heads_send.at[slot],
            recv_sem=heads_recv.at[slot],
            device_id=sibling,
            device_id_type=MESH,
        )

    each_relay((0,), start_relay)
    heads_copy(GATHERS - 1, heads, sibling).start()

    def copy(t, h, step):
        chunk = 2 * t + h
        a, b = (x, y) if h == 0 else (y, x)
        right, left = (a + 1) % SIDE, (a + 3) % SIDE
        up, down = (b + 1) % SIDE, (b + 3) % SIDE
        low, high = pl.ds(0, HALF), pl.ds(HALF, HALF)
        far_a, far_b = (a + 2) % SIDE, (b + 2) % SIDE
        source, target, device = [
            lambda: (part.at[chunk, far_a, :, :, low], from1.at[chunk, 0], plane_device(h, right, b)),
            lambda: (part.at[chunk, far_a, :, :, high], from1.at[chunk, 1], plane_device(h, left, b)),
            lambda: (part.at[chunk, right], from2.at[chunk, 0], plane_device(h, right, b)),
            lambda: (part.at[chunk, left], from2.at[chunk, 1], plane_device(h, left, b)),
            lambda: (part.at[chunk, a, far_b, :, low], from3.at[chunk, 0], plane_device(h, a, up)),
            lambda: (part.at[chunk, a, far_b, :, high], from3.at[chunk, 1], plane_device(h, a, down)),
            lambda: (part.at[chunk, a, up], from4.at[chunk, 0], plane_device(h, a, up)),
            lambda: (part.at[chunk, a, down], from4.at[chunk, 1], plane_device(h, a, down)),
            lambda: (both.at[section, chunk], both.at[section, chunk], other),
        ][step]()
        return pltpu.make_async_remote_copy(
            src_ref=source,
            dst_ref=target,
            send_sem=send_sem.at[chunk, step],
            recv_sem=recv_sem.at[chunk, step],
            device_id=device,
            device_id_type=MESH,
        )

    def arrive(t, h, steps):
        for step in steps:
            copy(t, h, step).wait_recv()

    def multiply(t):
        for h in range(2):
            weight_copy(t, h, 0).wait()
            weight_copy(t, h, 1).wait()
            lower = jnp.dot(
                heads[...], weight_buf[:, pl.ds(lower_start(t, h), WIDE)],
                preferred_element_type=jnp.float32,
            )
            upper = jnp.dot(
                heads[...], weight_buf[:, pl.ds(upper_start(t, h), WIDE)],
                preferred_element_type=jnp.float32,
            )
            for i in range(SIDE * SIDE):
                rows = slice(OWN * i, OWN * (i + 1))
                a, b = (i // SIDE, i % SIDE) if h == 0 else (i % SIDE, i // SIDE)
                part[2 * t + h, a, b] = stacked(lower[rows], upper[rows]).astype(jnp.bfloat16)
            copy(t, h, 0).start()
            copy(t, h, 1).start()

    def near_first(t):
        for h in range(2):
            chunk = 2 * t + h
            a = x if h == 0 else y
            right, left = (a + 1) % SIDE, (a + 3) % SIDE
            arrive(t, h, (0, 1))
            part[chunk, right, :, :, :HALF] = (
                wide(part[chunk, right, :, :, :HALF]) + wide(from1[chunk, 0])
            ).astype(jnp.bfloat16)
            copy(t, h, 2).start()
            part[chunk, left, :, :, HALF:] = (
                wide(part[chunk, left, :, :, HALF:]) + wide(from1[chunk, 1])
            ).astype(jnp.bfloat16)
            copy(t, h, 3).start()

    def far_second(t):
        for h in range(2):
            chunk = 2 * t + h
            a = x if h == 0 else y
            arrive(t, h, (2, 3))
            part[chunk, a] = (
                wide(part[chunk, a]) + (wide(from2[chunk, 0]) + wide(from2[chunk, 1]))
            ).astype(jnp.bfloat16)
            copy(t, h, 4).start()
            copy(t, h, 5).start()

    def near_second(t):
        for h in range(2):
            chunk = 2 * t + h
            a, b = (x, y) if h == 0 else (y, x)
            up, down = (b + 1) % SIDE, (b + 3) % SIDE
            arrive(t, h, (4, 5))
            part[chunk, a, up, :, :HALF] = (
                wide(part[chunk, a, up, :, :HALF]) + wide(from3[chunk, 0])
            ).astype(jnp.bfloat16)
            copy(t, h, 6).start()
            part[chunk, a, down, :, HALF:] = (
                wide(part[chunk, a, down, :, HALF:]) + wide(from3[chunk, 1])
            ).astype(jnp.bfloat16)
            copy(t, h, 7).start()

    def finish(t):
        for h in range(2):
            chunk = 2 * t + h
            a, b = (x, y) if h == 0 else (y, x)
            arrive(t, h, (6, 7))
            total = wide(part[chunk, a, b]) + (wide(from4[chunk, 0]) + wide(from4[chunk, 1]))
            stream = stacked(
                wide(residual[:, pl.ds(lower_start(t, h), WIDE)]),
                wide(residual[:, pl.ds(upper_start(t, h), WIDE)]),
            )
            total = total + jnp.where(section == 0, stream, 0.0)
            both[section, chunk] = total.astype(jnp.bfloat16)
            copy(t, h, 8).start()

    stages = (multiply, near_first, far_second, near_second, finish)

    def reduce_turn(n, carry):
        for late, stage in enumerate(stages):

            @pl.when(jnp.logical_and(n >= late, n < PAIRS + late))
            def _():
                stage(n - late)

            if late in (1, 2):

                @pl.when(n == 2 * late + 1)
                def _():
                    each_relay((late,), pass_relay)

        return carry

    lax.fori_loop(0, PAIRS + len(stages) - 1, reduce_turn, 0)

    heads_total[...] = jnp.zeros_like(heads_total)
    grads[...] = jnp.zeros_like(grads)
    zero = jnp.zeros((TALL, 128), jnp.float32)

    def row_mean(total):
        return both_halves(jnp.sum(total, axis=1, keepdims=True)) / (2 * CHUNKS * WIDE)

    def add_sums(t, total):
        for h in range(2):
            copy(t, h, 8).wait_recv()
            total = total + lanes(wide(both[0, 2 * t + h]))
        return total

    mean = row_mean(lax.fori_loop(0, PAIRS, add_sums, zero))

    def add_squares(t, total):
        for h in range(2):
            centred = wide(both[0, 2 * t + h]) - mean
            total = total + lanes(centred * centred)
        return total

    inv_scale = lax.rsqrt(row_mean(lax.fori_loop(0, PAIRS, add_squares, zero)) + EPSILON)

    def gain_rows(t, h):
        return stacked(
            jnp.broadcast_to(gain[:, pl.ds(lower_start(t, h), WIDE)], (OWN, WIDE)),
            jnp.broadcast_to(gain[:, pl.ds(upper_start(t, h), WIDE)], (OWN, WIDE)),
        )

    def add_means(t, totals):
        for h in range(2):
            unit = (wide(both[0, 2 * t + h]) - mean) * inv_scale
            scaled = gain_rows(t, h) * wide(both[1, 2 * t + h])
            totals = (totals[0] + lanes(scaled), totals[1] + lanes(scaled * unit))
        return totals

    sums = lax.fori_loop(0, PAIRS, add_means, (zero, zero))
    mean_scaled, mean_product = row_mean(sums[0]), row_mean(sums[1])

    def gather(p, h, step):
        chunk = 2 * p + h
        a, b = (x, y) if h == 0 else (y, x)
        right, left = (a + 1) % SIDE, (a + 3) % SIDE
        up, down = (b + 1) % SIDE, (b + 3) % SIDE
        low, high = pl.ds(0, HALF), pl.ds(HALF, HALF)
        block, device = [
            lambda: (values.at[chunk, b, a], plane_device(h, right, b)),
            lambda: (values.at[chunk, b, a], plane_device(h, left, b)),
            lambda: (values.at[chunk, b, left, :, low], plane_device(h, right, b)),
            lambda: (values.at[chunk, b, right, :, high], plane_device(h, left, b)),
            lambda: (values.at[chunk, b], plane_device(h, a, up)),
            lambda: (values.at[chunk, b], plane_device(h, a, down)),
            lambda: (values.at[chunk, down, :, :, low], plane_device(h, a, up)),
            lambda: (values.at[chunk, up, :, :, high], plane_device(h, a, down)),
        ][step]()
        return pltpu.make_async_remote_copy(
            src_ref=block,
            dst_ref=block,
            send_sem=gather_send.at[chunk, step],
            recv_sem=gather_recv.at[chunk, step],
            device_id=device,
            device_id_type=MESH,
        )

    def gather_stage(p, waits, starts):
        for h in range(2):
            for step in waits:
                gather(p, h, step).wait_recv()
            for step in starts:
                gather(p, h, step).start()

    def exchanged(target):
        slot = 2 * ((z + SIDE - 1 - target // 2) % SIDE) + core
        a, b = x + core * (y - x), y + core * (x - y)
        return pltpu.make_async_remote_copy(
            src_ref=exchange.at[target],
            dst_ref=values.at[CHUNKS + slot, b, a],
            send_sem=exchange_send.at[target],
            recv_sem=exchange_recv.at[slot],
            device_id={"grp": target},
            device_id_type=MESH,
        )

    def arrived_exchange(slot, h):
        a, b = (x, y) if h == 0 else (y, x)
        return pltpu.make_async_remote_copy(
            src_ref=exchange.at[0],
            dst_ref=values.at[CHUNKS + slot, b, a],
            send_sem=exchange_send.at[0],
            recv_sem=exchange_recv.at[slot],
            device_id=sibling,
            device_id_type=MESH,
        )

    def write(t, carry):
        kept = []
        for h in range(2):
            chunk = 2 * t + h
            a, b = (x, y) if h == 0 else (y, x)
            rows = gain_rows(t, h)
            unit = (wide(both[0, chunk]) - mean) * inv_scale
            d_normed = wide(both[1, chunk])
            normed = unit * rows
            grad = inv_scale * (rows * d_normed - mean_scaled - unit * mean_product)
            value = jnp.where(section == 0, grad, normed)
            values[chunk, b, a] = value.astype(jnp.bfloat16)
            gather(t, h, 0).start()
            gather(t, h, 1).start()
            kept.append(value)
            own_grad[:, pl.ds(lower_start(t, h), WIDE)] = grad[:OWN].astype(jnp.bfloat16)
            own_grad[:, pl.ds(upper_start(t, h), WIDE)] = grad[OWN:].astype(jnp.bfloat16)
            product = d_normed * unit
            gain_own[0, chunk, 0:1] = jnp.sum(product[:OWN], axis=0, keepdims=True)
            gain_own[0, chunk, 1:2] = jnp.sum(product[OWN:], axis=0, keepdims=True)
        for target, rows in ((t, slice(0, OWN)), (GROUPS - 1 - t, slice(OWN, TALL))):
            exchange[target] = stacked(kept[0][rows], kept[1][rows]).astype(jnp.bfloat16)

            @pl.when(target // 2 != z)
            def _():
                exchanged(target).start()
        return carry

    lax.fori_loop(0, PAIRS, write, 0)

    @pl.when(jnp.logical_or(z == 0, z == SIDE - 1))
    def _():
        for j in range(SIDE - 1):
            heads_copy(2 * j + core, heads, sibling).wait_recv()

    for j in range(SIDE - 1):
        passed_heads(j).start()
    own_grad_store = pltpu.make_async_copy(own_grad, grad_out, output_sem.at[0])
    own_grad_store.start()

    gain_partners = [
        {"tp": x * SIDE + y + 1 - 2 * (y % 2)},
        {"tp": x * SIDE + SIDE - 1 - y},
        {"tp": (x + 1 - 2 * (x % 2)) * SIDE + y},
        {"tp": (SIDE - 1 - x) * SIDE + y},
        sibling,
        {"grp": 2 * (z + 1 - 2 * (z % 2)) + core},
        {"grp": 2 * (SIDE - 1 - z) + core},
    ]

    def gain_copy(step):
        return pltpu.make_async_remote_copy(
            src_ref=gain_own.at[step],
            dst_ref=gain_got.at[step],
            send_sem=gain_send.at[step],
            recv_sem=gain_recv.at[step],
            device_id=gain_partners[step],
            device_id_type=MESH,
        )

    def sibling_copy(h):
        return pltpu.make_async_remote_copy(
            src_ref=to_sibling.at[h],
            dst_ref=from_sibling.at[h],
            send_sem=sibling_send.at[h],
            recv_sem=sibling_recv.at[h],
            device_id=sibling,
            device_id_type=MESH,
        )

    rows_dev = heads.shape[0]

    def unpack(p):
        for h in range(2):
            for i in range(0, SIDE * SIDE, 2):
                pair = []
                for at in (i, i + 1):
                    a, b = (at // SIDE, at % SIDE) if h == 0 else (at % SIDE, at // SIDE)
                    pair.append(wide(values[2 * p + h, b, a]))
                rows = slice(h * rows_dev + OWN * i, h * rows_dev + OWN * (i + 2))
                tokens[0, rows] = stacked(pair[0][:OWN], pair[1][:OWN]).astype(jnp.bfloat16)
                tokens[1, rows] = stacked(pair[0][OWN:], pair[1][OWN:]).astype(jnp.bfloat16)

    def add_grads(part_at, token_rows, head_rows):
        grads[part_at * WIDE : (part_at + 1) * WIDE] += grad_scale * lax.dot_general(
            token_rows, head_rows, (((0,), (0,)), ((), ())), preferred_element_type=jnp.float32
        )

    def use_rows(t):
        total = heads_total[...]
        for h in range(2):
            rows = slice(h * rows_dev, (h + 1) * rows_dev)
            for upper in range(2):
                start = upper_start(t, h) if upper else lower_start(t, h)
                total = total + lax.dot_general(
                    tokens[upper, rows], weight_buf[:, pl.ds(start, WIDE)],
                    (((1,), (1,)), ((), ())), preferred_element_type=jnp.float32,
                )
        heads_total[...] = total
        for upper in range(2):
            target = GROUPS - 1 - t if upper else t

            @pl.when(target == group)
            def _():
                for h in range(2):
                    add_grads(h, tokens[upper, h * rows_dev : (h + 1) * rows_dev], heads[...])

            @pl.when(target == 2 * z + 1 - core)
            def _():
                for h in range(2):
                    to_sibling[h] = tokens[upper, h * rows_dev : (h + 1) * rows_dev]
                    sibling_copy(h).start()

    def use_columns(j):
        heads_copy(2 * j + 1 - core, heads, sibling).wait_recv()
        head_rows = heads_all[pl.ds(2 * j, 2)].reshape(2 * rows_dev, -1)
        for upper in range(2):
            add_grads(upper, tokens[upper], head_rows)

    def use_sibling():
        heads_copy(GATHERS - 1, heads, sibling).wait_recv()
        for h in range(2):
            sibling_copy(h).wait_recv()
            add_grads(h, from_sibling[h], heads_all[GATHERS - 1])

    heads_store = pltpu.make_async_copy(heads_done, heads_out, output_sem.at[1])
    gain_store = pltpu.make_async_copy(gain_done, gain_out, output_sem.at[2])

    def inside(p, first=0):
        return jnp.logical_and(p >= first, p < GATHERS)

    def turn(n, carry):
        for step in range(len(gain_partners) + 1):

            @pl.when(n == step + 1)
            def _():
                if step > 0:
                    gain_copy(step - 1).wait_recv()
                    gain_own[step] = gain_own[step - 1] + gain_got[step - 1]
                if step < len(gain_partners):
                    gain_copy(step).start()

        @pl.when(inside(n, PAIRS))
        def _():
            for h in range(2):
                arrived_exchange(2 * (n - PAIRS) + h, h).wait_recv()
            gather_stage(n, (), (0, 1))

        @pl.when(inside(n - 1))
        def _():
            gather_stage(n - 1, (0, 1), (2, 3))

        @pl.when(inside(n - 2))
        def _():
            gather_stage(n - 2, (2, 3), (4, 5))

        @pl.when(inside(n - 3))
        def _():
            gather_stage(n - 3, (4, 5), (6, 7))

        @pl.when(inside(n - 4))
        def _():
            gather_stage(n - 4, (6, 7), ())
            unpack(n - 4)

            @pl.when(n - 4 < PAIRS)
            def _():
                use_rows(n - 4)

            @pl.when(n - 4 >= PAIRS)
            def _():
                use_columns(n - 4 - PAIRS)

            @pl.when(n - 4 == PAIRS)
            def _():
                use_sibling()
                heads_done[...] = heads_total[...].astype(jnp.bfloat16)
                heads_store.start()
                for t in range(PAIRS):
                    for h in range(2):
                        total = gain_own[len(gain_partners), 2 * t + h] * grad_scale
                        gain_done[:, pl.ds(lower_start(t, h), WIDE)] = total[0:1]
                        gain_done[:, pl.ds(upper_start(t, h), WIDE)] = total[1:2]
                gain_store.start()

        return carry

    lax.fori_loop(1, GATHERS + 4, turn, 0)
    grads_store = pltpu.make_async_copy(grads, grads_out, output_sem.at[3])
    grads_store.start()

    def sent(t, carry):
        for h in range(2):
            for step in range(9):
                copy(t, h, step).wait_send()
            target = t + h * (GROUPS - 1 - 2 * t)

            @pl.when(target // 2 != z)
            def _():
                exchanged(target).wait_send()
        return carry

    lax.fori_loop(0, PAIRS, sent, 0)

    def sent_gathers(p, carry):
        for h in range(2):
            for step in range(8):
                gather(p, h, step).wait_send()
        return carry

    lax.fori_loop(0, GATHERS, sent_gathers, 0)
    each_relay((0, 1, 2), lambda relay, slot: relay.wait_send())
    for j in range(SIDE - 1):
        passed_heads(j).wait_send()
    heads_copy(GATHERS - 1, heads, sibling).wait_send()
    for h in range(2):
        sibling_copy(h).wait_send()
    for step in range(len(gain_partners)):
        gain_copy(step).wait_send()
    for store in (own_grad_store, heads_store, gain_store, grads_store):
        store.wait()


def deliver_kernel(*refs):
    copies = [
        pltpu.make_async_copy(refs[at], refs[4 + at], refs[8].at[at]) for at in range(4)
    ]
    for copy in copies:
        copy.start()
    for copy in copies:
        copy.wait()


def delivered(results):
    hbm = pl.BlockSpec(memory_space=pl.ANY)
    return pl.pallas_call(
        deliver_kernel,
        out_shape=tuple(jax.ShapeDtypeStruct(result.shape, result.dtype) for result in results),
        in_specs=[hbm] * 4,
        out_specs=(hbm,) * 4,
        scratch_shapes=[pltpu.SemaphoreType.DMA((4,))],
        name="deliver",
    )(*results)


def fused(heads, weights, residual, gain):
    hbm = pl.BlockSpec(memory_space=pl.ANY)
    bf16, f32 = jnp.bfloat16, jnp.float32
    rows_dev, depth = heads.shape
    owned = weights.shape[1] // GROUPS
    dma = pltpu.SemaphoreType.DMA
    return pl.pallas_call(
        boundary_kernel,
        out_shape=(
            jax.ShapeDtypeStruct(heads.shape, bf16),
            jax.ShapeDtypeStruct((owned, depth), f32),
            jax.ShapeDtypeStruct(residual.shape, bf16),
            jax.ShapeDtypeStruct(gain.shape, f32),
        ),
        in_specs=[hbm] * 4,
        out_specs=(hbm,) * 4,
        scratch_shapes=[
            pltpu.VMEM(heads.shape, bf16),
            pltpu.VMEM(residual.shape, bf16),
            pltpu.VMEM(gain.shape, f32),
            pltpu.VMEM(heads.shape, bf16),
            pltpu.VMEM((owned, depth), f32),
            pltpu.VMEM(residual.shape, bf16),
            pltpu.VMEM(gain.shape, f32),
            pltpu.VMEM(weights.shape, bf16),
            pltpu.VMEM((CHUNKS, SIDE, SIDE, TALL, WIDE), bf16),
            pltpu.VMEM((CHUNKS, 2, SIDE, TALL, HALF), bf16),
            pltpu.VMEM((CHUNKS, 2, SIDE, TALL, WIDE), bf16),
            pltpu.VMEM((CHUNKS, 2, TALL, HALF), bf16),
            pltpu.VMEM((CHUNKS, 2, TALL, WIDE), bf16),
            pltpu.VMEM((2, CHUNKS, TALL, WIDE), bf16),
            pltpu.VMEM((2 * GATHERS, SIDE, SIDE, TALL, WIDE), bf16),
            pltpu.VMEM((GROUPS, TALL, WIDE), bf16),
            pltpu.VMEM((2, 2 * rows_dev, WIDE), bf16),
            pltpu.VMEM((2, rows_dev, WIDE), bf16),
            pltpu.VMEM((2, rows_dev, WIDE), bf16),
            pltpu.VMEM((GATHERS, rows_dev, depth), bf16),
            pltpu.VMEM((rows_dev, depth), f32),
            pltpu.VMEM((8, CHUNKS, 2, WIDE), f32),
            pltpu.VMEM((7, CHUNKS, 2, WIDE), f32),
            dma((3,)),
            dma((4,)),
            dma((CHUNKS, 2)),
            dma((CHUNKS, 9)),
            dma((CHUNKS, 9)),
            dma((2 * GATHERS, 8)),
            dma((2 * GATHERS, 8)),
            dma((GROUPS,)),
            dma((GROUPS - 2,)),
            dma((GATHERS + 6,)),
            dma((GATHERS,)),
            dma((2,)),
            dma((2,)),
            dma((7,)),
            dma((7,)),
        ],
        compiler_params=pltpu.CompilerParams(
            collective_id=0, has_side_effects=True, vmem_limit_bytes=60 * 1024 * 1024
        ),
        name="boundary",
    )(heads, weights, residual, gain)


def per_device(heads_in, weights, residual, norm_gain):
    heads_out, weight_grad, boundary_grad, gain_grad = delivered(
        fused(heads_in[0], weights[0], residual, norm_gain[None])
    )
    return (heads_out[None], weight_grad[None], boundary_grad, gain_grad[0])


def solution(mesh):
    placed = (P("section", "grp", "tp"), P("section", "tp", None), P(("grp", "tp"), None), P())
    return jax.shard_map(
        per_device,
        mesh=mesh,
        in_specs=placed,
        out_specs=(
            P("section", "grp", "tp"),
            P("section", "grp", "tp"),
            P(("grp", "tp"), None),
            P(),
        ),
        check_vma=False,
    )
```

```python
import math

import jax
import jax.numpy as jnp
from jax import lax
from jax.experimental import pallas as pl
from jax.experimental.pallas import tpu as pltpu
from jax.sharding import PartitionSpec as P

EPSILON = 1e-05
MESH = pl.DeviceIdType.MESH

SIDE = 4
GATHERS = 7
GROUPS = 8

PAIRS = 4
CHUNKS = 2 * PAIRS
WIDE = 512
HALF = WIDE // 2
OWN = 24
TALL = 2 * OWN


def lower_start(t, h):
    return pl.multiple_of((2 * t + h) * WIDE, WIDE)


def upper_start(t, h):
    return pl.multiple_of((2 * (2 * PAIRS - 1 - t) + h) * WIDE, WIDE)


def place_on_plane():
    tp = lax.axis_index("tp")
    return tp // SIDE, tp % SIDE


def plane_device(h, first, second):
    x, y = (first, second) if h == 0 else (second, first)
    return {"tp": x * SIDE + y}


def stacked(lower, upper):
    return jnp.concatenate([lower, upper], axis=0)


def both_halves(row_pair):
    total = row_pair[:OWN] + row_pair[OWN:]
    return stacked(total, total)


def lanes(value):
    return sum(value[:, 128 * i : 128 * (i + 1)] for i in range(value.shape[1] // 128))


def wide(value):
    return value.astype(jnp.float32)


def greet(peers):
    barrier = pltpu.get_barrier_semaphore()
    for peer in peers:
        pl.semaphore_signal(barrier, inc=1, device_id=peer, device_id_type=MESH)
    pl.semaphore_wait(barrier, len(peers))


def plane_neighbours(x, y):
    return [
        {"tp": ((x + 1) % SIDE) * SIDE + y},
        {"tp": ((x + 3) % SIDE) * SIDE + y},
        {"tp": x * SIDE + (y + 1) % SIDE},
        {"tp": x * SIDE + (y + 3) % SIDE},
    ]


def boundary_kernel(
    heads_in, weights, residual_in, gain_in, heads_out, grads_out, grad_out, gain_out,
    heads, residual, gain, heads_done, grads, own_grad, gain_done, weight_buf, part, from1, from2, from3, from4, both,
    values, exchange, tokens, to_sibling, from_sibling, heads_all, heads_total, gain_own, gain_got,
    input_sem, output_sem, weight_sem, send_sem, recv_sem, gather_send, gather_recv, exchange_send, exchange_recv,
    heads_send, heads_recv, sibling_send, sibling_recv, gain_send, gain_recv,
):
    x, y = place_on_plane()
    section = lax.axis_index("section")
    other = {"section": 1 - section}
    group = lax.axis_index("grp")
    z, core = group // 2, group % 2
    sibling = {"grp": 2 * z + 1 - core}
    grad_scale = 1.0 / math.sqrt(heads.shape[0] * GROUPS)

    def weight_copy(t, h, upper):
        start = upper_start(t, h) if upper else lower_start(t, h)
        cols = pl.ds(start, WIDE)
        return pltpu.make_async_copy(
            weights.at[:, cols], weight_buf.at[:, cols], weight_sem.at[2 * t + h, upper]
        )

    def start_weights(t, carry):
        for h in range(2):
            for upper in range(2):
                weight_copy(t, h, upper).start()
        return carry

    heads_load = pltpu.make_async_copy(heads_in, heads, input_sem.at[0])
    gain_load = pltpu.make_async_copy(gain_in, gain, input_sem.at[1])
    residual_load = pltpu.make_async_copy(residual_in, residual, input_sem.at[2])
    heads_load.start()
    lax.fori_loop(0, PAIRS, start_weights, 0)
    residual_load.start()
    gain_load.start()
    far_groups = [{"grp": 2 * ((z + hop) % SIDE) + k} for hop in range(1, SIDE) for k in range(2)]
    greet(plane_neighbours(x, y) + [other, sibling] + far_groups)
    heads_load.wait()
    residual_load.wait()
    gain_load.wait()

    def heads_copy(slot, source, device):
        return pltpu.make_async_remote_copy(
            src_ref=source,
            dst_ref=heads_all.at[slot],
            send_sem=heads_send.at[slot],
            recv_sem=heads_recv.at[slot],
            device_id=device,
            device_id_type=MESH,
        )

    def slot_of(origin, at):
        return 2 * ((origin + SIDE - 1 - at) % SIDE) + core

    def relayed_heads(origin, target, source, at):
        return pltpu.make_async_remote_copy(
            src_ref=source,
            dst_ref=heads_all.at[slot_of(origin, target)],
            send_sem=heads_send.at[GATHERS + at],
            recv_sem=heads_recv.at[slot_of(origin, target)],
            device_id={"grp": 2 * target + core},
            device_id_type=MESH,
        )

    relays = ((1, 0), (-1, 0), (1, 1), (-1, 1), (1, 2), (-1, 2))

    def each_relay(wanted, act):
        for at, (step, away) in enumerate(relays):
            if away not in wanted:
                continue
            first, last = (away, SIDE - 2) if step > 0 else (1, SIDE - 1 - away)

            @pl.when(jnp.logical_and(z >= first, z <= last))
            def _():
                origin = z - step * away
                source = heads_all.at[slot_of(origin, z)] if away else heads
                act(relayed_heads(origin, z + step, source, at), slot_of(origin, z))

    def start_relay(relay, slot):
        relay.start()

    def pass_relay(relay, slot):
        heads_copy(slot, heads, sibling).wait_recv()
        relay.start()

    def passed_heads(j):
        slot = 2 * j + core
        return pltpu.make_async_remote_copy(
            src_ref=heads_all.at[slot],
            dst_ref=heads_all.at[slot],
            send_sem=heads_send.at[slot],
            recv_sem=heads_recv.at[slot],
            device_id=sibling,
            device_id_type=MESH,
        )

    each_relay((0,), start_relay)
    heads_copy(GATHERS - 1, heads, sibling).start()

    def copy(t, h, step):
        chunk = 2 * t + h
        a, b = (x, y) if h == 0 else (y, x)
        right, left = (a + 1) % SIDE, (a + 3) % SIDE
        up, down = (b + 1) % SIDE, (b + 3) % SIDE
        low, high = pl.ds(0, HALF), pl.ds(HALF, HALF)
        far_a, far_b = (a + 2) % SIDE, (b + 2) % SIDE
        source, target, device = [
            lambda: (part.at[chunk, far_a, :, :, low], from1.at[chunk, 0], plane_device(h, right, b)),
            lambda: (part.at[chunk, far_a, :, :, high], from1.at[chunk, 1], plane_device(h, left, b)),
            lambda: (part.at[chunk, right], from2.at[chunk, 0], plane_device(h, right, b)),
            lambda: (part.at[chunk, left], from2.at[chunk, 1], plane_device(h, left, b)),
            lambda: (part.at[chunk, a, far_b, :, low], from3.at[chunk, 0], plane_device(h, a, up)),
            lambda: (part.at[chunk, a, far_b, :, high], from3.at[chunk, 1], plane_device(h, a, down)),
            lambda: (part.at[chunk, a, up], from4.at[chunk, 0], plane_device(h, a, up)),
            lambda: (part.at[chunk, a, down], from4.at[chunk, 1], plane_device(h, a, down)),
            lambda: (both.at[section, chunk], both.at[section, chunk], other),
        ][step]()
        return pltpu.make_async_remote_copy(
            src_ref=source,
            dst_ref=target,
            send_sem=send_sem.at[chunk, step],
            recv_sem=recv_sem.at[chunk, step],
            device_id=device,
            device_id_type=MESH,
        )

    def arrive(t, h, steps):
        for step in steps:
            copy(t, h, step).wait_recv()

    def multiply(t):
        for h in range(2):
            weight_copy(t, h, 0).wait()
            weight_copy(t, h, 1).wait()
            lower = jnp.dot(
                heads[...], weight_buf[:, pl.ds(lower_start(t, h), WIDE)],
                preferred_element_type=jnp.float32,
            )
            upper = jnp.dot(
                heads[...], weight_buf[:, pl.ds(upper_start(t, h), WIDE)],
                preferred_element_type=jnp.float32,
            )
            for i in range(SIDE * SIDE):
                rows = slice(OWN * i, OWN * (i + 1))
                a, b = (i // SIDE, i % SIDE) if h == 0 else (i % SIDE, i // SIDE)
                part[2 * t + h, a, b] = stacked(lower[rows], upper[rows]).astype(jnp.bfloat16)
            copy(t, h, 0).start()
            copy(t, h, 1).start()

    def near_first(t):
        for h in range(2):
            chunk = 2 * t + h
            a = x if h == 0 else y
            right, left = (a + 1) % SIDE, (a + 3) % SIDE
            arrive(t, h, (0, 1))
            part[chunk, right, :, :, :HALF] = (
                wide(part[chunk, right, :, :, :HALF]) + wide(from1[chunk, 0])
            ).astype(jnp.bfloat16)
            copy(t, h, 2).start()
            part[chunk, left, :, :, HALF:] = (
                wide(part[chunk, left, :, :, HALF:]) + wide(from1[chunk, 1])
            ).astype(jnp.bfloat16)
            copy(t, h, 3).start()

    def far_second(t):
        for h in range(2):
            chunk = 2 * t + h
            a = x if h == 0 else y
            arrive(t, h, (2, 3))
            part[chunk, a] = (
                wide(part[chunk, a]) + (wide(from2[chunk, 0]) + wide(from2[chunk, 1]))
            ).astype(jnp.bfloat16)
            copy(t, h, 4).start()
            copy(t, h, 5).start()

    def near_second(t):
        for h in range(2):
            chunk = 2 * t + h
            a, b = (x, y) if h == 0 else (y, x)
            up, down = (b + 1) % SIDE, (b + 3) % SIDE
            arrive(t, h, (4, 5))
            part[chunk, a, up, :, :HALF] = (
                wide(part[chunk, a, up, :, :HALF]) + wide(from3[chunk, 0])
            ).astype(jnp.bfloat16)
            copy(t, h, 6).start()
            part[chunk, a, down, :, HALF:] = (
                wide(part[chunk, a, down, :, HALF:]) + wide(from3[chunk, 1])
            ).astype(jnp.bfloat16)
            copy(t, h, 7).start()

    def finish(t):
        for h in range(2):
            chunk = 2 * t + h
            a, b = (x, y) if h == 0 else (y, x)
            arrive(t, h, (6, 7))
            total = wide(part[chunk, a, b]) + (wide(from4[chunk, 0]) + wide(from4[chunk, 1]))
            stream = stacked(
                wide(residual[:, pl.ds(lower_start(t, h), WIDE)]),
                wide(residual[:, pl.ds(upper_start(t, h), WIDE)]),
            )
            total = total + jnp.where(section == 0, stream, 0.0)
            both[section, chunk] = total.astype(jnp.bfloat16)
            copy(t, h, 8).start()

    stages = (multiply, near_first, far_second, near_second, finish)

    def reduce_turn(n, carry):
        for late, stage in enumerate(stages):

            @pl.when(jnp.logical_and(n >= late, n < PAIRS + late))
            def _():
                stage(n - late)

        return carry

    lax.fori_loop(0, PAIRS + len(stages) - 1, reduce_turn, 0)

    heads_total[...] = jnp.zeros_like(heads_total)
    grads[...] = jnp.zeros_like(grads)
    zero = jnp.zeros((TALL, 128), jnp.float32)

    def row_mean(total):
        return both_halves(jnp.sum(total, axis=1, keepdims=True)) / (2 * CHUNKS * WIDE)

    def add_sums(t, total):
        for h in range(2):
            copy(t, h, 8).wait_recv()
            total = total + lanes(wide(both[0, 2 * t + h]))
        return total

    mean = row_mean(lax.fori_loop(0, PAIRS, add_sums, zero))

    def add_squares(t, total):
        for h in range(2):
            centred = wide(both[0, 2 * t + h]) - mean
            total = total + lanes(centred * centred)
        return total

    inv_scale = lax.rsqrt(row_mean(lax.fori_loop(0, PAIRS, add_squares, zero)) + EPSILON)

    def gain_rows(t, h):
        return stacked(
            jnp.broadcast_to(gain[:, pl.ds(lower_start(t, h), WIDE)], (OWN, WIDE)),
            jnp.broadcast_to(gain[:, pl.ds(upper_start(t, h), WIDE)], (OWN, WIDE)),
        )

    def add_means(t, totals):
        for h in range(2):
            unit = (wide(both[0, 2 * t + h]) - mean) * inv_scale
            scaled = gain_rows(t, h) * wide(both[1, 2 * t + h])
            totals = (totals[0] + lanes(scaled), totals[1] + lanes(scaled * unit))
        return totals

    sums = lax.fori_loop(0, PAIRS, add_means, (zero, zero))
    mean_scaled, mean_product = row_mean(sums[0]), row_mean(sums[1])

    def gather(p, h, step):
        chunk = 2 * p + h
        a, b = (x, y) if h == 0 else (y, x)
        right, left = (a + 1) % SIDE, (a + 3) % SIDE
        up, down = (b + 1) % SIDE, (b + 3) % SIDE
        low, high = pl.ds(0, HALF), pl.ds(HALF, HALF)
        block, device = [
            lambda: (values.at[chunk, b, a], plane_device(h, right, b)),
            lambda: (values.at[chunk, b, a], plane_device(h, left, b)),
            lambda: (values.at[chunk, b, left, :, low], plane_device(h, right, b)),
            lambda: (values.at[chunk, b, right, :, high], plane_device(h, left, b)),
            lambda: (values.at[chunk, b], plane_device(h, a, up)),
            lambda: (values.at[chunk, b], plane_device(h, a, down)),
            lambda: (values.at[chunk, down, :, :, low], plane_device(h, a, up)),
            lambda: (values.at[chunk, up, :, :, high], plane_device(h, a, down)),
        ][step]()
        return pltpu.make_async_remote_copy(
            src_ref=block,
            dst_ref=block,
            send_sem=gather_send.at[chunk, step],
            recv_sem=gather_recv.at[chunk, step],
            device_id=device,
            device_id_type=MESH,
        )

    def gather_stage(p, waits, starts):
        for h in range(2):
            for step in waits:
                gather(p, h, step).wait_recv()
            for step in starts:
                gather(p, h, step).start()

    def exchanged(target):
        slot = 2 * ((z + SIDE - 1 - target // 2) % SIDE) + core
        a, b = x + core * (y - x), y + core * (x - y)
        return pltpu.make_async_remote_copy(
            src_ref=exchange.at[target],
            dst_ref=values.at[CHUNKS + slot, b, a],
            send_sem=exchange_send.at[target],
            recv_sem=exchange_recv.at[slot],
            device_id={"grp": target},
            device_id_type=MESH,
        )

    def arrived_exchange(slot, h):
        a, b = (x, y) if h == 0 else (y, x)
        return pltpu.make_async_remote_copy(
            src_ref=exchange.at[0],
            dst_ref=values.at[CHUNKS + slot, b, a],
            send_sem=exchange_send.at[0],
            recv_sem=exchange_recv.at[slot],
            device_id=sibling,
            device_id_type=MESH,
        )

    def write(t, carry):
        kept = []
        for h in range(2):
            chunk = 2 * t + h
            a, b = (x, y) if h == 0 else (y, x)
            rows = gain_rows(t, h)
            unit = (wide(both[0, chunk]) - mean) * inv_scale
            d_normed = wide(both[1, chunk])
            normed = unit * rows
            grad = inv_scale * (rows * d_normed - mean_scaled - unit * mean_product)
            value = jnp.where(section == 0, grad, normed)
            values[chunk, b, a] = value.astype(jnp.bfloat16)
            gather(t, h, 0).start()
            gather(t, h, 1).start()
            kept.append(value)
            own_grad[:, pl.ds(lower_start(t, h), WIDE)] = grad[:OWN].astype(jnp.bfloat16)
            own_grad[:, pl.ds(upper_start(t, h), WIDE)] = grad[OWN:].astype(jnp.bfloat16)
            product = d_normed * unit
            gain_own[0, chunk, 0:1] = jnp.sum(product[:OWN], axis=0, keepdims=True)
            gain_own[0, chunk, 1:2] = jnp.sum(product[OWN:], axis=0, keepdims=True)
        for target, rows in ((t, slice(0, OWN)), (GROUPS - 1 - t, slice(OWN, TALL))):
            exchange[target] = stacked(kept[0][rows], kept[1][rows]).astype(jnp.bfloat16)

            @pl.when(target // 2 != z)
            def _():
                exchanged(target).start()
        return carry

    lax.fori_loop(0, PAIRS, write, 0)

    each_relay((1,), pass_relay)
    own_grad_store = pltpu.make_async_copy(own_grad, grad_out, output_sem.at[0])
    own_grad_store.start()

    gain_partners = [
        {"tp": x * SIDE + y + 1 - 2 * (y % 2)},
        {"tp": x * SIDE + SIDE - 1 - y},
        {"tp": (x + 1 - 2 * (x % 2)) * SIDE + y},
        {"tp": (SIDE - 1 - x) * SIDE + y},
        sibling,
        {"grp": 2 * (z + 1 - 2 * (z % 2)) + core},
        {"grp": 2 * (SIDE - 1 - z) + core},
    ]

    def gain_copy(step):
        return pltpu.make_async_remote_copy(
            src_ref=gain_own.at[step],
            dst_ref=gain_got.at[step],
            send_sem=gain_send.at[step],
            recv_sem=gain_recv.at[step],
            device_id=gain_partners[step],
            device_id_type=MESH,
        )

    def sibling_copy(h):
        return pltpu.make_async_remote_copy(
            src_ref=to_sibling.at[h],
            dst_ref=from_sibling.at[h],
            send_sem=sibling_send.at[h],
            recv_sem=sibling_recv.at[h],
            device_id=sibling,
            device_id_type=MESH,
        )

    rows_dev = heads.shape[0]

    def unpack(p):
        for h in range(2):
            for i in range(0, SIDE * SIDE, 2):
                pair = []
                for at in (i, i + 1):
                    a, b = (at // SIDE, at % SIDE) if h == 0 else (at % SIDE, at // SIDE)
                    pair.append(wide(values[2 * p + h, b, a]))
                rows = slice(h * rows_dev + OWN * i, h * rows_dev + OWN * (i + 2))
                tokens[0, rows] = stacked(pair[0][:OWN], pair[1][:OWN]).astype(jnp.bfloat16)
                tokens[1, rows] = stacked(pair[0][OWN:], pair[1][OWN:]).astype(jnp.bfloat16)

    def add_grads(part_at, token_rows, head_rows):
        grads[part_at * WIDE : (part_at + 1) * WIDE] += grad_scale * lax.dot_general(
            token_rows, head_rows, (((0,), (0,)), ((), ())), preferred_element_type=jnp.float32
        )

    def use_rows(t):
        total = heads_total[...]
        for h in range(2):
            rows = slice(h * rows_dev, (h + 1) * rows_dev)
            for upper in range(2):
                start = upper_start(t, h) if upper else lower_start(t, h)
                total = total + lax.dot_general(
                    tokens[upper, rows], weight_buf[:, pl.ds(start, WIDE)],
                    (((1,), (1,)), ((), ())), preferred_element_type=jnp.float32,
                )
        heads_total[...] = total
        for upper in range(2):
            target = GROUPS - 1 - t if upper else t

            @pl.when(target == group)
            def _():
                for h in range(2):
                    add_grads(h, tokens[upper, h * rows_dev : (h + 1) * rows_dev], heads[...])

            @pl.when(target == 2 * z + 1 - core)
            def _():
                for h in range(2):
                    to_sibling[h] = tokens[upper, h * rows_dev : (h + 1) * rows_dev]
                    sibling_copy(h).start()

    def use_columns(j):
        heads_copy(2 * j + 1 - core, heads, sibling).wait_recv()
        head_rows = heads_all[pl.ds(2 * j, 2)].reshape(2 * rows_dev, -1)
        for upper in range(2):
            add_grads(upper, tokens[upper], head_rows)

    def use_sibling():
        heads_copy(GATHERS - 1, heads, sibling).wait_recv()
        for h in range(2):
            sibling_copy(h).wait_recv()
            add_grads(h, from_sibling[h], heads_all[GATHERS - 1])

    def pass_heads():
        @pl.when(jnp.logical_or(z == 0, z == SIDE - 1))
        def _():
            for j in range(SIDE - 1):
                heads_copy(2 * j + core, heads, sibling).wait_recv()

        for j in range(SIDE - 1):
            passed_heads(j).start()

    heads_store = pltpu.make_async_copy(heads_done, heads_out, output_sem.at[1])
    gain_store = pltpu.make_async_copy(gain_done, gain_out, output_sem.at[2])

    def inside(p, first=0):
        return jnp.logical_and(p >= first, p < GATHERS)

    def turn(n, carry):
        for step in range(len(gain_partners) + 1):

            @pl.when(n == step + 1)
            def _():
                if step > 0:
                    gain_copy(step - 1).wait_recv()
                    gain_own[step] = gain_own[step - 1] + gain_got[step - 1]
                if step < len(gain_partners):
                    gain_copy(step).start()

        @pl.when(n == 5)
        def _():
            each_relay((2,), pass_relay)

        @pl.when(n == 7)
        def _():
            pass_heads()

        @pl.when(inside(n, PAIRS))
        def _():
            for h in range(2):
                arrived_exchange(2 * (n - PAIRS) + h, h).wait_recv()
            gather_stage(n, (), (0, 1))

        @pl.when(inside(n - 1))
        def _():
            gather_stage(n - 1, (0, 1), (2, 3))

        @pl.when(inside(n - 2))
        def _():
            gather_stage(n - 2, (2, 3), (4, 5))

        @pl.when(inside(n - 3))
        def _():
            gather_stage(n - 3, (4, 5), (6, 7))

        @pl.when(inside(n - 4))
        def _():
            gather_stage(n - 4, (6, 7), ())
            unpack(n - 4)

            @pl.when(n - 4 < PAIRS)
            def _():
                use_rows(n - 4)

            @pl.when(n - 4 >= PAIRS)
            def _():
                use_columns(n - 4 - PAIRS)

            @pl.when(n - 4 == PAIRS)
            def _():
                use_sibling()
                heads_done[...] = heads_total[...].astype(jnp.bfloat16)
                heads_store.start()
                for t in range(PAIRS):
                    for h in range(2):
                        total = gain_own[len(gain_partners), 2 * t + h] * grad_scale
                        gain_done[:, pl.ds(lower_start(t, h), WIDE)] = total[0:1]
                        gain_done[:, pl.ds(upper_start(t, h), WIDE)] = total[1:2]
                gain_store.start()

        return carry

    lax.fori_loop(1, GATHERS + 4, turn, 0)
    grads_store = pltpu.make_async_copy(grads, grads_out, output_sem.at[3])
    grads_store.start()

    def sent(t, carry):
        for h in range(2):
            for step in range(9):
                copy(t, h, step).wait_send()
            target = t + h * (GROUPS - 1 - 2 * t)

            @pl.when(target // 2 != z)
            def _():
                exchanged(target).wait_send()
        return carry

    lax.fori_loop(0, PAIRS, sent, 0)

    def sent_gathers(p, carry):
        for h in range(2):
            for step in range(8):
                gather(p, h, step).wait_send()
        return carry

    lax.fori_loop(0, GATHERS, sent_gathers, 0)
    each_relay((0, 1, 2), lambda relay, slot: relay.wait_send())
    for j in range(SIDE - 1):
        passed_heads(j).wait_send()
    heads_copy(GATHERS - 1, heads, sibling).wait_send()
    for h in range(2):
        sibling_copy(h).wait_send()
    for step in range(len(gain_partners)):
        gain_copy(step).wait_send()
    for store in (own_grad_store, heads_store, gain_store, grads_store):
        store.wait()


def deliver_kernel(*refs):
    results, outputs, held = refs[:4], refs[4:8], refs[8:12]
    load_sem, store_sem = refs[12:]
    loads = [pltpu.make_async_copy(results[at], held[at], load_sem.at[at]) for at in range(4)]
    stores = [pltpu.make_async_copy(held[at], outputs[at], store_sem.at[at]) for at in range(4)]
    for load in loads:
        load.start()
    for load, store in zip(loads, stores):
        load.wait()
        store.start()
    for store in stores:
        store.wait()


def delivered(results):
    hbm = pl.BlockSpec(memory_space=pl.ANY)
    return pl.pallas_call(
        deliver_kernel,
        out_shape=tuple(jax.ShapeDtypeStruct(result.shape, result.dtype) for result in results),
        in_specs=[hbm] * 4,
        out_specs=(hbm,) * 4,
        scratch_shapes=[pltpu.VMEM(result.shape, result.dtype) for result in results]
        + [pltpu.SemaphoreType.DMA((4,))] * 2,
        name="deliver",
    )(*results)


def fused(heads, weights, residual, gain):
    hbm = pl.BlockSpec(memory_space=pl.ANY)
    bf16, f32 = jnp.bfloat16, jnp.float32
    rows_dev, depth = heads.shape
    owned = weights.shape[1] // GROUPS
    dma = pltpu.SemaphoreType.DMA
    return pl.pallas_call(
        boundary_kernel,
        out_shape=(
            jax.ShapeDtypeStruct(heads.shape, bf16),
            jax.ShapeDtypeStruct((owned, depth), f32),
            jax.ShapeDtypeStruct(residual.shape, bf16),
            jax.ShapeDtypeStruct(gain.shape, f32),
        ),
        in_specs=[hbm] * 4,
        out_specs=(hbm,) * 4,
        scratch_shapes=[
            pltpu.VMEM(heads.shape, bf16),
            pltpu.VMEM(residual.shape, bf16),
            pltpu.VMEM(gain.shape, f32),
            pltpu.VMEM(heads.shape, bf16),
            pltpu.VMEM((owned, depth), f32),
            pltpu.VMEM(residual.shape, bf16),
            pltpu.VMEM(gain.shape, f32),
            pltpu.VMEM(weights.shape, bf16),
            pltpu.VMEM((CHUNKS, SIDE, SIDE, TALL, WIDE), bf16),
            pltpu.VMEM((CHUNKS, 2, SIDE, TALL, HALF), bf16),
            pltpu.VMEM((CHUNKS, 2, SIDE, TALL, WIDE), bf16),
            pltpu.VMEM((CHUNKS, 2, TALL, HALF), bf16),
            pltpu.VMEM((CHUNKS, 2, TALL, WIDE), bf16),
            pltpu.VMEM((2, CHUNKS, TALL, WIDE), bf16),
            pltpu.VMEM((2 * GATHERS, SIDE, SIDE, TALL, WIDE), bf16),
            pltpu.VMEM((GROUPS, TALL, WIDE), bf16),
            pltpu.VMEM((2, 2 * rows_dev, WIDE), bf16),
            pltpu.VMEM((2, rows_dev, WIDE), bf16),
            pltpu.VMEM((2, rows_dev, WIDE), bf16),
            pltpu.VMEM((GATHERS, rows_dev, depth), bf16),
            pltpu.VMEM((rows_dev, depth), f32),
            pltpu.VMEM((8, CHUNKS, 2, WIDE), f32),
            pltpu.VMEM((7, CHUNKS, 2, WIDE), f32),
            dma((3,)),
            dma((4,)),
            dma((CHUNKS, 2)),
            dma((CHUNKS, 9)),
            dma((CHUNKS, 9)),
            dma((2 * GATHERS, 8)),
            dma((2 * GATHERS, 8)),
            dma((GROUPS,)),
            dma((GROUPS - 2,)),
            dma((GATHERS + 6,)),
            dma((GATHERS,)),
            dma((2,)),
            dma((2,)),
            dma((7,)),
            dma((7,)),
        ],
        compiler_params=pltpu.CompilerParams(
            collective_id=0, has_side_effects=True, vmem_limit_bytes=60 * 1024 * 1024
        ),
        name="boundary",
    )(heads, weights, residual, gain)


def per_device(heads_in, weights, residual, norm_gain):
    heads_out, weight_grad, boundary_grad, gain_grad = delivered(
        fused(heads_in[0], weights[0], residual, norm_gain[None])
    )
    return (heads_out[None], weight_grad[None], boundary_grad, gain_grad[0])


def solution(mesh):
    placed = (P("section", "grp", "tp"), P("section", "tp", None), P(("grp", "tp"), None), P())
    return jax.shard_map(
        per_device,
        mesh=mesh,
        in_specs=placed,
        out_specs=(
            P("section", "grp", "tp"),
            P("section", "grp", "tp"),
            P(("grp", "tp"), None),
            P(),
        ),
        check_vma=False,
    )
```

```python
import math

import jax
import jax.numpy as jnp
from jax import lax
from jax.experimental import pallas as pl
from jax.experimental.pallas import tpu as pltpu
from jax.sharding import PartitionSpec as P

EPSILON = 1e-05
MESH = pl.DeviceIdType.MESH

SIDE = 4
GROUPS = 8
ROW_GROUPS = 3
PAIRS = 2
UNITS = ROW_GROUPS * PAIRS
CHUNKS = 2 * UNITS
WIDE = 1024
HALF = WIDE // 2
FEW = 8
TALL = 2 * FEW
OWN = FEW * ROW_GROUPS
GATHERS = 2 * UNITS
SLOTS = GROUPS - 1
GAIN_STEPS = 7


def lower_start(t, h):
    return pl.multiple_of((2 * t + h) * WIDE, WIDE)


def upper_start(t, h):
    return pl.multiple_of((GROUPS - 1 - 2 * t - h) * WIDE, WIDE)


def plane_device(h, first, second):
    x, y = (first, second) if h == 0 else (second, first)
    return {"tp": x * SIDE + y}


def stacked(*parts):
    return jnp.concatenate(parts, axis=0)


def both_halves(row_pair):
    total = row_pair[:FEW] + row_pair[FEW:]
    return stacked(total, total)


def lanes(value):
    return sum(value[:, 128 * i : 128 * (i + 1)] for i in range(value.shape[1] // 128))


def wide(value):
    return value.astype(jnp.float32)


def narrow(value):
    return value.astype(jnp.bfloat16)


def remote(source, target, send_sem, recv_sem, device):
    return pltpu.make_async_remote_copy(
        src_ref=source,
        dst_ref=target,
        send_sem=send_sem,
        recv_sem=recv_sem,
        device_id=device,
        device_id_type=MESH,
    )


def greet(peers):
    barrier = pltpu.get_barrier_semaphore()
    for peer in peers:
        pl.semaphore_signal(barrier, inc=1, device_id=peer, device_id_type=MESH)
    pl.semaphore_wait(barrier, len(peers))


def boundary_kernel(
    heads_in, weights, residual_in, gain_in, heads_out, grads_out, grad_out, gain_out,
    heads, residual, gain, heads_done, grads, own_grad, gain_done,
    heads_rows, stream, grad_rows, weight_buf, part, from1, from2, from3, from4, both,
    values, columns, exchange, tokens, column_tokens, from_near, heads_all, heads_total, gain_own, gain_got,
    input_sem, output_sem, weight_sem, send_sem, recv_sem, value_send, value_recv, column_send, column_recv,
    exchange_send, exchange_recv, heads_send, heads_recv, near_send, near_recv, gain_send, gain_recv,
):
    tp = lax.axis_index("tp")
    x, y = tp // SIDE, tp % SIDE
    section = lax.axis_index("section")
    group = lax.axis_index("grp")
    z, core = group // 2, group % 2
    other = {"section": 1 - section}
    sibling_group = 2 * z + 1 - core
    sibling = {"grp": sibling_group}
    next_plane = z + 1 - 2 * (z % 2)
    rows_dev, depth = heads.shape
    rows_part = rows_dev // ROW_GROUPS
    grad_scale = 1.0 / math.sqrt(rows_dev * GROUPS)

    def axes(h):
        return (x, y) if h == 0 else (y, x)

    def weight_copy(t, h, upper):
        start = upper_start(t, h) if upper else lower_start(t, h)
        cols = pl.ds(start, WIDE)
        return pltpu.make_async_copy(
            weights.at[:, cols], weight_buf.at[:, cols], weight_sem.at[2 * t + h, upper]
        )

    def start_weights(t, carry):
        for h in range(2):
            for upper in range(2):
                weight_copy(t, h, upper).start()
        return carry

    loads = [
        pltpu.make_async_copy(source, target, input_sem.at[at])
        for at, (source, target) in enumerate(
            ((heads_in, heads), (residual_in, residual), (gain_in, gain))
        )
    ]
    for load in loads:
        load.start()
    lax.fori_loop(0, PAIRS, start_weights, 0)
    for load in loads:
        load.wait()
    for i in range(0, SIDE * SIDE, 2):
        pair = wide(heads[OWN * i : OWN * (i + 2)])
        for r in range(ROW_GROUPS):
            heads_rows[rows_part * r + FEW * i : rows_part * r + FEW * (i + 2)] = narrow(
                stacked(pair[FEW * r : FEW * (r + 1)], pair[OWN + FEW * r : OWN + FEW * (r + 1)])
            )

    def widen(at, carry):
        cols = pl.ds(pl.multiple_of(at * WIDE, WIDE), WIDE)
        rows = wide(residual[:, cols])
        for r in range(ROW_GROUPS):
            stream[r, :, cols] = rows[FEW * r : FEW * (r + 1)]
        return carry

    lax.fori_loop(0, GROUPS, widen, 0)
    heads_total[...] = jnp.zeros_like(heads_total)
    grads[...] = jnp.zeros_like(grads)
    gain_own[0] = jnp.zeros_like(gain_own[0])
    greet(
        [plane_device(0, (x + step) % SIDE, y) for step in (1, 3)]
        + [plane_device(0, x, (y + step) % SIDE) for step in (1, 3)]
        + [other, sibling]
        + [{"grp": 2 * ((z + hop) % SIDE) + k} for hop in range(1, SIDE) for k in range(2)]
    )

    def plane_slot(origin, at):
        return 2 * ((origin + SIDE - 1 - at) % SIDE)

    def heads_arrived(slot):
        remote(
            heads_rows, heads_all.at[slot], heads_send.at[SLOTS - 1], heads_recv.at[slot], sibling
        ).wait_recv()

    def sibling_heads():
        slot = SLOTS - 1
        return remote(
            heads_rows, heads_all.at[slot], heads_send.at[slot], heads_recv.at[slot], sibling
        )

    relays = ((1, 0), (-1, 0), (1, 1), (-1, 1), (1, 2), (-1, 2))

    def each_relay(wanted, act):
        for at, (step, away) in enumerate(relays):
            if away not in wanted:
                continue
            first, last = (away, SIDE - 2) if step > 0 else (1, SIDE - 1 - away)

            @pl.when(jnp.logical_and(z >= first, z <= last))
            def _():
                origin, target = z - step * away, z + step
                held = plane_slot(origin, z) + core
                slot = plane_slot(origin, target) + core
                act(
                    remote(
                        heads_all.at[held] if away else heads_rows,
                        heads_all.at[slot],
                        heads_send.at[SLOTS + at],
                        heads_recv.at[slot],
                        {"grp": 2 * target + core},
                    ),
                    held,
                )

    def start_relay(relay, held):
        relay.start()

    def pass_relay(relay, held):
        heads_arrived(held)
        relay.start()

    def passed_heads(j):
        slot = 2 * j + core
        held = heads_all.at[slot]
        return remote(held, held, heads_send.at[slot], heads_recv.at[slot], sibling)

    def pass_heads():
        @pl.when(jnp.logical_or(z == 0, z == SIDE - 1))
        def _():
            for j in range(SIDE - 1):
                heads_arrived(2 * j + core)

        for j in range(SIDE - 1):
            passed_heads(j).start()

    each_relay((0,), start_relay)
    sibling_heads().start()


    def copy(u, h, step):
        chunk = 2 * u + h
        a, b = axes(h)
        right, left = (a + 1) % SIDE, (a + 3) % SIDE
        up, down = (b + 1) % SIDE, (b + 3) % SIDE
        low, high = pl.ds(0, HALF), pl.ds(HALF, HALF)
        far_a, far_b = (a + 2) % SIDE, (b + 2) % SIDE
        source, target, device = [
            lambda: (part.at[chunk, far_a, :, :, low], from1.at[chunk, 0], plane_device(h, right, b)),
            lambda: (part.at[chunk, far_a, :, :, high], from1.at[chunk, 1], plane_device(h, left, b)),
            lambda: (part.at[chunk, right], from2.at[chunk, 0], plane_device(h, right, b)),
            lambda: (part.at[chunk, left], from2.at[chunk, 1], plane_device(h, left, b)),
            lambda: (part.at[chunk, a, far_b, :, low], from3.at[chunk, 0], plane_device(h, a, up)),
            lambda: (part.at[chunk, a, far_b, :, high], from3.at[chunk, 1], plane_device(h, a, down)),
            lambda: (part.at[chunk, a, up], from4.at[chunk, 0], plane_device(h, a, up)),
            lambda: (part.at[chunk, a, down], from4.at[chunk, 1], plane_device(h, a, down)),
            lambda: (both.at[section, chunk], both.at[section, chunk], other),
        ][step]()
        return remote(source, target, send_sem.at[chunk, step], recv_sem.at[chunk, step], device)

    def arrive(u, h, steps):
        for step in steps:
            copy(u, h, step).wait_recv()

    def multiply(t, carry):
        for h in range(2):
            weight_copy(t, h, 0).wait()
            weight_copy(t, h, 1).wait()
            for side in range(2):
                lower, upper = [
                    jnp.dot(
                        heads_rows[...],
                        weight_buf[:, pl.ds(pl.multiple_of(start + side * HALF, HALF), HALF)],
                        preferred_element_type=jnp.float32,
                    )
                    for start in (lower_start(t, h), upper_start(t, h))
                ]
                for r in range(ROW_GROUPS):
                    for i in range(SIDE * SIDE):
                        rows = slice(rows_part * r + FEW * i, rows_part * r + FEW * (i + 1))
                        a, b = (i // SIDE, i % SIDE) if h == 0 else (i % SIDE, i // SIDE)
                        part[2 * (PAIRS * r + t) + h, a, b, :, side * HALF : (side + 1) * HALF] = narrow(
                            stacked(lower[rows], upper[rows])
                        )
                    copy(PAIRS * r + t, h, side).start()
        return carry

    def near_first(u):
        for h in range(2):
            chunk = 2 * u + h
            a, b = axes(h)
            right, left = (a + 1) % SIDE, (a + 3) % SIDE
            arrive(u, h, (0, 1))
            part[chunk, right, :, :, :HALF] = narrow(
                wide(part[chunk, right, :, :, :HALF]) + wide(from1[chunk, 0])
            )
            copy(u, h, 2).start()
            part[chunk, left, :, :, HALF:] = narrow(
                wide(part[chunk, left, :, :, HALF:]) + wide(from1[chunk, 1])
            )
            copy(u, h, 3).start()

    def far_second(u):
        for h in range(2):
            chunk = 2 * u + h
            a, b = axes(h)
            arrive(u, h, (2, 3))
            part[chunk, a] = narrow(
                wide(part[chunk, a]) + (wide(from2[chunk, 0]) + wide(from2[chunk, 1]))
            )
            copy(u, h, 4).start()
            copy(u, h, 5).start()

    def near_second(u):
        for h in range(2):
            chunk = 2 * u + h
            a, b = axes(h)
            up, down = (b + 1) % SIDE, (b + 3) % SIDE
            arrive(u, h, (4, 5))
            part[chunk, a, up, :, :HALF] = narrow(
                wide(part[chunk, a, up, :, :HALF]) + wide(from3[chunk, 0])
            )
            copy(u, h, 6).start()
            part[chunk, a, down, :, HALF:] = narrow(
                wide(part[chunk, a, down, :, HALF:]) + wide(from3[chunk, 1])
            )
            copy(u, h, 7).start()

    def finish(u):
        r, t = u // PAIRS, u % PAIRS
        for h in range(2):
            chunk = 2 * u + h
            a, b = axes(h)
            arrive(u, h, (6, 7))
            total = wide(part[chunk, a, b]) + (wide(from4[chunk, 0]) + wide(from4[chunk, 1]))
            rows = stacked(
                stream[r, :, pl.ds(lower_start(t, h), WIDE)],
                stream[r, :, pl.ds(upper_start(t, h), WIDE)],
            )
            total = total + jnp.where(section == 0, rows, 0.0)
            both[section, chunk] = narrow(total)
            copy(u, h, 8).start()


    def gather_of(store, sends, recvs):
        half = store.shape[-1] // 2

        def gather(p, h, step):
            chunk = 2 * p + h
            a, b = axes(h)
            right, left = (a + 1) % SIDE, (a + 3) % SIDE
            up, down = (b + 1) % SIDE, (b + 3) % SIDE
            low, high = pl.ds(0, half), pl.ds(half, half)
            block, device = [
                lambda: (store.at[chunk, b, a], plane_device(h, right, b)),
                lambda: (store.at[chunk, b, a], plane_device(h, left, b)),
                lambda: (store.at[chunk, b, left, :, low], plane_device(h, right, b)),
                lambda: (store.at[chunk, b, right, :, high], plane_device(h, left, b)),
                lambda: (store.at[chunk, b], plane_device(h, a, up)),
                lambda: (store.at[chunk, b], plane_device(h, a, down)),
                lambda: (store.at[chunk, down, :, :, low], plane_device(h, a, up)),
                lambda: (store.at[chunk, up, :, :, high], plane_device(h, a, down)),
            ][step]()
            return remote(block, block, sends.at[chunk, step], recvs.at[chunk, step], device)

        return gather

    gather_values = gather_of(values, value_send, value_recv)
    gather_columns = gather_of(columns, column_send, column_recv)

    def exchanged(r, target):
        slot = 2 * (2 * r + z % 2) + core
        a, b = x + core * (y - x), y + core * (x - y)
        return remote(
            exchange.at[r, target],
            columns.at[slot, b, a],
            exchange_send.at[GROUPS * r + target],
            exchange_recv.at[slot],
            {"grp": target},
        )

    def exchange_arrived(p, h):
        a, b = axes(h)
        remote(
            exchange.at[0, 0],
            columns.at[2 * p + h, b, a],
            exchange_send.at[0],
            exchange_recv.at[2 * p + h],
            sibling,
        ).wait_recv()

    def gain_rows(t, h):
        return stacked(
            jnp.broadcast_to(gain[:, pl.ds(lower_start(t, h), WIDE)], (FEW, WIDE)),
            jnp.broadcast_to(gain[:, pl.ds(upper_start(t, h), WIDE)], (FEW, WIDE)),
        )

    def normalize(r):
        zero = jnp.zeros((TALL, 128), jnp.float32)
        chunks = [(t, h, 2 * (PAIRS * r + t) + h) for t in range(PAIRS) for h in range(2)]

        def row_mean(total):
            return both_halves(jnp.sum(total, axis=1, keepdims=True)) / (GROUPS * WIDE)

        total = zero
        for t, h, chunk in chunks:
            copy(PAIRS * r + t, h, 8).wait_recv()
            total = total + lanes(wide(both[0, chunk]))
        mean = row_mean(total)
        total = zero
        for t, h, chunk in chunks:
            centred = wide(both[0, chunk]) - mean
            total = total + lanes(centred * centred)
        inv_scale = lax.rsqrt(row_mean(total) + EPSILON)
        sum_scaled, sum_product = zero, zero
        for t, h, chunk in chunks:
            unit = (wide(both[0, chunk]) - mean) * inv_scale
            scaled = gain_rows(t, h) * wide(both[1, chunk])
            sum_scaled = sum_scaled + lanes(scaled)
            sum_product = sum_product + lanes(scaled * unit)
        mean_scaled, mean_product = row_mean(sum_scaled), row_mean(sum_product)
        for t, h, chunk in chunks:
            a, b = axes(h)
            rows = gain_rows(t, h)
            unit = (wide(both[0, chunk]) - mean) * inv_scale
            d_normed = wide(both[1, chunk])
            grad = inv_scale * (rows * d_normed - mean_scaled - unit * mean_product)
            value = jnp.where(section == 0, grad, unit * rows)
            values[chunk, b, a] = narrow(value)
            gather_values(PAIRS * r + t, h, 0).start()
            gather_values(PAIRS * r + t, h, 1).start()
            grad_rows[r, :, pl.ds(lower_start(t, h), WIDE)] = grad[:FEW]
            grad_rows[r, :, pl.ds(upper_start(t, h), WIDE)] = grad[FEW:]
            product = d_normed * unit
            for upper, target in enumerate((2 * t + h, GROUPS - 1 - 2 * t - h)):
                rows = slice(upper * FEW, (upper + 1) * FEW)
                gain_own[0, target] += jnp.sum(product[rows], axis=0, keepdims=True)
                exchange[r, target] = narrow(stacked(value[rows, :HALF], value[rows, HALF:]))

                @pl.when(target // SIDE != z // 2)
                def _():
                    exchanged(r, target).start()


    def near_copy(r, chunk, upper, target, slot):
        rows = pl.ds(pl.multiple_of(r * rows_part, rows_part), rows_part)
        return remote(
            tokens.at[chunk, upper, rows],
            from_near.at[slot, rows],
            near_send.at[GROUPS * r + target],
            near_recv.at[ROW_GROUPS * slot + r],
            {"grp": target},
        )

    def each_near(r, t, h, act):
        for upper, target in enumerate((2 * t + h, GROUPS - 1 - 2 * t - h)):
            for slot, wanted in ((0, target == sibling_group), (1 + core, target // 2 == next_plane)):

                @pl.when(wanted)
                def _():
                    act(near_copy(r, 2 * t + h, upper, target, slot))

    def split_blocks(store, chunk, h, target, first_row):
        for i in range(0, SIDE * SIDE, 2):
            pair = []
            for at in (i, i + 1):
                a, b = (at // SIDE, at % SIDE) if h == 0 else (at % SIDE, at // SIDE)
                pair.append(wide(store[chunk, b, a]))
            rows = pl.ds(pl.multiple_of(first_row + FEW * i, TALL), TALL)
            target[0, rows] = narrow(stacked(pair[0][:FEW], pair[1][:FEW]))
            target[1, rows] = narrow(stacked(pair[0][FEW:], pair[1][FEW:]))

    def add_grads(side, token_rows, head_rows):
        grads[side * HALF : (side + 1) * HALF] += grad_scale * lax.dot_general(
            token_rows, head_rows, (((0,), (0,)), ((), ())), preferred_element_type=jnp.float32
        )

    def use_rows(t, h):
        chunk = 2 * t + h
        total = heads_total[...]
        for upper, start in enumerate((lower_start(t, h), upper_start(t, h))):
            total = total + lax.dot_general(
                tokens[chunk, upper], weight_buf[:, pl.ds(start, WIDE)],
                (((1,), (1,)), ((), ())), preferred_element_type=jnp.float32,
            )
        heads_total[...] = total
        for upper, target in enumerate((chunk, GROUPS - 1 - chunk)):

            @pl.when(target == group)
            def _():
                for side in range(2):
                    add_grads(side, tokens[chunk, upper, :, side * HALF : (side + 1) * HALF], heads_rows[...])

    def use_columns(j):
        slot = plane_slot(2 * (1 - z // 2) + j, z)
        heads_arrived(slot + 1 - core)
        head_rows = heads_all[pl.ds(slot, 2)].reshape(2 * rows_dev, depth)
        for side in range(2):
            add_grads(side, column_tokens[j, side], head_rows)

    def use_near(slot, heads_slot):
        for r in range(ROW_GROUPS):
            near_copy(r, 0, 0, 0, slot).wait_recv()
        for side in range(2):
            add_grads(side, from_near[slot, :, side * HALF : (side + 1) * HALF], heads_all[heads_slot])

    def value_arrived(q):
        r, t = q // PAIRS, q % PAIRS
        for h in range(2):
            gather_values(q, h, 6).wait_recv()
            gather_values(q, h, 7).wait_recv()
            split_blocks(values, 2 * q + h, h, tokens.at[2 * t + h], r * rows_part)
            each_near(r, t, h, lambda near: near.start())

    def columns_arrived(p):
        r, j = p // 2, p % 2
        for h in range(2):
            gather_columns(p, h, 6).wait_recv()
            gather_columns(p, h, 7).wait_recv()
            split_blocks(columns, 2 * p + h, h, column_tokens.at[j], h * rows_dev + r * rows_part)

    gain_partners = [
        {"tp": x * SIDE + y + 1 - 2 * (y % 2)},
        {"tp": x * SIDE + SIDE - 1 - y},
        {"tp": (x + 1 - 2 * (x % 2)) * SIDE + y},
        {"tp": (SIDE - 1 - x) * SIDE + y},
        sibling,
        {"grp": 2 * next_plane + core},
        {"grp": 2 * (SIDE - 1 - z) + core},
    ]

    def gain_copy(step):
        return remote(
            gain_own.at[step], gain_got.at[step], gain_send.at[step], gain_recv.at[step], gain_partners[step]
        )

    own_grad_store, heads_store, gain_store, grads_store = [
        pltpu.make_async_copy(source, target, output_sem.at[at])
        for at, (source, target) in enumerate(
            ((own_grad, grad_out), (heads_done, heads_out), (gain_done, gain_out), (grads, grads_out))
        )
    ]

    def finish_rows():
        def join(at, carry):
            cols = pl.ds(pl.multiple_of(at * WIDE, WIDE), WIDE)
            own_grad[:, cols] = narrow(stacked(*(grad_rows[r, :, cols] for r in range(ROW_GROUPS))))
            return carry

        lax.fori_loop(0, GROUPS, join, 0)
        own_grad_store.start()

    def finish_heads():
        for i in range(0, SIDE * SIDE, 2):
            heads_done[OWN * i : OWN * (i + 2)] = narrow(
                stacked(
                    *(
                        heads_total[rows_part * r + FEW * at : rows_part * r + FEW * (at + 1)]
                        for at in (i, i + 1)
                        for r in range(ROW_GROUPS)
                    )
                )
            )
        heads_store.start()
        for target in range(GROUPS):
            gain_done[:, target * WIDE : (target + 1) * WIDE] = (
                gain_own[GAIN_STEPS, target] * grad_scale
            )
        gain_store.start()

    def within(value, count):
        return jnp.logical_and(value >= 0, value < count)

    def gather_stage(q, waits, starts):
        for gather, p in ((gather_values, q), (gather_columns, q - UNITS)):

            @pl.when(within(p, UNITS))
            def _():
                for h in range(2):
                    for step in waits:
                        gather(p, h, step).wait_recv()
                    for step in starts:
                        gather(p, h, step).start()

    NORM_TURN = 6
    LAST_NORM = NORM_TURN + PAIRS * (ROW_GROUPS - 1)
    GATHER_TURN = NORM_TURN + 1

    def turn(n, carry):
        for late, stage in ((0, near_first), (2, far_second), (3, near_second), (4, finish)):

            @pl.when(within(n - late, UNITS))
            def _():
                stage(n - late)

        @pl.when(jnp.logical_and(within(n - NORM_TURN, UNITS), (n - NORM_TURN) % PAIRS == 0))
        def _():
            normalize((n - NORM_TURN) // PAIRS)

        @pl.when(n == NORM_TURN)
        def _():
            each_relay((1,), pass_relay)

        @pl.when(n == LAST_NORM + 1)
        def _():
            finish_rows()
            each_relay((2,), pass_relay)

        @pl.when(n == LAST_NORM + 4)
        def _():
            pass_heads()

        for step in range(GAIN_STEPS + 1):

            @pl.when(n == LAST_NORM + 1 + step)
            def _():
                if step > 0:
                    gain_copy(step - 1).wait_recv()
                    gain_own[step] = gain_own[step - 1] + gain_got[step - 1]
                if step < GAIN_STEPS:
                    gain_copy(step).start()

        @pl.when(within(n - GATHER_TURN + 1 - UNITS, UNITS))
        def _():
            p = n - GATHER_TURN + 1 - UNITS
            for h in range(2):
                exchange_arrived(p, h)
                gather_columns(p, h, 0).start()
                gather_columns(p, h, 1).start()

        gather_stage(n - GATHER_TURN, (0, 1), (2, 3))
        gather_stage(n - GATHER_TURN - 1, (2, 3), (4, 5))
        gather_stage(n - GATHER_TURN - 3, (4, 5), (6, 7))
        done = n - GATHER_TURN - 4

        @pl.when(within(done, UNITS))
        def _():
            value_arrived(done)

            @pl.when(done >= UNITS - PAIRS)
            def _():
                for h in range(2):
                    use_rows(done - (UNITS - PAIRS), h)

        @pl.when(done == UNITS + 1)
        def _():
            finish_heads()

        @pl.when(done == GATHERS - 3)
        def _():
            heads_arrived(SLOTS - 1)
            use_near(0, SLOTS - 1)

        @pl.when(done == GATHERS - 1)
        def _():
            slot = plane_slot(next_plane, z)
            heads_arrived(slot + 1 - core)
            for k in range(2):
                use_near(1 + k, slot + k)

        @pl.when(within(done - UNITS, UNITS))
        def _():
            columns_arrived(done - UNITS)

            @pl.when(done >= GATHERS - 2)
            def _():
                use_columns(done - (GATHERS - 2))

        return carry

    lax.fori_loop(0, PAIRS, multiply, 0)
    lax.fori_loop(0, GATHER_TURN + 4 + GATHERS, turn, 0)
    grads_store.start()

    def sent(u, carry):
        r, t = u // PAIRS, u % PAIRS
        for h in range(2):
            for step in range(9):
                copy(u, h, step).wait_send()
            for step in range(8):
                gather_values(u, h, step).wait_send()
                gather_columns(u, h, step).wait_send()
            each_near(r, t, h, lambda near: near.wait_send())
            for target in (2 * t + h, GROUPS - 1 - 2 * t - h):

                @pl.when(target // SIDE != z // 2)
                def _():
                    exchanged(r, target).wait_send()

        return carry

    lax.fori_loop(0, UNITS, sent, 0)
    each_relay((0, 1, 2), lambda relay, held: relay.wait_send())
    for j in range(SIDE - 1):
        passed_heads(j).wait_send()
    sibling_heads().wait_send()
    for step in range(GAIN_STEPS):
        gain_copy(step).wait_send()
    for store in (own_grad_store, heads_store, gain_store, grads_store):
        store.wait()


def deliver_kernel(*refs):
    results, outputs, held = refs[:4], refs[4:8], refs[8:12]
    load_sem, store_sem = refs[12:]
    loads = [pltpu.make_async_copy(results[at], held[at], load_sem.at[at]) for at in range(4)]
    stores = [pltpu.make_async_copy(held[at], outputs[at], store_sem.at[at]) for at in range(4)]
    for load in loads:
        load.start()
    for load, store in zip(loads, stores):
        load.wait()
        store.start()
    for store in stores:
        store.wait()


def delivered(results):
    hbm = pl.BlockSpec(memory_space=pl.ANY)
    return pl.pallas_call(
        deliver_kernel,
        out_shape=tuple(jax.ShapeDtypeStruct(result.shape, result.dtype) for result in results),
        in_specs=[hbm] * 4,
        out_specs=(hbm,) * 4,
        scratch_shapes=[pltpu.VMEM(result.shape, result.dtype) for result in results]
        + [pltpu.SemaphoreType.DMA((4,))] * 2,
        name="deliver",
    )(*results)


def fused(heads, weights, residual, gain):
    hbm = pl.BlockSpec(memory_space=pl.ANY)
    bf16, f32 = jnp.bfloat16, jnp.float32
    rows_dev, depth = heads.shape
    owned = weights.shape[1] // GROUPS
    dma = pltpu.SemaphoreType.DMA
    return pl.pallas_call(
        boundary_kernel,
        out_shape=(
            jax.ShapeDtypeStruct(heads.shape, bf16),
            jax.ShapeDtypeStruct((owned, depth), f32),
            jax.ShapeDtypeStruct(residual.shape, bf16),
            jax.ShapeDtypeStruct(gain.shape, f32),
        ),
        in_specs=[hbm] * 4,
        out_specs=(hbm,) * 4,
        scratch_shapes=[
            pltpu.VMEM(heads.shape, bf16),
            pltpu.VMEM(residual.shape, bf16),
            pltpu.VMEM(gain.shape, f32),
            pltpu.VMEM(heads.shape, bf16),
            pltpu.VMEM((owned, depth), f32),
            pltpu.VMEM(residual.shape, bf16),
            pltpu.VMEM(gain.shape, f32),
            pltpu.VMEM(heads.shape, bf16),
            pltpu.VMEM((ROW_GROUPS, FEW, gain.shape[1]), f32),
            pltpu.VMEM((ROW_GROUPS, FEW, gain.shape[1]), f32),
            pltpu.VMEM(weights.shape, bf16),
            pltpu.VMEM((CHUNKS, SIDE, SIDE, TALL, WIDE), bf16),
            pltpu.VMEM((CHUNKS, 2, SIDE, TALL, HALF), bf16),
            pltpu.VMEM((CHUNKS, 2, SIDE, TALL, WIDE), bf16),
            pltpu.VMEM((CHUNKS, 2, TALL, HALF), bf16),
            pltpu.VMEM((CHUNKS, 2, TALL, WIDE), bf16),
            pltpu.VMEM((2, CHUNKS, TALL, WIDE), bf16),
            pltpu.VMEM((CHUNKS, SIDE, SIDE, TALL, WIDE), bf16),
            pltpu.VMEM((CHUNKS, SIDE, SIDE, TALL, HALF), bf16),
            pltpu.VMEM((ROW_GROUPS, GROUPS, TALL, HALF), bf16),
            pltpu.VMEM((2 * PAIRS, 2, rows_dev, WIDE), bf16),
            pltpu.VMEM((2, 2, 2 * rows_dev, HALF), bf16),
            pltpu.VMEM((3, rows_dev, WIDE), bf16),
            pltpu.VMEM((SLOTS, rows_dev, depth), bf16),
            pltpu.VMEM((rows_dev, depth), f32),
            pltpu.VMEM((GAIN_STEPS + 1, GROUPS, 1, WIDE), f32),
            pltpu.VMEM((GAIN_STEPS, GROUPS, 1, WIDE), f32),
            dma((3,)),
            dma((4,)),
            dma((2 * PAIRS, 2)),
            dma((CHUNKS, 9)),
            dma((CHUNKS, 9)),
            dma((CHUNKS, 8)),
            dma((CHUNKS, 8)),
            dma((CHUNKS, 8)),
            dma((CHUNKS, 8)),
            dma((ROW_GROUPS * GROUPS,)),
            dma((CHUNKS,)),
            dma((SLOTS + 6,)),
            dma((SLOTS,)),
            dma((ROW_GROUPS * GROUPS,)),
            dma((ROW_GROUPS * 3,)),
            dma((GAIN_STEPS,)),
            dma((GAIN_STEPS,)),
        ],
        compiler_params=pltpu.CompilerParams(
            collective_id=0, has_side_effects=True, vmem_limit_bytes=62 * 1024 * 1024
        ),
        name="boundary",
    )(heads, weights, residual, gain)


def per_device(heads_in, weights, residual, norm_gain):
    heads_out, weight_grad, boundary_grad, gain_grad = delivered(
        fused(heads_in[0], weights[0], residual, norm_gain[None])
    )
    return (heads_out[None], weight_grad[None], boundary_grad, gain_grad[0])


def solution(mesh):
    placed = (P("section", "grp", "tp"), P("section", "tp", None), P(("grp", "tp"), None), P())
    return jax.shard_map(
        per_device,
        mesh=mesh,
        in_specs=placed,
        out_specs=(
            P("section", "grp", "tp"),
            P("section", "grp", "tp"),
            P(("grp", "tp"), None),
            P(),
        ),
        check_vma=False,
    )
```

```python
import math

import jax
import jax.numpy as jnp
from jax import lax
from jax.experimental import pallas as pl
from jax.experimental.pallas import tpu as pltpu
from jax.sharding import PartitionSpec as P

EPSILON = 1e-05
MESH = pl.DeviceIdType.MESH

SIDE = 4
GROUPS = 8
UNITS = 8
FAR_UNITS = 4
CHUNKS = 2 * UNITS
FAR_CHUNKS = 2 * FAR_UNITS
WIDE = 256
HALF = WIDE // 2
UNIT_WIDE = 2 * WIDE
SHARD = 2 * UNIT_WIDE
OWN = 24
TALL = 2 * OWN
SLOTS = GROUPS - 1
GAIN_STEPS = 7


def lower_start(t, h=0):
    return pl.multiple_of(t * UNIT_WIDE + h * WIDE, WIDE)


def upper_start(t, h=0):
    return pl.multiple_of((GROUPS - 1 - t // 2) * SHARD + (t % 2) * UNIT_WIDE + h * WIDE, WIDE)


def plane_device(h, first, second):
    x, y = (first, second) if h == 0 else (second, first)
    return {"tp": x * SIDE + y}


def stacked(*parts):
    return jnp.concatenate(parts, axis=0)


def both_halves(row_pair):
    total = row_pair[:OWN] + row_pair[OWN:]
    return stacked(total, total)


def lanes(value):
    return sum(value[:, 128 * i : 128 * (i + 1)] for i in range(value.shape[1] // 128))


def wide(value):
    return value.astype(jnp.float32)


def narrow(value):
    return value.astype(jnp.bfloat16)


def remote(source, target, send_sem, recv_sem, device):
    return pltpu.make_async_remote_copy(
        src_ref=source,
        dst_ref=target,
        send_sem=send_sem,
        recv_sem=recv_sem,
        device_id=device,
        device_id_type=MESH,
    )


def greet(peers):
    barrier = pltpu.get_barrier_semaphore()
    for peer in peers:
        pl.semaphore_signal(barrier, inc=1, device_id=peer, device_id_type=MESH)
    pl.semaphore_wait(barrier, len(peers))


def boundary_kernel(
    heads_in, weights, residual_in, gain_in, heads_out, grads_out, grad_out, gain_out,
    heads, residual, gain, heads_done, grads, own_grad, gain_done,
    weight_buf, part, from1, from2, from3, from4, both,
    values, columns, exchange, tokens, column_tokens, from_near, heads_all, heads_total, gain_own, gain_got,
    input_sem, output_sem, weight_sem, send_sem, recv_sem, value_send, value_recv, column_send, column_recv,
    exchange_send, exchange_recv, heads_send, heads_recv, near_send, near_recv, gain_send, gain_recv,
):
    tp = lax.axis_index("tp")
    x, y = tp // SIDE, tp % SIDE
    section = lax.axis_index("section")
    group = lax.axis_index("grp")
    z, core = group // 2, group % 2
    other = {"section": 1 - section}
    sibling_group = 2 * z + 1 - core
    sibling = {"grp": sibling_group}
    next_plane = z + 1 - 2 * (z % 2)
    rows_dev, depth = heads.shape
    grad_scale = 1.0 / math.sqrt(rows_dev * GROUPS)

    def axes(h):
        return (x, y) if h == 0 else (y, x)

    def wait_arrived(size, sem):
        remote(size, size, heads_send.at[0], sem, sibling).wait_recv()

    def wait_sent(size, sem):
        remote(size, size, sem, heads_recv.at[0], sibling).wait_send()

    def weight_copy(t, upper):
        cols = pl.ds(upper_start(t) if upper else lower_start(t), UNIT_WIDE)
        return pltpu.make_async_copy(
            weights.at[:, cols], weight_buf.at[:, cols], weight_sem.at[t, upper]
        )

    def start_weights(t, carry):
        weight_copy(t, 0).start()
        weight_copy(t, 1).start()
        return carry

    heads_load, residual_load, gain_load = [
        pltpu.make_async_copy(source, target, input_sem.at[at])
        for at, (source, target) in enumerate(
            ((heads_in, heads), (residual_in, residual), (gain_in, gain))
        )
    ]
    heads_load.start()
    lax.fori_loop(0, UNITS, start_weights, 0)
    residual_load.start()
    gain_load.start()
    greet(
        [plane_device(0, (x + step) % SIDE, y) for step in (1, 3)]
        + [plane_device(0, x, (y + step) % SIDE) for step in (1, 3)]
        + [other, sibling]
        + [{"grp": 2 * ((z + hop) % SIDE) + k} for hop in range(1, SIDE) for k in range(2)]
    )
    heads_load.wait()

    def plane_slot(origin, at):
        return 2 * ((origin + SIDE - 1 - at) % SIDE)

    def heads_arrived(slot):
        remote(
            heads, heads_all.at[slot], heads_send.at[SLOTS - 1], heads_recv.at[slot], sibling
        ).wait_recv()

    def sibling_heads():
        slot = SLOTS - 1
        return remote(
            heads, heads_all.at[slot], heads_send.at[slot], heads_recv.at[slot], sibling
        )

    relays = ((1, 0), (-1, 0), (1, 1), (-1, 1), (1, 2), (-1, 2))

    def each_relay(wanted, act):
        for at, (step, away) in enumerate(relays):
            if away not in wanted:
                continue
            first, last = (away, SIDE - 2) if step > 0 else (1, SIDE - 1 - away)

            @pl.when(jnp.logical_and(z >= first, z <= last))
            def _():
                origin, target = z - step * away, z + step
                held = plane_slot(origin, z) + core
                slot = plane_slot(origin, target) + core
                act(
                    remote(
                        heads_all.at[held] if away else heads,
                        heads_all.at[slot],
                        heads_send.at[SLOTS + at],
                        heads_recv.at[slot],
                        {"grp": 2 * target + core},
                    ),
                    held,
                )

    def start_relay(relay, held):
        relay.start()

    def pass_relay(relay, held):
        heads_arrived(held)
        relay.start()

    def passed_heads(j):
        slot = 2 * j + core
        held = heads_all.at[slot]
        return remote(held, held, heads_send.at[slot], heads_recv.at[slot], sibling)

    def pass_heads():
        @pl.when(jnp.logical_or(z == 0, z == SIDE - 1))
        def _():
            for j in range(SIDE - 1):
                heads_arrived(2 * j + core)

        for j in range(SIDE - 1):
            passed_heads(j).start()

    each_relay((0,), start_relay)
    sibling_heads().start()


    def copy(u, h, step):
        chunk = 2 * u + h
        a, b = axes(h)
        right, left = (a + 1) % SIDE, (a + 3) % SIDE
        up, down = (b + 1) % SIDE, (b + 3) % SIDE
        low, high = pl.ds(0, HALF), pl.ds(HALF, HALF)
        far_a, far_b = (a + 2) % SIDE, (b + 2) % SIDE
        source, target, device = [
            lambda: (part.at[chunk, far_a, :, :, low], from1.at[chunk, 0], plane_device(h, right, b)),
            lambda: (part.at[chunk, far_a, :, :, high], from1.at[chunk, 1], plane_device(h, left, b)),
            lambda: (part.at[chunk, right], from2.at[chunk, 0], plane_device(h, right, b)),
            lambda: (part.at[chunk, left], from2.at[chunk, 1], plane_device(h, left, b)),
            lambda: (part.at[chunk, a, far_b, :, low], from3.at[chunk, 0], plane_device(h, a, up)),
            lambda: (part.at[chunk, a, far_b, :, high], from3.at[chunk, 1], plane_device(h, a, down)),
            lambda: (part.at[chunk, a, up], from4.at[chunk, 0], plane_device(h, a, up)),
            lambda: (part.at[chunk, a, down], from4.at[chunk, 1], plane_device(h, a, down)),
            lambda: (both.at[section, chunk], both.at[section, chunk], other),
        ][step]()
        return remote(source, target, send_sem.at[u], recv_sem.at[u, step // 2], device)

    reduce_sizes = [
        part.at[0, 0:2], part.at[0], part.at[0, 0, 0:2], part.at[0, 0], part.at[0, 0, 0:2]
    ]

    def arrive(u, stage):
        wait_arrived(reduce_sizes[stage], recv_sem.at[u, stage])

    def multiply(u):
        weight_copy(u, 0).wait()
        weight_copy(u, 1).wait()
        lower, upper = [
            jnp.dot(
                heads[...], weight_buf[:, pl.ds(start, UNIT_WIDE)],
                preferred_element_type=jnp.float32,
            )
            for start in (lower_start(u), upper_start(u))
        ]
        for h in range(2):
            cols = slice(h * WIDE, (h + 1) * WIDE)
            for i in range(SIDE * SIDE):
                rows = slice(OWN * i, OWN * (i + 1))
                a, b = (i // SIDE, i % SIDE) if h == 0 else (i % SIDE, i // SIDE)
                part[2 * u + h, a, b] = narrow(stacked(lower[rows, cols], upper[rows, cols]))
            copy(u, h, 0).start()
            copy(u, h, 1).start()

    def near_first(u):
        arrive(u, 0)
        for h in range(2):
            chunk = 2 * u + h
            a, b = axes(h)
            right, left = (a + 1) % SIDE, (a + 3) % SIDE
            part[chunk, right, :, :, :HALF] = narrow(
                wide(part[chunk, right, :, :, :HALF]) + wide(from1[chunk, 0])
            )
            copy(u, h, 2).start()
            part[chunk, left, :, :, HALF:] = narrow(
                wide(part[chunk, left, :, :, HALF:]) + wide(from1[chunk, 1])
            )
            copy(u, h, 3).start()

    def far_second(u):
        arrive(u, 1)
        for h in range(2):
            chunk = 2 * u + h
            a, b = axes(h)
            part[chunk, a] = narrow(
                wide(part[chunk, a]) + (wide(from2[chunk, 0]) + wide(from2[chunk, 1]))
            )
            copy(u, h, 4).start()
            copy(u, h, 5).start()

    def near_second(u):
        arrive(u, 2)
        for h in range(2):
            chunk = 2 * u + h
            a, b = axes(h)
            up, down = (b + 1) % SIDE, (b + 3) % SIDE
            part[chunk, a, up, :, :HALF] = narrow(
                wide(part[chunk, a, up, :, :HALF]) + wide(from3[chunk, 0])
            )
            copy(u, h, 6).start()
            part[chunk, a, down, :, HALF:] = narrow(
                wide(part[chunk, a, down, :, HALF:]) + wide(from3[chunk, 1])
            )
            copy(u, h, 7).start()

    def finish(u):
        arrive(u, 3)
        for h in range(2):
            chunk = 2 * u + h
            a, b = axes(h)
            total = wide(part[chunk, a, b]) + (wide(from4[chunk, 0]) + wide(from4[chunk, 1]))
            rows = stacked(
                wide(residual[:, pl.ds(lower_start(u, h), WIDE)]),
                wide(residual[:, pl.ds(upper_start(u, h), WIDE)]),
            )
            total = total + jnp.where(section == 0, rows, 0.0)
            both[section, chunk] = narrow(total)
            copy(u, h, 8).start()

    def within(value, count):
        return jnp.logical_and(value >= 0, value < count)

    stages = (multiply, near_first, far_second, near_second, finish)

    def reduce_turn(n, carry):
        for late, stage in enumerate(stages):

            @pl.when(within(n - late, UNITS))
            def _():
                stage(n - late)

        return carry

    residual_load.wait()
    gain_load.wait()
    lax.fori_loop(0, UNITS + len(stages) - 1, reduce_turn, 0)
    heads_total[...] = jnp.zeros_like(heads_total)
    grads[...] = jnp.zeros_like(grads)


    def gather_of(store, sends, recvs):
        half = store.shape[-1] // 2

        def gather(p, h, step):
            chunk = 2 * p + h
            a, b = axes(h)
            right, left = (a + 1) % SIDE, (a + 3) % SIDE
            up, down = (b + 1) % SIDE, (b + 3) % SIDE
            low, high = pl.ds(0, half), pl.ds(half, half)
            block, device = [
                lambda: (store.at[chunk, b, a], plane_device(h, right, b)),
                lambda: (store.at[chunk, b, a], plane_device(h, left, b)),
                lambda: (store.at[chunk, b, left, :, low], plane_device(h, right, b)),
                lambda: (store.at[chunk, b, right, :, high], plane_device(h, left, b)),
                lambda: (store.at[chunk, b], plane_device(h, a, up)),
                lambda: (store.at[chunk, b], plane_device(h, a, down)),
                lambda: (store.at[chunk, down, :, :, low], plane_device(h, a, up)),
                lambda: (store.at[chunk, up, :, :, high], plane_device(h, a, down)),
            ][step]()
            return remote(block, block, sends.at[p], recvs.at[p, step // 2], device)

        return gather

    gather_values = gather_of(values, value_send, value_recv)
    gather_columns = gather_of(columns, column_send, column_recv)

    gather_sizes = [values.at[0, 0], values.at[0, 0, 0:2], values.at[0], values.at[0, 0:2]]

    def exchanged(target, e):
        unit = 2 * (z % 2) + e
        a, b = x + core * (y - x), y + core * (x - y)
        return remote(
            exchange.at[target, e],
            columns.at[2 * unit + core, b, a],
            exchange_send.at[0],
            exchange_recv.at[unit],
            {"grp": target},
        )

    def gain_rows(t, h):
        return stacked(
            jnp.broadcast_to(gain[:, pl.ds(lower_start(t, h), WIDE)], (OWN, WIDE)),
            jnp.broadcast_to(gain[:, pl.ds(upper_start(t, h), WIDE)], (OWN, WIDE)),
        )

    zero = jnp.zeros((TALL, 128), jnp.float32)

    def row_mean(total):
        return both_halves(jnp.sum(total, axis=1, keepdims=True)) / (GROUPS * SHARD)

    def add_sums(t, total):
        arrive(t, 4)
        for h in range(2):
            total = total + lanes(wide(both[0, 2 * t + h]))
        return total

    mean = row_mean(lax.fori_loop(0, UNITS, add_sums, zero))

    def add_squares(t, total):
        for h in range(2):
            centred = wide(both[0, 2 * t + h]) - mean
            total = total + lanes(centred * centred)
        return total

    inv_scale = lax.rsqrt(row_mean(lax.fori_loop(0, UNITS, add_squares, zero)) + EPSILON)

    def add_means(t, totals):
        for h in range(2):
            unit = (wide(both[0, 2 * t + h]) - mean) * inv_scale
            scaled = gain_rows(t, h) * wide(both[1, 2 * t + h])
            totals = (totals[0] + lanes(scaled), totals[1] + lanes(scaled * unit))
        return totals

    sums = lax.fori_loop(0, UNITS, add_means, (zero, zero))
    mean_scaled, mean_product = row_mean(sums[0]), row_mean(sums[1])
    first_unit = SIDE * ((z // 2 + z % 2 + 1) % 2)

    def write(turn, carry):
        shard = (turn + first_unit // 2) % SIDE
        kept = []
        for v in range(2):
            t = 2 * shard + v
            for h in range(2):
                chunk = 2 * t + h
                a, b = axes(h)
                rows = gain_rows(t, h)
                unit = (wide(both[0, chunk]) - mean) * inv_scale
                d_normed = wide(both[1, chunk])
                grad = inv_scale * (rows * d_normed - mean_scaled - unit * mean_product)
                value = jnp.where(section == 0, grad, unit * rows)
                values[chunk, b, a] = narrow(value)
                gather_values(t, h, 0).start()
                gather_values(t, h, 1).start()
                kept.append(value)
                product = d_normed * unit
                for start, rows in (
                    (lower_start(t, h), slice(0, OWN)),
                    (upper_start(t, h), slice(OWN, TALL)),
                ):
                    own_grad[:, pl.ds(start, WIDE)] = narrow(grad[rows])
                    gain_own[0, :, pl.ds(start, WIDE)] = jnp.sum(product[rows], axis=0, keepdims=True)
        for target, rows in ((shard, slice(0, OWN)), (GROUPS - 1 - shard, slice(OWN, TALL))):
            for e in range(2):
                exchange[target, e] = narrow(stacked(kept[e][rows], kept[2 + e][rows]))

                @pl.when(target // SIDE != z // 2)
                def _():
                    exchanged(target, e).start()
        return carry

    lax.fori_loop(0, SIDE, write, 0)


    def near_copy(t, upper, target, slot):
        return remote(
            tokens.at[t, upper],
            from_near.at[slot, t % 2],
            near_send.at[0],
            near_recv.at[slot],
            {"grp": target},
        )

    def split_blocks(store, chunk, h, put):
        for i in range(0, SIDE * SIDE, 2):
            pair = []
            for at in (i, i + 1):
                a, b = (at // SIDE, at % SIDE) if h == 0 else (at % SIDE, at // SIDE)
                pair.append(wide(store[chunk, b, a]))
            put(0, slice(OWN * i, OWN * (i + 2)), narrow(stacked(pair[0][:OWN], pair[1][:OWN])))
            put(1, slice(OWN * i, OWN * (i + 2)), narrow(stacked(pair[0][OWN:], pair[1][OWN:])))

    def add_grads(start, token_rows, head_rows):
        rows = pl.ds(start, token_rows.shape[1])
        grads[rows] += grad_scale * lax.dot_general(
            token_rows, head_rows, (((0,), (0,)), ((), ())), preferred_element_type=jnp.float32
        )

    def use_values(t):
        for h in range(2):

            def put(upper, rows, block):
                tokens[t, upper, rows, h * WIDE : (h + 1) * WIDE] = block

            split_blocks(values, 2 * t + h, h, put)
        for upper, target in enumerate((t // 2, GROUPS - 1 - t // 2)):
            for slot, wanted in ((0, target == sibling_group), (1 + core, target // 2 == next_plane)):

                @pl.when(wanted)
                def _():
                    near_copy(t, upper, target, slot).start()

        total = heads_total[...]
        for upper, start in enumerate((lower_start(t), upper_start(t))):
            total = total + lax.dot_general(
                tokens[t, upper], weight_buf[:, pl.ds(start, UNIT_WIDE)],
                (((1,), (1,)), ((), ())), preferred_element_type=jnp.float32,
            )
        heads_total[...] = total
        for upper, target in enumerate((t // 2, GROUPS - 1 - t // 2)):

            @pl.when(target == group)
            def _():
                add_grads(pl.multiple_of((t % 2) * UNIT_WIDE, UNIT_WIDE), tokens[t, upper], heads[...])

    def use_columns(p):
        j, e = p // 2, p % 2
        for h in range(2):

            def put(side, rows, block):
                column_tokens[side, h * rows_dev + rows.start : h * rows_dev + rows.stop] = block

            split_blocks(columns, 2 * p + h, h, put)
        slot = plane_slot(2 * (1 - z // 2) + j, z)

        @pl.when(e == 0)
        def _():
            heads_arrived(slot + 1 - core)

        head_rows = heads_all[pl.ds(slot, 2)].reshape(2 * rows_dev, depth)
        for side in range(2):
            add_grads(pl.multiple_of(side * UNIT_WIDE + e * WIDE, WIDE), column_tokens[side], head_rows)

    def use_near(slot, heads_slot):
        wait_arrived(from_near.at[slot], near_recv.at[slot])
        for side in range(2):
            add_grads(side * UNIT_WIDE, from_near[slot, side], heads_all[heads_slot])

    gain_partners = [
        {"tp": x * SIDE + y + 1 - 2 * (y % 2)},
        {"tp": x * SIDE + SIDE - 1 - y},
        {"tp": (x + 1 - 2 * (x % 2)) * SIDE + y},
        {"tp": (SIDE - 1 - x) * SIDE + y},
        sibling,
        {"grp": 2 * next_plane + core},
        {"grp": 2 * (SIDE - 1 - z) + core},
    ]

    def gain_copy(step):
        return remote(
            gain_own.at[step], gain_got.at[step], gain_send.at[step], gain_recv.at[step], gain_partners[step]
        )

    own_grad_store, heads_store, gain_store, grads_store = [
        pltpu.make_async_copy(source, target, output_sem.at[at])
        for at, (source, target) in enumerate(
            ((own_grad, grad_out), (heads_done, heads_out), (gain_done, gain_out), (grads, grads_out))
        )
    ]

    def value_unit(q):
        return (q + first_unit) % UNITS

    def gather_stage(q, stage):
        def pass_on(gather, recvs, p):
            wait_arrived(gather_sizes[stage], recvs.at[p, stage])
            if stage < 3:
                for h in range(2):
                    gather(p, h, 2 * stage + 2).start()
                    gather(p, h, 2 * stage + 3).start()

        @pl.when(within(q, UNITS))
        def _():
            pass_on(gather_values, value_recv, value_unit(q))

        @pl.when(within(q - UNITS, FAR_UNITS))
        def _():
            pass_on(gather_columns, column_recv, q - UNITS)

    def gather_turn(n, carry):
        @pl.when(n == 4)
        def _():
            each_relay((2,), pass_relay)

        @pl.when(n == 9)
        def _():
            pass_heads()

        for step in range(GAIN_STEPS + 1):

            @pl.when(n == step + 1)
            def _():
                if step > 0:
                    gain_copy(step - 1).wait_recv()
                    gain_own[step] = gain_own[step - 1] + gain_got[step - 1]
                if step < GAIN_STEPS:
                    gain_copy(step).start()
                else:
                    gain_done[...] = gain_own[GAIN_STEPS] * grad_scale
                    gain_store.start()

        @pl.when(within(n + 1 - UNITS, FAR_UNITS))
        def _():
            p = n + 1 - UNITS
            wait_arrived(gather_sizes[1], exchange_recv.at[p])
            for h in range(2):
                gather_columns(p, h, 0).start()
                gather_columns(p, h, 1).start()

        @pl.when(n == UNITS + FAR_UNITS + 4)
        def _():
            near_heads = plane_slot(next_plane, z)
            heads_arrived(near_heads + 1 - core)
            for k in range(2):
                use_near(1 + k, near_heads + k)

        gather_stage(n, 0)
        gather_stage(n - 4, 2)
        gather_stage(n - 2, 1)
        gather_stage(n - 5, 3)
        done = n - 5

        @pl.when(within(done, UNITS))
        def _():
            use_values(value_unit(done))

        @pl.when(done == UNITS)
        def _():
            heads_done[...] = narrow(heads_total[...])
            heads_store.start()
            heads_arrived(SLOTS - 1)
            use_near(0, SLOTS - 1)

        @pl.when(within(done - UNITS, FAR_UNITS))
        def _():
            use_columns(done - UNITS)

        return carry

    own_grad_store.start()
    each_relay((1,), pass_relay)
    lax.fori_loop(0, UNITS + FAR_UNITS + 5, gather_turn, 0)
    grads_store.start()

    def reduce_sent(u, carry):
        wait_sent(part.at[0:2], send_sem.at[u])
        wait_sent(values.at[0:5, 0:3, 0:2], value_send.at[u])
        return carry

    def columns_sent(p, carry):
        wait_sent(values.at[0:5, 0:3, 0:2], column_send.at[p])
        return carry

    lax.fori_loop(0, UNITS, reduce_sent, 0)
    lax.fori_loop(0, FAR_UNITS, columns_sent, 0)
    wait_sent(exchange.at[0:SIDE], exchange_send.at[0])
    wait_sent(tokens.at[0:3], near_send.at[0])
    each_relay((0, 1, 2), lambda relay, held: relay.wait_send())
    for j in range(SIDE - 1):
        passed_heads(j).wait_send()
    sibling_heads().wait_send()
    for step in range(GAIN_STEPS):
        gain_copy(step).wait_send()
    for store in (own_grad_store, heads_store, gain_store, grads_store):
        store.wait()


def deliver_kernel(*refs):
    results, outputs, held = refs[:4], refs[4:8], refs[8:12]
    load_sem, store_sem = refs[12:]
    loads = [pltpu.make_async_copy(results[at], held[at], load_sem.at[at]) for at in range(4)]
    stores = [pltpu.make_async_copy(held[at], outputs[at], store_sem.at[at]) for at in range(4)]
    for load in loads:
        load.start()
    for load, store in zip(loads, stores):
        load.wait()
        store.start()
    for store in stores:
        store.wait()


def delivered(results):
    hbm = pl.BlockSpec(memory_space=pl.ANY)
    return pl.pallas_call(
        deliver_kernel,
        out_shape=tuple(jax.ShapeDtypeStruct(result.shape, result.dtype) for result in results),
        in_specs=[hbm] * 4,
        out_specs=(hbm,) * 4,
        scratch_shapes=[pltpu.VMEM(result.shape, result.dtype) for result in results]
        + [pltpu.SemaphoreType.DMA((4,))] * 2,
        name="deliver",
    )(*results)


def fused(heads, weights, residual, gain):
    hbm = pl.BlockSpec(memory_space=pl.ANY)
    bf16, f32 = jnp.bfloat16, jnp.float32
    rows_dev, depth = heads.shape
    owned = weights.shape[1] // GROUPS
    dma = pltpu.SemaphoreType.DMA
    return pl.pallas_call(
        boundary_kernel,
        out_shape=(
            jax.ShapeDtypeStruct(heads.shape, bf16),
            jax.ShapeDtypeStruct((owned, depth), f32),
            jax.ShapeDtypeStruct(residual.shape, bf16),
            jax.ShapeDtypeStruct(gain.shape, f32),
        ),
        in_specs=[hbm] * 4,
        out_specs=(hbm,) * 4,
        scratch_shapes=[
            pltpu.VMEM(heads.shape, bf16),
            pltpu.VMEM(residual.shape, bf16),
            pltpu.VMEM(gain.shape, f32),
            pltpu.VMEM(heads.shape, bf16),
            pltpu.VMEM((owned, depth), f32),
            pltpu.VMEM(residual.shape, bf16),
            pltpu.VMEM(gain.shape, f32),
            pltpu.VMEM(weights.shape, bf16),
            pltpu.VMEM((CHUNKS, SIDE, SIDE, TALL, WIDE), bf16),
            pltpu.VMEM((CHUNKS, 2, SIDE, TALL, HALF), bf16),
            pltpu.VMEM((CHUNKS, 2, SIDE, TALL, WIDE), bf16),
            pltpu.VMEM((CHUNKS, 2, TALL, HALF), bf16),
            pltpu.VMEM((CHUNKS, 2, TALL, WIDE), bf16),
            pltpu.VMEM((2, CHUNKS, TALL, WIDE), bf16),
            pltpu.VMEM((CHUNKS, SIDE, SIDE, TALL, WIDE), bf16),
            pltpu.VMEM((FAR_CHUNKS, SIDE, SIDE, TALL, WIDE), bf16),
            pltpu.VMEM((GROUPS, 2, TALL, WIDE), bf16),
            pltpu.VMEM((UNITS, 2, rows_dev, UNIT_WIDE), bf16),
            pltpu.VMEM((2, 2 * rows_dev, WIDE), bf16),
            pltpu.VMEM((3, 2, rows_dev, UNIT_WIDE), bf16),
            pltpu.VMEM((SLOTS, rows_dev, depth), bf16),
            pltpu.VMEM((rows_dev, depth), f32),
            pltpu.VMEM((GAIN_STEPS + 1,) + gain.shape, f32),
            pltpu.VMEM((GAIN_STEPS,) + gain.shape, f32),
            dma((3,)),
            dma((4,)),
            dma((UNITS, 2)),
            dma((UNITS,)),
            dma((UNITS, 5)),
            dma((UNITS,)),
            dma((UNITS, 4)),
            dma((FAR_UNITS,)),
            dma((FAR_UNITS, 4)),
            dma((1,)),
            dma((FAR_UNITS,)),
            dma((SLOTS + 6,)),
            dma((SLOTS,)),
            dma((1,)),
            dma((3,)),
            dma((GAIN_STEPS,)),
            dma((GAIN_STEPS,)),
        ],
        compiler_params=pltpu.CompilerParams(
            collective_id=0, has_side_effects=True, vmem_limit_bytes=62 * 1024 * 1024
        ),
        name="boundary",
    )(heads, weights, residual, gain)


def per_device(heads_in, weights, residual, norm_gain):
    heads_out, weight_grad, boundary_grad, gain_grad = delivered(
        fused(heads_in[0], weights[0], residual, norm_gain[None])
    )
    return (heads_out[None], weight_grad[None], boundary_grad, gain_grad[0])


def solution(mesh):
    placed = (P("section", "grp", "tp"), P("section", "tp", None), P(("grp", "tp"), None), P())
    return jax.shard_map(
        per_device,
        mesh=mesh,
        in_specs=placed,
        out_specs=(
            P("section", "grp", "tp"),
            P("section", "grp", "tp"),
            P(("grp", "tp"), None),
            P(),
        ),
        check_vma=False,
    )
```

```python
import math

import jax
import jax.numpy as jnp
from jax import lax
from jax.experimental import pallas as pl
from jax.experimental.pallas import tpu as pltpu
from jax.sharding import PartitionSpec as P

EPSILON = 1e-05
MESH = pl.DeviceIdType.MESH

SIDE = 4
GROUPS = 8
UNITS = 8
FAR_UNITS = 4
CHUNKS = 2 * UNITS
FAR_CHUNKS = 2 * FAR_UNITS
WIDE = 256
HALF = WIDE // 2
UNIT_WIDE = 2 * WIDE
SHARD = 2 * UNIT_WIDE
OWN = 24
TALL = 2 * OWN
SLOTS = GROUPS - 1
GAIN_STEPS = 7


def lower_start(t, h=0):
    return pl.multiple_of(t * UNIT_WIDE + h * WIDE, WIDE)


def upper_start(t, h=0):
    return pl.multiple_of((GROUPS - 1 - t // 2) * SHARD + (t % 2) * UNIT_WIDE + h * WIDE, WIDE)


def plane_device(h, first, second):
    x, y = (first, second) if h == 0 else (second, first)
    return {"tp": x * SIDE + y}


def stacked(*parts):
    return jnp.concatenate(parts, axis=0)


def both_halves(row_pair):
    total = row_pair[:OWN] + row_pair[OWN:]
    return stacked(total, total)


def lanes(value):
    return sum(value[:, 128 * i : 128 * (i + 1)] for i in range(value.shape[1] // 128))


def wide(value):
    return value.astype(jnp.float32)


def narrow(value):
    return value.astype(jnp.bfloat16)


def remote(source, target, send_sem, recv_sem, device):
    return pltpu.make_async_remote_copy(
        src_ref=source,
        dst_ref=target,
        send_sem=send_sem,
        recv_sem=recv_sem,
        device_id=device,
        device_id_type=MESH,
    )


def greet(peers):
    barrier = pltpu.get_barrier_semaphore()
    for peer in peers:
        pl.semaphore_signal(barrier, inc=1, device_id=peer, device_id_type=MESH)
    pl.semaphore_wait(barrier, len(peers))


def boundary_kernel(
    heads_in, weights, residual_in, gain_in, heads_out, grads_out, grad_out, gain_out,
    heads, residual, gain, heads_done, grads, own_grad, gain_done,
    heads_t, grads_t, weight_buf, part, from1, from2, from3, from4, both,
    values, columns, exchange, tokens, column_tokens, from_near, heads_all, heads_total, gain_own, gain_got,
    input_sem, output_sem, weight_sem, send_sem, recv_sem, value_send, value_recv, column_send, column_recv,
    exchange_send, exchange_recv, heads_send, heads_recv, near_send, near_recv, gain_send, gain_recv,
):
    tp = lax.axis_index("tp")
    x, y = tp // SIDE, tp % SIDE
    section = lax.axis_index("section")
    group = lax.axis_index("grp")
    z, core = group // 2, group % 2
    other = {"section": 1 - section}
    sibling_group = 2 * z + 1 - core
    sibling = {"grp": sibling_group}
    next_plane = z + 1 - 2 * (z % 2)
    rows_dev, depth = heads.shape
    grad_scale = 1.0 / math.sqrt(rows_dev * GROUPS)

    def axes(h):
        return (x, y) if h == 0 else (y, x)

    def wait_arrived(size, sem):
        remote(size, size, heads_send.at[0], sem, sibling).wait_recv()

    def wait_sent(size, sem):
        remote(size, size, sem, heads_recv.at[0], sibling).wait_send()

    def weight_copy(t, upper):
        cols = pl.ds(upper_start(t) if upper else lower_start(t), UNIT_WIDE)
        return pltpu.make_async_copy(
            weights.at[:, cols], weight_buf.at[:, cols], weight_sem.at[t, upper]
        )

    def start_weights(t, carry):
        weight_copy(t, 0).start()
        weight_copy(t, 1).start()
        return carry

    heads_load, residual_load, gain_load = [
        pltpu.make_async_copy(source, target, input_sem.at[at])
        for at, (source, target) in enumerate(
            ((heads_in, heads), (residual_in, residual), (gain_in, gain))
        )
    ]
    heads_load.start()
    lax.fori_loop(0, UNITS, start_weights, 0)
    residual_load.start()
    gain_load.start()
    greet(
        [plane_device(0, (x + step) % SIDE, y) for step in (1, 3)]
        + [plane_device(0, x, (y + step) % SIDE) for step in (1, 3)]
        + [other, sibling]
        + [{"grp": 2 * ((z + hop) % SIDE) + k} for hop in range(1, SIDE) for k in range(2)]
    )
    heads_load.wait()

    def plane_slot(origin, at):
        return 2 * ((origin + SIDE - 1 - at) % SIDE)

    def heads_arrived(slot):
        remote(
            heads_t, heads_all.at[slot], heads_send.at[SLOTS - 1], heads_recv.at[slot], sibling
        ).wait_recv()

    def sibling_heads():
        slot = SLOTS - 1
        return remote(
            heads_t, heads_all.at[slot], heads_send.at[slot], heads_recv.at[slot], sibling
        )

    relays = ((1, 0), (-1, 0), (1, 1), (-1, 1), (1, 2), (-1, 2))

    def each_relay(wanted, act):
        for at, (step, away) in enumerate(relays):
            if away not in wanted:
                continue
            first, last = (away, SIDE - 2) if step > 0 else (1, SIDE - 1 - away)

            @pl.when(jnp.logical_and(z >= first, z <= last))
            def _():
                origin, target = z - step * away, z + step
                held = plane_slot(origin, z) + core
                slot = plane_slot(origin, target) + core
                act(
                    remote(
                        heads_all.at[held] if away else heads_t,
                        heads_all.at[slot],
                        heads_send.at[SLOTS + at],
                        heads_recv.at[slot],
                        {"grp": 2 * target + core},
                    ),
                    held,
                )

    def start_relay(relay, held):
        relay.start()

    def pass_relay(relay, held):
        heads_arrived(held)
        relay.start()

    def passed_heads(j):
        slot = 2 * j + core
        held = heads_all.at[slot]
        return remote(held, held, heads_send.at[slot], heads_recv.at[slot], sibling)

    def pass_heads():
        @pl.when(jnp.logical_or(z == 0, z == SIDE - 1))
        def _():
            for j in range(SIDE - 1):
                heads_arrived(2 * j + core)

        for j in range(SIDE - 1):
            passed_heads(j).start()

    def send_heads():
        heads_t[...] = heads[...].T
        each_relay((0,), start_relay)
        sibling_heads().start()


    def copy(u, h, step):
        chunk = 2 * u + h
        a, b = axes(h)
        right, left = (a + 1) % SIDE, (a + 3) % SIDE
        up, down = (b + 1) % SIDE, (b + 3) % SIDE
        low, high = pl.ds(0, HALF), pl.ds(HALF, HALF)
        far_a, far_b = (a + 2) % SIDE, (b + 2) % SIDE
        source, target, device = [
            lambda: (part.at[chunk, far_a, :, :, low], from1.at[chunk, 0], plane_device(h, right, b)),
            lambda: (part.at[chunk, far_a, :, :, high], from1.at[chunk, 1], plane_device(h, left, b)),
            lambda: (part.at[chunk, right], from2.at[chunk, 0], plane_device(h, right, b)),
            lambda: (part.at[chunk, left], from2.at[chunk, 1], plane_device(h, left, b)),
            lambda: (part.at[chunk, a, far_b, :, low], from3.at[chunk, 0], plane_device(h, a, up)),
            lambda: (part.at[chunk, a, far_b, :, high], from3.at[chunk, 1], plane_device(h, a, down)),
            lambda: (part.at[chunk, a, up], from4.at[chunk, 0], plane_device(h, a, up)),
            lambda: (part.at[chunk, a, down], from4.at[chunk, 1], plane_device(h, a, down)),
            lambda: (both.at[section, chunk], both.at[section, chunk], other),
        ][step]()
        return remote(source, target, send_sem.at[u], recv_sem.at[u, step // 2], device)

    reduce_sizes = [
        part.at[0, 0:2], part.at[0], part.at[0, 0, 0:2], part.at[0, 0], part.at[0, 0, 0:2]
    ]

    def arrive(u, stage):
        wait_arrived(reduce_sizes[stage], recv_sem.at[u, stage])

    def multiply(u):
        weight_copy(u, 0).wait()
        weight_copy(u, 1).wait()
        lower, upper = [
            jnp.dot(
                heads[...], weight_buf[:, pl.ds(start, UNIT_WIDE)],
                preferred_element_type=jnp.float32,
            )
            for start in (lower_start(u), upper_start(u))
        ]
        for h in range(2):
            cols = slice(h * WIDE, (h + 1) * WIDE)
            for i in range(SIDE * SIDE):
                rows = slice(OWN * i, OWN * (i + 1))
                a, b = (i // SIDE, i % SIDE) if h == 0 else (i % SIDE, i // SIDE)
                part[2 * u + h, a, b] = narrow(stacked(lower[rows, cols], upper[rows, cols]))
            copy(u, h, 0).start()
            copy(u, h, 1).start()

    def near_first(u):
        arrive(u, 0)
        for h in range(2):
            chunk = 2 * u + h
            a, b = axes(h)
            right, left = (a + 1) % SIDE, (a + 3) % SIDE
            part[chunk, right, :, :, :HALF] = narrow(
                wide(part[chunk, right, :, :, :HALF]) + wide(from1[chunk, 0])
            )
            copy(u, h, 2).start()
            part[chunk, left, :, :, HALF:] = narrow(
                wide(part[chunk, left, :, :, HALF:]) + wide(from1[chunk, 1])
            )
            copy(u, h, 3).start()

    def far_second(u):
        arrive(u, 1)
        for h in range(2):
            chunk = 2 * u + h
            a, b = axes(h)
            part[chunk, a] = narrow(
                wide(part[chunk, a]) + (wide(from2[chunk, 0]) + wide(from2[chunk, 1]))
            )
            copy(u, h, 4).start()
            copy(u, h, 5).start()

    def near_second(u):
        arrive(u, 2)
        for h in range(2):
            chunk = 2 * u + h
            a, b = axes(h)
            up, down = (b + 1) % SIDE, (b + 3) % SIDE
            part[chunk, a, up, :, :HALF] = narrow(
                wide(part[chunk, a, up, :, :HALF]) + wide(from3[chunk, 0])
            )
            copy(u, h, 6).start()
            part[chunk, a, down, :, HALF:] = narrow(
                wide(part[chunk, a, down, :, HALF:]) + wide(from3[chunk, 1])
            )
            copy(u, h, 7).start()

    def finish(u):
        arrive(u, 3)
        for h in range(2):
            chunk = 2 * u + h
            a, b = axes(h)
            total = wide(part[chunk, a, b]) + (wide(from4[chunk, 0]) + wide(from4[chunk, 1]))
            rows = stacked(
                wide(residual[:, pl.ds(lower_start(u, h), WIDE)]),
                wide(residual[:, pl.ds(upper_start(u, h), WIDE)]),
            )
            total = total + jnp.where(section == 0, rows, 0.0)
            both[section, chunk] = narrow(total)
            copy(u, h, 8).start()

    def within(value, count):
        return jnp.logical_and(value >= 0, value < count)

    stages = (multiply, near_first, far_second, near_second, finish)

    def reduce_turn(n, carry):
        for late, stage in enumerate(stages):

            @pl.when(within(n - late, UNITS))
            def _():
                stage(n - late)

        @pl.when(n == 1)
        def _():
            send_heads()

        @pl.when(n == UNITS - 1)
        def _():
            each_relay((1,), pass_relay)

        return carry

    residual_load.wait()
    gain_load.wait()
    lax.fori_loop(0, UNITS + len(stages) - 1, reduce_turn, 0)
    heads_total[...] = jnp.zeros_like(heads_total)
    grads_t[...] = jnp.zeros_like(grads_t)


    def gather_of(store, sends, recvs):
        half = store.shape[-1] // 2

        def gather(p, h, step):
            chunk = 2 * p + h
            a, b = axes(h)
            right, left = (a + 1) % SIDE, (a + 3) % SIDE
            up, down = (b + 1) % SIDE, (b + 3) % SIDE
            low, high = pl.ds(0, half), pl.ds(half, half)
            block, device = [
                lambda: (store.at[chunk, b, a], plane_device(h, right, b)),
                lambda: (store.at[chunk, b, a], plane_device(h, left, b)),
                lambda: (store.at[chunk, b, left, :, low], plane_device(h, right, b)),
                lambda: (store.at[chunk, b, right, :, high], plane_device(h, left, b)),
                lambda: (store.at[chunk, b], plane_device(h, a, up)),
                lambda: (store.at[chunk, b], plane_device(h, a, down)),
                lambda: (store.at[chunk, down, :, :, low], plane_device(h, a, up)),
                lambda: (store.at[chunk, up, :, :, high], plane_device(h, a, down)),
            ][step]()
            return remote(block, block, sends.at[p], recvs.at[p, step // 2], device)

        return gather

    gather_values = gather_of(values, value_send, value_recv)
    gather_columns = gather_of(columns, column_send, column_recv)

    gather_sizes = [values.at[0, 0], values.at[0, 0, 0:2], values.at[0], values.at[0, 0:2]]

    def exchanged(target, e):
        unit = 2 * (z % 2) + e
        a, b = x + core * (y - x), y + core * (x - y)
        return remote(
            exchange.at[target, e],
            columns.at[2 * unit + core, b, a],
            exchange_send.at[0],
            exchange_recv.at[unit],
            {"grp": target},
        )

    def gain_rows(t, h):
        return stacked(
            jnp.broadcast_to(gain[:, pl.ds(lower_start(t, h), WIDE)], (OWN, WIDE)),
            jnp.broadcast_to(gain[:, pl.ds(upper_start(t, h), WIDE)], (OWN, WIDE)),
        )

    zero = jnp.zeros((TALL, 128), jnp.float32)

    def row_mean(total):
        return both_halves(jnp.sum(total, axis=1, keepdims=True)) / (GROUPS * SHARD)

    def add_sums(t, total):
        arrive(t, 4)
        for h in range(2):
            total = total + lanes(wide(both[0, 2 * t + h]))
        return total

    mean = row_mean(lax.fori_loop(0, UNITS, add_sums, zero))

    def add_squares(t, total):
        for h in range(2):
            centred = wide(both[0, 2 * t + h]) - mean
            total = total + lanes(centred * centred)
        return total

    inv_scale = lax.rsqrt(row_mean(lax.fori_loop(0, UNITS, add_squares, zero)) + EPSILON)

    def add_means(t, totals):
        for h in range(2):
            unit = (wide(both[0, 2 * t + h]) - mean) * inv_scale
            scaled = gain_rows(t, h) * wide(both[1, 2 * t + h])
            totals = (totals[0] + lanes(scaled), totals[1] + lanes(scaled * unit))
        return totals

    sums = lax.fori_loop(0, UNITS, add_means, (zero, zero))
    mean_scaled, mean_product = row_mean(sums[0]), row_mean(sums[1])
    first_unit = SIDE * ((z // 2 + z % 2 + 1) % 2)

    def write(turn, carry):
        shard = (turn + first_unit // 2) % SIDE
        kept = []
        for v in range(2):
            t = 2 * shard + v
            for h in range(2):
                chunk = 2 * t + h
                a, b = axes(h)
                rows = gain_rows(t, h)
                unit = (wide(both[0, chunk]) - mean) * inv_scale
                d_normed = wide(both[1, chunk])
                grad = inv_scale * (rows * d_normed - mean_scaled - unit * mean_product)
                value = jnp.where(section == 0, grad, unit * rows)
                values[chunk, b, a] = narrow(value)
                gather_values(t, h, 0).start()
                gather_values(t, h, 1).start()
                kept.append(value)
                product = d_normed * unit
                for start, rows in (
                    (lower_start(t, h), slice(0, OWN)),
                    (upper_start(t, h), slice(OWN, TALL)),
                ):
                    own_grad[:, pl.ds(start, WIDE)] = narrow(grad[rows])
                    gain_own[0, :, pl.ds(start, WIDE)] = jnp.sum(product[rows], axis=0, keepdims=True)
        for target, rows in ((shard, slice(0, OWN)), (GROUPS - 1 - shard, slice(OWN, TALL))):
            for e in range(2):
                exchange[target, e] = narrow(stacked(kept[e][rows], kept[2 + e][rows]))

                @pl.when(target // SIDE != z // 2)
                def _():
                    exchanged(target, e).start()
        return carry

    lax.fori_loop(0, SIDE, write, 0)


    def near_copy(t, upper, target, slot):
        return remote(
            tokens.at[t, upper],
            from_near.at[slot, t % 2],
            near_send.at[0],
            near_recv.at[slot],
            {"grp": target},
        )

    def split_blocks(store, chunk, h, put):
        for i in range(0, SIDE * SIDE, 2):
            pair = []
            for at in (i, i + 1):
                a, b = (at // SIDE, at % SIDE) if h == 0 else (at % SIDE, at // SIDE)
                pair.append(wide(store[chunk, b, a]))
            put(0, slice(OWN * i, OWN * (i + 2)), narrow(stacked(pair[0][:OWN], pair[1][:OWN])))
            put(1, slice(OWN * i, OWN * (i + 2)), narrow(stacked(pair[0][OWN:], pair[1][OWN:])))

    def add_grads(start, transposed_heads, token_rows):
        cols = pl.ds(start, token_rows.shape[1])
        grads_t[:, cols] += jnp.dot(
            transposed_heads, token_rows, preferred_element_type=jnp.float32
        )

    def store_grads(block):
        return pltpu.make_async_copy(
            grads.at[block * WIDE : (block + 1) * WIDE],
            grads_out.at[block * WIDE : (block + 1) * WIDE],
            output_sem.at[3 + block],
        )

    def finish_grads(blocks):
        for block in blocks:
            cols = slice(block * WIDE, (block + 1) * WIDE)
            grads[cols] = grad_scale * grads_t[:, cols].T
            store_grads(block).start()

    def use_values(t):
        for h in range(2):

            def put(upper, rows, block):
                tokens[t, upper, rows, h * WIDE : (h + 1) * WIDE] = block

            split_blocks(values, 2 * t + h, h, put)
        for upper, target in enumerate((t // 2, GROUPS - 1 - t // 2)):
            for slot, wanted in ((0, target == sibling_group), (1 + core, target // 2 == next_plane)):

                @pl.when(wanted)
                def _():
                    near_copy(t, upper, target, slot).start()

        total = heads_total[...]
        for upper, start in enumerate((lower_start(t), upper_start(t))):
            total = total + lax.dot_general(
                tokens[t, upper], weight_buf[:, pl.ds(start, UNIT_WIDE)],
                (((1,), (1,)), ((), ())), preferred_element_type=jnp.float32,
            )
        heads_total[...] = total
        for upper, target in enumerate((t // 2, GROUPS - 1 - t // 2)):

            @pl.when(target == group)
            def _():
                add_grads(pl.multiple_of((t % 2) * UNIT_WIDE, UNIT_WIDE), heads_t[...], tokens[t, upper])

    def use_columns(p):
        j, e = p // 2, p % 2
        for h in range(2):

            def put(side, rows, block):
                column_tokens[h, rows, side * WIDE : (side + 1) * WIDE] = block

            split_blocks(columns, 2 * p + h, h, put)
        slot = plane_slot(2 * (1 - z // 2) + j, z)

        @pl.when(e == 0)
        def _():
            heads_arrived(slot + 1 - core)

        total = jnp.dot(
            heads_all[slot], column_tokens[0], preferred_element_type=jnp.float32
        ) + jnp.dot(heads_all[slot + 1], column_tokens[1], preferred_element_type=jnp.float32)
        for side in range(2):
            cols = pl.ds(pl.multiple_of(side * UNIT_WIDE + e * WIDE, WIDE), WIDE)
            grads_t[:, cols] += total[:, side * WIDE : (side + 1) * WIDE]

    def use_near(slot, heads_slot):
        wait_arrived(from_near.at[slot], near_recv.at[slot])
        for side in range(2):
            add_grads(side * UNIT_WIDE, heads_all[heads_slot], from_near[slot, side])

    gain_partners = [
        {"tp": x * SIDE + y + 1 - 2 * (y % 2)},
        {"tp": x * SIDE + SIDE - 1 - y},
        {"tp": (x + 1 - 2 * (x % 2)) * SIDE + y},
        {"tp": (SIDE - 1 - x) * SIDE + y},
        sibling,
        {"grp": 2 * next_plane + core},
        {"grp": 2 * (SIDE - 1 - z) + core},
    ]

    def gain_copy(step):
        return remote(
            gain_own.at[step], gain_got.at[step], gain_send.at[step], gain_recv.at[step], gain_partners[step]
        )

    own_grad_store, heads_store, gain_store = [
        pltpu.make_async_copy(source, target, output_sem.at[at])
        for at, (source, target) in enumerate(
            ((own_grad, grad_out), (heads_done, heads_out), (gain_done, gain_out))
        )
    ]

    def value_unit(q):
        return (q + first_unit) % UNITS

    def gather_stage(q, stage):
        def pass_on(gather, recvs, p):
            wait_arrived(gather_sizes[stage], recvs.at[p, stage])
            if stage < 3:
                for h in range(2):
                    gather(p, h, 2 * stage + 2).start()
                    gather(p, h, 2 * stage + 3).start()

        @pl.when(within(q, UNITS))
        def _():
            pass_on(gather_values, value_recv, value_unit(q))

        @pl.when(within(q - UNITS, FAR_UNITS))
        def _():
            pass_on(gather_columns, column_recv, q - UNITS)

    def gather_turn(n, carry):
        @pl.when(n == 5)
        def _():
            pass_heads()

        for step in range(GAIN_STEPS + 1):

            @pl.when(n == step + 1)
            def _():
                if step > 0:
                    gain_copy(step - 1).wait_recv()
                    gain_own[step] = gain_own[step - 1] + gain_got[step - 1]
                if step < GAIN_STEPS:
                    gain_copy(step).start()
                else:
                    gain_done[...] = gain_own[GAIN_STEPS] * grad_scale
                    gain_store.start()

        @pl.when(within(n + 1 - UNITS, FAR_UNITS))
        def _():
            p = n + 1 - UNITS
            wait_arrived(gather_sizes[1], exchange_recv.at[p])
            for h in range(2):
                gather_columns(p, h, 0).start()
                gather_columns(p, h, 1).start()

        @pl.when(n == UNITS + FAR_UNITS + 4)
        def _():
            near_heads = plane_slot(next_plane, z)
            heads_arrived(near_heads + 1 - core)
            for k in range(2):
                use_near(1 + k, near_heads + k)
            finish_grads((0, 2))

        gather_stage(n, 0)
        gather_stage(n - 4, 2)
        gather_stage(n - 2, 1)
        gather_stage(n - 5, 3)
        done = n - 5

        @pl.when(within(done, UNITS))
        def _():
            use_values(value_unit(done))

        @pl.when(done == UNITS)
        def _():
            heads_done[...] = narrow(heads_total[...])
            heads_store.start()
            heads_arrived(SLOTS - 1)
            use_near(0, SLOTS - 1)

        @pl.when(within(done - UNITS, FAR_UNITS))
        def _():
            use_columns(done - UNITS)

        return carry

    own_grad_store.start()
    each_relay((2,), pass_relay)
    lax.fori_loop(0, UNITS + FAR_UNITS + 5, gather_turn, 0)
    finish_grads((1, 3))

    def reduce_sent(u, carry):
        wait_sent(part.at[0:2], send_sem.at[u])
        wait_sent(values.at[0:5, 0:3, 0:2], value_send.at[u])
        return carry

    def columns_sent(p, carry):
        wait_sent(values.at[0:5, 0:3, 0:2], column_send.at[p])
        return carry

    lax.fori_loop(0, UNITS, reduce_sent, 0)
    lax.fori_loop(0, FAR_UNITS, columns_sent, 0)
    wait_sent(exchange.at[0:SIDE], exchange_send.at[0])
    wait_sent(tokens.at[0:3], near_send.at[0])
    each_relay((0, 1, 2), lambda relay, held: relay.wait_send())
    for j in range(SIDE - 1):
        passed_heads(j).wait_send()
    sibling_heads().wait_send()
    for step in range(GAIN_STEPS):
        gain_copy(step).wait_send()
    for store in [own_grad_store, heads_store, gain_store] + [store_grads(i) for i in range(4)]:
        store.wait()


def deliver_kernel(*refs):
    results, outputs, held = refs[:4], refs[4:8], refs[8:12]
    load_sem, store_sem = refs[12:]
    loads = [pltpu.make_async_copy(results[at], held[at], load_sem.at[at]) for at in range(4)]
    stores = [pltpu.make_async_copy(held[at], outputs[at], store_sem.at[at]) for at in range(4)]
    for load in loads:
        load.start()
    for load, store in zip(loads, stores):
        load.wait()
        store.start()
    for store in stores:
        store.wait()


def delivered(results):
    hbm = pl.BlockSpec(memory_space=pl.ANY)
    return pl.pallas_call(
        deliver_kernel,
        out_shape=tuple(jax.ShapeDtypeStruct(result.shape, result.dtype) for result in results),
        in_specs=[hbm] * 4,
        out_specs=(hbm,) * 4,
        scratch_shapes=[pltpu.VMEM(result.shape, result.dtype) for result in results]
        + [pltpu.SemaphoreType.DMA((4,))] * 2,
        name="deliver",
    )(*results)


def fused(heads, weights, residual, gain):
    hbm = pl.BlockSpec(memory_space=pl.ANY)
    bf16, f32 = jnp.bfloat16, jnp.float32
    rows_dev, depth = heads.shape
    owned = weights.shape[1] // GROUPS
    dma = pltpu.SemaphoreType.DMA
    return pl.pallas_call(
        boundary_kernel,
        out_shape=(
            jax.ShapeDtypeStruct(heads.shape, bf16),
            jax.ShapeDtypeStruct((owned, depth), f32),
            jax.ShapeDtypeStruct(residual.shape, bf16),
            jax.ShapeDtypeStruct(gain.shape, f32),
        ),
        in_specs=[hbm] * 4,
        out_specs=(hbm,) * 4,
        scratch_shapes=[
            pltpu.VMEM(heads.shape, bf16),
            pltpu.VMEM(residual.shape, bf16),
            pltpu.VMEM(gain.shape, f32),
            pltpu.VMEM(heads.shape, bf16),
            pltpu.VMEM((owned, depth), f32),
            pltpu.VMEM(residual.shape, bf16),
            pltpu.VMEM(gain.shape, f32),
            pltpu.VMEM((depth, rows_dev), bf16),
            pltpu.VMEM((depth, owned), f32),
            pltpu.VMEM(weights.shape, bf16),
            pltpu.VMEM((CHUNKS, SIDE, SIDE, TALL, WIDE), bf16),
            pltpu.VMEM((CHUNKS, 2, SIDE, TALL, HALF), bf16),
            pltpu.VMEM((CHUNKS, 2, SIDE, TALL, WIDE), bf16),
            pltpu.VMEM((CHUNKS, 2, TALL, HALF), bf16),
            pltpu.VMEM((CHUNKS, 2, TALL, WIDE), bf16),
            pltpu.VMEM((2, CHUNKS, TALL, WIDE), bf16),
            pltpu.VMEM((CHUNKS, SIDE, SIDE, TALL, WIDE), bf16),
            pltpu.VMEM((FAR_CHUNKS, SIDE, SIDE, TALL, WIDE), bf16),
            pltpu.VMEM((GROUPS, 2, TALL, WIDE), bf16),
            pltpu.VMEM((UNITS, 2, rows_dev, UNIT_WIDE), bf16),
            pltpu.VMEM((2, rows_dev, UNIT_WIDE), bf16),
            pltpu.VMEM((3, 2, rows_dev, UNIT_WIDE), bf16),
            pltpu.VMEM((SLOTS, depth, rows_dev), bf16),
            pltpu.VMEM((rows_dev, depth), f32),
            pltpu.VMEM((GAIN_STEPS + 1,) + gain.shape, f32),
            pltpu.VMEM((GAIN_STEPS,) + gain.shape, f32),
            dma((3,)),
            dma((7,)),
            dma((UNITS, 2)),
            dma((UNITS,)),
            dma((UNITS, 5)),
            dma((UNITS,)),
            dma((UNITS, 4)),
            dma((FAR_UNITS,)),
            dma((FAR_UNITS, 4)),
            dma((1,)),
            dma((FAR_UNITS,)),
            dma((SLOTS + 6,)),
            dma((SLOTS,)),
            dma((1,)),
            dma((3,)),
            dma((GAIN_STEPS,)),
            dma((GAIN_STEPS,)),
        ],
        compiler_params=pltpu.CompilerParams(
            collective_id=0, has_side_effects=True, vmem_limit_bytes=62 * 1024 * 1024
        ),
        name="boundary",
    )(heads, weights, residual, gain)


def per_device(heads_in, weights, residual, norm_gain):
    heads_out, weight_grad, boundary_grad, gain_grad = delivered(
        fused(heads_in[0], weights[0], residual, norm_gain[None])
    )
    return (heads_out[None], weight_grad[None], boundary_grad, gain_grad[0])


def solution(mesh):
    placed = (P("section", "grp", "tp"), P("section", "tp", None), P(("grp", "tp"), None), P())
    return jax.shard_map(
        per_device,
        mesh=mesh,
        in_specs=placed,
        out_specs=(
            P("section", "grp", "tp"),
            P("section", "grp", "tp"),
            P(("grp", "tp"), None),
            P(),
        ),
        check_vma=False,
    )
```

```python
import math

import jax
import jax.numpy as jnp
from jax import lax
from jax.experimental import pallas as pl
from jax.experimental.pallas import tpu as pltpu
from jax.sharding import PartitionSpec as P

EPSILON = 1e-05
MESH = pl.DeviceIdType.MESH

SIDE = 4
GROUPS = 8
UNITS = 8
FAR_UNITS = 5
CHUNKS = 2 * UNITS
FAR_CHUNKS = 2 * FAR_UNITS
WIDE = 256
HALF = WIDE // 2
UNIT_WIDE = 2 * WIDE
SHARD = 2 * UNIT_WIDE
OWN = 24
TALL = 2 * OWN
SLOTS = GROUPS - 1
GAIN_STEPS = 7


def lower_start(t, h=0):
    return pl.multiple_of(t * UNIT_WIDE + h * WIDE, WIDE)


def upper_start(t, h=0):
    return pl.multiple_of((GROUPS - 1 - t // 2) * SHARD + (t % 2) * UNIT_WIDE + h * WIDE, WIDE)


def plane_device(h, first, second):
    x, y = (first, second) if h == 0 else (second, first)
    return {"tp": x * SIDE + y}


def stacked(*parts):
    return jnp.concatenate(parts, axis=0)


def both_halves(row_pair):
    total = row_pair[:OWN] + row_pair[OWN:]
    return stacked(total, total)


def lanes(value):
    return sum(value[:, 128 * i : 128 * (i + 1)] for i in range(value.shape[1] // 128))


def wide(value):
    return value.astype(jnp.float32)


def narrow(value):
    return value.astype(jnp.bfloat16)


def remote(source, target, send_sem, recv_sem, device):
    return pltpu.make_async_remote_copy(
        src_ref=source,
        dst_ref=target,
        send_sem=send_sem,
        recv_sem=recv_sem,
        device_id=device,
        device_id_type=MESH,
    )


def greet(peers):
    barrier = pltpu.get_barrier_semaphore()
    for peer in peers:
        pl.semaphore_signal(barrier, inc=1, device_id=peer, device_id_type=MESH)
    pl.semaphore_wait(barrier, len(peers))


def boundary_kernel(
    heads_in, weights, residual_in, gain_in, heads_out, grads_out, grad_out, gain_out,
    heads, residual, gain, heads_done, grads, own_grad, gain_done,
    heads_t, grads_t, weight_buf, part, from1, from2, from3, from4, both,
    values, columns, exchange, tokens, column_tokens, from_near, heads_all, heads_total, gain_own, gain_got,
    input_sem, output_sem, weight_sem, send_sem, recv_sem, value_send, value_recv, column_send, column_recv,
    exchange_send, exchange_recv, heads_send, heads_recv, near_send, near_recv, gain_send, gain_recv,
):
    tp = lax.axis_index("tp")
    x, y = tp // SIDE, tp % SIDE
    section = lax.axis_index("section")
    group = lax.axis_index("grp")
    z, core = group // 2, group % 2
    other = {"section": 1 - section}
    sibling_group = 2 * z + 1 - core
    sibling = {"grp": sibling_group}
    next_plane = z + 1 - 2 * (z % 2)
    rows_dev, depth = heads.shape
    grad_scale = 1.0 / math.sqrt(rows_dev * GROUPS)

    def axes(h):
        return (x, y) if h == 0 else (y, x)

    def wait_arrived(size, sem):
        remote(size, size, heads_send.at[0], sem, sibling).wait_recv()

    def wait_sent(size, sem):
        remote(size, size, sem, heads_recv.at[0], sibling).wait_send()

    def weight_copy(t, upper):
        cols = pl.ds(upper_start(t) if upper else lower_start(t), UNIT_WIDE)
        return pltpu.make_async_copy(
            weights.at[:, cols], weight_buf.at[:, cols], weight_sem.at[t, upper]
        )

    def start_weights(t, carry):
        weight_copy(t, 0).start()
        weight_copy(t, 1).start()
        return carry

    heads_load, residual_load, gain_load = [
        pltpu.make_async_copy(source, target, input_sem.at[at])
        for at, (source, target) in enumerate(
            ((heads_in, heads), (residual_in, residual), (gain_in, gain))
        )
    ]
    heads_load.start()
    lax.fori_loop(0, UNITS, start_weights, 0)
    residual_load.start()
    gain_load.start()
    greet(
        [plane_device(0, (x + step) % SIDE, y) for step in (1, 3)]
        + [plane_device(0, x, (y + step) % SIDE) for step in (1, 3)]
        + [other, sibling]
        + [{"grp": 2 * ((z + hop) % SIDE) + k} for hop in range(1, SIDE) for k in range(2)]
    )
    heads_load.wait()

    def plane_slot(origin, at):
        return 2 * ((origin + SIDE - 1 - at) % SIDE)

    def heads_arrived(slot):
        remote(
            heads_t, heads_all.at[slot], heads_send.at[SLOTS - 1], heads_recv.at[slot], sibling
        ).wait_recv()

    def sibling_heads():
        slot = SLOTS - 1
        return remote(
            heads_t, heads_all.at[slot], heads_send.at[slot], heads_recv.at[slot], sibling
        )

    relays = ((1, 0), (-1, 0), (1, 1), (-1, 1), (1, 2), (-1, 2))

    def each_relay(wanted, act):
        for at, (step, away) in enumerate(relays):
            if away not in wanted:
                continue
            first, last = (away, SIDE - 2) if step > 0 else (1, SIDE - 1 - away)

            @pl.when(jnp.logical_and(z >= first, z <= last))
            def _():
                origin, target = z - step * away, z + step
                held = plane_slot(origin, z) + core
                slot = plane_slot(origin, target) + core
                act(
                    remote(
                        heads_all.at[held] if away else heads_t,
                        heads_all.at[slot],
                        heads_send.at[SLOTS + at],
                        heads_recv.at[slot],
                        {"grp": 2 * target + core},
                    ),
                    held,
                )

    def start_relay(relay, held):
        relay.start()

    def pass_relay(relay, held):
        heads_arrived(held)
        relay.start()

    def passed_heads(j):
        slot = 2 * j + core
        held = heads_all.at[slot]
        return remote(held, held, heads_send.at[slot], heads_recv.at[slot], sibling)

    def pass_heads():
        @pl.when(jnp.logical_or(z == 0, z == SIDE - 1))
        def _():
            for j in range(SIDE - 1):
                heads_arrived(2 * j + core)

        for j in range(SIDE - 1):
            passed_heads(j).start()

    def send_heads():
        heads_t[...] = heads[...].T
        each_relay((0,), start_relay)
        sibling_heads().start()


    def copy(u, h, step):
        chunk = 2 * u + h
        a, b = axes(h)
        right, left = (a + 1) % SIDE, (a + 3) % SIDE
        up, down = (b + 1) % SIDE, (b + 3) % SIDE
        low, high = pl.ds(0, HALF), pl.ds(HALF, HALF)
        far_a, far_b = (a + 2) % SIDE, (b + 2) % SIDE
        source, target, device = [
            lambda: (part.at[chunk, far_a, :, :, low], from1.at[chunk, 0], plane_device(h, right, b)),
            lambda: (part.at[chunk, far_a, :, :, high], from1.at[chunk, 1], plane_device(h, left, b)),
            lambda: (part.at[chunk, right], from2.at[chunk, 0], plane_device(h, right, b)),
            lambda: (part.at[chunk, left], from2.at[chunk, 1], plane_device(h, left, b)),
            lambda: (part.at[chunk, a, far_b, :, low], from3.at[chunk, 0], plane_device(h, a, up)),
            lambda: (part.at[chunk, a, far_b, :, high], from3.at[chunk, 1], plane_device(h, a, down)),
            lambda: (part.at[chunk, a, up], from4.at[chunk, 0], plane_device(h, a, up)),
            lambda: (part.at[chunk, a, down], from4.at[chunk, 1], plane_device(h, a, down)),
            lambda: (both.at[section, chunk], both.at[section, chunk], other),
        ][step]()
        return remote(source, target, send_sem.at[u], recv_sem.at[u, step // 2], device)

    reduce_sizes = [
        part.at[0, 0:2], part.at[0], part.at[0, 0, 0:2], part.at[0, 0], part.at[0, 0, 0:2]
    ]

    def arrive(u, stage):
        wait_arrived(reduce_sizes[stage], recv_sem.at[u, stage])

    def multiply(u):
        weight_copy(u, 0).wait()
        weight_copy(u, 1).wait()
        lower, upper = [
            jnp.dot(
                heads[...], weight_buf[:, pl.ds(start, UNIT_WIDE)],
                preferred_element_type=jnp.float32,
            )
            for start in (lower_start(u), upper_start(u))
        ]
        for h in range(2):
            cols = slice(h * WIDE, (h + 1) * WIDE)
            for i in range(SIDE * SIDE):
                rows = slice(OWN * i, OWN * (i + 1))
                a, b = (i // SIDE, i % SIDE) if h == 0 else (i % SIDE, i // SIDE)
                part[2 * u + h, a, b] = narrow(stacked(lower[rows, cols], upper[rows, cols]))
            copy(u, h, 0).start()
            copy(u, h, 1).start()

    def near_first(u):
        arrive(u, 0)
        for h in range(2):
            chunk = 2 * u + h
            a, b = axes(h)
            right, left = (a + 1) % SIDE, (a + 3) % SIDE
            part[chunk, right, :, :, :HALF] = narrow(
                wide(part[chunk, right, :, :, :HALF]) + wide(from1[chunk, 0])
            )
            copy(u, h, 2).start()
            part[chunk, left, :, :, HALF:] = narrow(
                wide(part[chunk, left, :, :, HALF:]) + wide(from1[chunk, 1])
            )
            copy(u, h, 3).start()

    def far_second(u):
        arrive(u, 1)
        for h in range(2):
            chunk = 2 * u + h
            a, b = axes(h)
            part[chunk, a] = narrow(
                wide(part[chunk, a]) + (wide(from2[chunk, 0]) + wide(from2[chunk, 1]))
            )
            copy(u, h, 4).start()
            copy(u, h, 5).start()

    def near_second(u):
        arrive(u, 2)
        for h in range(2):
            chunk = 2 * u + h
            a, b = axes(h)
            up, down = (b + 1) % SIDE, (b + 3) % SIDE
            part[chunk, a, up, :, :HALF] = narrow(
                wide(part[chunk, a, up, :, :HALF]) + wide(from3[chunk, 0])
            )
            copy(u, h, 6).start()
            part[chunk, a, down, :, HALF:] = narrow(
                wide(part[chunk, a, down, :, HALF:]) + wide(from3[chunk, 1])
            )
            copy(u, h, 7).start()

    def finish(u):
        arrive(u, 3)
        for h in range(2):
            chunk = 2 * u + h
            a, b = axes(h)
            total = wide(part[chunk, a, b]) + (wide(from4[chunk, 0]) + wide(from4[chunk, 1]))
            rows = stacked(
                wide(residual[:, pl.ds(lower_start(u, h), WIDE)]),
                wide(residual[:, pl.ds(upper_start(u, h), WIDE)]),
            )
            total = total + jnp.where(section == 0, rows, 0.0)
            both[section, chunk] = narrow(total)
            copy(u, h, 8).start()

    def within(value, count):
        return jnp.logical_and(value >= 0, value < count)

    stages = (multiply, near_first, far_second, near_second, finish)

    def reduce_turn(n, carry):
        for late, stage in enumerate(stages):

            @pl.when(within(n - late, UNITS))
            def _():
                stage(n - late)

        @pl.when(n == 1)
        def _():
            send_heads()

        @pl.when(n == UNITS - 1)
        def _():
            each_relay((1,), pass_relay)

        return carry

    residual_load.wait()
    gain_load.wait()
    lax.fori_loop(0, UNITS + len(stages) - 1, reduce_turn, 0)
    heads_total[...] = jnp.zeros_like(heads_total)
    grads_t[...] = jnp.zeros_like(grads_t)


    def gather_of(store, sends, recvs):
        half = store.shape[-1] // 2

        def gather(p, h, step):
            chunk = 2 * p + h
            a, b = axes(h)
            right, left = (a + 1) % SIDE, (a + 3) % SIDE
            up, down = (b + 1) % SIDE, (b + 3) % SIDE
            low, high = pl.ds(0, half), pl.ds(half, half)
            block, device = [
                lambda: (store.at[chunk, b, a], plane_device(h, right, b)),
                lambda: (store.at[chunk, b, a], plane_device(h, left, b)),
                lambda: (store.at[chunk, b, left, :, low], plane_device(h, right, b)),
                lambda: (store.at[chunk, b, right, :, high], plane_device(h, left, b)),
                lambda: (store.at[chunk, b], plane_device(h, a, up)),
                lambda: (store.at[chunk, b], plane_device(h, a, down)),
                lambda: (store.at[chunk, down, :, :, low], plane_device(h, a, up)),
                lambda: (store.at[chunk, up, :, :, high], plane_device(h, a, down)),
            ][step]()
            return remote(block, block, sends.at[p], recvs.at[p, step // 2], device)

        return gather

    gather_values = gather_of(values, value_send, value_recv)
    gather_columns = gather_of(columns, column_send, column_recv)

    gather_sizes = [values.at[0, 0], values.at[0, 0, 0:2], values.at[0], values.at[0, 0:2]]

    def exchanged(target, e):
        unit = 2 * (z % 2) + e if e < 2 else FAR_UNITS - 1
        a, b = x + core * (y - x), y + core * (x - y)
        return remote(
            exchange.at[target, e],
            columns.at[2 * unit + core, b, a],
            exchange_send.at[0],
            exchange_recv.at[unit],
            {"grp": target},
        )

    def gain_rows(t, h):
        return stacked(
            jnp.broadcast_to(gain[:, pl.ds(lower_start(t, h), WIDE)], (OWN, WIDE)),
            jnp.broadcast_to(gain[:, pl.ds(upper_start(t, h), WIDE)], (OWN, WIDE)),
        )

    zero = jnp.zeros((TALL, 128), jnp.float32)

    def row_mean(total):
        return both_halves(jnp.sum(total, axis=1, keepdims=True)) / (GROUPS * SHARD)

    def add_sums(t, total):
        arrive(t, 4)
        for h in range(2):
            total = total + lanes(wide(both[0, 2 * t + h]))
        return total

    mean = row_mean(lax.fori_loop(0, UNITS, add_sums, zero))

    def add_squares(t, total):
        for h in range(2):
            centred = wide(both[0, 2 * t + h]) - mean
            total = total + lanes(centred * centred)
        return total

    inv_scale = lax.rsqrt(row_mean(lax.fori_loop(0, UNITS, add_squares, zero)) + EPSILON)

    def add_means(t, totals):
        for h in range(2):
            unit = (wide(both[0, 2 * t + h]) - mean) * inv_scale
            scaled = gain_rows(t, h) * wide(both[1, 2 * t + h])
            totals = (totals[0] + lanes(scaled), totals[1] + lanes(scaled * unit))
        return totals

    sums = lax.fori_loop(0, UNITS, add_means, (zero, zero))
    mean_scaled, mean_product = row_mean(sums[0]), row_mean(sums[1])
    first_unit = SIDE * ((z // 2 + z % 2 + 1) % 2)

    def write(turn, carry):
        shard = (turn + first_unit // 2) % SIDE
        kept = []
        for v in range(2):
            t = 2 * shard + v
            for h in range(2):
                chunk = 2 * t + h
                a, b = axes(h)
                rows = gain_rows(t, h)
                unit = (wide(both[0, chunk]) - mean) * inv_scale
                d_normed = wide(both[1, chunk])
                grad = inv_scale * (rows * d_normed - mean_scaled - unit * mean_product)
                value = jnp.where(section == 0, grad, unit * rows)
                values[chunk, b, a] = narrow(value)
                gather_values(t, h, 0).start()
                gather_values(t, h, 1).start()
                kept.append(value)
                product = d_normed * unit
                for start, rows in (
                    (lower_start(t, h), slice(0, OWN)),
                    (upper_start(t, h), slice(OWN, TALL)),
                ):
                    own_grad[:, pl.ds(start, WIDE)] = narrow(grad[rows])
                    gain_own[0, :, pl.ds(start, WIDE)] = jnp.sum(product[rows], axis=0, keepdims=True)
        for target, rows in ((shard, slice(0, OWN)), (GROUPS - 1 - shard, slice(OWN, TALL))):
            for e, (first, second) in enumerate(((0, 2), (1, 3), (2, 3))):
                exchange[target, e] = narrow(stacked(kept[first][rows], kept[second][rows]))
                wanted = target // SIDE != z // 2 if e < 2 else target // 2 == next_plane

                @pl.when(wanted)
                def _():
                    exchanged(target, e).start()
        return carry

    lax.fori_loop(0, SIDE, write, 0)


    def near_copy(t, upper, target, slot):
        return remote(
            tokens.at[t, upper],
            from_near.at[slot],
            near_send.at[0],
            near_recv.at[slot],
            {"grp": target},
        )

    def split_blocks(store, chunk, h, put):
        for i in range(0, SIDE * SIDE, 2):
            pair = []
            for at in (i, i + 1):
                a, b = (at // SIDE, at % SIDE) if h == 0 else (at % SIDE, at // SIDE)
                pair.append(wide(store[chunk, b, a]))
            put(0, slice(OWN * i, OWN * (i + 2)), narrow(stacked(pair[0][:OWN], pair[1][:OWN])))
            put(1, slice(OWN * i, OWN * (i + 2)), narrow(stacked(pair[0][OWN:], pair[1][OWN:])))

    def add_grads(start, transposed_heads, token_rows):
        cols = pl.ds(start, token_rows.shape[1])
        grads_t[:, cols] += jnp.dot(
            transposed_heads, token_rows, preferred_element_type=jnp.float32
        )

    def store_grads(block):
        return pltpu.make_async_copy(
            grads.at[block * WIDE : (block + 1) * WIDE],
            grads_out.at[block * WIDE : (block + 1) * WIDE],
            output_sem.at[3 + block],
        )

    def finish_grads(blocks):
        for block in blocks:
            cols = slice(block * WIDE, (block + 1) * WIDE)
            grads[cols] = grad_scale * grads_t[:, cols].T
            store_grads(block).start()

    def use_values(t):
        for h in range(2):

            def put(upper, rows, block):
                tokens[t, upper, rows, h * WIDE : (h + 1) * WIDE] = block

            split_blocks(values, 2 * t + h, h, put)
        for upper, target in enumerate((t // 2, GROUPS - 1 - t // 2)):
            to_next = jnp.logical_and(target // 2 == next_plane, t % 2 == 0)
            for slot, wanted in ((t % 2, target == sibling_group), (2 + core, to_next)):

                @pl.when(wanted)
                def _():
                    near_copy(t, upper, target, slot).start()

        total = heads_total[...]
        for upper, start in enumerate((lower_start(t), upper_start(t))):
            total = total + lax.dot_general(
                tokens[t, upper], weight_buf[:, pl.ds(start, UNIT_WIDE)],
                (((1,), (1,)), ((), ())), preferred_element_type=jnp.float32,
            )
        heads_total[...] = total
        for upper, target in enumerate((t // 2, GROUPS - 1 - t // 2)):

            @pl.when(target == group)
            def _():
                add_grads(pl.multiple_of((t % 2) * UNIT_WIDE, UNIT_WIDE), heads_t[...], tokens[t, upper])

    def use_columns(p):
        last = p // (FAR_UNITS - 1)
        plane = (1 - last) * (2 * (1 - z // 2) + p // 2) + last * next_plane
        for h in range(2):

            def put(side, rows, block):
                column_tokens[h, rows, side * WIDE : (side + 1) * WIDE] = block

            split_blocks(columns, 2 * p + h, h, put)
        slot = plane_slot(plane, z)

        @pl.when(jnp.logical_and(p % 2 == 0, last == 0))
        def _():
            heads_arrived(slot + 1 - core)

        total = jnp.dot(
            heads_all[slot], column_tokens[0], preferred_element_type=jnp.float32
        ) + jnp.dot(heads_all[slot + 1], column_tokens[1], preferred_element_type=jnp.float32)
        for side in range(2):
            start = (1 - last) * (side * UNIT_WIDE + (p % 2) * WIDE) + last * (UNIT_WIDE + side * WIDE)
            cols = pl.ds(pl.multiple_of(start, WIDE), WIDE)
            grads_t[:, cols] += total[:, side * WIDE : (side + 1) * WIDE]

    def use_near(slot, heads_slot, start):
        wait_arrived(from_near.at[slot], near_recv.at[slot])
        add_grads(start, heads_all[heads_slot], from_near[slot])

    gain_partners = [
        {"tp": x * SIDE + y + 1 - 2 * (y % 2)},
        {"tp": x * SIDE + SIDE - 1 - y},
        {"tp": (x + 1 - 2 * (x % 2)) * SIDE + y},
        {"tp": (SIDE - 1 - x) * SIDE + y},
        sibling,
        {"grp": 2 * next_plane + core},
        {"grp": 2 * (SIDE - 1 - z) + core},
    ]

    def gain_copy(step):
        return remote(
            gain_own.at[step], gain_got.at[step], gain_send.at[step], gain_recv.at[step], gain_partners[step]
        )

    own_grad_store, heads_store, gain_store = [
        pltpu.make_async_copy(source, target, output_sem.at[at])
        for at, (source, target) in enumerate(
            ((own_grad, grad_out), (heads_done, heads_out), (gain_done, gain_out))
        )
    ]

    near_heads = plane_slot(next_plane, z)

    def value_unit(q):
        return (q + first_unit) % UNITS

    def gather_stage(q, stage):
        def pass_on(gather, recvs, p):
            wait_arrived(gather_sizes[stage], recvs.at[p, stage])
            if stage < 3:
                for h in range(2):
                    gather(p, h, 2 * stage + 2).start()
                    gather(p, h, 2 * stage + 3).start()

        @pl.when(within(q, UNITS))
        def _():
            pass_on(gather_values, value_recv, value_unit(q))

        @pl.when(within(q - UNITS, FAR_UNITS))
        def _():
            pass_on(gather_columns, column_recv, q - UNITS)

    def gather_turn(n, carry):
        @pl.when(n == 5)
        def _():
            pass_heads()

        for step in range(GAIN_STEPS + 1):

            @pl.when(n == step + 1)
            def _():
                if step > 0:
                    gain_copy(step - 1).wait_recv()
                    gain_own[step] = gain_own[step - 1] + gain_got[step - 1]
                if step < GAIN_STEPS:
                    gain_copy(step).start()
                else:
                    gain_done[...] = gain_own[GAIN_STEPS] * grad_scale
                    gain_store.start()

        @pl.when(within(n + 1 - UNITS, FAR_UNITS))
        def _():
            p = n + 1 - UNITS
            wait_arrived(gather_sizes[1], exchange_recv.at[p])
            for h in range(2):
                gather_columns(p, h, 0).start()
                gather_columns(p, h, 1).start()

        @pl.when(n == UNITS + FAR_UNITS + 4)
        def _():
            finish_grads((0, 1))

        gather_stage(n, 0)
        gather_stage(n - 4, 2)
        gather_stage(n - 2, 1)
        gather_stage(n - 5, 3)
        done = n - 5

        @pl.when(within(done, UNITS))
        def _():
            use_values(value_unit(done))

        @pl.when(done == UNITS)
        def _():
            heads_done[...] = narrow(heads_total[...])
            heads_store.start()
            heads_arrived(SLOTS - 1)
            use_near(0, SLOTS - 1, 0)
            use_near(1, SLOTS - 1, UNIT_WIDE)
            heads_arrived(near_heads + 1 - core)

        @pl.when(done == UNITS + 2)
        def _():
            for k in range(2):
                use_near(2 + k, near_heads + k, 0)

        @pl.when(within(done - UNITS, FAR_UNITS))
        def _():
            use_columns(done - UNITS)

        return carry

    own_grad_store.start()
    each_relay((2,), pass_relay)
    lax.fori_loop(0, UNITS + FAR_UNITS + 5, gather_turn, 0)
    finish_grads((2, 3))

    def reduce_sent(u, carry):
        wait_sent(part.at[0:2], send_sem.at[u])
        wait_sent(values.at[0:5, 0:3, 0:2], value_send.at[u])
        return carry

    def columns_sent(p, carry):
        wait_sent(values.at[0:5, 0:3, 0:2], column_send.at[p])
        return carry

    lax.fori_loop(0, UNITS, reduce_sent, 0)
    lax.fori_loop(0, FAR_UNITS, columns_sent, 0)
    wait_sent(exchange.at[0:5, 0:2], exchange_send.at[0])
    wait_sent(tokens.at[0:2], near_send.at[0])
    each_relay((0, 1, 2), lambda relay, held: relay.wait_send())
    for j in range(SIDE - 1):
        passed_heads(j).wait_send()
    sibling_heads().wait_send()
    for step in range(GAIN_STEPS):
        gain_copy(step).wait_send()
    for store in [own_grad_store, heads_store, gain_store] + [store_grads(i) for i in range(4)]:
        store.wait()


def deliver_kernel(*refs):
    results, outputs, held = refs[:4], refs[4:8], refs[8:12]
    load_sem, store_sem = refs[12:]
    loads = [pltpu.make_async_copy(results[at], held[at], load_sem.at[at]) for at in range(4)]
    stores = [pltpu.make_async_copy(held[at], outputs[at], store_sem.at[at]) for at in range(4)]
    for load in loads:
        load.start()
    for load, store in zip(loads, stores):
        load.wait()
        store.start()
    for store in stores:
        store.wait()


def delivered(results):
    hbm = pl.BlockSpec(memory_space=pl.ANY)
    return pl.pallas_call(
        deliver_kernel,
        out_shape=tuple(jax.ShapeDtypeStruct(result.shape, result.dtype) for result in results),
        in_specs=[hbm] * 4,
        out_specs=(hbm,) * 4,
        scratch_shapes=[pltpu.VMEM(result.shape, result.dtype) for result in results]
        + [pltpu.SemaphoreType.DMA((4,))] * 2,
        name="deliver",
    )(*results)


def fused(heads, weights, residual, gain):
    hbm = pl.BlockSpec(memory_space=pl.ANY)
    bf16, f32 = jnp.bfloat16, jnp.float32
    rows_dev, depth = heads.shape
    owned = weights.shape[1] // GROUPS
    dma = pltpu.SemaphoreType.DMA
    return pl.pallas_call(
        boundary_kernel,
        out_shape=(
            jax.ShapeDtypeStruct(heads.shape, bf16),
            jax.ShapeDtypeStruct((owned, depth), f32),
            jax.ShapeDtypeStruct(residual.shape, bf16),
            jax.ShapeDtypeStruct(gain.shape, f32),
        ),
        in_specs=[hbm] * 4,
        out_specs=(hbm,) * 4,
        scratch_shapes=[
            pltpu.VMEM(heads.shape, bf16),
            pltpu.VMEM(residual.shape, bf16),
            pltpu.VMEM(gain.shape, f32),
            pltpu.VMEM(heads.shape, bf16),
            pltpu.VMEM((owned, depth), f32),
            pltpu.VMEM(residual.shape, bf16),
            pltpu.VMEM(gain.shape, f32),
            pltpu.VMEM((depth, rows_dev), bf16),
            pltpu.VMEM((depth, owned), f32),
            pltpu.VMEM(weights.shape, bf16),
            pltpu.VMEM((CHUNKS, SIDE, SIDE, TALL, WIDE), bf16),
            pltpu.VMEM((CHUNKS, 2, SIDE, TALL, HALF), bf16),
            pltpu.VMEM((CHUNKS, 2, SIDE, TALL, WIDE), bf16),
            pltpu.VMEM((CHUNKS, 2, TALL, HALF), bf16),
            pltpu.VMEM((CHUNKS, 2, TALL, WIDE), bf16),
            pltpu.VMEM((2, CHUNKS, TALL, WIDE), bf16),
            pltpu.VMEM((CHUNKS, SIDE, SIDE, TALL, WIDE), bf16),
            pltpu.VMEM((FAR_CHUNKS, SIDE, SIDE, TALL, WIDE), bf16),
            pltpu.VMEM((GROUPS, 3, TALL, WIDE), bf16),
            pltpu.VMEM((UNITS, 2, rows_dev, UNIT_WIDE), bf16),
            pltpu.VMEM((2, rows_dev, UNIT_WIDE), bf16),
            pltpu.VMEM((4, rows_dev, UNIT_WIDE), bf16),
            pltpu.VMEM((SLOTS, depth, rows_dev), bf16),
            pltpu.VMEM((rows_dev, depth), f32),
            pltpu.VMEM((GAIN_STEPS + 1,) + gain.shape, f32),
            pltpu.VMEM((GAIN_STEPS,) + gain.shape, f32),
            dma((3,)),
            dma((7,)),
            dma((UNITS, 2)),
            dma((UNITS,)),
            dma((UNITS, 5)),
            dma((UNITS,)),
            dma((UNITS, 4)),
            dma((FAR_UNITS,)),
            dma((FAR_UNITS, 4)),
            dma((1,)),
            dma((FAR_UNITS,)),
            dma((SLOTS + 6,)),
            dma((SLOTS,)),
            dma((1,)),
            dma((4,)),
            dma((GAIN_STEPS,)),
            dma((GAIN_STEPS,)),
        ],
        compiler_params=pltpu.CompilerParams(
            collective_id=0, has_side_effects=True, vmem_limit_bytes=62 * 1024 * 1024
        ),
        name="boundary",
    )(heads, weights, residual, gain)


def per_device(heads_in, weights, residual, norm_gain):
    heads_out, weight_grad, boundary_grad, gain_grad = delivered(
        fused(heads_in[0], weights[0], residual, norm_gain[None])
    )
    return (heads_out[None], weight_grad[None], boundary_grad, gain_grad[0])


def solution(mesh):
    placed = (P("section", "grp", "tp"), P("section", "tp", None), P(("grp", "tp"), None), P())
    return jax.shard_map(
        per_device,
        mesh=mesh,
        in_specs=placed,
        out_specs=(
            P("section", "grp", "tp"),
            P("section", "grp", "tp"),
            P(("grp", "tp"), None),
            P(),
        ),
        check_vma=False,
    )
```

```python
import math

import jax
import jax.numpy as jnp
from jax import lax
from jax.experimental import pallas as pl
from jax.experimental.pallas import tpu as pltpu
from jax.sharding import PartitionSpec as P

EPSILON = 1e-05
MESH = pl.DeviceIdType.MESH

SIDE = 4
GROUPS = 8
UNITS = 8
FAR_UNITS = 5
CHUNKS = 2 * UNITS
ALL_UNITS = UNITS + FAR_UNITS
GATHER_GROUPS = ((0, 2), (2, UNITS - 2), (UNITS, FAR_UNITS))
WIDE = 256
UNIT_WIDE = 2 * WIDE
SHARD = 2 * UNIT_WIDE
OWN = 24
TALL = 2 * OWN
SLOTS = GROUPS - 1
GAIN_STEPS = 7


def lower_start(t, h=0):
    return pl.multiple_of(t * UNIT_WIDE + h * WIDE, WIDE)


def upper_start(t, h=0):
    return pl.multiple_of((GROUPS - 1 - t // 2) * SHARD + (t % 2) * UNIT_WIDE + h * WIDE, WIDE)


def plane_device(h, first, second):
    x, y = (first, second) if h == 0 else (second, first)
    return {"tp": x * SIDE + y}


def stacked(*parts):
    return jnp.concatenate(parts, axis=0)


def both_halves(row_pair):
    total = row_pair[:OWN] + row_pair[OWN:]
    return stacked(total, total)


def lanes(value):
    return sum(value[:, 128 * i : 128 * (i + 1)] for i in range(value.shape[1] // 128))


def wide(value):
    return value.astype(jnp.float32)


def narrow(value):
    return value.astype(jnp.bfloat16)


def remote(source, target, send_sem, recv_sem, device):
    return pltpu.make_async_remote_copy(
        src_ref=source,
        dst_ref=target,
        send_sem=send_sem,
        recv_sem=recv_sem,
        device_id=device,
        device_id_type=MESH,
    )


def greet(peers):
    barrier = pltpu.get_barrier_semaphore()
    for peer in peers:
        pl.semaphore_signal(barrier, inc=1, device_id=peer, device_id_type=MESH)
    pl.semaphore_wait(barrier, len(peers))


def boundary_kernel(
    heads_in, weights, residual_in, gain_in, heads_out, grads_out, grad_out, gain_out,
    heads, residual, gain, heads_done, grads, own_grad, gain_done,
    heads_t, grads_t, weight_buf, part, from1, from2, from3, from4, both,
    values, exchange, tokens, column_tokens, from_near, heads_all, heads_total, gain_own, gain_got,
    input_sem, output_sem, weight_sem, send_sem, recv_sem, group_send, group_recv, unit_send, unit_recv,
    exchange_send, exchange_recv, heads_send, heads_recv, near_send, near_recv, gain_send, gain_recv,
):
    tp = lax.axis_index("tp")
    x, y = tp // SIDE, tp % SIDE
    section = lax.axis_index("section")
    group = lax.axis_index("grp")
    z, core = group // 2, group % 2
    other = {"section": 1 - section}
    sibling_group = 2 * z + 1 - core
    sibling = {"grp": sibling_group}
    next_plane = z + 1 - 2 * (z % 2)
    rows_dev, depth = heads.shape
    grad_scale = 1.0 / math.sqrt(rows_dev * GROUPS)

    def axes(h):
        return (x, y) if h == 0 else (y, x)

    def wait_arrived(size, sem):
        remote(size, size, heads_send.at[0], sem, sibling).wait_recv()

    def wait_sent(size, sem):
        remote(size, size, sem, heads_recv.at[0], sibling).wait_send()

    def weight_copy(t, upper):
        cols = pl.ds(upper_start(t) if upper else lower_start(t), UNIT_WIDE)
        return pltpu.make_async_copy(
            weights.at[:, cols], weight_buf.at[:, cols], weight_sem.at[t, upper]
        )

    def start_weights(t, carry):
        weight_copy(t, 0).start()
        weight_copy(t, 1).start()
        return carry

    heads_load, residual_load, gain_load = [
        pltpu.make_async_copy(source, target, input_sem.at[at])
        for at, (source, target) in enumerate(
            ((heads_in, heads), (residual_in, residual), (gain_in, gain))
        )
    ]
    heads_load.start()
    lax.fori_loop(0, UNITS, start_weights, 0)
    residual_load.start()
    gain_load.start()
    greet(
        [plane_device(0, (x + step) % SIDE, y) for step in (1, 3)]
        + [plane_device(0, x, (y + step) % SIDE) for step in (1, 3)]
        + [other, sibling]
        + [{"grp": 2 * ((z + hop) % SIDE) + k} for hop in range(1, SIDE) for k in range(2)]
    )
    heads_load.wait()

    def plane_slot(origin, at):
        return 2 * ((origin + SIDE - 1 - at) % SIDE)

    def heads_arrived(slot):
        remote(
            heads_t, heads_all.at[slot], heads_send.at[SLOTS - 1], heads_recv.at[slot], sibling
        ).wait_recv()

    def sibling_heads():
        slot = SLOTS - 1
        return remote(
            heads_t, heads_all.at[slot], heads_send.at[slot], heads_recv.at[slot], sibling
        )

    relays = ((1, 0), (-1, 0), (1, 1), (-1, 1), (1, 2), (-1, 2))

    def each_relay(wanted, act):
        for at, (step, away) in enumerate(relays):
            if away not in wanted:
                continue
            first, last = (away, SIDE - 2) if step > 0 else (1, SIDE - 1 - away)

            @pl.when(jnp.logical_and(z >= first, z <= last))
            def _():
                origin, target = z - step * away, z + step
                held = plane_slot(origin, z) + core
                slot = plane_slot(origin, target) + core
                act(
                    remote(
                        heads_all.at[held] if away else heads_t,
                        heads_all.at[slot],
                        heads_send.at[SLOTS + at],
                        heads_recv.at[slot],
                        {"grp": 2 * target + core},
                    ),
                    held,
                )

    def start_relay(relay, held):
        relay.start()

    def pass_relay(relay, held):
        heads_arrived(held)
        relay.start()

    def passed_heads(j):
        slot = 2 * j + core
        held = heads_all.at[slot]
        return remote(held, held, heads_send.at[slot], heads_recv.at[slot], sibling)

    def pass_heads():
        @pl.when(jnp.logical_or(z == 0, z == SIDE - 1))
        def _():
            for j in range(SIDE - 1):
                heads_arrived(2 * j + core)

        for j in range(SIDE - 1):
            passed_heads(j).start()

    def send_heads():
        heads_t[...] = heads[...].T
        each_relay((0,), start_relay)
        sibling_heads().start()


    def copy(u, h, step):
        chunk = 2 * u + h
        a, b = axes(h)
        right, left = (a + 1) % SIDE, (a + 3) % SIDE
        up, down = (b + 1) % SIDE, (b + 3) % SIDE
        far_a, far_b = (a + 2) % SIDE, (b + 2) % SIDE
        odd = u % 2
        way_a, way_b = (a + 1 + 2 * odd) % SIDE, (b + 1 + 2 * odd) % SIDE
        source, target, device = [
            lambda: (part.at[chunk, far_a], from1.at[chunk], plane_device(h, way_a, b)),
            lambda: (part.at[chunk, right], from2.at[chunk, 0], plane_device(h, right, b)),
            lambda: (part.at[chunk, left], from2.at[chunk, 1], plane_device(h, left, b)),
            lambda: (part.at[chunk, a, far_b], from3.at[chunk], plane_device(h, a, way_b)),
            lambda: (part.at[chunk, a, up], from4.at[chunk, 0], plane_device(h, a, up)),
            lambda: (part.at[chunk, a, down], from4.at[chunk, 1], plane_device(h, a, down)),
            lambda: (both.at[section, chunk], both.at[section, chunk], other),
        ][step]()
        stage = (0, 1, 1, 2, 3, 3, 4)[step]
        return remote(source, target, send_sem.at[u], recv_sem.at[u, stage], device)

    reduce_sizes = [
        part.at[0, 0:2], part.at[0], part.at[0, 0, 0:2], part.at[0, 0], part.at[0, 0, 0:2]
    ]

    def arrive(u, stage):
        wait_arrived(reduce_sizes[stage], recv_sem.at[u, stage])

    def multiply(u):
        weight_copy(u, 0).wait()
        weight_copy(u, 1).wait()
        lower, upper = [
            jnp.dot(
                heads[...], weight_buf[:, pl.ds(start, UNIT_WIDE)],
                preferred_element_type=jnp.float32,
            )
            for start in (lower_start(u), upper_start(u))
        ]
        for h in range(2):
            cols = slice(h * WIDE, (h + 1) * WIDE)
            for i in range(SIDE * SIDE):
                rows = slice(OWN * i, OWN * (i + 1))
                a, b = (i // SIDE, i % SIDE) if h == 0 else (i % SIDE, i // SIDE)
                part[2 * u + h, a, b] = narrow(stacked(lower[rows, cols], upper[rows, cols]))
            copy(u, h, 0).start()

    def near_first(u):
        arrive(u, 0)
        for h in range(2):
            chunk = 2 * u + h
            near = (axes(h)[0] + 1 + 2 * (u % 2)) % SIDE
            part[chunk, near] = narrow(wide(part[chunk, near]) + wide(from1[chunk]))
            copy(u, h, 1).start()
            copy(u, h, 2).start()

    def far_second(u):
        arrive(u, 1)
        for h in range(2):
            chunk = 2 * u + h
            a, b = axes(h)
            part[chunk, a] = narrow(
                wide(part[chunk, a]) + (wide(from2[chunk, 0]) + wide(from2[chunk, 1]))
            )
            copy(u, h, 3).start()

    def near_second(u):
        arrive(u, 2)
        for h in range(2):
            chunk = 2 * u + h
            a, b = axes(h)
            near = (b + 1 + 2 * (u % 2)) % SIDE
            part[chunk, a, near] = narrow(wide(part[chunk, a, near]) + wide(from3[chunk]))
            copy(u, h, 4).start()
            copy(u, h, 5).start()

    def finish(u):
        arrive(u, 3)
        for h in range(2):
            chunk = 2 * u + h
            a, b = axes(h)
            total = wide(part[chunk, a, b]) + (wide(from4[chunk, 0]) + wide(from4[chunk, 1]))
            rows = stacked(
                wide(residual[:, pl.ds(lower_start(u, h), WIDE)]),
                wide(residual[:, pl.ds(upper_start(u, h), WIDE)]),
            )
            total = total + jnp.where(section == 0, rows, 0.0)
            both[section, chunk] = narrow(total)
            copy(u, h, 6).start()

    def within(value, count):
        return jnp.logical_and(value >= 0, value < count)

    stages = (multiply, near_first, far_second, near_second, finish)

    def reduce_turn(n, carry):
        for late, stage in enumerate(stages):

            @pl.when(within(n - late, UNITS))
            def _():
                stage(n - late)

        @pl.when(n == 1)
        def _():
            send_heads()

        @pl.when(n == UNITS - 1)
        def _():
            each_relay((1,), pass_relay)

        return carry

    residual_load.wait()
    gain_load.wait()
    lax.fori_loop(0, UNITS + len(stages) - 1, reduce_turn, 0)
    heads_total[...] = jnp.zeros_like(heads_total)
    grads_t[...] = jnp.zeros_like(grads_t)


    def gather_first(group, h, step):
        first, count = GATHER_GROUPS[group]
        a, b = axes(h)
        right, left = (a + 1) % SIDE, (a + 3) % SIDE
        half = (count + 1) // 2
        block, way = [
            lambda: (values.at[h, first : first + count, b, a], right),
            lambda: (values.at[h, first : first + count, b, a], left),
            lambda: (values.at[h, first : first + half, b, left], right),
            lambda: (values.at[h, first + half : first + count, b, right], left),
        ][step]()
        sems = group_send.at[group], group_recv.at[group, step // 2]
        return remote(block, block, *sems, plane_device(h, way, b))

    def gather_second(q, h, step):
        a, b = axes(h)
        up, down = (b + 1) % SIDE, (b + 3) % SIDE
        odd = q % 2
        block, way = [
            lambda: (values.at[h, q, b], up),
            lambda: (values.at[h, q, b], down),
            lambda: (values.at[h, q, (b + 3 + 2 * odd) % SIDE], (b + 1 + 2 * odd) % SIDE),
        ][step]()
        sems = unit_send.at[q], unit_recv.at[q, step // 2]
        return remote(block, block, *sems, plane_device(h, a, way))

    def start_group(group, steps):
        for h in range(2):
            for step in steps:
                gather_first(group, h, step).start()

    def start_unit(q, steps):
        for h in range(2):
            for step in steps:
                gather_second(q, h, step).start()

    def exchanged(target, e):
        unit = 2 * (z % 2) + e if e < 2 else FAR_UNITS - 1
        a, b = x + core * (y - x), y + core * (x - y)
        return remote(
            exchange.at[target, e],
            values.at[core, UNITS + unit, b, a],
            exchange_send.at[0],
            exchange_recv.at[0],
            {"grp": target},
        )

    def gain_rows(t, h):
        return stacked(
            jnp.broadcast_to(gain[:, pl.ds(lower_start(t, h), WIDE)], (OWN, WIDE)),
            jnp.broadcast_to(gain[:, pl.ds(upper_start(t, h), WIDE)], (OWN, WIDE)),
        )

    zero = jnp.zeros((TALL, 128), jnp.float32)

    def row_mean(total):
        return both_halves(jnp.sum(total, axis=1, keepdims=True)) / (GROUPS * SHARD)

    def add_sums(t, total):
        arrive(t, 4)
        for h in range(2):
            total = total + lanes(wide(both[0, 2 * t + h]))
        return total

    mean = row_mean(lax.fori_loop(0, UNITS, add_sums, zero))

    def add_squares(t, total):
        for h in range(2):
            centred = wide(both[0, 2 * t + h]) - mean
            total = total + lanes(centred * centred)
        return total

    inv_scale = lax.rsqrt(row_mean(lax.fori_loop(0, UNITS, add_squares, zero)) + EPSILON)

    def add_means(t, totals):
        for h in range(2):
            unit = (wide(both[0, 2 * t + h]) - mean) * inv_scale
            scaled = gain_rows(t, h) * wide(both[1, 2 * t + h])
            totals = (totals[0] + lanes(scaled), totals[1] + lanes(scaled * unit))
        return totals

    sums = lax.fori_loop(0, UNITS, add_means, (zero, zero))
    mean_scaled, mean_product = row_mean(sums[0]), row_mean(sums[1])
    first_unit = SIDE * ((z // 2 + z % 2 + 1) % 2)

    def write(turn, carry):
        shard = (turn + first_unit // 2) % SIDE
        kept = []
        for v in range(2):
            t = 2 * shard + v
            for h in range(2):
                chunk = 2 * t + h
                a, b = axes(h)
                rows = gain_rows(t, h)
                unit = (wide(both[0, chunk]) - mean) * inv_scale
                d_normed = wide(both[1, chunk])
                grad = inv_scale * (rows * d_normed - mean_scaled - unit * mean_product)
                value = jnp.where(section == 0, grad, unit * rows)
                values[h, 2 * turn + v, b, a] = narrow(value)
                kept.append(value)
                product = d_normed * unit
                for start, rows in (
                    (lower_start(t, h), slice(0, OWN)),
                    (upper_start(t, h), slice(OWN, TALL)),
                ):
                    own_grad[:, pl.ds(start, WIDE)] = narrow(grad[rows])
                    gain_own[0, :, pl.ds(start, WIDE)] = jnp.sum(product[rows], axis=0, keepdims=True)
        for target, rows in ((shard, slice(0, OWN)), (GROUPS - 1 - shard, slice(OWN, TALL))):
            for e, (first, second) in enumerate(((0, 2), (1, 3), (2, 3))):
                exchange[target, e] = narrow(stacked(kept[first][rows], kept[second][rows]))
                wanted = target // SIDE != z // 2 if e < 2 else target // 2 == next_plane

                @pl.when(wanted)
                def _():
                    exchanged(target, e).start()

        @pl.when(turn == 0)
        def _():
            start_group(0, (0, 1))

        return carry

    lax.fori_loop(0, SIDE, write, 0)
    start_group(1, (0, 1))


    def near_copy(t, upper, target, slot):
        return remote(
            tokens.at[t, upper],
            from_near.at[slot],
            near_send.at[0],
            near_recv.at[slot],
            {"grp": target},
        )

    def split_blocks(q, h, put):
        for i in range(0, SIDE * SIDE, 2):
            pair = []
            for at in (i, i + 1):
                a, b = (at // SIDE, at % SIDE) if h == 0 else (at % SIDE, at // SIDE)
                pair.append(wide(values[h, q, b, a]))
            put(0, slice(OWN * i, OWN * (i + 2)), narrow(stacked(pair[0][:OWN], pair[1][:OWN])))
            put(1, slice(OWN * i, OWN * (i + 2)), narrow(stacked(pair[0][OWN:], pair[1][OWN:])))

    def add_grads(start, transposed_heads, token_rows):
        cols = pl.ds(start, token_rows.shape[1])
        grads_t[:, cols] += jnp.dot(
            transposed_heads, token_rows, preferred_element_type=jnp.float32
        )

    def store_grads(block):
        return pltpu.make_async_copy(
            grads.at[block * WIDE : (block + 1) * WIDE],
            grads_out.at[block * WIDE : (block + 1) * WIDE],
            output_sem.at[3 + block],
        )

    def finish_grads(blocks):
        for block in blocks:
            cols = slice(block * WIDE, (block + 1) * WIDE)
            grads[cols] = grad_scale * grads_t[:, cols].T
            store_grads(block).start()

    def use_values(q):
        t = (q + first_unit) % UNITS
        for h in range(2):

            def put(upper, rows, block):
                tokens[t, upper, rows, h * WIDE : (h + 1) * WIDE] = block

            split_blocks(q, h, put)
        for upper, target in enumerate((t // 2, GROUPS - 1 - t // 2)):
            to_next = jnp.logical_and(target // 2 == next_plane, t % 2 == 0)
            for slot, wanted in ((t % 2, target == sibling_group), (2 + core, to_next)):

                @pl.when(wanted)
                def _():
                    near_copy(t, upper, target, slot).start()

        total = heads_total[...]
        for upper, start in enumerate((lower_start(t), upper_start(t))):
            total = total + lax.dot_general(
                tokens[t, upper], weight_buf[:, pl.ds(start, UNIT_WIDE)],
                (((1,), (1,)), ((), ())), preferred_element_type=jnp.float32,
            )
        heads_total[...] = total
        for upper, target in enumerate((t // 2, GROUPS - 1 - t // 2)):

            @pl.when(target == group)
            def _():
                add_grads(pl.multiple_of((t % 2) * UNIT_WIDE, UNIT_WIDE), heads_t[...], tokens[t, upper])

    def use_columns(p):
        last = p // (FAR_UNITS - 1)
        plane = (1 - last) * (2 * (1 - z // 2) + p // 2) + last * next_plane
        for h in range(2):

            def put(side, rows, block):
                column_tokens[h, rows, side * WIDE : (side + 1) * WIDE] = block

            split_blocks(UNITS + p, h, put)
        slot = plane_slot(plane, z)

        @pl.when(jnp.logical_and(p % 2 == 0, last == 0))
        def _():
            heads_arrived(slot + 1 - core)

        total = jnp.dot(
            heads_all[slot], column_tokens[0], preferred_element_type=jnp.float32
        ) + jnp.dot(heads_all[slot + 1], column_tokens[1], preferred_element_type=jnp.float32)
        for side in range(2):
            start = (1 - last) * (side * UNIT_WIDE + (p % 2) * WIDE) + last * (UNIT_WIDE + side * WIDE)
            cols = pl.ds(pl.multiple_of(start, WIDE), WIDE)
            grads_t[:, cols] += total[:, side * WIDE : (side + 1) * WIDE]

    def use_near(slot, heads_slot, start):
        wait_arrived(from_near.at[slot], near_recv.at[slot])
        add_grads(start, heads_all[heads_slot], from_near[slot])

    gain_partners = [
        {"tp": x * SIDE + y + 1 - 2 * (y % 2)},
        {"tp": x * SIDE + SIDE - 1 - y},
        {"tp": (x + 1 - 2 * (x % 2)) * SIDE + y},
        {"tp": (SIDE - 1 - x) * SIDE + y},
        sibling,
        {"grp": 2 * next_plane + core},
        {"grp": 2 * (SIDE - 1 - z) + core},
    ]

    def gain_copy(step):
        return remote(
            gain_own.at[step], gain_got.at[step], gain_send.at[step], gain_recv.at[step], gain_partners[step]
        )

    own_grad_store, heads_store, gain_store = [
        pltpu.make_async_copy(source, target, output_sem.at[at])
        for at, (source, target) in enumerate(
            ((own_grad, grad_out), (heads_done, heads_out), (gain_done, gain_out))
        )
    ]

    near_heads = plane_slot(next_plane, z)

    def gather_turn(n, carry):
        @pl.when(n == 5)
        def _():
            pass_heads()

        for step in range(GAIN_STEPS + 1):

            @pl.when(n == step + 1)
            def _():
                if step > 0:
                    gain_copy(step - 1).wait_recv()
                    gain_own[step] = gain_own[step - 1] + gain_got[step - 1]
                if step < GAIN_STEPS:
                    gain_copy(step).start()
                else:
                    gain_done[...] = gain_own[GAIN_STEPS] * grad_scale
                    gain_store.start()

        @pl.when(n == 3)
        def _():
            wait_arrived(values.at[0:2, 0:FAR_UNITS, 0, 0], exchange_recv.at[0])
            start_group(2, (0, 1))

        for group, at in enumerate((0, 1, 5)):
            count = GATHER_GROUPS[group][1]

            @pl.when(n == at)
            def _():
                wait_arrived(values.at[0:2, 0:count, 0, 0:2], group_recv.at[group, 0])
                start_group(group, (2, 3))

        @pl.when(within(n - 2, ALL_UNITS))
        def _():
            wait_arrived(values.at[0:2, 0:2, 0], unit_recv.at[n - 2, 0])
            start_unit(n - 2, (2,))

        for group, (first, count) in enumerate(GATHER_GROUPS):

            @pl.when(n == first)
            def _():
                wait_arrived(values.at[0:2, 0:count, 0, 0], group_recv.at[group, 1])

        @pl.when(n < ALL_UNITS)
        def _():
            start_unit(n, (0, 1))

        done = n - 3

        @pl.when(done == ALL_UNITS - 1)
        def _():
            finish_grads((0, 1))

        @pl.when(within(done, ALL_UNITS))
        def _():
            wait_arrived(values.at[0:2, 0, 0], unit_recv.at[done, 1])

        @pl.when(within(done, UNITS))
        def _():
            use_values(done)

        @pl.when(done == UNITS)
        def _():
            heads_done[...] = narrow(heads_total[...])
            heads_store.start()
            heads_arrived(SLOTS - 1)
            use_near(0, SLOTS - 1, 0)
            use_near(1, SLOTS - 1, UNIT_WIDE)
            heads_arrived(near_heads + 1 - core)

        @pl.when(done == UNITS + 2)
        def _():
            for k in range(2):
                use_near(2 + k, near_heads + k, 0)

        @pl.when(within(done - UNITS, FAR_UNITS))
        def _():
            use_columns(done - UNITS)

        return carry

    own_grad_store.start()
    each_relay((2,), pass_relay)
    lax.fori_loop(0, ALL_UNITS + 3, gather_turn, 0)
    finish_grads((2, 3))

    def reduce_sent(u, carry):
        wait_sent(part.at[0:2], send_sem.at[u])
        return carry

    def gather_sent(q, carry):
        wait_sent(values.at[0:2, 0:3, 0], unit_send.at[q])
        return carry

    lax.fori_loop(0, UNITS, reduce_sent, 0)
    lax.fori_loop(0, ALL_UNITS, gather_sent, 0)
    for group, (first, count) in enumerate(GATHER_GROUPS):
        wait_sent(values.at[0:2, 0:count, 0, 0:3], group_send.at[group])
    wait_sent(exchange.at[0:5, 0:2], exchange_send.at[0])
    wait_sent(tokens.at[0:2], near_send.at[0])
    each_relay((0, 1, 2), lambda relay, held: relay.wait_send())
    for j in range(SIDE - 1):
        passed_heads(j).wait_send()
    sibling_heads().wait_send()
    for step in range(GAIN_STEPS):
        gain_copy(step).wait_send()
    for store in [own_grad_store, heads_store, gain_store] + [store_grads(i) for i in range(4)]:
        store.wait()


def deliver_kernel(*refs):
    results, outputs, held = refs[:4], refs[4:8], refs[8:12]
    load_sem, store_sem = refs[12:]
    loads = [pltpu.make_async_copy(results[at], held[at], load_sem.at[at]) for at in range(4)]
    stores = [pltpu.make_async_copy(held[at], outputs[at], store_sem.at[at]) for at in range(4)]
    for load in loads:
        load.start()
    for load, store in zip(loads, stores):
        load.wait()
        store.start()
    for store in stores:
        store.wait()


def delivered(results):
    hbm = pl.BlockSpec(memory_space=pl.ANY)
    return pl.pallas_call(
        deliver_kernel,
        out_shape=tuple(jax.ShapeDtypeStruct(result.shape, result.dtype) for result in results),
        in_specs=[hbm] * 4,
        out_specs=(hbm,) * 4,
        scratch_shapes=[pltpu.VMEM(result.shape, result.dtype) for result in results]
        + [pltpu.SemaphoreType.DMA((4,))] * 2,
        name="deliver",
    )(*results)


def fused(heads, weights, residual, gain):
    hbm = pl.BlockSpec(memory_space=pl.ANY)
    bf16, f32 = jnp.bfloat16, jnp.float32
    rows_dev, depth = heads.shape
    owned = weights.shape[1] // GROUPS
    dma = pltpu.SemaphoreType.DMA
    return pl.pallas_call(
        boundary_kernel,
        out_shape=(
            jax.ShapeDtypeStruct(heads.shape, bf16),
            jax.ShapeDtypeStruct((owned, depth), f32),
            jax.ShapeDtypeStruct(residual.shape, bf16),
            jax.ShapeDtypeStruct(gain.shape, f32),
        ),
        in_specs=[hbm] * 4,
        out_specs=(hbm,) * 4,
        scratch_shapes=[
            pltpu.VMEM(heads.shape, bf16),
            pltpu.VMEM(residual.shape, bf16),
            pltpu.VMEM(gain.shape, f32),
            pltpu.VMEM(heads.shape, bf16),
            pltpu.VMEM((owned, depth), f32),
            pltpu.VMEM(residual.shape, bf16),
            pltpu.VMEM(gain.shape, f32),
            pltpu.VMEM((depth, rows_dev), bf16),
            pltpu.VMEM((depth, owned), f32),
            pltpu.VMEM(weights.shape, bf16),
            pltpu.VMEM((CHUNKS, SIDE, SIDE, TALL, WIDE), bf16),
            pltpu.VMEM((CHUNKS, SIDE, TALL, WIDE), bf16),
            pltpu.VMEM((CHUNKS, 2, SIDE, TALL, WIDE), bf16),
            pltpu.VMEM((CHUNKS, TALL, WIDE), bf16),
            pltpu.VMEM((CHUNKS, 2, TALL, WIDE), bf16),
            pltpu.VMEM((2, CHUNKS, TALL, WIDE), bf16),
            pltpu.VMEM((2, ALL_UNITS, SIDE, SIDE, TALL, WIDE), bf16),
            pltpu.VMEM((GROUPS, 3, TALL, WIDE), bf16),
            pltpu.VMEM((UNITS, 2, rows_dev, UNIT_WIDE), bf16),
            pltpu.VMEM((2, rows_dev, UNIT_WIDE), bf16),
            pltpu.VMEM((4, rows_dev, UNIT_WIDE), bf16),
            pltpu.VMEM((SLOTS, depth, rows_dev), bf16),
            pltpu.VMEM((rows_dev, depth), f32),
            pltpu.VMEM((GAIN_STEPS + 1,) + gain.shape, f32),
            pltpu.VMEM((GAIN_STEPS,) + gain.shape, f32),
            dma((3,)),
            dma((7,)),
            dma((UNITS, 2)),
            dma((UNITS,)),
            dma((UNITS, 5)),
            dma((len(GATHER_GROUPS),)),
            dma((len(GATHER_GROUPS), 2)),
            dma((ALL_UNITS,)),
            dma((ALL_UNITS, 2)),
            dma((1,)),
            dma((1,)),
            dma((SLOTS + 6,)),
            dma((SLOTS,)),
            dma((1,)),
            dma((4,)),
            dma((GAIN_STEPS,)),
            dma((GAIN_STEPS,)),
        ],
        compiler_params=pltpu.CompilerParams(
            collective_id=0, has_side_effects=True, vmem_limit_bytes=62 * 1024 * 1024
        ),
        name="boundary",
    )(heads, weights, residual, gain)


def per_device(heads_in, weights, residual, norm_gain):
    heads_out, weight_grad, boundary_grad, gain_grad = delivered(
        fused(heads_in[0], weights[0], residual, norm_gain[None])
    )
    return (heads_out[None], weight_grad[None], boundary_grad, gain_grad[0])


def solution(mesh):
    placed = (P("section", "grp", "tp"), P("section", "tp", None), P(("grp", "tp"), None), P())
    return jax.shard_map(
        per_device,
        mesh=mesh,
        in_specs=placed,
        out_specs=(
            P("section", "grp", "tp"),
            P("section", "grp", "tp"),
            P(("grp", "tp"), None),
            P(),
        ),
        check_vma=False,
    )
```

```python
import math

import jax
import jax.numpy as jnp
from jax import lax
from jax.experimental import pallas as pl
from jax.experimental.pallas import tpu as pltpu
from jax.sharding import PartitionSpec as P

EPSILON = 1e-05
MESH = pl.DeviceIdType.MESH

SIDE = 4
GROUPS = 8
UNITS = 8
FAR_UNITS = 5
CHUNKS = 2 * UNITS
FAR_CHUNKS = 2 * FAR_UNITS
WIDE = 256
HALF = WIDE // 2
UNIT_WIDE = 2 * WIDE
SHARD = 2 * UNIT_WIDE
OWN = 24
TALL = 2 * OWN
SLOTS = GROUPS - 1
GAIN_STEPS = 7


def lower_start(t, h=0):
    return pl.multiple_of(t * UNIT_WIDE + h * WIDE, WIDE)


def upper_start(t, h=0):
    return pl.multiple_of((GROUPS - 1 - t // 2) * SHARD + (t % 2) * UNIT_WIDE + h * WIDE, WIDE)


def plane_device(h, first, second):
    x, y = (first, second) if h == 0 else (second, first)
    return {"tp": x * SIDE + y}


def stacked(*parts):
    return jnp.concatenate(parts, axis=0)


def both_halves(row_pair):
    total = row_pair[:OWN] + row_pair[OWN:]
    return stacked(total, total)


def lanes(value):
    return sum(value[:, 128 * i : 128 * (i + 1)] for i in range(value.shape[1] // 128))


def wide(value):
    return value.astype(jnp.float32)


def narrow(value):
    return value.astype(jnp.bfloat16)


def remote(source, target, send_sem, recv_sem, device):
    return pltpu.make_async_remote_copy(
        src_ref=source,
        dst_ref=target,
        send_sem=send_sem,
        recv_sem=recv_sem,
        device_id=device,
        device_id_type=MESH,
    )


def greet(peers):
    barrier = pltpu.get_barrier_semaphore()
    for peer in peers:
        pl.semaphore_signal(barrier, inc=1, device_id=peer, device_id_type=MESH)
    pl.semaphore_wait(barrier, len(peers))


def boundary_kernel(
    heads_in, weights, residual_in, gain_in, heads_out, grads_out, grad_out, gain_out,
    heads, residual, gain, heads_done, grads, own_grad, gain_done,
    heads_t, grads_t, weight_buf, part, from1, from2, from3, from4, both,
    values, columns, exchange, tokens, column_tokens, from_near, heads_all, heads_total, gain_own, gain_got,
    input_sem, output_sem, weight_sem, send_sem, recv_sem, value_send, value_recv, column_send, column_recv,
    exchange_send, exchange_recv, heads_send, heads_recv, near_send, near_recv, gain_send, gain_recv,
):
    tp = lax.axis_index("tp")
    x, y = tp // SIDE, tp % SIDE
    section = lax.axis_index("section")
    group = lax.axis_index("grp")
    z, core = group // 2, group % 2
    other = {"section": 1 - section}
    sibling_group = 2 * z + 1 - core
    sibling = {"grp": sibling_group}
    next_plane = z + 1 - 2 * (z % 2)
    rows_dev, depth = heads.shape
    grad_scale = 1.0 / math.sqrt(rows_dev * GROUPS)

    def axes(h):
        return (x, y) if h == 0 else (y, x)

    def wait_arrived(size, sem):
        remote(size, size, heads_send.at[0], sem, sibling).wait_recv()

    def wait_sent(size, sem):
        remote(size, size, sem, heads_recv.at[0], sibling).wait_send()

    def weight_copy(t, upper):
        cols = pl.ds(upper_start(t) if upper else lower_start(t), UNIT_WIDE)
        return pltpu.make_async_copy(
            weights.at[:, cols], weight_buf.at[:, cols], weight_sem.at[t, upper]
        )

    def start_weights(t, carry):
        weight_copy(t, 0).start()
        weight_copy(t, 1).start()
        return carry

    heads_load, residual_load, gain_load = [
        pltpu.make_async_copy(source, target, input_sem.at[at])
        for at, (source, target) in enumerate(
            ((heads_in, heads), (residual_in, residual), (gain_in, gain))
        )
    ]
    heads_load.start()
    lax.fori_loop(0, UNITS, start_weights, 0)
    residual_load.start()
    gain_load.start()
    greet(
        [plane_device(0, (x + step) % SIDE, y) for step in (1, 3)]
        + [plane_device(0, x, (y + step) % SIDE) for step in (1, 3)]
        + [other, sibling]
        + [{"grp": 2 * ((z + hop) % SIDE) + k} for hop in range(1, SIDE) for k in range(2)]
    )
    heads_load.wait()

    def plane_slot(origin, at):
        return 2 * ((origin + SIDE - 1 - at) % SIDE)

    def heads_arrived(slot):
        remote(
            heads_t, heads_all.at[slot], heads_send.at[SLOTS - 1], heads_recv.at[slot], sibling
        ).wait_recv()

    def sibling_heads():
        slot = SLOTS - 1
        return remote(
            heads_t, heads_all.at[slot], heads_send.at[slot], heads_recv.at[slot], sibling
        )

    relays = ((1, 0), (-1, 0), (1, 1), (-1, 1), (1, 2), (-1, 2))

    def each_relay(wanted, act):
        for at, (step, away) in enumerate(relays):
            if away not in wanted:
                continue
            first, last = (away, SIDE - 2) if step > 0 else (1, SIDE - 1 - away)

            @pl.when(jnp.logical_and(z >= first, z <= last))
            def _():
                origin, target = z - step * away, z + step
                held = plane_slot(origin, z) + core
                slot = plane_slot(origin, target) + core
                act(
                    remote(
                        heads_all.at[held] if away else heads_t,
                        heads_all.at[slot],
                        heads_send.at[SLOTS + at],
                        heads_recv.at[slot],
                        {"grp": 2 * target + core},
                    ),
                    held,
                )

    def start_relay(relay, held):
        relay.start()

    def pass_relay(relay, held):
        heads_arrived(held)
        relay.start()

    def passed_heads(j):
        slot = 2 * j + core
        held = heads_all.at[slot]
        return remote(held, held, heads_send.at[slot], heads_recv.at[slot], sibling)

    def pass_heads():
        @pl.when(jnp.logical_or(z == 0, z == SIDE - 1))
        def _():
            for j in range(SIDE - 1):
                heads_arrived(2 * j + core)

        for j in range(SIDE - 1):
            passed_heads(j).start()

    def send_heads():
        heads_t[...] = heads[...].T
        each_relay((0,), start_relay)
        sibling_heads().start()


    def copy(u, h, step):
        chunk = 2 * u + h
        a, b = axes(h)
        right, left = (a + 1) % SIDE, (a + 3) % SIDE
        up, down = (b + 1) % SIDE, (b + 3) % SIDE
        low, high = pl.ds(0, HALF), pl.ds(HALF, HALF)
        far_a, far_b = (a + 2) % SIDE, (b + 2) % SIDE
        source, target, device = [
            lambda: (part.at[chunk, far_a, :, :, low], from1.at[chunk, 0], plane_device(h, right, b)),
            lambda: (part.at[chunk, far_a, :, :, high], from1.at[chunk, 1], plane_device(h, left, b)),
            lambda: (part.at[chunk, right], from2.at[chunk, 0], plane_device(h, right, b)),
            lambda: (part.at[chunk, left], from2.at[chunk, 1], plane_device(h, left, b)),
            lambda: (part.at[chunk, a, far_b, :, low], from3.at[chunk, 0], plane_device(h, a, up)),
            lambda: (part.at[chunk, a, far_b, :, high], from3.at[chunk, 1], plane_device(h, a, down)),
            lambda: (part.at[chunk, a, up], from4.at[chunk, 0], plane_device(h, a, up)),
            lambda: (part.at[chunk, a, down], from4.at[chunk, 1], plane_device(h, a, down)),
            lambda: (both.at[section, chunk], both.at[section, chunk], other),
        ][step]()
        return remote(source, target, send_sem.at[u], recv_sem.at[u, step // 2], device)

    reduce_sizes = [
        part.at[0, 0:2], part.at[0], part.at[0, 0, 0:2], part.at[0, 0], part.at[0, 0, 0:2]
    ]

    def arrive(u, stage):
        wait_arrived(reduce_sizes[stage], recv_sem.at[u, stage])

    def multiply(u):
        weight_copy(u, 0).wait()
        weight_copy(u, 1).wait()
        lower, upper = [
            jnp.dot(
                heads[...], weight_buf[:, pl.ds(start, UNIT_WIDE)],
                preferred_element_type=jnp.float32,
            )
            for start in (lower_start(u), upper_start(u))
        ]
        for h in range(2):
            cols = slice(h * WIDE, (h + 1) * WIDE)
            for i in range(SIDE * SIDE):
                rows = slice(OWN * i, OWN * (i + 1))
                a, b = (i // SIDE, i % SIDE) if h == 0 else (i % SIDE, i // SIDE)
                part[2 * u + h, a, b] = narrow(stacked(lower[rows, cols], upper[rows, cols]))
            copy(u, h, 0).start()
            copy(u, h, 1).start()

    def transpose_weights(u):
        for start in (lower_start(u), upper_start(u)):
            cols = pl.ds(start, UNIT_WIDE)
            weight_buf[:, cols] = weight_buf[:, cols].T

    def near_first(u):
        arrive(u, 0)
        for h in range(2):
            chunk = 2 * u + h
            a, b = axes(h)
            right, left = (a + 1) % SIDE, (a + 3) % SIDE
            part[chunk, right, :, :, :HALF] = narrow(
                wide(part[chunk, right, :, :, :HALF]) + wide(from1[chunk, 0])
            )
            copy(u, h, 2).start()
            part[chunk, left, :, :, HALF:] = narrow(
                wide(part[chunk, left, :, :, HALF:]) + wide(from1[chunk, 1])
            )
            copy(u, h, 3).start()

    def far_second(u):
        arrive(u, 1)
        for h in range(2):
            chunk = 2 * u + h
            a, b = axes(h)
            part[chunk, a] = narrow(
                wide(part[chunk, a]) + (wide(from2[chunk, 0]) + wide(from2[chunk, 1]))
            )
            copy(u, h, 4).start()
            copy(u, h, 5).start()

    def near_second(u):
        arrive(u, 2)
        for h in range(2):
            chunk = 2 * u + h
            a, b = axes(h)
            up, down = (b + 1) % SIDE, (b + 3) % SIDE
            part[chunk, a, up, :, :HALF] = narrow(
                wide(part[chunk, a, up, :, :HALF]) + wide(from3[chunk, 0])
            )
            copy(u, h, 6).start()
            part[chunk, a, down, :, HALF:] = narrow(
                wide(part[chunk, a, down, :, HALF:]) + wide(from3[chunk, 1])
            )
            copy(u, h, 7).start()

    def finish(u):
        arrive(u, 3)
        for h in range(2):
            chunk = 2 * u + h
            a, b = axes(h)
            total = wide(part[chunk, a, b]) + (wide(from4[chunk, 0]) + wide(from4[chunk, 1]))
            rows = stacked(
                wide(residual[:, pl.ds(lower_start(u, h), WIDE)]),
                wide(residual[:, pl.ds(upper_start(u, h), WIDE)]),
            )
            total = total + jnp.where(section == 0, rows, 0.0)
            both[section, chunk] = narrow(total)
            copy(u, h, 8).start()

    def within(value, count):
        return jnp.logical_and(value >= 0, value < count)

    stages = (multiply, near_first, far_second, near_second, finish)
    TRANSPOSE_TURN = 4

    def reduce_turn(n, carry):
        for late, stage in enumerate(stages):

            @pl.when(within(n - late, UNITS))
            def _():
                stage(n - late)

        @pl.when(within(n - TRANSPOSE_TURN, UNITS))
        def _():
            transpose_weights(n - TRANSPOSE_TURN)

        @pl.when(n == 1)
        def _():
            send_heads()

        @pl.when(n == UNITS - 1)
        def _():
            each_relay((1,), pass_relay)

        return carry

    residual_load.wait()
    gain_load.wait()
    lax.fori_loop(0, UNITS + len(stages) - 1, reduce_turn, 0)
    heads_total[...] = jnp.zeros_like(heads_total)
    grads_t[...] = jnp.zeros_like(grads_t)


    def gather_of(store, sends, recvs):
        half = store.shape[-1] // 2

        def gather(p, h, step):
            chunk = 2 * p + h
            a, b = axes(h)
            right, left = (a + 1) % SIDE, (a + 3) % SIDE
            up, down = (b + 1) % SIDE, (b + 3) % SIDE
            low, high = pl.ds(0, half), pl.ds(half, half)
            block, device = [
                lambda: (store.at[chunk, b, a], plane_device(h, right, b)),
                lambda: (store.at[chunk, b, a], plane_device(h, left, b)),
                lambda: (store.at[chunk, b, left, :, low], plane_device(h, right, b)),
                lambda: (store.at[chunk, b, right, :, high], plane_device(h, left, b)),
                lambda: (store.at[chunk, b], plane_device(h, a, up)),
                lambda: (store.at[chunk, b], plane_device(h, a, down)),
                lambda: (store.at[chunk, down, :, :, low], plane_device(h, a, up)),
                lambda: (store.at[chunk, up, :, :, high], plane_device(h, a, down)),
            ][step]()
            return remote(block, block, sends.at[p], recvs.at[p, step // 2], device)

        return gather

    gather_values = gather_of(values, value_send, value_recv)
    gather_columns = gather_of(columns, column_send, column_recv)

    gather_sizes = [values.at[0, 0], values.at[0, 0, 0:2], values.at[0], values.at[0, 0:2]]

    def exchanged(target, e):
        unit = 2 * (z % 2) + e if e < 2 else FAR_UNITS - 1
        a, b = x + core * (y - x), y + core * (x - y)
        return remote(
            exchange.at[target, e],
            columns.at[2 * unit + core, b, a],
            exchange_send.at[0],
            exchange_recv.at[unit],
            {"grp": target},
        )

    def gain_rows(t, h):
        return stacked(
            jnp.broadcast_to(gain[:, pl.ds(lower_start(t, h), WIDE)], (OWN, WIDE)),
            jnp.broadcast_to(gain[:, pl.ds(upper_start(t, h), WIDE)], (OWN, WIDE)),
        )

    zero = jnp.zeros((TALL, 128), jnp.float32)

    def row_mean(total):
        return both_halves(jnp.sum(total, axis=1, keepdims=True)) / (GROUPS * SHARD)

    def add_sums(t, total):
        arrive(t, 4)
        for h in range(2):
            total = total + lanes(wide(both[0, 2 * t + h]))
        return total

    mean = row_mean(lax.fori_loop(0, UNITS, add_sums, zero))

    def add_squares(t, total):
        for h in range(2):
            centred = wide(both[0, 2 * t + h]) - mean
            total = total + lanes(centred * centred)
        return total

    inv_scale = lax.rsqrt(row_mean(lax.fori_loop(0, UNITS, add_squares, zero)) + EPSILON)

    def add_means(t, totals):
        for h in range(2):
            unit = (wide(both[0, 2 * t + h]) - mean) * inv_scale
            scaled = gain_rows(t, h) * wide(both[1, 2 * t + h])
            totals = (totals[0] + lanes(scaled), totals[1] + lanes(scaled * unit))
        return totals

    sums = lax.fori_loop(0, UNITS, add_means, (zero, zero))
    mean_scaled, mean_product = row_mean(sums[0]), row_mean(sums[1])
    first_unit = SIDE * ((z // 2 + z % 2 + 1) % 2)

    def write(turn, carry):
        shard = (turn + first_unit // 2) % SIDE
        kept = []
        for v in range(2):
            t = 2 * shard + v
            for h in range(2):
                chunk = 2 * t + h
                a, b = axes(h)
                rows = gain_rows(t, h)
                unit = (wide(both[0, chunk]) - mean) * inv_scale
                d_normed = wide(both[1, chunk])
                grad = inv_scale * (rows * d_normed - mean_scaled - unit * mean_product)
                value = jnp.where(section == 0, grad, unit * rows)
                values[chunk, b, a] = narrow(value)
                gather_values(t, h, 0).start()
                gather_values(t, h, 1).start()
                kept.append(value)
                product = d_normed * unit
                for start, rows in (
                    (lower_start(t, h), slice(0, OWN)),
                    (upper_start(t, h), slice(OWN, TALL)),
                ):
                    own_grad[:, pl.ds(start, WIDE)] = narrow(grad[rows])
                    gain_own[0, :, pl.ds(start, WIDE)] = jnp.sum(product[rows], axis=0, keepdims=True)
        for target, rows in ((shard, slice(0, OWN)), (GROUPS - 1 - shard, slice(OWN, TALL))):
            for e, (first, second) in enumerate(((0, 2), (1, 3), (2, 3))):
                exchange[target, e] = narrow(stacked(kept[first][rows], kept[second][rows]))
                wanted = target // SIDE != z // 2 if e < 2 else target // 2 == next_plane

                @pl.when(wanted)
                def _():
                    exchanged(target, e).start()
        return carry

    lax.fori_loop(0, SIDE, write, 0)


    def near_copy(t, upper, target, slot):
        return remote(
            tokens.at[t, upper],
            from_near.at[slot],
            near_send.at[0],
            near_recv.at[slot],
            {"grp": target},
        )

    def split_blocks(store, chunk, h, put):
        for i in range(0, SIDE * SIDE, 2):
            pair = []
            for at in (i, i + 1):
                a, b = (at // SIDE, at % SIDE) if h == 0 else (at % SIDE, at // SIDE)
                pair.append(wide(store[chunk, b, a]))
            put(0, slice(OWN * i, OWN * (i + 2)), narrow(stacked(pair[0][:OWN], pair[1][:OWN])))
            put(1, slice(OWN * i, OWN * (i + 2)), narrow(stacked(pair[0][OWN:], pair[1][OWN:])))

    def add_grads(start, transposed_heads, token_rows):
        cols = pl.ds(start, token_rows.shape[1])
        grads_t[:, cols] += jnp.dot(
            transposed_heads, token_rows, preferred_element_type=jnp.float32
        )

    def store_grads(block):
        return pltpu.make_async_copy(
            grads.at[block * WIDE : (block + 1) * WIDE],
            grads_out.at[block * WIDE : (block + 1) * WIDE],
            output_sem.at[3 + block],
        )

    def finish_grads(blocks):
        for block in blocks:
            cols = slice(block * WIDE, (block + 1) * WIDE)
            grads[cols] = grad_scale * grads_t[:, cols].T
            store_grads(block).start()

    def use_values(t):
        for h in range(2):

            def put(upper, rows, block):
                tokens[t, upper, rows, h * WIDE : (h + 1) * WIDE] = block

            split_blocks(values, 2 * t + h, h, put)
        for upper, target in enumerate((t // 2, GROUPS - 1 - t // 2)):
            to_next = jnp.logical_and(target // 2 == next_plane, t % 2 == 0)
            for slot, wanted in ((t % 2, target == sibling_group), (2 + core, to_next)):

                @pl.when(wanted)
                def _():
                    near_copy(t, upper, target, slot).start()

        total = heads_total[...]
        for upper, start in enumerate((lower_start(t), upper_start(t))):
            total = total + jnp.dot(
                tokens[t, upper], weight_buf[:, pl.ds(start, UNIT_WIDE)],
                preferred_element_type=jnp.float32,
            )
        heads_total[...] = total
        for upper, target in enumerate((t // 2, GROUPS - 1 - t // 2)):

            @pl.when(target == group)
            def _():
                add_grads(pl.multiple_of((t % 2) * UNIT_WIDE, UNIT_WIDE), heads_t[...], tokens[t, upper])

    def use_columns(p):
        last = p // (FAR_UNITS - 1)
        plane = (1 - last) * (2 * (1 - z // 2) + p // 2) + last * next_plane
        for h in range(2):

            def put(side, rows, block):
                column_tokens[h, rows, side * WIDE : (side + 1) * WIDE] = block

            split_blocks(columns, 2 * p + h, h, put)
        slot = plane_slot(plane, z)

        @pl.when(jnp.logical_and(p % 2 == 0, last == 0))
        def _():
            heads_arrived(slot + 1 - core)

        total = jnp.dot(
            heads_all[slot], column_tokens[0], preferred_element_type=jnp.float32
        ) + jnp.dot(heads_all[slot + 1], column_tokens[1], preferred_element_type=jnp.float32)
        for side in range(2):
            start = (1 - last) * (side * UNIT_WIDE + (p % 2) * WIDE) + last * (UNIT_WIDE + side * WIDE)
            cols = pl.ds(pl.multiple_of(start, WIDE), WIDE)
            grads_t[:, cols] += total[:, side * WIDE : (side + 1) * WIDE]

    def use_near(slot, heads_slot, start):
        wait_arrived(from_near.at[slot], near_recv.at[slot])
        add_grads(start, heads_all[heads_slot], from_near[slot])

    gain_partners = [
        {"tp": x * SIDE + y + 1 - 2 * (y % 2)},
        {"tp": x * SIDE + SIDE - 1 - y},
        {"tp": (x + 1 - 2 * (x % 2)) * SIDE + y},
        {"tp": (SIDE - 1 - x) * SIDE + y},
        sibling,
        {"grp": 2 * next_plane + core},
        {"grp": 2 * (SIDE - 1 - z) + core},
    ]

    def gain_copy(step):
        return remote(
            gain_own.at[step], gain_got.at[step], gain_send.at[step], gain_recv.at[step], gain_partners[step]
        )

    own_grad_store, heads_store, gain_store = [
        pltpu.make_async_copy(source, target, output_sem.at[at])
        for at, (source, target) in enumerate(
            ((own_grad, grad_out), (heads_done, heads_out), (gain_done, gain_out))
        )
    ]

    near_heads = plane_slot(next_plane, z)

    def value_unit(q):
        return (q + first_unit) % UNITS

    def gather_stage(q, stage):
        def pass_on(gather, recvs, p):
            wait_arrived(gather_sizes[stage], recvs.at[p, stage])
            if stage < 3:
                for h in range(2):
                    gather(p, h, 2 * stage + 2).start()
                    gather(p, h, 2 * stage + 3).start()

        @pl.when(within(q, UNITS))
        def _():
            pass_on(gather_values, value_recv, value_unit(q))

        @pl.when(within(q - UNITS, FAR_UNITS))
        def _():
            pass_on(gather_columns, column_recv, q - UNITS)

    def gather_turn(n, carry):
        @pl.when(n == 5)
        def _():
            pass_heads()

        for step in range(GAIN_STEPS + 1):

            @pl.when(n == step + 1)
            def _():
                if step > 0:
                    gain_copy(step - 1).wait_recv()
                    gain_own[step] = gain_own[step - 1] + gain_got[step - 1]
                if step < GAIN_STEPS:
                    gain_copy(step).start()
                else:
                    gain_done[...] = gain_own[GAIN_STEPS] * grad_scale
                    gain_store.start()

        @pl.when(within(n + 1 - UNITS, FAR_UNITS))
        def _():
            p = n + 1 - UNITS
            wait_arrived(gather_sizes[1], exchange_recv.at[p])
            for h in range(2):
                gather_columns(p, h, 0).start()
                gather_columns(p, h, 1).start()

        @pl.when(n == UNITS + FAR_UNITS + 4)
        def _():
            finish_grads((0, 1))

        gather_stage(n, 0)
        gather_stage(n - 4, 2)
        gather_stage(n - 2, 1)
        gather_stage(n - 5, 3)
        done = n - 5

        @pl.when(within(done, UNITS))
        def _():
            use_values(value_unit(done))

        @pl.when(done == UNITS)
        def _():
            heads_done[...] = narrow(heads_total[...])
            heads_store.start()
            heads_arrived(SLOTS - 1)
            use_near(0, SLOTS - 1, 0)
            use_near(1, SLOTS - 1, UNIT_WIDE)
            heads_arrived(near_heads + 1 - core)

        @pl.when(done == UNITS + 2)
        def _():
            for k in range(2):
                use_near(2 + k, near_heads + k, 0)

        @pl.when(within(done - UNITS, FAR_UNITS))
        def _():
            use_columns(done - UNITS)

        return carry

    own_grad_store.start()
    each_relay((2,), pass_relay)
    lax.fori_loop(0, UNITS + FAR_UNITS + 5, gather_turn, 0)
    finish_grads((2, 3))

    def reduce_sent(u, carry):
        wait_sent(part.at[0:2], send_sem.at[u])
        wait_sent(values.at[0:5, 0:3, 0:2], value_send.at[u])
        return carry

    def columns_sent(p, carry):
        wait_sent(values.at[0:5, 0:3, 0:2], column_send.at[p])
        return carry

    lax.fori_loop(0, UNITS, reduce_sent, 0)
    lax.fori_loop(0, FAR_UNITS, columns_sent, 0)
    wait_sent(exchange.at[0:5, 0:2], exchange_send.at[0])
    wait_sent(tokens.at[0:2], near_send.at[0])
    each_relay((0, 1, 2), lambda relay, held: relay.wait_send())
    for j in range(SIDE - 1):
        passed_heads(j).wait_send()
    sibling_heads().wait_send()
    for step in range(GAIN_STEPS):
        gain_copy(step).wait_send()
    for store in [own_grad_store, heads_store, gain_store] + [store_grads(i) for i in range(4)]:
        store.wait()


def deliver_kernel(*refs):
    results, outputs, held = refs[:4], refs[4:8], refs[8:12]
    load_sem, store_sem = refs[12:]
    loads = [pltpu.make_async_copy(results[at], held[at], load_sem.at[at]) for at in range(4)]
    stores = [pltpu.make_async_copy(held[at], outputs[at], store_sem.at[at]) for at in range(4)]
    for load in loads:
        load.start()
    for load, store in zip(loads, stores):
        load.wait()
        store.start()
    for store in stores:
        store.wait()


def delivered(results):
    hbm = pl.BlockSpec(memory_space=pl.ANY)
    return pl.pallas_call(
        deliver_kernel,
        out_shape=tuple(jax.ShapeDtypeStruct(result.shape, result.dtype) for result in results),
        in_specs=[hbm] * 4,
        out_specs=(hbm,) * 4,
        scratch_shapes=[pltpu.VMEM(result.shape, result.dtype) for result in results]
        + [pltpu.SemaphoreType.DMA((4,))] * 2,
        name="deliver",
    )(*results)


def fused(heads, weights, residual, gain):
    hbm = pl.BlockSpec(memory_space=pl.ANY)
    bf16, f32 = jnp.bfloat16, jnp.float32
    rows_dev, depth = heads.shape
    owned = weights.shape[1] // GROUPS
    dma = pltpu.SemaphoreType.DMA
    return pl.pallas_call(
        boundary_kernel,
        out_shape=(
            jax.ShapeDtypeStruct(heads.shape, bf16),
            jax.ShapeDtypeStruct((owned, depth), f32),
            jax.ShapeDtypeStruct(residual.shape, bf16),
            jax.ShapeDtypeStruct(gain.shape, f32),
        ),
        in_specs=[hbm] * 4,
        out_specs=(hbm,) * 4,
        scratch_shapes=[
            pltpu.VMEM(heads.shape, bf16),
            pltpu.VMEM(residual.shape, bf16),
            pltpu.VMEM(gain.shape, f32),
            pltpu.VMEM(heads.shape, bf16),
            pltpu.VMEM((owned, depth), f32),
            pltpu.VMEM(residual.shape, bf16),
            pltpu.VMEM(gain.shape, f32),
            pltpu.VMEM((depth, rows_dev), bf16),
            pltpu.VMEM((depth, owned), f32),
            pltpu.VMEM(weights.shape, bf16),
            pltpu.VMEM((CHUNKS, SIDE, SIDE, TALL, WIDE), bf16),
            pltpu.VMEM((CHUNKS, 2, SIDE, TALL, HALF), bf16),
            pltpu.VMEM((CHUNKS, 2, SIDE, TALL, WIDE), bf16),
            pltpu.VMEM((CHUNKS, 2, TALL, HALF), bf16),
            pltpu.VMEM((CHUNKS, 2, TALL, WIDE), bf16),
            pltpu.VMEM((2, CHUNKS, TALL, WIDE), bf16),
            pltpu.VMEM((CHUNKS, SIDE, SIDE, TALL, WIDE), bf16),
            pltpu.VMEM((FAR_CHUNKS, SIDE, SIDE, TALL, WIDE), bf16),
            pltpu.VMEM((GROUPS, 3, TALL, WIDE), bf16),
            pltpu.VMEM((UNITS, 2, rows_dev, UNIT_WIDE), bf16),
            pltpu.VMEM((2, rows_dev, UNIT_WIDE), bf16),
            pltpu.VMEM((4, rows_dev, UNIT_WIDE), bf16),
            pltpu.VMEM((SLOTS, depth, rows_dev), bf16),
            pltpu.VMEM((rows_dev, depth), f32),
            pltpu.VMEM((GAIN_STEPS + 1,) + gain.shape, f32),
            pltpu.VMEM((GAIN_STEPS,) + gain.shape, f32),
            dma((3,)),
            dma((7,)),
            dma((UNITS, 2)),
            dma((UNITS,)),
            dma((UNITS, 5)),
            dma((UNITS,)),
            dma((UNITS, 4)),
            dma((FAR_UNITS,)),
            dma((FAR_UNITS, 4)),
            dma((1,)),
            dma((FAR_UNITS,)),
            dma((SLOTS + 6,)),
            dma((SLOTS,)),
            dma((1,)),
            dma((4,)),
            dma((GAIN_STEPS,)),
            dma((GAIN_STEPS,)),
        ],
        compiler_params=pltpu.CompilerParams(
            collective_id=0, has_side_effects=True, vmem_limit_bytes=62 * 1024 * 1024
        ),
        name="boundary",
    )(heads, weights, residual, gain)


def per_device(heads_in, weights, residual, norm_gain):
    heads_out, weight_grad, boundary_grad, gain_grad = delivered(
        fused(heads_in[0], weights[0], residual, norm_gain[None])
    )
    return (heads_out[None], weight_grad[None], boundary_grad, gain_grad[0])


def solution(mesh):
    placed = (P("section", "grp", "tp"), P("section", "tp", None), P(("grp", "tp"), None), P())
    return jax.shard_map(
        per_device,
        mesh=mesh,
        in_specs=placed,
        out_specs=(
            P("section", "grp", "tp"),
            P("section", "grp", "tp"),
            P(("grp", "tp"), None),
            P(),
        ),
        check_vma=False,
    )
```

```python
import math

import jax
import jax.numpy as jnp
from jax import lax
from jax.experimental import pallas as pl
from jax.experimental.pallas import tpu as pltpu
from jax.sharding import PartitionSpec as P

EPSILON = 1e-05
MESH = pl.DeviceIdType.MESH

SIDE = 4
GROUPS = 8
UNITS = 8
FAR_UNITS = 5
CHUNKS = 2 * UNITS
FAR_CHUNKS = 2 * FAR_UNITS
WIDE = 256
HALF = WIDE // 2
UNIT_WIDE = 2 * WIDE
SHARD = 2 * UNIT_WIDE
OWN = 24
TALL = 2 * OWN
SLOTS = GROUPS - 1
GAIN_STEPS = 7


def lower_start(t, h=0):
    return pl.multiple_of(t * UNIT_WIDE + h * WIDE, WIDE)


def upper_start(t, h=0):
    return pl.multiple_of((GROUPS - 1 - t // 2) * SHARD + (t % 2) * UNIT_WIDE + h * WIDE, WIDE)


def plane_device(h, first, second):
    x, y = (first, second) if h == 0 else (second, first)
    return {"tp": x * SIDE + y}


def stacked(*parts):
    return jnp.concatenate(parts, axis=0)


def both_halves(row_pair):
    total = row_pair[:OWN] + row_pair[OWN:]
    return stacked(total, total)


def lanes(value):
    return sum(value[:, 128 * i : 128 * (i + 1)] for i in range(value.shape[1] // 128))


def wide(value):
    return value.astype(jnp.float32)


def narrow(value):
    return value.astype(jnp.bfloat16)


def remote(source, target, send_sem, recv_sem, device):
    return pltpu.make_async_remote_copy(
        src_ref=source,
        dst_ref=target,
        send_sem=send_sem,
        recv_sem=recv_sem,
        device_id=device,
        device_id_type=MESH,
    )


def greet(peers):
    barrier = pltpu.get_barrier_semaphore()
    for peer in peers:
        pl.semaphore_signal(barrier, inc=1, device_id=peer, device_id_type=MESH)
    pl.semaphore_wait(barrier, len(peers))


def boundary_kernel(
    heads_in, weights, residual_in, gain_in, heads_out, grads_out, grad_out, gain_out,
    heads, residual, gain, heads_done, grads, own_grad, gain_done,
    heads_t, grads_t, weight_buf, part, from1, from2, from3, from4, both,
    values, columns, exchange, tokens, column_tokens, from_near, heads_all, heads_total, gain_own, gain_got,
    input_sem, output_sem, weight_sem, send_sem, recv_sem, value_send, value_recv, column_send, column_recv,
    exchange_send, exchange_recv, heads_send, heads_recv, near_send, near_recv, gain_send, gain_recv,
):
    tp = lax.axis_index("tp")
    x, y = tp // SIDE, tp % SIDE
    section = lax.axis_index("section")
    group = lax.axis_index("grp")
    z, core = group // 2, group % 2
    other = {"section": 1 - section}
    sibling_group = 2 * z + 1 - core
    sibling = {"grp": sibling_group}
    next_plane = z + 1 - 2 * (z % 2)
    rows_dev, depth = heads.shape
    grad_scale = 1.0 / math.sqrt(rows_dev * GROUPS)

    def axes(h):
        return (x, y) if h == 0 else (y, x)

    def wait_arrived(size, sem):
        remote(size, size, heads_send.at[0], sem, sibling).wait_recv()

    def wait_sent(size, sem):
        remote(size, size, sem, heads_recv.at[0], sibling).wait_send()

    def weight_copy(t, upper):
        cols = pl.ds(upper_start(t) if upper else lower_start(t), UNIT_WIDE)
        return pltpu.make_async_copy(
            weights.at[:, cols], weight_buf.at[:, cols], weight_sem.at[t, upper]
        )

    def start_weights(t, carry):
        weight_copy(t, 0).start()
        weight_copy(t, 1).start()
        return carry

    heads_load, residual_load, gain_load = [
        pltpu.make_async_copy(source, target, input_sem.at[at])
        for at, (source, target) in enumerate(
            ((heads_in, heads), (residual_in, residual), (gain_in, gain))
        )
    ]
    heads_load.start()
    lax.fori_loop(0, UNITS, start_weights, 0)
    residual_load.start()
    gain_load.start()
    greet(
        [plane_device(0, (x + step) % SIDE, y) for step in (1, 3)]
        + [plane_device(0, x, (y + step) % SIDE) for step in (1, 3)]
        + [other, sibling]
        + [{"grp": 2 * ((z + hop) % SIDE) + k} for hop in range(1, SIDE) for k in range(2)]
    )
    heads_load.wait()

    def plane_slot(origin, at):
        return 2 * ((origin + SIDE - 1 - at) % SIDE)

    def heads_arrived(slot):
        remote(
            heads_t, heads_all.at[slot], heads_send.at[SLOTS - 1], heads_recv.at[slot], sibling
        ).wait_recv()

    def sibling_heads():
        slot = SLOTS - 1
        return remote(
            heads_t, heads_all.at[slot], heads_send.at[slot], heads_recv.at[slot], sibling
        )

    relays = ((1, 0), (-1, 0), (1, 1), (-1, 1), (1, 2), (-1, 2))

    def each_relay(wanted, act):
        for at, (step, away) in enumerate(relays):
            if away not in wanted:
                continue
            first, last = (away, SIDE - 2) if step > 0 else (1, SIDE - 1 - away)

            @pl.when(jnp.logical_and(z >= first, z <= last))
            def _():
                origin, target = z - step * away, z + step
                held = plane_slot(origin, z) + core
                slot = plane_slot(origin, target) + core
                act(
                    remote(
                        heads_all.at[held] if away else heads_t,
                        heads_all.at[slot],
                        heads_send.at[SLOTS + at],
                        heads_recv.at[slot],
                        {"grp": 2 * target + core},
                    ),
                    held,
                )

    def start_relay(relay, held):
        relay.start()

    def pass_relay(relay, held):
        heads_arrived(held)
        relay.start()

    def passed_heads(j):
        slot = 2 * j + core
        held = heads_all.at[slot]
        return remote(held, held, heads_send.at[slot], heads_recv.at[slot], sibling)

    def pass_heads(late):
        for j in range(SIDE - 1):
            far = jnp.logical_or(
                jnp.logical_and(z == 0, j == SIDE - 2), jnp.logical_and(z == SIDE - 1, j == 0)
            )

            @pl.when(far if late else jnp.logical_not(far))
            def _():
                @pl.when(jnp.logical_or(z == 0, z == SIDE - 1))
                def _():
                    heads_arrived(2 * j + core)

                passed_heads(j).start()

    def send_heads():
        heads_t[...] = heads[...].T
        each_relay((0,), start_relay)
        sibling_heads().start()


    def copy(u, h, step):
        chunk = 2 * u + h
        a, b = axes(h)
        right, left = (a + 1) % SIDE, (a + 3) % SIDE
        up, down = (b + 1) % SIDE, (b + 3) % SIDE
        low, high = pl.ds(0, HALF), pl.ds(HALF, HALF)
        far_a, far_b = (a + 2) % SIDE, (b + 2) % SIDE
        source, target, device = [
            lambda: (part.at[chunk, far_a, :, :, low], from1.at[chunk, 0], plane_device(h, right, b)),
            lambda: (part.at[chunk, far_a, :, :, high], from1.at[chunk, 1], plane_device(h, left, b)),
            lambda: (part.at[chunk, right], from2.at[chunk, 0], plane_device(h, right, b)),
            lambda: (part.at[chunk, left], from2.at[chunk, 1], plane_device(h, left, b)),
            lambda: (part.at[chunk, a, far_b, :, low], from3.at[chunk, 0], plane_device(h, a, up)),
            lambda: (part.at[chunk, a, far_b, :, high], from3.at[chunk, 1], plane_device(h, a, down)),
            lambda: (part.at[chunk, a, up], from4.at[chunk, 0], plane_device(h, a, up)),
            lambda: (part.at[chunk, a, down], from4.at[chunk, 1], plane_device(h, a, down)),
            lambda: (both.at[section, chunk], both.at[section, chunk], other),
        ][step]()
        return remote(source, target, send_sem.at[u], recv_sem.at[u, step // 2], device)

    reduce_sizes = [
        part.at[0, 0:2], part.at[0], part.at[0, 0, 0:2], part.at[0, 0], part.at[0, 0, 0:2]
    ]

    def arrive(u, stage):
        wait_arrived(reduce_sizes[stage], recv_sem.at[u, stage])

    def multiply(u):
        weight_copy(u, 0).wait()
        weight_copy(u, 1).wait()
        lower, upper = [
            jnp.dot(
                heads[...], weight_buf[:, pl.ds(start, UNIT_WIDE)],
                preferred_element_type=jnp.float32,
            )
            for start in (lower_start(u), upper_start(u))
        ]
        for h in range(2):
            cols = slice(h * WIDE, (h + 1) * WIDE)
            for i in range(SIDE * SIDE):
                rows = slice(OWN * i, OWN * (i + 1))
                a, b = (i // SIDE, i % SIDE) if h == 0 else (i % SIDE, i // SIDE)
                part[2 * u + h, a, b] = narrow(stacked(lower[rows, cols], upper[rows, cols]))
            copy(u, h, 0).start()
            copy(u, h, 1).start()

    def near_first(u):
        arrive(u, 0)
        for h in range(2):
            chunk = 2 * u + h
            a, b = axes(h)
            right, left = (a + 1) % SIDE, (a + 3) % SIDE
            part[chunk, right, :, :, :HALF] = narrow(
                wide(part[chunk, right, :, :, :HALF]) + wide(from1[chunk, 0])
            )
            copy(u, h, 2).start()
            part[chunk, left, :, :, HALF:] = narrow(
                wide(part[chunk, left, :, :, HALF:]) + wide(from1[chunk, 1])
            )
            copy(u, h, 3).start()

    def far_second(u):
        arrive(u, 1)
        for h in range(2):
            chunk = 2 * u + h
            a, b = axes(h)
            part[chunk, a] = narrow(
                wide(part[chunk, a]) + (wide(from2[chunk, 0]) + wide(from2[chunk, 1]))
            )
            copy(u, h, 4).start()
            copy(u, h, 5).start()

    def near_second(u):
        arrive(u, 2)
        for h in range(2):
            chunk = 2 * u + h
            a, b = axes(h)
            up, down = (b + 1) % SIDE, (b + 3) % SIDE
            part[chunk, a, up, :, :HALF] = narrow(
                wide(part[chunk, a, up, :, :HALF]) + wide(from3[chunk, 0])
            )
            copy(u, h, 6).start()
            part[chunk, a, down, :, HALF:] = narrow(
                wide(part[chunk, a, down, :, HALF:]) + wide(from3[chunk, 1])
            )
            copy(u, h, 7).start()

    def finish(u):
        arrive(u, 3)
        for h in range(2):
            chunk = 2 * u + h
            a, b = axes(h)
            total = wide(part[chunk, a, b]) + (wide(from4[chunk, 0]) + wide(from4[chunk, 1]))
            rows = stacked(
                wide(residual[:, pl.ds(lower_start(u, h), WIDE)]),
                wide(residual[:, pl.ds(upper_start(u, h), WIDE)]),
            )
            total = total + jnp.where(section == 0, rows, 0.0)
            both[section, chunk] = narrow(total)
            copy(u, h, 8).start()

    def within(value, count):
        return jnp.logical_and(value >= 0, value < count)

    stages = (multiply, near_first, far_second, near_second, finish)

    def reduce_turn(n, carry):
        for late, stage in enumerate(stages):

            @pl.when(within(n - late, UNITS))
            def _():
                stage(n - late)

        for away, at in ((1, 4), (2, 9)):

            @pl.when(n == at)
            def _():
                each_relay((away,), pass_relay)

        return carry

    send_heads()
    residual_load.wait()
    gain_load.wait()
    lax.fori_loop(0, UNITS + len(stages) - 1, reduce_turn, 0)
    pass_heads(False)
    heads_total[...] = jnp.zeros_like(heads_total)
    grads_t[...] = jnp.zeros_like(grads_t)


    def gather_of(store, sends, recvs):
        half = store.shape[-1] // 2

        def gather(p, h, step):
            chunk = 2 * p + h
            a, b = axes(h)
            right, left = (a + 1) % SIDE, (a + 3) % SIDE
            up, down = (b + 1) % SIDE, (b + 3) % SIDE
            low, high = pl.ds(0, half), pl.ds(half, half)
            block, device = [
                lambda: (store.at[chunk, b, a], plane_device(h, right, b)),
                lambda: (store.at[chunk, b, a], plane_device(h, left, b)),
                lambda: (store.at[chunk, b, left, :, low], plane_device(h, right, b)),
                lambda: (store.at[chunk, b, right, :, high], plane_device(h, left, b)),
                lambda: (store.at[chunk, b], plane_device(h, a, up)),
                lambda: (store.at[chunk, b], plane_device(h, a, down)),
                lambda: (store.at[chunk, down, :, :, low], plane_device(h, a, up)),
                lambda: (store.at[chunk, up, :, :, high], plane_device(h, a, down)),
            ][step]()
            return remote(block, block, sends.at[p], recvs.at[p, step // 2], device)

        return gather

    gather_values = gather_of(values, value_send, value_recv)
    gather_columns = gather_of(columns, column_send, column_recv)

    gather_sizes = [values.at[0, 0], values.at[0, 0, 0:2], values.at[0], values.at[0, 0:2]]

    def exchanged(target, e):
        unit = 2 * (z % 2) + e if e < 2 else FAR_UNITS - 1
        a, b = x + core * (y - x), y + core * (x - y)
        return remote(
            exchange.at[target, e],
            columns.at[2 * unit + core, b, a],
            exchange_send.at[0],
            exchange_recv.at[unit],
            {"grp": target},
        )

    def gain_rows(t, h):
        return stacked(
            jnp.broadcast_to(gain[:, pl.ds(lower_start(t, h), WIDE)], (OWN, WIDE)),
            jnp.broadcast_to(gain[:, pl.ds(upper_start(t, h), WIDE)], (OWN, WIDE)),
        )

    zero = jnp.zeros((TALL, 128), jnp.float32)

    def row_mean(total):
        return both_halves(jnp.sum(total, axis=1, keepdims=True)) / (GROUPS * SHARD)

    def add_sums(t, total):
        arrive(t, 4)
        for h in range(2):
            total = total + lanes(wide(both[0, 2 * t + h]))
        return total

    mean = row_mean(lax.fori_loop(0, UNITS, add_sums, zero))

    def add_squares(t, total):
        for h in range(2):
            centred = wide(both[0, 2 * t + h]) - mean
            total = total + lanes(centred * centred)
        return total

    inv_scale = lax.rsqrt(row_mean(lax.fori_loop(0, UNITS, add_squares, zero)) + EPSILON)

    def add_means(t, totals):
        for h in range(2):
            unit = (wide(both[0, 2 * t + h]) - mean) * inv_scale
            scaled = gain_rows(t, h) * wide(both[1, 2 * t + h])
            totals = (totals[0] + lanes(scaled), totals[1] + lanes(scaled * unit))
        return totals

    sums = lax.fori_loop(0, UNITS, add_means, (zero, zero))
    mean_scaled, mean_product = row_mean(sums[0]), row_mean(sums[1])
    first_unit = SIDE * ((z // 2 + z % 2 + 1) % 2)

    def write(turn, carry):
        shard = (turn + first_unit // 2) % SIDE
        kept = []
        for v in range(2):
            t = 2 * shard + v
            for h in range(2):
                chunk = 2 * t + h
                a, b = axes(h)
                rows = gain_rows(t, h)
                unit = (wide(both[0, chunk]) - mean) * inv_scale
                d_normed = wide(both[1, chunk])
                grad = inv_scale * (rows * d_normed - mean_scaled - unit * mean_product)
                value = jnp.where(section == 0, grad, unit * rows)
                values[chunk, b, a] = narrow(value)
                gather_values(t, h, 0).start()
                gather_values(t, h, 1).start()
                kept.append(value)
                product = d_normed * unit
                for start, rows in (
                    (lower_start(t, h), slice(0, OWN)),
                    (upper_start(t, h), slice(OWN, TALL)),
                ):
                    own_grad[:, pl.ds(start, WIDE)] = narrow(grad[rows])
                    gain_own[0, :, pl.ds(start, WIDE)] = jnp.sum(product[rows], axis=0, keepdims=True)
        for target, rows in ((shard, slice(0, OWN)), (GROUPS - 1 - shard, slice(OWN, TALL))):
            for e, (first, second) in enumerate(((0, 2), (1, 3), (2, 3))):
                exchange[target, e] = narrow(stacked(kept[first][rows], kept[second][rows]))
                wanted = target // SIDE != z // 2 if e < 2 else target // 2 == next_plane

                @pl.when(wanted)
                def _():
                    exchanged(target, e).start()
        return carry

    lax.fori_loop(0, SIDE, write, 0)


    def near_copy(t, upper, target, slot):
        return remote(
            tokens.at[t, upper],
            from_near.at[slot],
            near_send.at[0],
            near_recv.at[slot],
            {"grp": target},
        )

    def split_blocks(store, chunk, h, put):
        for i in range(0, SIDE * SIDE, 2):
            pair = []
            for at in (i, i + 1):
                a, b = (at // SIDE, at % SIDE) if h == 0 else (at % SIDE, at // SIDE)
                pair.append(wide(store[chunk, b, a]))
            put(0, slice(OWN * i, OWN * (i + 2)), narrow(stacked(pair[0][:OWN], pair[1][:OWN])))
            put(1, slice(OWN * i, OWN * (i + 2)), narrow(stacked(pair[0][OWN:], pair[1][OWN:])))

    def add_grads(start, transposed_heads, token_rows):
        cols = pl.ds(start, token_rows.shape[1])
        grads_t[:, cols] += jnp.dot(
            transposed_heads, token_rows, preferred_element_type=jnp.float32
        )

    def store_grads(block):
        return pltpu.make_async_copy(
            grads.at[block * WIDE : (block + 1) * WIDE],
            grads_out.at[block * WIDE : (block + 1) * WIDE],
            output_sem.at[3 + block],
        )

    def finish_grads(blocks):
        for block in blocks:
            cols = slice(block * WIDE, (block + 1) * WIDE)
            grads[cols] = grad_scale * grads_t[:, cols].T
            store_grads(block).start()

    def use_values(t):
        for h in range(2):

            def put(upper, rows, block):
                tokens[t, upper, rows, h * WIDE : (h + 1) * WIDE] = block

            split_blocks(values, 2 * t + h, h, put)
        for upper, target in enumerate((t // 2, GROUPS - 1 - t // 2)):
            to_next = jnp.logical_and(target // 2 == next_plane, t % 2 == 0)
            for slot, wanted in ((t % 2, target == sibling_group), (2 + core, to_next)):

                @pl.when(wanted)
                def _():
                    near_copy(t, upper, target, slot).start()

        total = heads_total[...]
        for upper, start in enumerate((lower_start(t), upper_start(t))):
            total = total + lax.dot_general(
                tokens[t, upper], weight_buf[:, pl.ds(start, UNIT_WIDE)],
                (((1,), (1,)), ((), ())), preferred_element_type=jnp.float32,
            )
        heads_total[...] = total
        for upper, target in enumerate((t // 2, GROUPS - 1 - t // 2)):

            @pl.when(target == group)
            def _():
                add_grads(pl.multiple_of((t % 2) * UNIT_WIDE, UNIT_WIDE), heads_t[...], tokens[t, upper])

    def use_columns(p):
        last = p // (FAR_UNITS - 1)
        plane = (1 - last) * (2 * (1 - z // 2) + p // 2) + last * next_plane
        for h in range(2):

            def put(side, rows, block):
                column_tokens[h, rows, side * WIDE : (side + 1) * WIDE] = block

            split_blocks(columns, 2 * p + h, h, put)
        slot = plane_slot(plane, z)

        @pl.when(jnp.logical_and(p % 2 == 0, last == 0))
        def _():
            heads_arrived(slot + 1 - core)

        total = jnp.dot(
            heads_all[slot], column_tokens[0], preferred_element_type=jnp.float32
        ) + jnp.dot(heads_all[slot + 1], column_tokens[1], preferred_element_type=jnp.float32)
        for side in range(2):
            start = (1 - last) * (side * UNIT_WIDE + (p % 2) * WIDE) + last * (UNIT_WIDE + side * WIDE)
            cols = pl.ds(pl.multiple_of(start, WIDE), WIDE)
            grads_t[:, cols] += total[:, side * WIDE : (side + 1) * WIDE]

    def use_near(slot, heads_slot, start):
        wait_arrived(from_near.at[slot], near_recv.at[slot])
        add_grads(start, heads_all[heads_slot], from_near[slot])

    gain_partners = [
        {"tp": x * SIDE + y + 1 - 2 * (y % 2)},
        {"tp": x * SIDE + SIDE - 1 - y},
        {"tp": (x + 1 - 2 * (x % 2)) * SIDE + y},
        {"tp": (SIDE - 1 - x) * SIDE + y},
        sibling,
        {"grp": 2 * next_plane + core},
        {"grp": 2 * (SIDE - 1 - z) + core},
    ]

    def gain_copy(step):
        return remote(
            gain_own.at[step], gain_got.at[step], gain_send.at[step], gain_recv.at[step], gain_partners[step]
        )

    own_grad_store, heads_store, gain_store = [
        pltpu.make_async_copy(source, target, output_sem.at[at])
        for at, (source, target) in enumerate(
            ((own_grad, grad_out), (heads_done, heads_out), (gain_done, gain_out))
        )
    ]

    near_heads = plane_slot(next_plane, z)

    def value_unit(q):
        return (q + first_unit) % UNITS

    def gather_stage(q, stage):
        def pass_on(gather, recvs, p):
            wait_arrived(gather_sizes[stage], recvs.at[p, stage])
            if stage < 3:
                for h in range(2):
                    gather(p, h, 2 * stage + 2).start()
                    gather(p, h, 2 * stage + 3).start()

        @pl.when(within(q, UNITS))
        def _():
            pass_on(gather_values, value_recv, value_unit(q))

        @pl.when(within(q - UNITS, FAR_UNITS))
        def _():
            pass_on(gather_columns, column_recv, q - UNITS)

    def gather_turn(n, carry):
        @pl.when(n == 4)
        def _():
            pass_heads(True)

        for step in range(GAIN_STEPS + 1):

            @pl.when(n == step + 1)
            def _():
                if step > 0:
                    gain_copy(step - 1).wait_recv()
                    gain_own[step] = gain_own[step - 1] + gain_got[step - 1]
                if step < GAIN_STEPS:
                    gain_copy(step).start()
                else:
                    gain_done[...] = gain_own[GAIN_STEPS] * grad_scale
                    gain_store.start()

        @pl.when(within(n + 1 - UNITS, FAR_UNITS))
        def _():
            p = n + 1 - UNITS
            wait_arrived(gather_sizes[1], exchange_recv.at[p])
            for h in range(2):
                gather_columns(p, h, 0).start()
                gather_columns(p, h, 1).start()

        @pl.when(n == UNITS + FAR_UNITS + 4)
        def _():
            finish_grads((0, 1))

        gather_stage(n, 0)
        gather_stage(n - 4, 2)
        gather_stage(n - 2, 1)
        gather_stage(n - 5, 3)
        done = n - 5

        @pl.when(within(done, UNITS))
        def _():
            use_values(value_unit(done))

        @pl.when(done == UNITS)
        def _():
            heads_done[...] = narrow(heads_total[...])
            heads_store.start()
            heads_arrived(SLOTS - 1)
            use_near(0, SLOTS - 1, 0)
            use_near(1, SLOTS - 1, UNIT_WIDE)
            heads_arrived(near_heads + 1 - core)

        @pl.when(done == UNITS + 2)
        def _():
            for k in range(2):
                use_near(2 + k, near_heads + k, 0)

        @pl.when(within(done - UNITS, FAR_UNITS))
        def _():
            use_columns(done - UNITS)

        return carry

    own_grad_store.start()
    lax.fori_loop(0, UNITS + FAR_UNITS + 5, gather_turn, 0)
    finish_grads((2, 3))

    def reduce_sent(u, carry):
        wait_sent(part.at[0:2], send_sem.at[u])
        wait_sent(values.at[0:5, 0:3, 0:2], value_send.at[u])
        return carry

    def columns_sent(p, carry):
        wait_sent(values.at[0:5, 0:3, 0:2], column_send.at[p])
        return carry

    lax.fori_loop(0, UNITS, reduce_sent, 0)
    lax.fori_loop(0, FAR_UNITS, columns_sent, 0)
    wait_sent(exchange.at[0:5, 0:2], exchange_send.at[0])
    wait_sent(tokens.at[0:2], near_send.at[0])
    each_relay((0, 1, 2), lambda relay, held: relay.wait_send())
    for j in range(SIDE - 1):
        passed_heads(j).wait_send()
    sibling_heads().wait_send()
    for step in range(GAIN_STEPS):
        gain_copy(step).wait_send()
    for store in [own_grad_store, heads_store, gain_store] + [store_grads(i) for i in range(4)]:
        store.wait()


def deliver_kernel(*refs):
    results, outputs, held = refs[:4], refs[4:8], refs[8:12]
    load_sem, store_sem = refs[12:]
    loads = [pltpu.make_async_copy(results[at], held[at], load_sem.at[at]) for at in range(4)]
    stores = [pltpu.make_async_copy(held[at], outputs[at], store_sem.at[at]) for at in range(4)]
    for load in loads:
        load.start()
    for load, store in zip(loads, stores):
        load.wait()
        store.start()
    for store in stores:
        store.wait()


def delivered(results):
    hbm = pl.BlockSpec(memory_space=pl.ANY)
    return pl.pallas_call(
        deliver_kernel,
        out_shape=tuple(jax.ShapeDtypeStruct(result.shape, result.dtype) for result in results),
        in_specs=[hbm] * 4,
        out_specs=(hbm,) * 4,
        scratch_shapes=[pltpu.VMEM(result.shape, result.dtype) for result in results]
        + [pltpu.SemaphoreType.DMA((4,))] * 2,
        name="deliver",
    )(*results)


def fused(heads, weights, residual, gain):
    hbm = pl.BlockSpec(memory_space=pl.ANY)
    bf16, f32 = jnp.bfloat16, jnp.float32
    rows_dev, depth = heads.shape
    owned = weights.shape[1] // GROUPS
    dma = pltpu.SemaphoreType.DMA
    return pl.pallas_call(
        boundary_kernel,
        out_shape=(
            jax.ShapeDtypeStruct(heads.shape, bf16),
            jax.ShapeDtypeStruct((owned, depth), f32),
            jax.ShapeDtypeStruct(residual.shape, bf16),
            jax.ShapeDtypeStruct(gain.shape, f32),
        ),
        in_specs=[hbm] * 4,
        out_specs=(hbm,) * 4,
        scratch_shapes=[
            pltpu.VMEM(heads.shape, bf16),
            pltpu.VMEM(residual.shape, bf16),
            pltpu.VMEM(gain.shape, f32),
            pltpu.VMEM(heads.shape, bf16),
            pltpu.VMEM((owned, depth), f32),
            pltpu.VMEM(residual.shape, bf16),
            pltpu.VMEM(gain.shape, f32),
            pltpu.VMEM((depth, rows_dev), bf16),
            pltpu.VMEM((depth, owned), f32),
            pltpu.VMEM(weights.shape, bf16),
            pltpu.VMEM((CHUNKS, SIDE, SIDE, TALL, WIDE), bf16),
            pltpu.VMEM((CHUNKS, 2, SIDE, TALL, HALF), bf16),
            pltpu.VMEM((CHUNKS, 2, SIDE, TALL, WIDE), bf16),
            pltpu.VMEM((CHUNKS, 2, TALL, HALF), bf16),
            pltpu.VMEM((CHUNKS, 2, TALL, WIDE), bf16),
            pltpu.VMEM((2, CHUNKS, TALL, WIDE), bf16),
            pltpu.VMEM((CHUNKS, SIDE, SIDE, TALL, WIDE), bf16),
            pltpu.VMEM((FAR_CHUNKS, SIDE, SIDE, TALL, WIDE), bf16),
            pltpu.VMEM((GROUPS, 3, TALL, WIDE), bf16),
            pltpu.VMEM((UNITS, 2, rows_dev, UNIT_WIDE), bf16),
            pltpu.VMEM((2, rows_dev, UNIT_WIDE), bf16),
            pltpu.VMEM((4, rows_dev, UNIT_WIDE), bf16),
            pltpu.VMEM((SLOTS, depth, rows_dev), bf16),
            pltpu.VMEM((rows_dev, depth), f32),
            pltpu.VMEM((GAIN_STEPS + 1,) + gain.shape, f32),
            pltpu.VMEM((GAIN_STEPS,) + gain.shape, f32),
            dma((3,)),
            dma((7,)),
            dma((UNITS, 2)),
            dma((UNITS,)),
            dma((UNITS, 5)),
            dma((UNITS,)),
            dma((UNITS, 4)),
            dma((FAR_UNITS,)),
            dma((FAR_UNITS, 4)),
            dma((1,)),
            dma((FAR_UNITS,)),
            dma((SLOTS + 6,)),
            dma((SLOTS,)),
            dma((1,)),
            dma((4,)),
            dma((GAIN_STEPS,)),
            dma((GAIN_STEPS,)),
        ],
        compiler_params=pltpu.CompilerParams(
            collective_id=0, has_side_effects=True, vmem_limit_bytes=62 * 1024 * 1024
        ),
        name="boundary",
    )(heads, weights, residual, gain)


def per_device(heads_in, weights, residual, norm_gain):
    heads_out, weight_grad, boundary_grad, gain_grad = delivered(
        fused(heads_in[0], weights[0], residual, norm_gain[None])
    )
    return (heads_out[None], weight_grad[None], boundary_grad, gain_grad[0])


def solution(mesh):
    placed = (P("section", "grp", "tp"), P("section", "tp", None), P(("grp", "tp"), None), P())
    return jax.shard_map(
        per_device,
        mesh=mesh,
        in_specs=placed,
        out_specs=(
            P("section", "grp", "tp"),
            P("section", "grp", "tp"),
            P(("grp", "tp"), None),
            P(),
        ),
        check_vma=False,
    )
```

```python
import math

import jax
import jax.numpy as jnp
from jax import lax
from jax.experimental import pallas as pl
from jax.experimental.pallas import tpu as pltpu
from jax.sharding import PartitionSpec as P

EPSILON = 1e-05
MESH = pl.DeviceIdType.MESH

SIDE = 4
GROUPS = 8
UNITS = 8
FAR_UNITS = 5
CHUNKS = 2 * UNITS
FAR_CHUNKS = 2 * FAR_UNITS
WIDE = 256
HALF = WIDE // 2
UNIT_WIDE = 2 * WIDE
SHARD = 2 * UNIT_WIDE
OWN = 24
TALL = 2 * OWN
SLOTS = GROUPS - 1
GAIN_STEPS = 7


def lower_start(t, h=0):
    return pl.multiple_of(t * UNIT_WIDE + h * WIDE, WIDE)


def upper_start(t, h=0):
    return pl.multiple_of((GROUPS - 1 - t // 2) * SHARD + (t % 2) * UNIT_WIDE + h * WIDE, WIDE)


def plane_device(h, first, second):
    x, y = (first, second) if h == 0 else (second, first)
    return {"tp": x * SIDE + y}


def stacked(*parts):
    return jnp.concatenate(parts, axis=0)


def both_halves(row_pair):
    total = row_pair[:OWN] + row_pair[OWN:]
    return stacked(total, total)


def lanes(value):
    return sum(value[:, 128 * i : 128 * (i + 1)] for i in range(value.shape[1] // 128))


def wide(value):
    return value.astype(jnp.float32)


def narrow(value):
    return value.astype(jnp.bfloat16)


def remote(source, target, send_sem, recv_sem, device):
    return pltpu.make_async_remote_copy(
        src_ref=source,
        dst_ref=target,
        send_sem=send_sem,
        recv_sem=recv_sem,
        device_id=device,
        device_id_type=MESH,
    )


def greet(peers):
    barrier = pltpu.get_barrier_semaphore()
    for peer in peers:
        pl.semaphore_signal(barrier, inc=1, device_id=peer, device_id_type=MESH)
    pl.semaphore_wait(barrier, len(peers))


def boundary_kernel(
    heads_in, weights, residual_in, gain_in, heads_out, grads_out, grad_out, gain_out,
    heads, residual, gain, heads_done, grads, own_grad, gain_done,
    heads_t, grads_t, weight_buf, part, from1, from2, from3, from4, both,
    values, columns, exchange, tokens, column_tokens, from_near, heads_all, heads_total, gain_own, gain_got,
    input_sem, output_sem, weight_sem, send_sem, recv_sem, value_send, value_recv, column_send, column_recv,
    exchange_send, exchange_recv, heads_send, heads_recv, near_send, near_recv, gain_send, gain_recv,
):
    tp = lax.axis_index("tp")
    x, y = tp // SIDE, tp % SIDE
    section = lax.axis_index("section")
    group = lax.axis_index("grp")
    z, core = group // 2, group % 2
    other = {"section": 1 - section}
    sibling_group = 2 * z + 1 - core
    sibling = {"grp": sibling_group}
    next_plane = z + 1 - 2 * (z % 2)
    rows_dev, depth = heads.shape
    grad_scale = 1.0 / math.sqrt(rows_dev * GROUPS)

    def axes(h):
        return (x, y) if h == 0 else (y, x)

    def wait_arrived(size, sem):
        remote(size, size, heads_send.at[0], sem, sibling).wait_recv()

    def wait_sent(size, sem):
        remote(size, size, sem, heads_recv.at[0], sibling).wait_send()

    def weight_copy(t, upper):
        cols = pl.ds(upper_start(t) if upper else lower_start(t), UNIT_WIDE)
        return pltpu.make_async_copy(
            weights.at[:, cols], weight_buf.at[:, cols], weight_sem.at[t, upper]
        )

    def start_weights(t, carry):
        weight_copy(t, 0).start()
        weight_copy(t, 1).start()
        return carry

    heads_load, residual_load, gain_load = [
        pltpu.make_async_copy(source, target, input_sem.at[at])
        for at, (source, target) in enumerate(
            ((heads_in, heads), (residual_in, residual), (gain_in, gain))
        )
    ]
    heads_load.start()
    lax.fori_loop(0, UNITS, start_weights, 0)
    residual_load.start()
    gain_load.start()
    greet(
        [plane_device(0, (x + step) % SIDE, y) for step in (1, 3)]
        + [plane_device(0, x, (y + step) % SIDE) for step in (1, 3)]
        + [other, sibling]
        + [{"grp": 2 * ((z + hop) % SIDE) + k} for hop in range(1, SIDE) for k in range(2)]
    )
    heads_load.wait()

    def plane_slot(origin, at):
        return 2 * ((origin + SIDE - 1 - at) % SIDE)

    def heads_arrived(slot):
        remote(
            heads_t, heads_all.at[slot], heads_send.at[SLOTS - 1], heads_recv.at[slot], sibling
        ).wait_recv()

    def sibling_heads():
        slot = SLOTS - 1
        return remote(
            heads_t, heads_all.at[slot], heads_send.at[slot], heads_recv.at[slot], sibling
        )

    relays = ((1, 0), (-1, 0), (1, 1), (-1, 1), (1, 2), (-1, 2))

    def each_relay(wanted, act):
        for at, (step, away) in enumerate(relays):
            if away not in wanted:
                continue
            first, last = (away, SIDE - 2) if step > 0 else (1, SIDE - 1 - away)

            @pl.when(jnp.logical_and(z >= first, z <= last))
            def _():
                origin, target = z - step * away, z + step
                held = plane_slot(origin, z) + core
                slot = plane_slot(origin, target) + core
                act(
                    remote(
                        heads_all.at[held] if away else heads_t,
                        heads_all.at[slot],
                        heads_send.at[SLOTS + at],
                        heads_recv.at[slot],
                        {"grp": 2 * target + core},
                    ),
                    held,
                )

    def start_relay(relay, held):
        relay.start()

    def pass_relay(relay, held):
        heads_arrived(held)
        relay.start()

    def passed_heads(j):
        slot = 2 * j + core
        held = heads_all.at[slot]
        return remote(held, held, heads_send.at[slot], heads_recv.at[slot], sibling)

    def pass_heads(neighbours):
        for j in range(SIDE - 1):
            origin = (z + 1 + j) % SIDE
            near = jnp.logical_or(origin == z + 1, origin == z - 1)

            @pl.when(near if neighbours else jnp.logical_not(near))
            def _():
                @pl.when(jnp.logical_or(z == 0, z == SIDE - 1))
                def _():
                    heads_arrived(2 * j + core)

                passed_heads(j).start()

    def send_heads():
        heads_t[...] = heads[...].T
        each_relay((0,), start_relay)
        sibling_heads().start()


    def copy(u, h, step):
        chunk = 2 * u + h
        a, b = axes(h)
        right, left = (a + 1) % SIDE, (a + 3) % SIDE
        up, down = (b + 1) % SIDE, (b + 3) % SIDE
        low, high = pl.ds(0, HALF), pl.ds(HALF, HALF)
        far_a, far_b = (a + 2) % SIDE, (b + 2) % SIDE
        source, target, device = [
            lambda: (part.at[chunk, far_a, :, :, low], from1.at[chunk, 0], plane_device(h, right, b)),
            lambda: (part.at[chunk, far_a, :, :, high], from1.at[chunk, 1], plane_device(h, left, b)),
            lambda: (part.at[chunk, right], from2.at[chunk, 0], plane_device(h, right, b)),
            lambda: (part.at[chunk, left], from2.at[chunk, 1], plane_device(h, left, b)),
            lambda: (part.at[chunk, a, far_b, :, low], from3.at[chunk, 0], plane_device(h, a, up)),
            lambda: (part.at[chunk, a, far_b, :, high], from3.at[chunk, 1], plane_device(h, a, down)),
            lambda: (part.at[chunk, a, up], from4.at[chunk, 0], plane_device(h, a, up)),
            lambda: (part.at[chunk, a, down], from4.at[chunk, 1], plane_device(h, a, down)),
            lambda: (both.at[section, chunk], both.at[section, chunk], other),
        ][step]()
        return remote(source, target, send_sem.at[u], recv_sem.at[u, step // 2], device)

    reduce_sizes = [
        part.at[0, 0:2], part.at[0], part.at[0, 0, 0:2], part.at[0, 0], part.at[0, 0, 0:2]
    ]

    def arrive(u, stage):
        wait_arrived(reduce_sizes[stage], recv_sem.at[u, stage])

    def multiply(u):
        weight_copy(u, 0).wait()
        weight_copy(u, 1).wait()
        lower, upper = [
            jnp.dot(
                heads[...], weight_buf[:, pl.ds(start, UNIT_WIDE)],
                preferred_element_type=jnp.float32,
            )
            for start in (lower_start(u), upper_start(u))
        ]
        for h in range(2):
            cols = slice(h * WIDE, (h + 1) * WIDE)
            for i in range(SIDE * SIDE):
                rows = slice(OWN * i, OWN * (i + 1))
                a, b = (i // SIDE, i % SIDE) if h == 0 else (i % SIDE, i // SIDE)
                part[2 * u + h, a, b] = narrow(stacked(lower[rows, cols], upper[rows, cols]))
            copy(u, h, 0).start()
            copy(u, h, 1).start()

    def near_first(u):
        arrive(u, 0)
        for h in range(2):
            chunk = 2 * u + h
            a, b = axes(h)
            right, left = (a + 1) % SIDE, (a + 3) % SIDE
            part[chunk, right, :, :, :HALF] = narrow(
                wide(part[chunk, right, :, :, :HALF]) + wide(from1[chunk, 0])
            )
            copy(u, h, 2).start()
            part[chunk, left, :, :, HALF:] = narrow(
                wide(part[chunk, left, :, :, HALF:]) + wide(from1[chunk, 1])
            )
            copy(u, h, 3).start()

    def far_second(u):
        arrive(u, 1)
        for h in range(2):
            chunk = 2 * u + h
            a, b = axes(h)
            part[chunk, a] = narrow(
                wide(part[chunk, a]) + (wide(from2[chunk, 0]) + wide(from2[chunk, 1]))
            )
            copy(u, h, 4).start()
            copy(u, h, 5).start()

    def near_second(u):
        arrive(u, 2)
        for h in range(2):
            chunk = 2 * u + h
            a, b = axes(h)
            up, down = (b + 1) % SIDE, (b + 3) % SIDE
            part[chunk, a, up, :, :HALF] = narrow(
                wide(part[chunk, a, up, :, :HALF]) + wide(from3[chunk, 0])
            )
            copy(u, h, 6).start()
            part[chunk, a, down, :, HALF:] = narrow(
                wide(part[chunk, a, down, :, HALF:]) + wide(from3[chunk, 1])
            )
            copy(u, h, 7).start()

    def finish(u):
        arrive(u, 3)
        for h in range(2):
            chunk = 2 * u + h
            a, b = axes(h)
            total = wide(part[chunk, a, b]) + (wide(from4[chunk, 0]) + wide(from4[chunk, 1]))
            rows = stacked(
                wide(residual[:, pl.ds(lower_start(u, h), WIDE)]),
                wide(residual[:, pl.ds(upper_start(u, h), WIDE)]),
            )
            total = total + jnp.where(section == 0, rows, 0.0)
            both[section, chunk] = narrow(total)
            copy(u, h, 8).start()

    def within(value, count):
        return jnp.logical_and(value >= 0, value < count)

    stages = (multiply, near_first, far_second, near_second, finish)

    def reduce_turn(n, carry):
        for late, stage in enumerate(stages):

            @pl.when(within(n - late, UNITS))
            def _():
                stage(n - late)

        @pl.when(n == 1)
        def _():
            send_heads()

        @pl.when(n == UNITS - 1)
        def _():
            each_relay((1,), pass_relay)

        return carry

    residual_load.wait()
    gain_load.wait()
    lax.fori_loop(0, UNITS + len(stages) - 1, reduce_turn, 0)
    pass_heads(True)
    heads_total[...] = jnp.zeros_like(heads_total)
    grads_t[...] = jnp.zeros_like(grads_t)


    def gather_of(store, sends, recvs):
        half = store.shape[-1] // 2

        def gather(p, h, step):
            chunk = 2 * p + h
            a, b = axes(h)
            right, left = (a + 1) % SIDE, (a + 3) % SIDE
            up, down = (b + 1) % SIDE, (b + 3) % SIDE
            low, high = pl.ds(0, half), pl.ds(half, half)
            block, device = [
                lambda: (store.at[chunk, b, a], plane_device(h, right, b)),
                lambda: (store.at[chunk, b, a], plane_device(h, left, b)),
                lambda: (store.at[chunk, b, left, :, low], plane_device(h, right, b)),
                lambda: (store.at[chunk, b, right, :, high], plane_device(h, left, b)),
                lambda: (store.at[chunk, b], plane_device(h, a, up)),
                lambda: (store.at[chunk, b], plane_device(h, a, down)),
                lambda: (store.at[chunk, down, :, :, low], plane_device(h, a, up)),
                lambda: (store.at[chunk, up, :, :, high], plane_device(h, a, down)),
            ][step]()
            return remote(block, block, sends.at[p], recvs.at[p, step // 2], device)

        return gather

    gather_values = gather_of(values, value_send, value_recv)
    gather_columns = gather_of(columns, column_send, column_recv)

    gather_sizes = [values.at[0, 0], values.at[0, 0, 0:2], values.at[0], values.at[0, 0:2]]

    def exchanged(target, e):
        unit = 2 * (z % 2) + e if e < 2 else FAR_UNITS - 1
        a, b = x + core * (y - x), y + core * (x - y)
        return remote(
            exchange.at[target, e],
            columns.at[2 * unit + core, b, a],
            exchange_send.at[0],
            exchange_recv.at[unit],
            {"grp": target},
        )

    def gain_rows(t, h):
        return stacked(
            jnp.broadcast_to(gain[:, pl.ds(lower_start(t, h), WIDE)], (OWN, WIDE)),
            jnp.broadcast_to(gain[:, pl.ds(upper_start(t, h), WIDE)], (OWN, WIDE)),
        )

    zero = jnp.zeros((TALL, 128), jnp.float32)

    def row_mean(total):
        return both_halves(jnp.sum(total, axis=1, keepdims=True)) / (GROUPS * SHARD)

    def add_sums(t, total):
        arrive(t, 4)
        for h in range(2):
            total = total + lanes(wide(both[0, 2 * t + h]))
        return total

    mean = row_mean(lax.fori_loop(0, UNITS, add_sums, zero))

    def add_squares(t, total):
        for h in range(2):
            centred = wide(both[0, 2 * t + h]) - mean
            total = total + lanes(centred * centred)
        return total

    inv_scale = lax.rsqrt(row_mean(lax.fori_loop(0, UNITS, add_squares, zero)) + EPSILON)

    def add_means(t, totals):
        for h in range(2):
            unit = (wide(both[0, 2 * t + h]) - mean) * inv_scale
            scaled = gain_rows(t, h) * wide(both[1, 2 * t + h])
            totals = (totals[0] + lanes(scaled), totals[1] + lanes(scaled * unit))
        return totals

    sums = lax.fori_loop(0, UNITS, add_means, (zero, zero))
    mean_scaled, mean_product = row_mean(sums[0]), row_mean(sums[1])
    first_unit = SIDE * ((z // 2 + z % 2 + 1) % 2)

    def write(turn, carry):
        shard = (turn + first_unit // 2) % SIDE
        kept = []
        for v in range(2):
            t = 2 * shard + v
            for h in range(2):
                chunk = 2 * t + h
                a, b = axes(h)
                rows = gain_rows(t, h)
                unit = (wide(both[0, chunk]) - mean) * inv_scale
                d_normed = wide(both[1, chunk])
                grad = inv_scale * (rows * d_normed - mean_scaled - unit * mean_product)
                value = jnp.where(section == 0, grad, unit * rows)
                values[chunk, b, a] = narrow(value)
                gather_values(t, h, 0).start()
                gather_values(t, h, 1).start()
                kept.append(value)
                product = d_normed * unit
                for start, rows in (
                    (lower_start(t, h), slice(0, OWN)),
                    (upper_start(t, h), slice(OWN, TALL)),
                ):
                    own_grad[:, pl.ds(start, WIDE)] = narrow(grad[rows])
                    gain_own[0, :, pl.ds(start, WIDE)] = jnp.sum(product[rows], axis=0, keepdims=True)
        for target, rows in ((shard, slice(0, OWN)), (GROUPS - 1 - shard, slice(OWN, TALL))):
            for e, (first, second) in enumerate(((0, 2), (1, 3), (2, 3))):
                exchange[target, e] = narrow(stacked(kept[first][rows], kept[second][rows]))
                wanted = target // SIDE != z // 2 if e < 2 else target // 2 == next_plane

                @pl.when(wanted)
                def _():
                    exchanged(target, e).start()
        return carry

    lax.fori_loop(0, SIDE, write, 0)


    def near_copy(t, upper, target, slot):
        return remote(
            tokens.at[t, upper],
            from_near.at[slot],
            near_send.at[0],
            near_recv.at[slot],
            {"grp": target},
        )

    def split_blocks(store, chunk, h, put):
        for i in range(0, SIDE * SIDE, 2):
            pair = []
            for at in (i, i + 1):
                a, b = (at // SIDE, at % SIDE) if h == 0 else (at % SIDE, at // SIDE)
                pair.append(wide(store[chunk, b, a]))
            put(0, slice(OWN * i, OWN * (i + 2)), narrow(stacked(pair[0][:OWN], pair[1][:OWN])))
            put(1, slice(OWN * i, OWN * (i + 2)), narrow(stacked(pair[0][OWN:], pair[1][OWN:])))

    def add_grads(start, transposed_heads, token_rows):
        cols = pl.ds(start, token_rows.shape[1])
        grads_t[:, cols] += jnp.dot(
            transposed_heads, token_rows, preferred_element_type=jnp.float32
        )

    def store_grads(block):
        return pltpu.make_async_copy(
            grads.at[block * WIDE : (block + 1) * WIDE],
            grads_out.at[block * WIDE : (block + 1) * WIDE],
            output_sem.at[3 + block],
        )

    def finish_grads(blocks):
        for block in blocks:
            cols = slice(block * WIDE, (block + 1) * WIDE)
            grads[cols] = grad_scale * grads_t[:, cols].T
            store_grads(block).start()

    def use_values(t):
        for h in range(2):

            def put(upper, rows, block):
                tokens[t, upper, rows, h * WIDE : (h + 1) * WIDE] = block

            split_blocks(values, 2 * t + h, h, put)
        for upper, target in enumerate((t // 2, GROUPS - 1 - t // 2)):
            to_next = jnp.logical_and(target // 2 == next_plane, t % 2 == 0)
            for slot, wanted in ((t % 2, target == sibling_group), (2 + core, to_next)):

                @pl.when(wanted)
                def _():
                    near_copy(t, upper, target, slot).start()

        total = heads_total[...]
        for upper, start in enumerate((lower_start(t), upper_start(t))):
            total = total + lax.dot_general(
                tokens[t, upper], weight_buf[:, pl.ds(start, UNIT_WIDE)],
                (((1,), (1,)), ((), ())), preferred_element_type=jnp.float32,
            )
        heads_total[...] = total
        for upper, target in enumerate((t // 2, GROUPS - 1 - t // 2)):

            @pl.when(target == group)
            def _():
                add_grads(pl.multiple_of((t % 2) * UNIT_WIDE, UNIT_WIDE), heads_t[...], tokens[t, upper])

    def use_columns(p):
        last = p // (FAR_UNITS - 1)
        plane = (1 - last) * (2 * (1 - z // 2) + p // 2) + last * next_plane
        for h in range(2):

            def put(side, rows, block):
                column_tokens[h, rows, side * WIDE : (side + 1) * WIDE] = block

            split_blocks(columns, 2 * p + h, h, put)
        slot = plane_slot(plane, z)

        @pl.when(jnp.logical_and(p % 2 == 0, last == 0))
        def _():
            heads_arrived(slot + 1 - core)

        total = jnp.dot(
            heads_all[slot], column_tokens[0], preferred_element_type=jnp.float32
        ) + jnp.dot(heads_all[slot + 1], column_tokens[1], preferred_element_type=jnp.float32)
        for side in range(2):
            start = (1 - last) * (side * UNIT_WIDE + (p % 2) * WIDE) + last * (UNIT_WIDE + side * WIDE)
            cols = pl.ds(pl.multiple_of(start, WIDE), WIDE)
            grads_t[:, cols] += total[:, side * WIDE : (side + 1) * WIDE]

    def use_near(slot, heads_slot, start):
        wait_arrived(from_near.at[slot], near_recv.at[slot])
        add_grads(start, heads_all[heads_slot], from_near[slot])

    gain_partners = [
        {"tp": x * SIDE + y + 1 - 2 * (y % 2)},
        {"tp": x * SIDE + SIDE - 1 - y},
        {"tp": (x + 1 - 2 * (x % 2)) * SIDE + y},
        {"tp": (SIDE - 1 - x) * SIDE + y},
        sibling,
        {"grp": 2 * next_plane + core},
        {"grp": 2 * (SIDE - 1 - z) + core},
    ]

    def gain_copy(step):
        return remote(
            gain_own.at[step], gain_got.at[step], gain_send.at[step], gain_recv.at[step], gain_partners[step]
        )

    own_grad_store, heads_store, gain_store = [
        pltpu.make_async_copy(source, target, output_sem.at[at])
        for at, (source, target) in enumerate(
            ((own_grad, grad_out), (heads_done, heads_out), (gain_done, gain_out))
        )
    ]

    near_heads = plane_slot(next_plane, z)

    def value_unit(q):
        return (q + first_unit) % UNITS

    def gather_stage(q, stage):
        def pass_on(gather, recvs, p):
            wait_arrived(gather_sizes[stage], recvs.at[p, stage])
            if stage < 3:
                for h in range(2):
                    gather(p, h, 2 * stage + 2).start()
                    gather(p, h, 2 * stage + 3).start()

        @pl.when(within(q, UNITS))
        def _():
            pass_on(gather_values, value_recv, value_unit(q))

        @pl.when(within(q - UNITS, FAR_UNITS))
        def _():
            pass_on(gather_columns, column_recv, q - UNITS)

    def gather_turn(n, carry):
        @pl.when(n == 5)
        def _():
            pass_heads(False)

        for step in range(GAIN_STEPS + 1):

            @pl.when(n == step + 1)
            def _():
                if step > 0:
                    gain_copy(step - 1).wait_recv()
                    gain_own[step] = gain_own[step - 1] + gain_got[step - 1]
                if step < GAIN_STEPS:
                    gain_copy(step).start()
                else:
                    gain_done[...] = gain_own[GAIN_STEPS] * grad_scale
                    gain_store.start()

        @pl.when(within(n + 1 - UNITS, FAR_UNITS))
        def _():
            p = n + 1 - UNITS
            wait_arrived(gather_sizes[1], exchange_recv.at[p])
            for h in range(2):
                gather_columns(p, h, 0).start()
                gather_columns(p, h, 1).start()

        @pl.when(n == UNITS + FAR_UNITS + 4)
        def _():
            finish_grads((0, 1))

        gather_stage(n, 0)
        gather_stage(n - 4, 2)
        gather_stage(n - 2, 1)
        gather_stage(n - 5, 3)
        done = n - 5

        @pl.when(within(done, UNITS))
        def _():
            use_values(value_unit(done))

        @pl.when(done == UNITS)
        def _():
            heads_done[...] = narrow(heads_total[...])
            heads_store.start()
            heads_arrived(SLOTS - 1)
            use_near(0, SLOTS - 1, 0)
            use_near(1, SLOTS - 1, UNIT_WIDE)
            heads_arrived(near_heads + 1 - core)

        @pl.when(done == UNITS + 2)
        def _():
            for k in range(2):
                use_near(2 + k, near_heads + k, 0)

        @pl.when(within(done - UNITS, FAR_UNITS))
        def _():
            use_columns(done - UNITS)

        return carry

    own_grad_store.start()
    each_relay((2,), pass_relay)
    lax.fori_loop(0, UNITS + FAR_UNITS + 5, gather_turn, 0)
    finish_grads((2, 3))

    def reduce_sent(u, carry):
        wait_sent(part.at[0:2], send_sem.at[u])
        wait_sent(values.at[0:5, 0:3, 0:2], value_send.at[u])
        return carry

    def columns_sent(p, carry):
        wait_sent(values.at[0:5, 0:3, 0:2], column_send.at[p])
        return carry

    lax.fori_loop(0, UNITS, reduce_sent, 0)
    lax.fori_loop(0, FAR_UNITS, columns_sent, 0)
    wait_sent(exchange.at[0:5, 0:2], exchange_send.at[0])
    wait_sent(tokens.at[0:2], near_send.at[0])
    each_relay((0, 1, 2), lambda relay, held: relay.wait_send())
    for j in range(SIDE - 1):
        passed_heads(j).wait_send()
    sibling_heads().wait_send()
    for step in range(GAIN_STEPS):
        gain_copy(step).wait_send()
    for store in [own_grad_store, heads_store, gain_store] + [store_grads(i) for i in range(4)]:
        store.wait()


def deliver_kernel(*refs):
    results, outputs, held = refs[:4], refs[4:8], refs[8:12]
    load_sem, store_sem = refs[12:]
    pieces = [(1, pl.ds(block * WIDE, WIDE)) for block in range(SIDE)]
    pieces += [(at, pl.ds(0, results[at].shape[0])) for at in (0, 2, 3)]

    def copies(sources, targets, sems):
        return [
            pltpu.make_async_copy(sources[at].at[rows], targets[at].at[rows], sems.at[i])
            for i, (at, rows) in enumerate(pieces)
        ]

    loads, stores = copies(results, held, load_sem), copies(held, outputs, store_sem)
    for load in loads:
        load.start()
    for load, store in zip(loads, stores):
        load.wait()
        store.start()
    for store in stores:
        store.wait()


def delivered(results):
    hbm = pl.BlockSpec(memory_space=pl.ANY)
    return pl.pallas_call(
        deliver_kernel,
        out_shape=tuple(jax.ShapeDtypeStruct(result.shape, result.dtype) for result in results),
        in_specs=[hbm] * 4,
        out_specs=(hbm,) * 4,
        scratch_shapes=[pltpu.VMEM(result.shape, result.dtype) for result in results]
        + [pltpu.SemaphoreType.DMA((SIDE + 3,))] * 2,
        name="deliver",
    )(*results)


def fused(heads, weights, residual, gain):
    hbm = pl.BlockSpec(memory_space=pl.ANY)
    bf16, f32 = jnp.bfloat16, jnp.float32
    rows_dev, depth = heads.shape
    owned = weights.shape[1] // GROUPS
    dma = pltpu.SemaphoreType.DMA
    return pl.pallas_call(
        boundary_kernel,
        out_shape=(
            jax.ShapeDtypeStruct(heads.shape, bf16),
            jax.ShapeDtypeStruct((owned, depth), f32),
            jax.ShapeDtypeStruct(residual.shape, bf16),
            jax.ShapeDtypeStruct(gain.shape, f32),
        ),
        in_specs=[hbm] * 4,
        out_specs=(hbm,) * 4,
        scratch_shapes=[
            pltpu.VMEM(heads.shape, bf16),
            pltpu.VMEM(residual.shape, bf16),
            pltpu.VMEM(gain.shape, f32),
            pltpu.VMEM(heads.shape, bf16),
            pltpu.VMEM((owned, depth), f32),
            pltpu.VMEM(residual.shape, bf16),
            pltpu.VMEM(gain.shape, f32),
            pltpu.VMEM((depth, rows_dev), bf16),
            pltpu.VMEM((depth, owned), f32),
            pltpu.VMEM(weights.shape, bf16),
            pltpu.VMEM((CHUNKS, SIDE, SIDE, TALL, WIDE), bf16),
            pltpu.VMEM((CHUNKS, 2, SIDE, TALL, HALF), bf16),
            pltpu.VMEM((CHUNKS, 2, SIDE, TALL, WIDE), bf16),
            pltpu.VMEM((CHUNKS, 2, TALL, HALF), bf16),
            pltpu.VMEM((CHUNKS, 2, TALL, WIDE), bf16),
            pltpu.VMEM((2, CHUNKS, TALL, WIDE), bf16),
            pltpu.VMEM((CHUNKS, SIDE, SIDE, TALL, WIDE), bf16),
            pltpu.VMEM((FAR_CHUNKS, SIDE, SIDE, TALL, WIDE), bf16),
            pltpu.VMEM((GROUPS, 3, TALL, WIDE), bf16),
            pltpu.VMEM((UNITS, 2, rows_dev, UNIT_WIDE), bf16),
            pltpu.VMEM((2, rows_dev, UNIT_WIDE), bf16),
            pltpu.VMEM((4, rows_dev, UNIT_WIDE), bf16),
            pltpu.VMEM((SLOTS, depth, rows_dev), bf16),
            pltpu.VMEM((rows_dev, depth), f32),
            pltpu.VMEM((GAIN_STEPS + 1,) + gain.shape, f32),
            pltpu.VMEM((GAIN_STEPS,) + gain.shape, f32),
            dma((3,)),
            dma((7,)),
            dma((UNITS, 2)),
            dma((UNITS,)),
            dma((UNITS, 5)),
            dma((UNITS,)),
            dma((UNITS, 4)),
            dma((FAR_UNITS,)),
            dma((FAR_UNITS, 4)),
            dma((1,)),
            dma((FAR_UNITS,)),
            dma((SLOTS + 6,)),
            dma((SLOTS,)),
            dma((1,)),
            dma((4,)),
            dma((GAIN_STEPS,)),
            dma((GAIN_STEPS,)),
        ],
        compiler_params=pltpu.CompilerParams(
            collective_id=0, has_side_effects=True, vmem_limit_bytes=62 * 1024 * 1024
        ),
        name="boundary",
    )(heads, weights, residual, gain)


def per_device(heads_in, weights, residual, norm_gain):
    heads_out, weight_grad, boundary_grad, gain_grad = delivered(
        fused(heads_in[0], weights[0], residual, norm_gain[None])
    )
    return (heads_out[None], weight_grad[None], boundary_grad, gain_grad[0])


def solution(mesh):
    placed = (P("section", "grp", "tp"), P("section", "tp", None), P(("grp", "tp"), None), P())
    return jax.shard_map(
        per_device,
        mesh=mesh,
        in_specs=placed,
        out_specs=(
            P("section", "grp", "tp"),
            P("section", "grp", "tp"),
            P(("grp", "tp"), None),
            P(),
        ),
        check_vma=False,
    )
```

```python
import math

import jax
import jax.numpy as jnp
from jax import lax
from jax.experimental import pallas as pl
from jax.experimental.pallas import tpu as pltpu
from jax.sharding import PartitionSpec as P

EPSILON = 1e-05
MESH = pl.DeviceIdType.MESH

SIDE = 4
GROUPS = 8
UNITS = 8
FAR_UNITS = 5
CHUNKS = 2 * UNITS
FAR_CHUNKS = 2 * FAR_UNITS
WIDE = 256
HALF = WIDE // 2
UNIT_WIDE = 2 * WIDE
SHARD = 2 * UNIT_WIDE
OWN = 24
TALL = 2 * OWN
SLOTS = GROUPS - 1
GAIN_STEPS = 7


def lower_start(t, h=0):
    return pl.multiple_of(t * UNIT_WIDE + h * WIDE, WIDE)


def upper_start(t, h=0):
    return pl.multiple_of((GROUPS - 1 - t // 2) * SHARD + (t % 2) * UNIT_WIDE + h * WIDE, WIDE)


def plane_device(h, first, second):
    x, y = (first, second) if h == 0 else (second, first)
    return {"tp": x * SIDE + y}


def stacked(*parts):
    return jnp.concatenate(parts, axis=0)


def both_halves(row_pair):
    total = row_pair[:OWN] + row_pair[OWN:]
    return stacked(total, total)


def lanes(value):
    return sum(value[:, 128 * i : 128 * (i + 1)] for i in range(value.shape[1] // 128))


def wide(value):
    return value.astype(jnp.float32)


def narrow(value):
    return value.astype(jnp.bfloat16)


def remote(source, target, send_sem, recv_sem, device):
    return pltpu.make_async_remote_copy(
        src_ref=source,
        dst_ref=target,
        send_sem=send_sem,
        recv_sem=recv_sem,
        device_id=device,
        device_id_type=MESH,
    )


def greet(peers):
    barrier = pltpu.get_barrier_semaphore()
    for peer in peers:
        pl.semaphore_signal(barrier, inc=1, device_id=peer, device_id_type=MESH)
    pl.semaphore_wait(barrier, len(peers))


def boundary_kernel(
    heads_in, weights, residual_in, gain_in, heads_out, grads_out, grad_out, gain_out,
    heads, residual, gain, heads_done, grads, own_grad, gain_done,
    heads_t, grads_t, weight_buf, part, from1, from2, from3, from4, both,
    values, columns, exchange, tokens, column_tokens, from_near, heads_all, heads_total, gain_own, gain_got,
    input_sem, output_sem, weight_sem, send_sem, recv_sem, value_send, value_recv, column_send, column_recv,
    exchange_send, exchange_recv, heads_send, heads_recv, near_send, near_recv, gain_send, gain_recv,
):
    tp = lax.axis_index("tp")
    x, y = tp // SIDE, tp % SIDE
    section = lax.axis_index("section")
    group = lax.axis_index("grp")
    z, core = group // 2, group % 2
    other = {"section": 1 - section}
    sibling_group = 2 * z + 1 - core
    sibling = {"grp": sibling_group}
    next_plane = z + 1 - 2 * (z % 2)
    rows_dev, depth = heads.shape
    grad_scale = 1.0 / math.sqrt(rows_dev * GROUPS)

    def axes(h):
        return (x, y) if h == 0 else (y, x)

    def wait_arrived(size, sem):
        remote(size, size, heads_send.at[0], sem, sibling).wait_recv()

    def wait_sent(size, sem):
        remote(size, size, sem, heads_recv.at[0], sibling).wait_send()

    def weight_copy(t, upper):
        cols = pl.ds(upper_start(t) if upper else lower_start(t), UNIT_WIDE)
        return pltpu.make_async_copy(
            weights.at[:, cols], weight_buf.at[:, cols], weight_sem.at[t, upper]
        )

    def start_weights(t, carry):
        weight_copy(t, 0).start()
        weight_copy(t, 1).start()
        return carry

    heads_load, residual_load, gain_load = [
        pltpu.make_async_copy(source, target, input_sem.at[at])
        for at, (source, target) in enumerate(
            ((heads_in, heads), (residual_in, residual), (gain_in, gain))
        )
    ]
    heads_load.start()
    lax.fori_loop(0, UNITS, start_weights, 0)
    residual_load.start()
    gain_load.start()
    greet(
        [plane_device(0, (x + step) % SIDE, y) for step in (1, 3)]
        + [plane_device(0, x, (y + step) % SIDE) for step in (1, 3)]
        + [other, sibling]
        + [{"grp": 2 * ((z + hop) % SIDE) + k} for hop in range(1, SIDE) for k in range(2)]
    )
    heads_load.wait()

    def plane_slot(origin, at):
        return 2 * ((origin + SIDE - 1 - at) % SIDE)

    def heads_arrived(slot):
        remote(
            heads_t, heads_all.at[slot], heads_send.at[SLOTS - 1], heads_recv.at[slot], sibling
        ).wait_recv()

    def sibling_heads():
        slot = SLOTS - 1
        return remote(
            heads_t, heads_all.at[slot], heads_send.at[slot], heads_recv.at[slot], sibling
        )

    relays = ((1, 0), (-1, 0), (1, 1), (-1, 1), (1, 2), (-1, 2))

    def each_relay(wanted, act):
        for at, (step, away) in enumerate(relays):
            if away not in wanted:
                continue
            first, last = (away, SIDE - 2) if step > 0 else (1, SIDE - 1 - away)

            @pl.when(jnp.logical_and(z >= first, z <= last))
            def _():
                origin, target = z - step * away, z + step
                held = plane_slot(origin, z) + core
                slot = plane_slot(origin, target) + core
                act(
                    remote(
                        heads_all.at[held] if away else heads_t,
                        heads_all.at[slot],
                        heads_send.at[SLOTS + at],
                        heads_recv.at[slot],
                        {"grp": 2 * target + core},
                    ),
                    held,
                )

    def start_relay(relay, held):
        relay.start()

    def pass_relay(relay, held):
        heads_arrived(held)
        relay.start()

    def passed_heads(j):
        slot = 2 * j + core
        held = heads_all.at[slot]
        return remote(held, held, heads_send.at[slot], heads_recv.at[slot], sibling)

    def pass_heads(neighbours):
        for j in range(SIDE - 1):
            origin = (z + 1 + j) % SIDE
            near = jnp.logical_or(origin == z + 1, origin == z - 1)

            @pl.when(near if neighbours else jnp.logical_not(near))
            def _():
                @pl.when(jnp.logical_or(z == 0, z == SIDE - 1))
                def _():
                    heads_arrived(2 * j + core)

                passed_heads(j).start()

    def send_heads():
        heads_t[...] = heads[...].T
        each_relay((0,), start_relay)
        sibling_heads().start()


    def copy(u, h, step):
        chunk = 2 * u + h
        a, b = axes(h)
        right, left = (a + 1) % SIDE, (a + 3) % SIDE
        up, down = (b + 1) % SIDE, (b + 3) % SIDE
        low, high = pl.ds(0, HALF), pl.ds(HALF, HALF)
        far_a, far_b = (a + 2) % SIDE, (b + 2) % SIDE
        source, target, device = [
            lambda: (part.at[chunk, far_a, :, :, low], from1.at[chunk, 0], plane_device(h, right, b)),
            lambda: (part.at[chunk, far_a, :, :, high], from1.at[chunk, 1], plane_device(h, left, b)),
            lambda: (part.at[chunk, right], from2.at[chunk, 0], plane_device(h, right, b)),
            lambda: (part.at[chunk, left], from2.at[chunk, 1], plane_device(h, left, b)),
            lambda: (part.at[chunk, a, far_b, :, low], from3.at[chunk, 0], plane_device(h, a, up)),
            lambda: (part.at[chunk, a, far_b, :, high], from3.at[chunk, 1], plane_device(h, a, down)),
            lambda: (part.at[chunk, a, up], from4.at[chunk, 0], plane_device(h, a, up)),
            lambda: (part.at[chunk, a, down], from4.at[chunk, 1], plane_device(h, a, down)),
            lambda: (both.at[section, chunk], both.at[section, chunk], other),
        ][step]()
        return remote(source, target, send_sem.at[u], recv_sem.at[u, step // 2], device)

    reduce_sizes = [
        part.at[0, 0:2], part.at[0], part.at[0, 0, 0:2], part.at[0, 0], part.at[0, 0, 0:2]
    ]

    def arrive(u, stage):
        wait_arrived(reduce_sizes[stage], recv_sem.at[u, stage])

    def multiply(u):
        weight_copy(u, 0).wait()
        weight_copy(u, 1).wait()
        lower, upper = [
            jnp.dot(
                heads[...], weight_buf[:, pl.ds(start, UNIT_WIDE)],
                preferred_element_type=jnp.float32,
            )
            for start in (lower_start(u), upper_start(u))
        ]
        for h in range(2):
            cols = slice(h * WIDE, (h + 1) * WIDE)
            for i in range(SIDE * SIDE):
                rows = slice(OWN * i, OWN * (i + 1))
                a, b = (i // SIDE, i % SIDE) if h == 0 else (i % SIDE, i // SIDE)
                part[2 * u + h, a, b] = narrow(stacked(lower[rows, cols], upper[rows, cols]))
            copy(u, h, 0).start()
            copy(u, h, 1).start()

    def near_first(u):
        arrive(u, 0)
        for h in range(2):
            chunk = 2 * u + h
            a, b = axes(h)
            right, left = (a + 1) % SIDE, (a + 3) % SIDE
            part[chunk, right, :, :, :HALF] = narrow(
                wide(part[chunk, right, :, :, :HALF]) + wide(from1[chunk, 0])
            )
            copy(u, h, 2).start()
            part[chunk, left, :, :, HALF:] = narrow(
                wide(part[chunk, left, :, :, HALF:]) + wide(from1[chunk, 1])
            )
            copy(u, h, 3).start()

    def far_second(u):
        arrive(u, 1)
        for h in range(2):
            chunk = 2 * u + h
            a, b = axes(h)
            part[chunk, a] = narrow(
                wide(part[chunk, a]) + (wide(from2[chunk, 0]) + wide(from2[chunk, 1]))
            )
            copy(u, h, 4).start()
            copy(u, h, 5).start()

    def near_second(u):
        arrive(u, 2)
        for h in range(2):
            chunk = 2 * u + h
            a, b = axes(h)
            up, down = (b + 1) % SIDE, (b + 3) % SIDE
            part[chunk, a, up, :, :HALF] = narrow(
                wide(part[chunk, a, up, :, :HALF]) + wide(from3[chunk, 0])
            )
            copy(u, h, 6).start()
            part[chunk, a, down, :, HALF:] = narrow(
                wide(part[chunk, a, down, :, HALF:]) + wide(from3[chunk, 1])
            )
            copy(u, h, 7).start()

    def finish(u):
        arrive(u, 3)
        for h in range(2):
            chunk = 2 * u + h
            a, b = axes(h)
            total = wide(part[chunk, a, b]) + (wide(from4[chunk, 0]) + wide(from4[chunk, 1]))
            rows = stacked(
                wide(residual[:, pl.ds(lower_start(u, h), WIDE)]),
                wide(residual[:, pl.ds(upper_start(u, h), WIDE)]),
            )
            total = total + jnp.where(section == 0, rows, 0.0)
            both[section, chunk] = narrow(total)
            copy(u, h, 8).start()

    def within(value, count):
        return jnp.logical_and(value >= 0, value < count)

    stages = (multiply, near_first, far_second, near_second, finish)
    APART = 2

    def reduce_turn(n, carry):
        for at, stage in enumerate(stages):

            @pl.when(within(n - APART * at, UNITS))
            def _():
                stage(n - APART * at)

        @pl.when(n == 1)
        def _():
            send_heads()

        @pl.when(n == UNITS + 2)
        def _():
            each_relay((1,), pass_relay)

        return carry

    residual_load.wait()
    gain_load.wait()
    lax.fori_loop(0, UNITS + APART * (len(stages) - 1), reduce_turn, 0)
    pass_heads(True)
    heads_total[...] = jnp.zeros_like(heads_total)
    grads_t[...] = jnp.zeros_like(grads_t)


    def gather_of(store, sends, recvs):
        half = store.shape[-1] // 2

        def gather(p, h, step):
            chunk = 2 * p + h
            a, b = axes(h)
            right, left = (a + 1) % SIDE, (a + 3) % SIDE
            up, down = (b + 1) % SIDE, (b + 3) % SIDE
            low, high = pl.ds(0, half), pl.ds(half, half)
            block, device = [
                lambda: (store.at[chunk, b, a], plane_device(h, right, b)),
                lambda: (store.at[chunk, b, a], plane_device(h, left, b)),
                lambda: (store.at[chunk, b, left, :, low], plane_device(h, right, b)),
                lambda: (store.at[chunk, b, right, :, high], plane_device(h, left, b)),
                lambda: (store.at[chunk, b], plane_device(h, a, up)),
                lambda: (store.at[chunk, b], plane_device(h, a, down)),
                lambda: (store.at[chunk, down, :, :, low], plane_device(h, a, up)),
                lambda: (store.at[chunk, up, :, :, high], plane_device(h, a, down)),
            ][step]()
            return remote(block, block, sends.at[p], recvs.at[p, step // 2], device)

        return gather

    gather_values = gather_of(values, value_send, value_recv)
    gather_columns = gather_of(columns, column_send, column_recv)

    gather_sizes = [values.at[0, 0], values.at[0, 0, 0:2], values.at[0], values.at[0, 0:2]]

    def exchanged(target, e):
        unit = 2 * (z % 2) + e if e < 2 else FAR_UNITS - 1
        a, b = x + core * (y - x), y + core * (x - y)
        return remote(
            exchange.at[target, e],
            columns.at[2 * unit + core, b, a],
            exchange_send.at[0],
            exchange_recv.at[unit],
            {"grp": target},
        )

    def gain_rows(t, h):
        return stacked(
            jnp.broadcast_to(gain[:, pl.ds(lower_start(t, h), WIDE)], (OWN, WIDE)),
            jnp.broadcast_to(gain[:, pl.ds(upper_start(t, h), WIDE)], (OWN, WIDE)),
        )

    zero = jnp.zeros((TALL, 128), jnp.float32)

    def row_mean(total):
        return both_halves(jnp.sum(total, axis=1, keepdims=True)) / (GROUPS * SHARD)

    def add_sums(t, total):
        arrive(t, 4)
        for h in range(2):
            total = total + lanes(wide(both[0, 2 * t + h]))
        return total

    mean = row_mean(lax.fori_loop(0, UNITS, add_sums, zero))

    def add_squares(t, total):
        for h in range(2):
            centred = wide(both[0, 2 * t + h]) - mean
            total = total + lanes(centred * centred)
        return total

    inv_scale = lax.rsqrt(row_mean(lax.fori_loop(0, UNITS, add_squares, zero)) + EPSILON)

    def add_means(t, totals):
        for h in range(2):
            unit = (wide(both[0, 2 * t + h]) - mean) * inv_scale
            scaled = gain_rows(t, h) * wide(both[1, 2 * t + h])
            totals = (totals[0] + lanes(scaled), totals[1] + lanes(scaled * unit))
        return totals

    sums = lax.fori_loop(0, UNITS, add_means, (zero, zero))
    mean_scaled, mean_product = row_mean(sums[0]), row_mean(sums[1])
    first_unit = SIDE * ((z // 2 + z % 2 + 1) % 2)

    def write(turn, carry):
        shard = (turn + first_unit // 2) % SIDE
        kept = []
        for v in range(2):
            t = 2 * shard + v
            for h in range(2):
                chunk = 2 * t + h
                a, b = axes(h)
                rows = gain_rows(t, h)
                unit = (wide(both[0, chunk]) - mean) * inv_scale
                d_normed = wide(both[1, chunk])
                grad = inv_scale * (rows * d_normed - mean_scaled - unit * mean_product)
                value = jnp.where(section == 0, grad, unit * rows)
                values[chunk, b, a] = narrow(value)
                gather_values(t, h, 0).start()
                gather_values(t, h, 1).start()
                kept.append(value)
                product = d_normed * unit
                for start, rows in (
                    (lower_start(t, h), slice(0, OWN)),
                    (upper_start(t, h), slice(OWN, TALL)),
                ):
                    own_grad[:, pl.ds(start, WIDE)] = narrow(grad[rows])
                    gain_own[0, :, pl.ds(start, WIDE)] = jnp.sum(product[rows], axis=0, keepdims=True)
        for target, rows in ((shard, slice(0, OWN)), (GROUPS - 1 - shard, slice(OWN, TALL))):
            for e, (first, second) in enumerate(((0, 2), (1, 3), (2, 3))):
                exchange[target, e] = narrow(stacked(kept[first][rows], kept[second][rows]))
                wanted = target // SIDE != z // 2 if e < 2 else target // 2 == next_plane

                @pl.when(wanted)
                def _():
                    exchanged(target, e).start()
        return carry

    lax.fori_loop(0, SIDE, write, 0)


    def near_copy(t, upper, target, slot):
        return remote(
            tokens.at[t, upper],
            from_near.at[slot],
            near_send.at[0],
            near_recv.at[slot],
            {"grp": target},
        )

    def split_blocks(store, chunk, h, put):
        for i in range(0, SIDE * SIDE, 2):
            pair = []
            for at in (i, i + 1):
                a, b = (at // SIDE, at % SIDE) if h == 0 else (at % SIDE, at // SIDE)
                pair.append(wide(store[chunk, b, a]))
            put(0, slice(OWN * i, OWN * (i + 2)), narrow(stacked(pair[0][:OWN], pair[1][:OWN])))
            put(1, slice(OWN * i, OWN * (i + 2)), narrow(stacked(pair[0][OWN:], pair[1][OWN:])))

    def add_grads(start, transposed_heads, token_rows):
        cols = pl.ds(start, token_rows.shape[1])
        grads_t[:, cols] += jnp.dot(
            transposed_heads, token_rows, preferred_element_type=jnp.float32
        )

    def store_grads(block):
        return pltpu.make_async_copy(
            grads.at[block * WIDE : (block + 1) * WIDE],
            grads_out.at[block * WIDE : (block + 1) * WIDE],
            output_sem.at[3 + block],
        )

    def finish_grads(blocks):
        for block in blocks:
            cols = slice(block * WIDE, (block + 1) * WIDE)
            grads[cols] = grad_scale * grads_t[:, cols].T
            store_grads(block).start()

    def use_values(t):
        for h in range(2):

            def put(upper, rows, block):
                tokens[t, upper, rows, h * WIDE : (h + 1) * WIDE] = block

            split_blocks(values, 2 * t + h, h, put)
        for upper, target in enumerate((t // 2, GROUPS - 1 - t // 2)):
            to_next = jnp.logical_and(target // 2 == next_plane, t % 2 == 0)
            for slot, wanted in ((t % 2, target == sibling_group), (2 + core, to_next)):

                @pl.when(wanted)
                def _():
                    near_copy(t, upper, target, slot).start()

        total = heads_total[...]
        for upper, start in enumerate((lower_start(t), upper_start(t))):
            total = total + lax.dot_general(
                tokens[t, upper], weight_buf[:, pl.ds(start, UNIT_WIDE)],
                (((1,), (1,)), ((), ())), preferred_element_type=jnp.float32,
            )
        heads_total[...] = total
        for upper, target in enumerate((t // 2, GROUPS - 1 - t // 2)):

            @pl.when(target == group)
            def _():
                add_grads(pl.multiple_of((t % 2) * UNIT_WIDE, UNIT_WIDE), heads_t[...], tokens[t, upper])

    def use_columns(p):
        last = p // (FAR_UNITS - 1)
        plane = (1 - last) * (2 * (1 - z // 2) + p // 2) + last * next_plane
        for h in range(2):

            def put(side, rows, block):
                column_tokens[h, rows, side * WIDE : (side + 1) * WIDE] = block

            split_blocks(columns, 2 * p + h, h, put)
        slot = plane_slot(plane, z)

        @pl.when(jnp.logical_and(p % 2 == 0, last == 0))
        def _():
            heads_arrived(slot + 1 - core)

        total = jnp.dot(
            heads_all[slot], column_tokens[0], preferred_element_type=jnp.float32
        ) + jnp.dot(heads_all[slot + 1], column_tokens[1], preferred_element_type=jnp.float32)
        for side in range(2):
            start = (1 - last) * (side * UNIT_WIDE + (p % 2) * WIDE) + last * (UNIT_WIDE + side * WIDE)
            cols = pl.ds(pl.multiple_of(start, WIDE), WIDE)
            grads_t[:, cols] += total[:, side * WIDE : (side + 1) * WIDE]

    def use_near(slot, heads_slot, start):
        wait_arrived(from_near.at[slot], near_recv.at[slot])
        add_grads(start, heads_all[heads_slot], from_near[slot])

    gain_partners = [
        {"tp": x * SIDE + y + 1 - 2 * (y % 2)},
        {"tp": x * SIDE + SIDE - 1 - y},
        {"tp": (x + 1 - 2 * (x % 2)) * SIDE + y},
        {"tp": (SIDE - 1 - x) * SIDE + y},
        sibling,
        {"grp": 2 * next_plane + core},
        {"grp": 2 * (SIDE - 1 - z) + core},
    ]

    def gain_copy(step):
        return remote(
            gain_own.at[step], gain_got.at[step], gain_send.at[step], gain_recv.at[step], gain_partners[step]
        )

    own_grad_store, heads_store, gain_store = [
        pltpu.make_async_copy(source, target, output_sem.at[at])
        for at, (source, target) in enumerate(
            ((own_grad, grad_out), (heads_done, heads_out), (gain_done, gain_out))
        )
    ]

    near_heads = plane_slot(next_plane, z)

    def value_unit(q):
        return (q + first_unit) % UNITS

    def gather_stage(q, stage):
        def pass_on(gather, recvs, p):
            wait_arrived(gather_sizes[stage], recvs.at[p, stage])
            if stage < 3:
                for h in range(2):
                    gather(p, h, 2 * stage + 2).start()
                    gather(p, h, 2 * stage + 3).start()

        @pl.when(within(q, UNITS))
        def _():
            pass_on(gather_values, value_recv, value_unit(q))

        @pl.when(within(q - UNITS, FAR_UNITS))
        def _():
            pass_on(gather_columns, column_recv, q - UNITS)

    def gather_turn(n, carry):
        @pl.when(n == 8)
        def _():
            pass_heads(False)

        for step in range(GAIN_STEPS + 1):

            @pl.when(n == step + 6)
            def _():
                if step > 0:
                    gain_copy(step - 1).wait_recv()
                    gain_own[step] = gain_own[step - 1] + gain_got[step - 1]
                if step < GAIN_STEPS:
                    gain_copy(step).start()
                else:
                    gain_done[...] = gain_own[GAIN_STEPS] * grad_scale
                    gain_store.start()

        @pl.when(within(n + 2 - UNITS, FAR_UNITS))
        def _():
            p = n + 2 - UNITS
            wait_arrived(gather_sizes[1], exchange_recv.at[p])
            for h in range(2):
                gather_columns(p, h, 0).start()
                gather_columns(p, h, 1).start()

        @pl.when(n == UNITS + FAR_UNITS + 7)
        def _():
            finish_grads((0, 1))

        gather_stage(n, 0)
        gather_stage(n - 6, 2)
        gather_stage(n - 3, 1)
        gather_stage(n - 8, 3)
        done = n - 8

        @pl.when(within(done, UNITS))
        def _():
            use_values(value_unit(done))

        @pl.when(done == UNITS)
        def _():
            heads_done[...] = narrow(heads_total[...])
            heads_store.start()
            heads_arrived(SLOTS - 1)
            use_near(0, SLOTS - 1, 0)
            use_near(1, SLOTS - 1, UNIT_WIDE)
            heads_arrived(near_heads + 1 - core)

        @pl.when(done == UNITS + 2)
        def _():
            for k in range(2):
                use_near(2 + k, near_heads + k, 0)

        @pl.when(within(done - UNITS, FAR_UNITS))
        def _():
            use_columns(done - UNITS)

        return carry

    own_grad_store.start()
    each_relay((2,), pass_relay)
    lax.fori_loop(0, UNITS + FAR_UNITS + 8, gather_turn, 0)
    finish_grads((2, 3))

    def reduce_sent(u, carry):
        wait_sent(part.at[0:2], send_sem.at[u])
        wait_sent(values.at[0:5, 0:3, 0:2], value_send.at[u])
        return carry

    def columns_sent(p, carry):
        wait_sent(values.at[0:5, 0:3, 0:2], column_send.at[p])
        return carry

    lax.fori_loop(0, UNITS, reduce_sent, 0)
    lax.fori_loop(0, FAR_UNITS, columns_sent, 0)
    wait_sent(exchange.at[0:5, 0:2], exchange_send.at[0])
    wait_sent(tokens.at[0:2], near_send.at[0])
    each_relay((0, 1, 2), lambda relay, held: relay.wait_send())
    for j in range(SIDE - 1):
        passed_heads(j).wait_send()
    sibling_heads().wait_send()
    for step in range(GAIN_STEPS):
        gain_copy(step).wait_send()
    for store in [own_grad_store, heads_store, gain_store] + [store_grads(i) for i in range(4)]:
        store.wait()


def deliver_kernel(*refs):
    results, outputs, held = refs[:4], refs[4:8], refs[8:12]
    load_sem, store_sem = refs[12:]
    pieces = [(1, pl.ds(block * WIDE, WIDE)) for block in range(SIDE)]
    pieces += [(at, pl.ds(0, results[at].shape[0])) for at in (0, 2, 3)]

    def copies(sources, targets, sems):
        return [
            pltpu.make_async_copy(sources[at].at[rows], targets[at].at[rows], sems.at[i])
            for i, (at, rows) in enumerate(pieces)
        ]

    loads, stores = copies(results, held, load_sem), copies(held, outputs, store_sem)
    for load in loads:
        load.start()
    for load, store in zip(loads, stores):
        load.wait()
        store.start()
    for store in stores:
        store.wait()


def delivered(results):
    hbm = pl.BlockSpec(memory_space=pl.ANY)
    return pl.pallas_call(
        deliver_kernel,
        out_shape=tuple(jax.ShapeDtypeStruct(result.shape, result.dtype) for result in results),
        in_specs=[hbm] * 4,
        out_specs=(hbm,) * 4,
        scratch_shapes=[pltpu.VMEM(result.shape, result.dtype) for result in results]
        + [pltpu.SemaphoreType.DMA((SIDE + 3,))] * 2,
        name="deliver",
    )(*results)


def fused(heads, weights, residual, gain):
    hbm = pl.BlockSpec(memory_space=pl.ANY)
    bf16, f32 = jnp.bfloat16, jnp.float32
    rows_dev, depth = heads.shape
    owned = weights.shape[1] // GROUPS
    dma = pltpu.SemaphoreType.DMA
    return pl.pallas_call(
        boundary_kernel,
        out_shape=(
            jax.ShapeDtypeStruct(heads.shape, bf16),
            jax.ShapeDtypeStruct((owned, depth), f32),
            jax.ShapeDtypeStruct(residual.shape, bf16),
            jax.ShapeDtypeStruct(gain.shape, f32),
        ),
        in_specs=[hbm] * 4,
        out_specs=(hbm,) * 4,
        scratch_shapes=[
            pltpu.VMEM(heads.shape, bf16),
            pltpu.VMEM(residual.shape, bf16),
            pltpu.VMEM(gain.shape, f32),
            pltpu.VMEM(heads.shape, bf16),
            pltpu.VMEM((owned, depth), f32),
            pltpu.VMEM(residual.shape, bf16),
            pltpu.VMEM(gain.shape, f32),
            pltpu.VMEM((depth, rows_dev), bf16),
            pltpu.VMEM((depth, owned), f32),
            pltpu.VMEM(weights.shape, bf16),
            pltpu.VMEM((CHUNKS, SIDE, SIDE, TALL, WIDE), bf16),
            pltpu.VMEM((CHUNKS, 2, SIDE, TALL, HALF), bf16),
            pltpu.VMEM((CHUNKS, 2, SIDE, TALL, WIDE), bf16),
            pltpu.VMEM((CHUNKS, 2, TALL, HALF), bf16),
            pltpu.VMEM((CHUNKS, 2, TALL, WIDE), bf16),
            pltpu.VMEM((2, CHUNKS, TALL, WIDE), bf16),
            pltpu.VMEM((CHUNKS, SIDE, SIDE, TALL, WIDE), bf16),
            pltpu.VMEM((FAR_CHUNKS, SIDE, SIDE, TALL, WIDE), bf16),
            pltpu.VMEM((GROUPS, 3, TALL, WIDE), bf16),
            pltpu.VMEM((UNITS, 2, rows_dev, UNIT_WIDE), bf16),
            pltpu.VMEM((2, rows_dev, UNIT_WIDE), bf16),
            pltpu.VMEM((4, rows_dev, UNIT_WIDE), bf16),
            pltpu.VMEM((SLOTS, depth, rows_dev), bf16),
            pltpu.VMEM((rows_dev, depth), f32),
            pltpu.VMEM((GAIN_STEPS + 1,) + gain.shape, f32),
            pltpu.VMEM((GAIN_STEPS,) + gain.shape, f32),
            dma((3,)),
            dma((7,)),
            dma((UNITS, 2)),
            dma((UNITS,)),
            dma((UNITS, 5)),
            dma((UNITS,)),
            dma((UNITS, 4)),
            dma((FAR_UNITS,)),
            dma((FAR_UNITS, 4)),
            dma((1,)),
            dma((FAR_UNITS,)),
            dma((SLOTS + 6,)),
            dma((SLOTS,)),
            dma((1,)),
            dma((4,)),
            dma((GAIN_STEPS,)),
            dma((GAIN_STEPS,)),
        ],
        compiler_params=pltpu.CompilerParams(
            collective_id=0, has_side_effects=True, vmem_limit_bytes=62 * 1024 * 1024
        ),
        name="boundary",
    )(heads, weights, residual, gain)


def per_device(heads_in, weights, residual, norm_gain):
    heads_out, weight_grad, boundary_grad, gain_grad = delivered(
        fused(heads_in[0], weights[0], residual, norm_gain[None])
    )
    return (heads_out[None], weight_grad[None], boundary_grad, gain_grad[0])


def solution(mesh):
    placed = (P("section", "grp", "tp"), P("section", "tp", None), P(("grp", "tp"), None), P())
    return jax.shard_map(
        per_device,
        mesh=mesh,
        in_specs=placed,
        out_specs=(
            P("section", "grp", "tp"),
            P("section", "grp", "tp"),
            P(("grp", "tp"), None),
            P(),
        ),
        check_vma=False,
    )
```

```python
import math

import jax
import jax.numpy as jnp
from jax import lax
from jax.experimental import pallas as pl
from jax.experimental.pallas import tpu as pltpu
from jax.sharding import PartitionSpec as P

EPSILON = 1e-05
MESH = pl.DeviceIdType.MESH

SIDE = 4
GROUPS = 8
UNITS = 8
FAR_UNITS = 5
CHUNKS = 2 * UNITS
FAR_CHUNKS = 2 * FAR_UNITS
WIDE = 256
HALF = WIDE // 2
UNIT_WIDE = 2 * WIDE
SHARD = 2 * UNIT_WIDE
OWN = 24
TALL = 2 * OWN
SLOTS = GROUPS - 1
GAIN_STEPS = 7


def lower_start(t, h=0):
    return pl.multiple_of(t * UNIT_WIDE + h * WIDE, WIDE)


def upper_start(t, h=0):
    return pl.multiple_of((GROUPS - 1 - t // 2) * SHARD + (t % 2) * UNIT_WIDE + h * WIDE, WIDE)


def plane_device(h, first, second):
    x, y = (first, second) if h == 0 else (second, first)
    return {"tp": x * SIDE + y}


def stacked(*parts):
    return jnp.concatenate(parts, axis=0)


def both_halves(row_pair):
    total = row_pair[:OWN] + row_pair[OWN:]
    return stacked(total, total)


def lanes(value):
    return sum(value[:, 128 * i : 128 * (i + 1)] for i in range(value.shape[1] // 128))


def wide(value):
    return value.astype(jnp.float32)


def narrow(value):
    return value.astype(jnp.bfloat16)


def remote(source, target, send_sem, recv_sem, device):
    return pltpu.make_async_remote_copy(
        src_ref=source,
        dst_ref=target,
        send_sem=send_sem,
        recv_sem=recv_sem,
        device_id=device,
        device_id_type=MESH,
    )


def greet(peers):
    barrier = pltpu.get_barrier_semaphore()
    for peer in peers:
        pl.semaphore_signal(barrier, inc=1, device_id=peer, device_id_type=MESH)
    pl.semaphore_wait(barrier, len(peers))


def boundary_kernel(
    heads_in, weights, residual_in, gain_in, heads_out, grads_out, grad_out, gain_out,
    heads, residual, gain, heads_done, grads, own_grad, gain_done,
    heads_t, grads_t, weight_buf, part, from1, from2, from3, from4, both,
    values, columns, exchange, tokens, column_tokens, from_near, heads_all, heads_total, gain_own, gain_got,
    input_sem, output_sem, weight_sem, send_sem, recv_sem, value_send, value_recv, column_send, column_recv,
    exchange_send, exchange_recv, heads_send, heads_recv, near_send, near_recv, gain_send, gain_recv,
):
    tp = lax.axis_index("tp")
    x, y = tp // SIDE, tp % SIDE
    section = lax.axis_index("section")
    group = lax.axis_index("grp")
    z, core = group // 2, group % 2
    other = {"section": 1 - section}
    sibling_group = 2 * z + 1 - core
    sibling = {"grp": sibling_group}
    next_plane = z + 1 - 2 * (z % 2)
    rows_dev, depth = heads.shape
    grad_scale = 1.0 / math.sqrt(rows_dev * GROUPS)

    def axes(h):
        return (x, y) if h == 0 else (y, x)

    def wait_arrived(size, sem):
        remote(size, size, heads_send.at[0], sem, sibling).wait_recv()

    def wait_sent(size, sem):
        remote(size, size, sem, heads_recv.at[0], sibling).wait_send()

    def weight_copy(t, upper):
        cols = pl.ds(upper_start(t) if upper else lower_start(t), UNIT_WIDE)
        return pltpu.make_async_copy(
            weights.at[:, cols], weight_buf.at[:, cols], weight_sem.at[t, upper]
        )

    def start_weights(t, carry):
        weight_copy(t, 0).start()
        weight_copy(t, 1).start()
        return carry

    heads_load, residual_load, gain_load = [
        pltpu.make_async_copy(source, target, input_sem.at[at])
        for at, (source, target) in enumerate(
            ((heads_in, heads), (residual_in, residual), (gain_in, gain))
        )
    ]
    heads_load.start()
    lax.fori_loop(0, UNITS, start_weights, 0)
    residual_load.start()
    gain_load.start()
    greet(
        [plane_device(0, (x + step) % SIDE, y) for step in (1, 3)]
        + [plane_device(0, x, (y + step) % SIDE) for step in (1, 3)]
        + [other, sibling]
        + [{"grp": 2 * ((z + hop) % SIDE) + k} for hop in range(1, SIDE) for k in range(2)]
    )
    heads_load.wait()

    def plane_slot(origin, at):
        return 2 * ((origin + SIDE - 1 - at) % SIDE)

    def heads_arrived(slot):
        remote(
            heads_t, heads_all.at[slot], heads_send.at[SLOTS - 1], heads_recv.at[slot], sibling
        ).wait_recv()

    def sibling_heads():
        slot = SLOTS - 1
        return remote(
            heads_t, heads_all.at[slot], heads_send.at[slot], heads_recv.at[slot], sibling
        )

    relays = ((1, 0), (-1, 0), (1, 1), (-1, 1), (1, 2), (-1, 2))

    def each_relay(wanted, act):
        for at, (step, away) in enumerate(relays):
            if away not in wanted:
                continue
            first, last = (away, SIDE - 2) if step > 0 else (1, SIDE - 1 - away)

            @pl.when(jnp.logical_and(z >= first, z <= last))
            def _():
                origin, target = z - step * away, z + step
                held = plane_slot(origin, z) + core
                slot = plane_slot(origin, target) + core
                act(
                    remote(
                        heads_all.at[held] if away else heads_t,
                        heads_all.at[slot],
                        heads_send.at[SLOTS + at],
                        heads_recv.at[slot],
                        {"grp": 2 * target + core},
                    ),
                    held,
                )

    def start_relay(relay, held):
        relay.start()

    def pass_relay(relay, held):
        heads_arrived(held)
        relay.start()

    def passed_heads(j):
        slot = 2 * j + core
        held = heads_all.at[slot]
        return remote(held, held, heads_send.at[slot], heads_recv.at[slot], sibling)

    def pass_heads(neighbours):
        for j in range(SIDE - 1):
            origin = (z + 1 + j) % SIDE
            near = jnp.logical_or(origin == z + 1, origin == z - 1)

            @pl.when(near if neighbours else jnp.logical_not(near))
            def _():
                @pl.when(jnp.logical_or(z == 0, z == SIDE - 1))
                def _():
                    heads_arrived(2 * j + core)

                passed_heads(j).start()

    def send_heads():
        heads_t[...] = heads[...].T
        each_relay((0,), start_relay)
        sibling_heads().start()


    def copy(u, h, step):
        chunk = 2 * u + h
        a, b = axes(h)
        right, left = (a + 1) % SIDE, (a + 3) % SIDE
        up, down = (b + 1) % SIDE, (b + 3) % SIDE
        low, high = pl.ds(0, HALF), pl.ds(HALF, HALF)
        far_a, far_b = (a + 2) % SIDE, (b + 2) % SIDE
        source, target, device = [
            lambda: (part.at[chunk, far_a, :, :, low], from1.at[chunk, 0], plane_device(h, right, b)),
            lambda: (part.at[chunk, far_a, :, :, high], from1.at[chunk, 1], plane_device(h, left, b)),
            lambda: (part.at[chunk, right], from2.at[chunk, 0], plane_device(h, right, b)),
            lambda: (part.at[chunk, left], from2.at[chunk, 1], plane_device(h, left, b)),
            lambda: (part.at[chunk, a, far_b, :, low], from3.at[chunk, 0], plane_device(h, a, up)),
            lambda: (part.at[chunk, a, far_b, :, high], from3.at[chunk, 1], plane_device(h, a, down)),
            lambda: (part.at[chunk, a, up], from4.at[chunk, 0], plane_device(h, a, up)),
            lambda: (part.at[chunk, a, down], from4.at[chunk, 1], plane_device(h, a, down)),
            lambda: (both.at[section, chunk], both.at[section, chunk], other),
        ][step]()
        return remote(source, target, send_sem.at[u], recv_sem.at[u, step // 2], device)

    reduce_sizes = [
        part.at[0, 0:2], part.at[0], part.at[0, 0, 0:2], part.at[0, 0], part.at[0, 0, 0:2]
    ]

    def arrive(u, stage):
        wait_arrived(reduce_sizes[stage], recv_sem.at[u, stage])

    def multiply(u):
        weight_copy(u, 0).wait()
        weight_copy(u, 1).wait()
        lower, upper = [
            jnp.dot(
                heads[...], weight_buf[:, pl.ds(start, UNIT_WIDE)],
                preferred_element_type=jnp.float32,
            )
            for start in (lower_start(u), upper_start(u))
        ]
        for h in range(2):
            cols = slice(h * WIDE, (h + 1) * WIDE)
            for i in range(SIDE * SIDE):
                rows = slice(OWN * i, OWN * (i + 1))
                a, b = (i // SIDE, i % SIDE) if h == 0 else (i % SIDE, i // SIDE)
                part[2 * u + h, a, b] = narrow(stacked(lower[rows, cols], upper[rows, cols]))
            copy(u, h, 0).start()
            copy(u, h, 1).start()

    def near_first(u):
        arrive(u, 0)
        for h in range(2):
            chunk = 2 * u + h
            a, b = axes(h)
            right, left = (a + 1) % SIDE, (a + 3) % SIDE
            part[chunk, right, :, :, :HALF] = narrow(
                wide(part[chunk, right, :, :, :HALF]) + wide(from1[chunk, 0])
            )
            copy(u, h, 2).start()
            part[chunk, left, :, :, HALF:] = narrow(
                wide(part[chunk, left, :, :, HALF:]) + wide(from1[chunk, 1])
            )
            copy(u, h, 3).start()

    def far_second(u):
        arrive(u, 1)
        for h in range(2):
            chunk = 2 * u + h
            a, b = axes(h)
            part[chunk, a] = narrow(
                wide(part[chunk, a]) + (wide(from2[chunk, 0]) + wide(from2[chunk, 1]))
            )
            copy(u, h, 4).start()
            copy(u, h, 5).start()

    def near_second(u):
        arrive(u, 2)
        for h in range(2):
            chunk = 2 * u + h
            a, b = axes(h)
            up, down = (b + 1) % SIDE, (b + 3) % SIDE
            part[chunk, a, up, :, :HALF] = narrow(
                wide(part[chunk, a, up, :, :HALF]) + wide(from3[chunk, 0])
            )
            copy(u, h, 6).start()
            part[chunk, a, down, :, HALF:] = narrow(
                wide(part[chunk, a, down, :, HALF:]) + wide(from3[chunk, 1])
            )
            copy(u, h, 7).start()

    def finish(u):
        arrive(u, 3)
        for h in range(2):
            chunk = 2 * u + h
            a, b = axes(h)
            total = wide(part[chunk, a, b]) + (wide(from4[chunk, 0]) + wide(from4[chunk, 1]))
            rows = stacked(
                wide(residual[:, pl.ds(lower_start(u, h), WIDE)]),
                wide(residual[:, pl.ds(upper_start(u, h), WIDE)]),
            )
            total = total + jnp.where(section == 0, rows, 0.0)
            both[section, chunk] = narrow(total)
            copy(u, h, 8).start()

    def within(value, count):
        return jnp.logical_and(value >= 0, value < count)

    stages = (multiply, near_first, far_second, near_second, finish)
    APART = 2

    def reduce_turn(n, carry):
        for at, stage in enumerate(stages):

            @pl.when(within(n - APART * at, UNITS))
            def _():
                stage(n - APART * at)

        @pl.when(n == 1)
        def _():
            send_heads()

        @pl.when(n == UNITS + 2)
        def _():
            each_relay((1,), pass_relay)

        return carry

    residual_load.wait()
    gain_load.wait()
    lax.fori_loop(0, UNITS + APART * (len(stages) - 1), reduce_turn, 0)
    pass_heads(True)
    heads_total[...] = jnp.zeros_like(heads_total)
    grads_t[...] = jnp.zeros_like(grads_t)


    def gather_of(store, sends, recvs):
        half = store.shape[-1] // 2

        def gather(p, h, step):
            chunk = 2 * p + h
            a, b = axes(h)
            right, left = (a + 1) % SIDE, (a + 3) % SIDE
            up, down = (b + 1) % SIDE, (b + 3) % SIDE
            low, high = pl.ds(0, half), pl.ds(half, half)
            block, device = [
                lambda: (store.at[chunk, b, a], plane_device(h, right, b)),
                lambda: (store.at[chunk, b, a], plane_device(h, left, b)),
                lambda: (store.at[chunk, b, left, :, low], plane_device(h, right, b)),
                lambda: (store.at[chunk, b, right, :, high], plane_device(h, left, b)),
                lambda: (store.at[chunk, b], plane_device(h, a, up)),
                lambda: (store.at[chunk, b], plane_device(h, a, down)),
                lambda: (store.at[chunk, down, :, :, low], plane_device(h, a, up)),
                lambda: (store.at[chunk, up, :, :, high], plane_device(h, a, down)),
            ][step]()
            return remote(block, block, sends.at[p], recvs.at[p, step // 2], device)

        return gather

    gather_values = gather_of(values, value_send, value_recv)
    gather_columns = gather_of(columns, column_send, column_recv)

    gather_sizes = [values.at[0, 0], values.at[0, 0, 0:2], values.at[0], values.at[0, 0:2]]

    def exchanged(target, e):
        unit = 2 * (z % 2) + e if e < 2 else FAR_UNITS - 1
        a, b = x + core * (y - x), y + core * (x - y)
        return remote(
            exchange.at[target, e],
            columns.at[2 * unit + core, b, a],
            exchange_send.at[0],
            exchange_recv.at[unit],
            {"grp": target},
        )

    def gain_rows(t, h):
        return stacked(
            jnp.broadcast_to(gain[:, pl.ds(lower_start(t, h), WIDE)], (OWN, WIDE)),
            jnp.broadcast_to(gain[:, pl.ds(upper_start(t, h), WIDE)], (OWN, WIDE)),
        )

    zero = jnp.zeros((TALL, 128), jnp.float32)

    def row_mean(total):
        return both_halves(jnp.sum(total, axis=1, keepdims=True)) / (GROUPS * SHARD)

    def add_sums(t, total):
        arrive(t, 4)
        for h in range(2):
            total = total + lanes(wide(both[0, 2 * t + h]))
        return total

    mean = row_mean(lax.fori_loop(0, UNITS, add_sums, zero))

    def add_squares(t, total):
        for h in range(2):
            centred = wide(both[0, 2 * t + h]) - mean
            total = total + lanes(centred * centred)
        return total

    inv_scale = lax.rsqrt(row_mean(lax.fori_loop(0, UNITS, add_squares, zero)) + EPSILON)

    def add_means(t, totals):
        for h in range(2):
            unit = (wide(both[0, 2 * t + h]) - mean) * inv_scale
            scaled = gain_rows(t, h) * wide(both[1, 2 * t + h])
            totals = (totals[0] + lanes(scaled), totals[1] + lanes(scaled * unit))
        return totals

    sums = lax.fori_loop(0, UNITS, add_means, (zero, zero))
    mean_scaled, mean_product = row_mean(sums[0]), row_mean(sums[1])
    first_unit = SIDE * ((z // 2 + z % 2 + 1) % 2)

    def write(turn, carry):
        shard = (turn + first_unit // 2) % SIDE
        kept = []
        for v in range(2):
            t = 2 * shard + v
            for h in range(2):
                chunk = 2 * t + h
                a, b = axes(h)
                rows = gain_rows(t, h)
                unit = (wide(both[0, chunk]) - mean) * inv_scale
                d_normed = wide(both[1, chunk])
                grad = inv_scale * (rows * d_normed - mean_scaled - unit * mean_product)
                value = jnp.where(section == 0, grad, unit * rows)
                values[chunk, b, a] = narrow(value)
                gather_values(t, h, 0).start()
                gather_values(t, h, 1).start()
                kept.append(value)
                product = d_normed * unit
                for start, rows in (
                    (lower_start(t, h), slice(0, OWN)),
                    (upper_start(t, h), slice(OWN, TALL)),
                ):
                    own_grad[:, pl.ds(start, WIDE)] = narrow(grad[rows])
                    gain_own[0, :, pl.ds(start, WIDE)] = jnp.sum(product[rows], axis=0, keepdims=True)
        for target, rows in ((shard, slice(0, OWN)), (GROUPS - 1 - shard, slice(OWN, TALL))):
            for e, (first, second) in enumerate(((0, 2), (1, 3), (2, 3))):
                exchange[target, e] = narrow(stacked(kept[first][rows], kept[second][rows]))
                wanted = target // SIDE != z // 2 if e < 2 else target // 2 == next_plane

                @pl.when(wanted)
                def _():
                    exchanged(target, e).start()
        return carry

    lax.fori_loop(0, SIDE, write, 0)


    def near_copy(t, upper, target, slot):
        return remote(
            tokens.at[t, upper],
            from_near.at[slot],
            near_send.at[0],
            near_recv.at[slot],
            {"grp": target},
        )

    def split_blocks(store, chunk, h, put):
        for i in range(0, SIDE * SIDE, 2):
            pair = []
            for at in (i, i + 1):
                a, b = (at // SIDE, at % SIDE) if h == 0 else (at % SIDE, at // SIDE)
                pair.append(wide(store[chunk, b, a]))
            put(0, slice(OWN * i, OWN * (i + 2)), narrow(stacked(pair[0][:OWN], pair[1][:OWN])))
            put(1, slice(OWN * i, OWN * (i + 2)), narrow(stacked(pair[0][OWN:], pair[1][OWN:])))

    def add_grads(start, transposed_heads, token_rows):
        cols = pl.ds(start, token_rows.shape[1])
        grads_t[:, cols] += jnp.dot(
            transposed_heads, token_rows, preferred_element_type=jnp.float32
        )

    def store_grads(block):
        return pltpu.make_async_copy(
            grads.at[block * WIDE : (block + 1) * WIDE],
            grads_out.at[block * WIDE : (block + 1) * WIDE],
            output_sem.at[3 + block],
        )

    def finish_grads(blocks):
        for block in blocks:
            cols = slice(block * WIDE, (block + 1) * WIDE)
            grads[cols] = grad_scale * grads_t[:, cols].T
            store_grads(block).start()

    def use_values(t):
        for h in range(2):

            def put(upper, rows, block):
                tokens[t, upper, rows, h * WIDE : (h + 1) * WIDE] = block

            split_blocks(values, 2 * t + h, h, put)
        for upper, target in enumerate((t // 2, GROUPS - 1 - t // 2)):
            to_next = jnp.logical_and(target // 2 == next_plane, t % 2 == 0)
            for slot, wanted in ((t % 2, target == sibling_group), (2 + core, to_next)):

                @pl.when(wanted)
                def _():
                    near_copy(t, upper, target, slot).start()

        total = heads_total[...]
        for upper, start in enumerate((lower_start(t), upper_start(t))):
            total = total + lax.dot_general(
                tokens[t, upper], weight_buf[:, pl.ds(start, UNIT_WIDE)],
                (((1,), (1,)), ((), ())), preferred_element_type=jnp.float32,
            )
        heads_total[...] = total
        for upper, target in enumerate((t // 2, GROUPS - 1 - t // 2)):

            @pl.when(target == group)
            def _():
                add_grads(pl.multiple_of((t % 2) * UNIT_WIDE, UNIT_WIDE), heads_t[...], tokens[t, upper])

    def use_columns(p):
        last = p // (FAR_UNITS - 1)
        plane = (1 - last) * (2 * (1 - z // 2) + p // 2) + last * next_plane
        for h in range(2):

            def put(side, rows, block):
                column_tokens[h, rows, side * WIDE : (side + 1) * WIDE] = block

            split_blocks(columns, 2 * p + h, h, put)
        slot = plane_slot(plane, z)

        @pl.when(jnp.logical_and(p % 2 == 0, last == 0))
        def _():
            heads_arrived(slot + 1 - core)

        total = jnp.dot(
            heads_all[slot], column_tokens[0], preferred_element_type=jnp.float32
        ) + jnp.dot(heads_all[slot + 1], column_tokens[1], preferred_element_type=jnp.float32)
        for side in range(2):
            start = (1 - last) * (side * UNIT_WIDE + (p % 2) * WIDE) + last * (UNIT_WIDE + side * WIDE)
            cols = pl.ds(pl.multiple_of(start, WIDE), WIDE)
            grads_t[:, cols] += total[:, side * WIDE : (side + 1) * WIDE]

    def use_near(slot, heads_slot, start):
        wait_arrived(from_near.at[slot], near_recv.at[slot])
        add_grads(start, heads_all[heads_slot], from_near[slot])

    gain_partners = [
        {"tp": x * SIDE + y + 1 - 2 * (y % 2)},
        {"tp": x * SIDE + SIDE - 1 - y},
        {"tp": (x + 1 - 2 * (x % 2)) * SIDE + y},
        {"tp": (SIDE - 1 - x) * SIDE + y},
        sibling,
        {"grp": 2 * next_plane + core},
        {"grp": 2 * (SIDE - 1 - z) + core},
    ]

    def gain_copy(step):
        return remote(
            gain_own.at[step], gain_got.at[step], gain_send.at[step], gain_recv.at[step], gain_partners[step]
        )

    own_grad_store, heads_store, gain_store = [
        pltpu.make_async_copy(source, target, output_sem.at[at])
        for at, (source, target) in enumerate(
            ((own_grad, grad_out), (heads_done, heads_out), (gain_done, gain_out))
        )
    ]

    near_heads = plane_slot(next_plane, z)

    def value_unit(q):
        return (q + first_unit) % UNITS

    def gather_stage(q, stage):
        def pass_on(gather, recvs, p):
            wait_arrived(gather_sizes[stage], recvs.at[p, stage])
            if stage < 3:
                for h in range(2):
                    gather(p, h, 2 * stage + 2).start()
                    gather(p, h, 2 * stage + 3).start()

        @pl.when(within(q, UNITS))
        def _():
            pass_on(gather_values, value_recv, value_unit(q))

        @pl.when(within(q - UNITS, FAR_UNITS))
        def _():
            pass_on(gather_columns, column_recv, q - UNITS)

    def gather_turn(n, carry):
        @pl.when(n == 5)
        def _():
            pass_heads(False)

        for step in range(GAIN_STEPS + 1):

            @pl.when(n == step + 1)
            def _():
                if step > 0:
                    gain_copy(step - 1).wait_recv()
                    gain_own[step] = gain_own[step - 1] + gain_got[step - 1]
                if step < GAIN_STEPS:
                    gain_copy(step).start()
                else:
                    gain_done[...] = gain_own[GAIN_STEPS] * grad_scale
                    gain_store.start()

        @pl.when(within(n + 1 - UNITS, FAR_UNITS))
        def _():
            p = n + 1 - UNITS
            wait_arrived(gather_sizes[1], exchange_recv.at[p])
            for h in range(2):
                gather_columns(p, h, 0).start()
                gather_columns(p, h, 1).start()

        @pl.when(n == UNITS + FAR_UNITS + 4)
        def _():
            finish_grads((0, 1))

        gather_stage(n, 0)
        gather_stage(n - 4, 2)
        gather_stage(n - 2, 1)
        gather_stage(n - 5, 3)
        done = n - 5

        @pl.when(within(done, UNITS))
        def _():
            use_values(value_unit(done))

        @pl.when(done == UNITS)
        def _():
            heads_done[...] = narrow(heads_total[...])
            heads_store.start()
            heads_arrived(SLOTS - 1)
            use_near(0, SLOTS - 1, 0)
            use_near(1, SLOTS - 1, UNIT_WIDE)
            heads_arrived(near_heads + 1 - core)

        @pl.when(done == UNITS + 2)
        def _():
            for k in range(2):
                use_near(2 + k, near_heads + k, 0)

        @pl.when(within(done - UNITS, FAR_UNITS))
        def _():
            use_columns(done - UNITS)

        return carry

    own_grad_store.start()
    each_relay((2,), pass_relay)
    lax.fori_loop(0, UNITS + FAR_UNITS + 5, gather_turn, 0)
    finish_grads((2, 3))

    def reduce_sent(u, carry):
        wait_sent(part.at[0:2], send_sem.at[u])
        wait_sent(values.at[0:5, 0:3, 0:2], value_send.at[u])
        return carry

    def columns_sent(p, carry):
        wait_sent(values.at[0:5, 0:3, 0:2], column_send.at[p])
        return carry

    lax.fori_loop(0, UNITS, reduce_sent, 0)
    lax.fori_loop(0, FAR_UNITS, columns_sent, 0)
    wait_sent(exchange.at[0:5, 0:2], exchange_send.at[0])
    wait_sent(tokens.at[0:2], near_send.at[0])
    each_relay((0, 1, 2), lambda relay, held: relay.wait_send())
    for j in range(SIDE - 1):
        passed_heads(j).wait_send()
    sibling_heads().wait_send()
    for step in range(GAIN_STEPS):
        gain_copy(step).wait_send()
    for store in [own_grad_store, heads_store, gain_store] + [store_grads(i) for i in range(4)]:
        store.wait()


def deliver_kernel(*refs):
    results, outputs, held = refs[:4], refs[4:8], refs[8:12]
    load_sem, store_sem = refs[12:]
    pieces = [(1, pl.ds(block * WIDE, WIDE)) for block in range(SIDE)]
    pieces += [(at, pl.ds(0, results[at].shape[0])) for at in (0, 2, 3)]

    def copies(sources, targets, sems):
        return [
            pltpu.make_async_copy(sources[at].at[rows], targets[at].at[rows], sems.at[i])
            for i, (at, rows) in enumerate(pieces)
        ]

    loads, stores = copies(results, held, load_sem), copies(held, outputs, store_sem)
    for load in loads:
        load.start()
    for load, store in zip(loads, stores):
        load.wait()
        store.start()
    for store in stores:
        store.wait()


def delivered(results):
    hbm = pl.BlockSpec(memory_space=pl.ANY)
    return pl.pallas_call(
        deliver_kernel,
        out_shape=tuple(jax.ShapeDtypeStruct(result.shape, result.dtype) for result in results),
        in_specs=[hbm] * 4,
        out_specs=(hbm,) * 4,
        scratch_shapes=[pltpu.VMEM(result.shape, result.dtype) for result in results]
        + [pltpu.SemaphoreType.DMA((SIDE + 3,))] * 2,
        name="deliver",
    )(*results)


def fused(heads, weights, residual, gain):
    hbm = pl.BlockSpec(memory_space=pl.ANY)
    bf16, f32 = jnp.bfloat16, jnp.float32
    rows_dev, depth = heads.shape
    owned = weights.shape[1] // GROUPS
    dma = pltpu.SemaphoreType.DMA
    return pl.pallas_call(
        boundary_kernel,
        out_shape=(
            jax.ShapeDtypeStruct(heads.shape, bf16),
            jax.ShapeDtypeStruct((owned, depth), f32),
            jax.ShapeDtypeStruct(residual.shape, bf16),
            jax.ShapeDtypeStruct(gain.shape, f32),
        ),
        in_specs=[hbm] * 4,
        out_specs=(hbm,) * 4,
        scratch_shapes=[
            pltpu.VMEM(heads.shape, bf16),
            pltpu.VMEM(residual.shape, bf16),
            pltpu.VMEM(gain.shape, f32),
            pltpu.VMEM(heads.shape, bf16),
            pltpu.VMEM((owned, depth), f32),
            pltpu.VMEM(residual.shape, bf16),
            pltpu.VMEM(gain.shape, f32),
            pltpu.VMEM((depth, rows_dev), bf16),
            pltpu.VMEM((depth, owned), f32),
            pltpu.VMEM(weights.shape, bf16),
            pltpu.VMEM((CHUNKS, SIDE, SIDE, TALL, WIDE), bf16),
            pltpu.VMEM((CHUNKS, 2, SIDE, TALL, HALF), bf16),
            pltpu.VMEM((CHUNKS, 2, SIDE, TALL, WIDE), bf16),
            pltpu.VMEM((CHUNKS, 2, TALL, HALF), bf16),
            pltpu.VMEM((CHUNKS, 2, TALL, WIDE), bf16),
            pltpu.VMEM((2, CHUNKS, TALL, WIDE), bf16),
            pltpu.VMEM((CHUNKS, SIDE, SIDE, TALL, WIDE), bf16),
            pltpu.VMEM((FAR_CHUNKS, SIDE, SIDE, TALL, WIDE), bf16),
            pltpu.VMEM((GROUPS, 3, TALL, WIDE), bf16),
            pltpu.VMEM((UNITS, 2, rows_dev, UNIT_WIDE), bf16),
            pltpu.VMEM((2, rows_dev, UNIT_WIDE), bf16),
            pltpu.VMEM((4, rows_dev, UNIT_WIDE), bf16),
            pltpu.VMEM((SLOTS, depth, rows_dev), bf16),
            pltpu.VMEM((rows_dev, depth), f32),
            pltpu.VMEM((GAIN_STEPS + 1,) + gain.shape, f32),
            pltpu.VMEM((GAIN_STEPS,) + gain.shape, f32),
            dma((3,)),
            dma((7,)),
            dma((UNITS, 2)),
            dma((UNITS,)),
            dma((UNITS, 5)),
            dma((UNITS,)),
            dma((UNITS, 4)),
            dma((FAR_UNITS,)),
            dma((FAR_UNITS, 4)),
            dma((1,)),
            dma((FAR_UNITS,)),
            dma((SLOTS + 6,)),
            dma((SLOTS,)),
            dma((1,)),
            dma((4,)),
            dma((GAIN_STEPS,)),
            dma((GAIN_STEPS,)),
        ],
        compiler_params=pltpu.CompilerParams(
            collective_id=0, has_side_effects=True, vmem_limit_bytes=62 * 1024 * 1024
        ),
        name="boundary",
    )(heads, weights, residual, gain)


def per_device(heads_in, weights, residual, norm_gain):
    heads_out, weight_grad, boundary_grad, gain_grad = delivered(
        fused(heads_in[0], weights[0], residual, norm_gain[None])
    )
    return (heads_out[None], weight_grad[None], boundary_grad, gain_grad[0])


def solution(mesh):
    placed = (P("section", "grp", "tp"), P("section", "tp", None), P(("grp", "tp"), None), P())
    return jax.shard_map(
        per_device,
        mesh=mesh,
        in_specs=placed,
        out_specs=(
            P("section", "grp", "tp"),
            P("section", "grp", "tp"),
            P(("grp", "tp"), None),
            P(),
        ),
        check_vma=False,
    )
```

```python
import math

import jax
import jax.numpy as jnp
from jax import lax
from jax.experimental import pallas as pl
from jax.experimental.pallas import tpu as pltpu
from jax.sharding import PartitionSpec as P

EPSILON = 1e-05
MESH = pl.DeviceIdType.MESH

SIDE = 4
GROUPS = 8
UNITS = 8
FAR_UNITS = 5
CHUNKS = 2 * UNITS
FAR_CHUNKS = 2 * FAR_UNITS
WIDE = 256
HALF = WIDE // 2
UNIT_WIDE = 2 * WIDE
SHARD = 2 * UNIT_WIDE
OWN = 24
TALL = 2 * OWN
SLOTS = GROUPS - 1
GAIN_STEPS = 7


def lower_start(t, h=0):
    return pl.multiple_of(t * UNIT_WIDE + h * WIDE, WIDE)


def upper_start(t, h=0):
    return pl.multiple_of((GROUPS - 1 - t // 2) * SHARD + (t % 2) * UNIT_WIDE + h * WIDE, WIDE)


def plane_device(h, first, second):
    x, y = (first, second) if h == 0 else (second, first)
    return {"tp": x * SIDE + y}


def stacked(*parts):
    return jnp.concatenate(parts, axis=0)


def both_halves(row_pair):
    total = row_pair[:OWN] + row_pair[OWN:]
    return stacked(total, total)


def lanes(value):
    return sum(value[:, 128 * i : 128 * (i + 1)] for i in range(value.shape[1] // 128))


def wide(value):
    return value.astype(jnp.float32)


def narrow(value):
    return value.astype(jnp.bfloat16)


def remote(source, target, send_sem, recv_sem, device):
    return pltpu.make_async_remote_copy(
        src_ref=source,
        dst_ref=target,
        send_sem=send_sem,
        recv_sem=recv_sem,
        device_id=device,
        device_id_type=MESH,
    )


def greet(peers):
    barrier = pltpu.get_barrier_semaphore()
    for peer in peers:
        pl.semaphore_signal(barrier, inc=1, device_id=peer, device_id_type=MESH)
    pl.semaphore_wait(barrier, len(peers))


def boundary_kernel(
    heads_in, weights, residual_in, gain_in, heads_out, grads_out, grad_out, gain_out,
    heads, residual, gain, heads_done, grads, own_grad, gain_done,
    heads_t, grads_t, weight_buf, part, from1, from2, from3, from4, both,
    values, columns, exchange, tokens, column_tokens, from_near, heads_all, heads_total, gain_own, gain_got,
    input_sem, output_sem, weight_sem, send_sem, recv_sem, value_send, value_recv, column_send, column_recv,
    exchange_send, exchange_recv, heads_send, heads_recv, near_send, near_recv, gain_send, gain_recv,
):
    tp = lax.axis_index("tp")
    x, y = tp // SIDE, tp % SIDE
    section = lax.axis_index("section")
    group = lax.axis_index("grp")
    z, core = group // 2, group % 2
    other = {"section": 1 - section}
    sibling_group = 2 * z + 1 - core
    sibling = {"grp": sibling_group}
    next_plane = z + 1 - 2 * (z % 2)
    rows_dev, depth = heads.shape
    grad_scale = 1.0 / math.sqrt(rows_dev * GROUPS)

    def axes(h):
        return (x, y) if h == 0 else (y, x)

    def wait_arrived(size, sem):
        remote(size, size, heads_send.at[0], sem, sibling).wait_recv()

    def wait_sent(size, sem):
        remote(size, size, sem, heads_recv.at[0], sibling).wait_send()

    def weight_copy(t, upper):
        cols = pl.ds(upper_start(t) if upper else lower_start(t), UNIT_WIDE)
        return pltpu.make_async_copy(
            weights.at[:, cols], weight_buf.at[:, cols], weight_sem.at[t, upper]
        )

    def start_weights(t, carry):
        weight_copy(t, 0).start()
        weight_copy(t, 1).start()
        return carry

    heads_load, residual_load, gain_load = [
        pltpu.make_async_copy(source, target, input_sem.at[at])
        for at, (source, target) in enumerate(
            ((heads_in, heads), (residual_in, residual), (gain_in, gain))
        )
    ]
    heads_load.start()
    lax.fori_loop(0, UNITS, start_weights, 0)
    residual_load.start()
    gain_load.start()
    greet(
        [plane_device(0, (x + step) % SIDE, y) for step in (1, 3)]
        + [plane_device(0, x, (y + step) % SIDE) for step in (1, 3)]
        + [other, sibling]
        + [{"grp": 2 * ((z + hop) % SIDE) + k} for hop in range(1, SIDE) for k in range(2)]
    )
    heads_load.wait()

    def plane_slot(origin, at):
        return 2 * ((origin + SIDE - 1 - at) % SIDE)

    def heads_arrived(slot):
        remote(
            heads_t, heads_all.at[slot], heads_send.at[SLOTS - 1], heads_recv.at[slot], sibling
        ).wait_recv()

    def sibling_heads():
        slot = SLOTS - 1
        return remote(
            heads_t, heads_all.at[slot], heads_send.at[slot], heads_recv.at[slot], sibling
        )

    relays = ((1, 0), (-1, 0), (1, 1), (-1, 1), (1, 2), (-1, 2))

    def each_relay(wanted, act):
        for at, (step, away) in enumerate(relays):
            if away not in wanted:
                continue
            first, last = (away, SIDE - 2) if step > 0 else (1, SIDE - 1 - away)

            @pl.when(jnp.logical_and(z >= first, z <= last))
            def _():
                origin, target = z - step * away, z + step
                held = plane_slot(origin, z) + core
                slot = plane_slot(origin, target) + core
                act(
                    remote(
                        heads_all.at[held] if away else heads_t,
                        heads_all.at[slot],
                        heads_send.at[SLOTS + at],
                        heads_recv.at[slot],
                        {"grp": 2 * target + core},
                    ),
                    held,
                )

    def start_relay(relay, held):
        relay.start()

    def pass_relay(relay, held):
        heads_arrived(held)
        relay.start()

    def passed_heads(j):
        slot = 2 * j + core
        held = heads_all.at[slot]
        return remote(held, held, heads_send.at[slot], heads_recv.at[slot], sibling)

    def pass_heads(neighbours):
        for j in range(SIDE - 1):
            origin = (z + 1 + j) % SIDE
            near = jnp.logical_or(origin == z + 1, origin == z - 1)

            @pl.when(near if neighbours else jnp.logical_not(near))
            def _():
                @pl.when(jnp.logical_or(z == 0, z == SIDE - 1))
                def _():
                    heads_arrived(2 * j + core)

                passed_heads(j).start()

    def send_heads():
        heads_t[...] = heads[...].T
        each_relay((0,), start_relay)
        sibling_heads().start()


    def copy(u, h, step):
        chunk = 2 * u + h
        a, b = axes(h)
        right, left = (a + 1) % SIDE, (a + 3) % SIDE
        up, down = (b + 1) % SIDE, (b + 3) % SIDE
        low, high = pl.ds(0, HALF), pl.ds(HALF, HALF)
        far_a, far_b = (a + 2) % SIDE, (b + 2) % SIDE
        source, target, device = [
            lambda: (part.at[chunk, far_a, :, :, low], from1.at[chunk, 0], plane_device(h, right, b)),
            lambda: (part.at[chunk, far_a, :, :, high], from1.at[chunk, 1], plane_device(h, left, b)),
            lambda: (part.at[chunk, right], from2.at[chunk, 0], plane_device(h, right, b)),
            lambda: (part.at[chunk, left], from2.at[chunk, 1], plane_device(h, left, b)),
            lambda: (part.at[chunk, a, far_b, :, low], from3.at[chunk, 0], plane_device(h, a, up)),
            lambda: (part.at[chunk, a, far_b, :, high], from3.at[chunk, 1], plane_device(h, a, down)),
            lambda: (part.at[chunk, a, up], from4.at[chunk, 0], plane_device(h, a, up)),
            lambda: (part.at[chunk, a, down], from4.at[chunk, 1], plane_device(h, a, down)),
            lambda: (both.at[section, chunk], both.at[section, chunk], other),
        ][step]()
        return remote(source, target, send_sem.at[u], recv_sem.at[u, step // 2], device)

    reduce_sizes = [
        part.at[0, 0:2], part.at[0], part.at[0, 0, 0:2], part.at[0, 0], part.at[0, 0, 0:2]
    ]

    def arrive(u, stage):
        wait_arrived(reduce_sizes[stage], recv_sem.at[u, stage])

    def multiply(u):
        weight_copy(u, 0).wait()
        weight_copy(u, 1).wait()
        lower, upper = [
            jnp.dot(
                heads[...], weight_buf[:, pl.ds(start, UNIT_WIDE)],
                preferred_element_type=jnp.float32,
            )
            for start in (lower_start(u), upper_start(u))
        ]
        for h in range(2):
            cols = slice(h * WIDE, (h + 1) * WIDE)
            for i in range(SIDE * SIDE):
                rows = slice(OWN * i, OWN * (i + 1))
                a, b = (i // SIDE, i % SIDE) if h == 0 else (i % SIDE, i // SIDE)
                part[2 * u + h, a, b] = narrow(stacked(lower[rows, cols], upper[rows, cols]))
            copy(u, h, 0).start()
            copy(u, h, 1).start()

    def near_first(u):
        arrive(u, 0)
        for h in range(2):
            chunk = 2 * u + h
            a, b = axes(h)
            right, left = (a + 1) % SIDE, (a + 3) % SIDE
            part[chunk, right, :, :, :HALF] = narrow(
                wide(part[chunk, right, :, :, :HALF]) + wide(from1[chunk, 0])
            )
            copy(u, h, 2).start()
            part[chunk, left, :, :, HALF:] = narrow(
                wide(part[chunk, left, :, :, HALF:]) + wide(from1[chunk, 1])
            )
            copy(u, h, 3).start()

    def far_second(u):
        arrive(u, 1)
        for h in range(2):
            chunk = 2 * u + h
            a, b = axes(h)
            part[chunk, a] = narrow(
                wide(part[chunk, a]) + (wide(from2[chunk, 0]) + wide(from2[chunk, 1]))
            )
            copy(u, h, 4).start()
            copy(u, h, 5).start()

    def near_second(u):
        arrive(u, 2)
        for h in range(2):
            chunk = 2 * u + h
            a, b = axes(h)
            up, down = (b + 1) % SIDE, (b + 3) % SIDE
            part[chunk, a, up, :, :HALF] = narrow(
                wide(part[chunk, a, up, :, :HALF]) + wide(from3[chunk, 0])
            )
            copy(u, h, 6).start()
            part[chunk, a, down, :, HALF:] = narrow(
                wide(part[chunk, a, down, :, HALF:]) + wide(from3[chunk, 1])
            )
            copy(u, h, 7).start()

    def finish(u):
        arrive(u, 3)
        for h in range(2):
            chunk = 2 * u + h
            a, b = axes(h)
            total = wide(part[chunk, a, b]) + (wide(from4[chunk, 0]) + wide(from4[chunk, 1]))
            rows = stacked(
                wide(residual[:, pl.ds(lower_start(u, h), WIDE)]),
                wide(residual[:, pl.ds(upper_start(u, h), WIDE)]),
            )
            total = total + jnp.where(section == 0, rows, 0.0)
            both[section, chunk] = narrow(total)
            copy(u, h, 8).start()

    def within(value, count):
        return jnp.logical_and(value >= 0, value < count)

    stages = (multiply, near_first, far_second, near_second, finish)

    def reduce_turn(n, carry):
        for late, stage in enumerate(stages):

            @pl.when(within(n - late, UNITS))
            def _():
                stage(n - late)

        @pl.when(n == 1)
        def _():
            send_heads()

        @pl.when(n == UNITS - 1)
        def _():
            each_relay((1,), pass_relay)

        return carry

    residual_load.wait()
    gain_load.wait()
    lax.fori_loop(0, UNITS + len(stages) - 1, reduce_turn, 0)
    pass_heads(True)
    heads_total[...] = jnp.zeros_like(heads_total)
    grads_t[...] = jnp.zeros_like(grads_t)


    def gather_of(store, sends, recvs):
        half = store.shape[-1] // 2

        def gather(p, h, step):
            chunk = 2 * p + h
            a, b = axes(h)
            right, left = (a + 1) % SIDE, (a + 3) % SIDE
            up, down = (b + 1) % SIDE, (b + 3) % SIDE
            low, high = pl.ds(0, half), pl.ds(half, half)
            block, device = [
                lambda: (store.at[chunk, b, a], plane_device(h, right, b)),
                lambda: (store.at[chunk, b, a], plane_device(h, left, b)),
                lambda: (store.at[chunk, b, left, :, low], plane_device(h, right, b)),
                lambda: (store.at[chunk, b, right, :, high], plane_device(h, left, b)),
                lambda: (store.at[chunk, b], plane_device(h, a, up)),
                lambda: (store.at[chunk, b], plane_device(h, a, down)),
                lambda: (store.at[chunk, down, :, :, low], plane_device(h, a, up)),
                lambda: (store.at[chunk, up, :, :, high], plane_device(h, a, down)),
            ][step]()
            return remote(block, block, sends.at[p], recvs.at[p, step // 2], device)

        return gather

    gather_values = gather_of(values, value_send, value_recv)
    gather_columns = gather_of(columns, column_send, column_recv)

    gather_sizes = [values.at[0, 0], values.at[0, 0, 0:2], values.at[0], values.at[0, 0:2]]

    def exchanged(target, e):
        unit = 2 * (z % 2) + e if e < 2 else FAR_UNITS - 1
        a, b = x + core * (y - x), y + core * (x - y)
        return remote(
            exchange.at[target, e],
            columns.at[2 * unit + core, b, a],
            exchange_send.at[0],
            exchange_recv.at[unit],
            {"grp": target},
        )

    def gain_rows(t, h):
        return stacked(
            jnp.broadcast_to(gain[:, pl.ds(lower_start(t, h), WIDE)], (OWN, WIDE)),
            jnp.broadcast_to(gain[:, pl.ds(upper_start(t, h), WIDE)], (OWN, WIDE)),
        )

    zero = jnp.zeros((TALL, 128), jnp.float32)

    def row_mean(total):
        return both_halves(jnp.sum(total, axis=1, keepdims=True)) / (GROUPS * SHARD)

    def add_sums(t, total):
        arrive(t, 4)
        for h in range(2):
            total = total + lanes(wide(both[0, 2 * t + h]))
        return total

    mean = row_mean(lax.fori_loop(0, UNITS, add_sums, zero))

    def add_squares(t, total):
        for h in range(2):
            centred = wide(both[0, 2 * t + h]) - mean
            total = total + lanes(centred * centred)
        return total

    inv_scale = lax.rsqrt(row_mean(lax.fori_loop(0, UNITS, add_squares, zero)) + EPSILON)

    def add_means(t, totals):
        for h in range(2):
            unit = (wide(both[0, 2 * t + h]) - mean) * inv_scale
            scaled = gain_rows(t, h) * wide(both[1, 2 * t + h])
            totals = (totals[0] + lanes(scaled), totals[1] + lanes(scaled * unit))
        return totals

    sums = lax.fori_loop(0, UNITS, add_means, (zero, zero))
    mean_scaled, mean_product = row_mean(sums[0]), row_mean(sums[1])
    first_unit = SIDE * ((z // 2 + z % 2 + 1) % 2)

    def write(turn, carry):
        shard = (turn + first_unit // 2) % SIDE
        kept = []
        for v in range(2):
            t = 2 * shard + v
            for h in range(2):
                chunk = 2 * t + h
                a, b = axes(h)
                rows = gain_rows(t, h)
                unit = (wide(both[0, chunk]) - mean) * inv_scale
                d_normed = wide(both[1, chunk])
                grad = inv_scale * (rows * d_normed - mean_scaled - unit * mean_product)
                value = jnp.where(section == 0, grad, unit * rows)
                values[chunk, b, a] = narrow(value)
                gather_values(t, h, 0).start()
                gather_values(t, h, 1).start()
                kept.append(value)
                product = d_normed * unit
                for start, rows in (
                    (lower_start(t, h), slice(0, OWN)),
                    (upper_start(t, h), slice(OWN, TALL)),
                ):
                    own_grad[:, pl.ds(start, WIDE)] = narrow(grad[rows])
                    gain_own[0, :, pl.ds(start, WIDE)] = jnp.sum(product[rows], axis=0, keepdims=True)
        for target, rows in ((shard, slice(0, OWN)), (GROUPS - 1 - shard, slice(OWN, TALL))):
            for e, (first, second) in enumerate(((0, 2), (1, 3), (2, 3))):
                exchange[target, e] = narrow(stacked(kept[first][rows], kept[second][rows]))
                wanted = target // SIDE != z // 2 if e < 2 else target // 2 == next_plane

                @pl.when(wanted)
                def _():
                    exchanged(target, e).start()
        return carry

    lax.fori_loop(0, SIDE, write, 0)


    def near_copy(t, upper, target, slot):
        return remote(
            tokens.at[t, upper],
            from_near.at[slot],
            near_send.at[0],
            near_recv.at[slot],
            {"grp": target},
        )

    def split_blocks(store, chunk, h, put):
        for i in range(0, SIDE * SIDE, 2):
            pair = []
            for at in (i, i + 1):
                a, b = (at // SIDE, at % SIDE) if h == 0 else (at % SIDE, at // SIDE)
                pair.append(wide(store[chunk, b, a]))
            put(0, slice(OWN * i, OWN * (i + 2)), narrow(stacked(pair[0][:OWN], pair[1][:OWN])))
            put(1, slice(OWN * i, OWN * (i + 2)), narrow(stacked(pair[0][OWN:], pair[1][OWN:])))

    def add_grads(start, transposed_heads, token_rows):
        cols = pl.ds(start, token_rows.shape[1])
        grads_t[:, cols] += jnp.dot(
            transposed_heads, token_rows, preferred_element_type=jnp.float32
        )

    def store_grads(block):
        return pltpu.make_async_copy(
            grads.at[block * WIDE : (block + 1) * WIDE],
            grads_out.at[block * WIDE : (block + 1) * WIDE],
            output_sem.at[3 + block],
        )

    def finish_grads(blocks):
        for block in blocks:
            cols = slice(block * WIDE, (block + 1) * WIDE)
            grads[cols] = grad_scale * grads_t[:, cols].T
            store_grads(block).start()

    def use_values(t):
        for h in range(2):

            def put(upper, rows, block):
                tokens[t, upper, rows, h * WIDE : (h + 1) * WIDE] = block

            split_blocks(values, 2 * t + h, h, put)
        for upper, target in enumerate((t // 2, GROUPS - 1 - t // 2)):
            to_next = jnp.logical_and(target // 2 == next_plane, t % 2 == 0)
            for slot, wanted in ((t % 2, target == sibling_group), (2 + core, to_next)):

                @pl.when(wanted)
                def _():
                    near_copy(t, upper, target, slot).start()

        total = heads_total[...]
        for upper, start in enumerate((lower_start(t), upper_start(t))):
            total = total + lax.dot_general(
                tokens[t, upper], weight_buf[:, pl.ds(start, UNIT_WIDE)],
                (((1,), (1,)), ((), ())), preferred_element_type=jnp.float32,
            )
        heads_total[...] = total
        for upper, target in enumerate((t // 2, GROUPS - 1 - t // 2)):

            @pl.when(target == group)
            def _():
                add_grads(pl.multiple_of((t % 2) * UNIT_WIDE, UNIT_WIDE), heads_t[...], tokens[t, upper])

    def use_columns(p):
        last = p // (FAR_UNITS - 1)
        plane = (1 - last) * (2 * (1 - z // 2) + p // 2) + last * next_plane
        for h in range(2):

            def put(side, rows, block):
                column_tokens[h, rows, side * WIDE : (side + 1) * WIDE] = block

            split_blocks(columns, 2 * p + h, h, put)
        slot = plane_slot(plane, z)

        @pl.when(jnp.logical_and(p % 2 == 0, last == 0))
        def _():
            heads_arrived(slot + 1 - core)

        total = jnp.dot(
            heads_all[slot], column_tokens[0], preferred_element_type=jnp.float32
        ) + jnp.dot(heads_all[slot + 1], column_tokens[1], preferred_element_type=jnp.float32)
        for side in range(2):
            start = (1 - last) * (side * UNIT_WIDE + (p % 2) * WIDE) + last * (UNIT_WIDE + side * WIDE)
            cols = pl.ds(pl.multiple_of(start, WIDE), WIDE)
            grads_t[:, cols] += total[:, side * WIDE : (side + 1) * WIDE]

    def use_near(slot, heads_slot, start):
        wait_arrived(from_near.at[slot], near_recv.at[slot])
        add_grads(start, heads_all[heads_slot], from_near[slot])

    gain_partners = [
        {"tp": x * SIDE + y + 1 - 2 * (y % 2)},
        {"tp": x * SIDE + SIDE - 1 - y},
        {"tp": (x + 1 - 2 * (x % 2)) * SIDE + y},
        {"tp": (SIDE - 1 - x) * SIDE + y},
        sibling,
        {"grp": 2 * next_plane + core},
        {"grp": 2 * (SIDE - 1 - z) + core},
    ]

    def gain_copy(step):
        return remote(
            gain_own.at[step], gain_got.at[step], gain_send.at[step], gain_recv.at[step], gain_partners[step]
        )

    own_grad_store, heads_store, gain_store = [
        pltpu.make_async_copy(source, target, output_sem.at[at])
        for at, (source, target) in enumerate(
            ((own_grad, grad_out), (heads_done, heads_out), (gain_done, gain_out))
        )
    ]

    near_heads = plane_slot(next_plane, z)

    def value_unit(q):
        return (q + first_unit) % UNITS

    def gather_stage(q, stage):
        def pass_on(gather, recvs, p):
            wait_arrived(gather_sizes[stage], recvs.at[p, stage])
            if stage < 3:
                for h in range(2):
                    gather(p, h, 2 * stage + 2).start()
                    gather(p, h, 2 * stage + 3).start()

        @pl.when(within(q, UNITS))
        def _():
            pass_on(gather_values, value_recv, value_unit(q))

        @pl.when(within(q - UNITS, FAR_UNITS))
        def _():
            pass_on(gather_columns, column_recv, q - UNITS)

    def gather_turn(n, carry):
        @pl.when(n == 8)
        def _():
            pass_heads(False)

        for step in range(GAIN_STEPS + 1):

            @pl.when(n == step + 6)
            def _():
                if step > 0:
                    gain_copy(step - 1).wait_recv()
                    gain_own[step] = gain_own[step - 1] + gain_got[step - 1]
                if step < GAIN_STEPS:
                    gain_copy(step).start()
                else:
                    gain_done[...] = gain_own[GAIN_STEPS] * grad_scale
                    gain_store.start()

        @pl.when(within(n + 2 - UNITS, FAR_UNITS))
        def _():
            p = n + 2 - UNITS
            wait_arrived(gather_sizes[1], exchange_recv.at[p])
            for h in range(2):
                gather_columns(p, h, 0).start()
                gather_columns(p, h, 1).start()

        @pl.when(n == UNITS + FAR_UNITS + 7)
        def _():
            finish_grads((0, 1))

        gather_stage(n, 0)
        gather_stage(n - 6, 2)
        gather_stage(n - 3, 1)
        gather_stage(n - 8, 3)
        done = n - 8

        @pl.when(within(done, UNITS))
        def _():
            use_values(value_unit(done))

        @pl.when(done == UNITS)
        def _():
            heads_done[...] = narrow(heads_total[...])
            heads_store.start()
            heads_arrived(SLOTS - 1)
            use_near(0, SLOTS - 1, 0)
            use_near(1, SLOTS - 1, UNIT_WIDE)
            heads_arrived(near_heads + 1 - core)

        @pl.when(done == UNITS + 2)
        def _():
            for k in range(2):
                use_near(2 + k, near_heads + k, 0)

        @pl.when(within(done - UNITS, FAR_UNITS))
        def _():
            use_columns(done - UNITS)

        return carry

    own_grad_store.start()
    each_relay((2,), pass_relay)
    lax.fori_loop(0, UNITS + FAR_UNITS + 8, gather_turn, 0)
    finish_grads((2, 3))

    def reduce_sent(u, carry):
        wait_sent(part.at[0:2], send_sem.at[u])
        wait_sent(values.at[0:5, 0:3, 0:2], value_send.at[u])
        return carry

    def columns_sent(p, carry):
        wait_sent(values.at[0:5, 0:3, 0:2], column_send.at[p])
        return carry

    lax.fori_loop(0, UNITS, reduce_sent, 0)
    lax.fori_loop(0, FAR_UNITS, columns_sent, 0)
    wait_sent(exchange.at[0:5, 0:2], exchange_send.at[0])
    wait_sent(tokens.at[0:2], near_send.at[0])
    each_relay((0, 1, 2), lambda relay, held: relay.wait_send())
    for j in range(SIDE - 1):
        passed_heads(j).wait_send()
    sibling_heads().wait_send()
    for step in range(GAIN_STEPS):
        gain_copy(step).wait_send()
    for store in [own_grad_store, heads_store, gain_store] + [store_grads(i) for i in range(4)]:
        store.wait()


def deliver_kernel(*refs):
    results, outputs, held = refs[:4], refs[4:8], refs[8:12]
    load_sem, store_sem = refs[12:]
    pieces = [(1, pl.ds(block * WIDE, WIDE)) for block in range(SIDE)]
    pieces += [(at, pl.ds(0, results[at].shape[0])) for at in (0, 2, 3)]

    def copies(sources, targets, sems):
        return [
            pltpu.make_async_copy(sources[at].at[rows], targets[at].at[rows], sems.at[i])
            for i, (at, rows) in enumerate(pieces)
        ]

    loads, stores = copies(results, held, load_sem), copies(held, outputs, store_sem)
    for load in loads:
        load.start()
    for load, store in zip(loads, stores):
        load.wait()
        store.start()
    for store in stores:
        store.wait()


def delivered(results):
    hbm = pl.BlockSpec(memory_space=pl.ANY)
    return pl.pallas_call(
        deliver_kernel,
        out_shape=tuple(jax.ShapeDtypeStruct(result.shape, result.dtype) for result in results),
        in_specs=[hbm] * 4,
        out_specs=(hbm,) * 4,
        scratch_shapes=[pltpu.VMEM(result.shape, result.dtype) for result in results]
        + [pltpu.SemaphoreType.DMA((SIDE + 3,))] * 2,
        name="deliver",
    )(*results)


def fused(heads, weights, residual, gain):
    hbm = pl.BlockSpec(memory_space=pl.ANY)
    bf16, f32 = jnp.bfloat16, jnp.float32
    rows_dev, depth = heads.shape
    owned = weights.shape[1] // GROUPS
    dma = pltpu.SemaphoreType.DMA
    return pl.pallas_call(
        boundary_kernel,
        out_shape=(
            jax.ShapeDtypeStruct(heads.shape, bf16),
            jax.ShapeDtypeStruct((owned, depth), f32),
            jax.ShapeDtypeStruct(residual.shape, bf16),
            jax.ShapeDtypeStruct(gain.shape, f32),
        ),
        in_specs=[hbm] * 4,
        out_specs=(hbm,) * 4,
        scratch_shapes=[
            pltpu.VMEM(heads.shape, bf16),
            pltpu.VMEM(residual.shape, bf16),
            pltpu.VMEM(gain.shape, f32),
            pltpu.VMEM(heads.shape, bf16),
            pltpu.VMEM((owned, depth), f32),
            pltpu.VMEM(residual.shape, bf16),
            pltpu.VMEM(gain.shape, f32),
            pltpu.VMEM((depth, rows_dev), bf16),
            pltpu.VMEM((depth, owned), f32),
            pltpu.VMEM(weights.shape, bf16),
            pltpu.VMEM((CHUNKS, SIDE, SIDE, TALL, WIDE), bf16),
            pltpu.VMEM((CHUNKS, 2, SIDE, TALL, HALF), bf16),
            pltpu.VMEM((CHUNKS, 2, SIDE, TALL, WIDE), bf16),
            pltpu.VMEM((CHUNKS, 2, TALL, HALF), bf16),
            pltpu.VMEM((CHUNKS, 2, TALL, WIDE), bf16),
            pltpu.VMEM((2, CHUNKS, TALL, WIDE), bf16),
            pltpu.VMEM((CHUNKS, SIDE, SIDE, TALL, WIDE), bf16),
            pltpu.VMEM((FAR_CHUNKS, SIDE, SIDE, TALL, WIDE), bf16),
            pltpu.VMEM((GROUPS, 3, TALL, WIDE), bf16),
            pltpu.VMEM((UNITS, 2, rows_dev, UNIT_WIDE), bf16),
            pltpu.VMEM((2, rows_dev, UNIT_WIDE), bf16),
            pltpu.VMEM((4, rows_dev, UNIT_WIDE), bf16),
            pltpu.VMEM((SLOTS, depth, rows_dev), bf16),
            pltpu.VMEM((rows_dev, depth), f32),
            pltpu.VMEM((GAIN_STEPS + 1,) + gain.shape, f32),
            pltpu.VMEM((GAIN_STEPS,) + gain.shape, f32),
            dma((3,)),
            dma((7,)),
            dma((UNITS, 2)),
            dma((UNITS,)),
            dma((UNITS, 5)),
            dma((UNITS,)),
            dma((UNITS, 4)),
            dma((FAR_UNITS,)),
            dma((FAR_UNITS, 4)),
            dma((1,)),
            dma((FAR_UNITS,)),
            dma((SLOTS + 6,)),
            dma((SLOTS,)),
            dma((1,)),
            dma((4,)),
            dma((GAIN_STEPS,)),
            dma((GAIN_STEPS,)),
        ],
        compiler_params=pltpu.CompilerParams(
            collective_id=0, has_side_effects=True, vmem_limit_bytes=62 * 1024 * 1024
        ),
        name="boundary",
    )(heads, weights, residual, gain)


def per_device(heads_in, weights, residual, norm_gain):
    heads_out, weight_grad, boundary_grad, gain_grad = delivered(
        fused(heads_in[0], weights[0], residual, norm_gain[None])
    )
    return (heads_out[None], weight_grad[None], boundary_grad, gain_grad[0])


def solution(mesh):
    placed = (P("section", "grp", "tp"), P("section", "tp", None), P(("grp", "tp"), None), P())
    return jax.shard_map(
        per_device,
        mesh=mesh,
        in_specs=placed,
        out_specs=(
            P("section", "grp", "tp"),
            P("section", "grp", "tp"),
            P(("grp", "tp"), None),
            P(),
        ),
        check_vma=False,
    )
```
